32 devices in a mesh: users: 16 (over z, y, core), items: 2 (over x).
Axes of the slice: x: 2, y: 2, z: 4, core: 2. Of those that a mesh axis runs over, the one named last changes fastest.
Arguments:
- interactions: bfloat16 [3, 20480, 512], P(None, 'users', 'items')
- matchings: int32 [3], replicated, may hold values from 1 to 15, as said below
- user_shape: bfloat16 [20480, 128], P('users'), may hold values from 0.5 to 2
- item_shape: bfloat16 [8192, 128], P(('users', 'items')), may hold values from 0.5 to 2
Outputs:
- user_log: bfloat16 [20480, 128], P('users')
- item_log: bfloat16 [8192, 128], P(('users', 'items'))
The draws below stay inside these ranges and needn't reach their ends.
Inputs may be any that keep to these rules, and one draw needn't show every extreme that they name: matchings[0] and matchings[1] are two different values of 1 to 14, and the last matching is 15.
All inputs are finite; a program needn't handle non-finite values.
Results may differ from the reference program's by a relative error of at most 0.0012.
The reference program's roundings to bfloat16 on the way (of `user_exp` and `ratios`) count: a program that leaves them out, or rounds other values in their place, can miss the bound.
Values sent between devices are 32-bit elements; how exact they have to be, the bound alone decides.
No kernel may reach another device: no remote copies, remote signals or barrier semaphores. Data moves between devices by JAX's collectives and lax.ppermute only.
A program may use at most 64 MiB of HBM per device.

```python
import math
import jax
import jax.numpy as jnp
from jax import lax

K = 128
U_DEV = 1280
I_BLK = 256
STRATA = 3
USERS = 20480
COLS = 512
ITEMS = 8192
N_USERS = 16
N_ITEMS = 2


def draw_interactions(key, part):
    count_key = jax.random.fold_in(key, 11)
    heavy_key = jax.random.fold_in(key, 12)
    shape = (STRATA, USERS, COLS)
    counts = jax.random.randint(count_key, shape, 0, 4).astype(jnp.float32)
    heavy = jnp.exp(jax.random.uniform(heavy_key, (1, USERS, 1), jnp.float32, 0.0, math.log(8.0)))
    return (counts * heavy).astype(jnp.bfloat16)


def draw_matchings(key, part):
    key = jax.random.fold_in(key, 21)
    order = jax.random.permutation(key, N_USERS - 2).astype(jnp.int32) + 1
    first_two = order[:2]
    middle = jax.random.randint(jax.random.fold_in(key, 22), (STRATA - 3,), 1, N_USERS).astype(jnp.int32)
    last = jnp.full((1,), N_USERS - 1, jnp.int32)
    return jnp.concatenate([first_two, middle, last]).astype(jnp.int32)


def block_scale(stream_key, shape, shards, low, largest):
    factor_of = 1.0
    for axis_at, shards_of in shards:
        steps = jax.random.uniform(jax.random.fold_in(jax.random.fold_in(stream_key, 6), axis_at), (shards_of,), jnp.float32, low / len(shards), largest / len(shards))
        factor_of = factor_of * jnp.repeat(jnp.exp(steps), shape[axis_at] // shards_of).reshape((-1,) + (1,) * (len(shape) - 1 - axis_at))
    return factor_of


def setup_inputs(seed: int = 0) -> dict:
    key_list = jax.random.split(jax.random.key(seed), 5)
    return {
        "interactions": draw_interactions(jax.random.fold_in(key_list[4], 71), 0),
        "matchings": draw_matchings(jax.random.fold_in(key_list[4], 71), 0),
        "user_shape": jnp.clip(jnp.exp(math.log(2.0) - 1.3862944 * jax.random.uniform(key_list[2], (USERS, K), jnp.float32) ** block_scale(key_list[2], (USERS, K), ((0, 16),), -0.2, 0.2)), 0.5, 2.0).astype(jnp.bfloat16),
        "item_shape": jnp.clip(jnp.exp(math.log(2.0) - 1.3862944 * jax.random.uniform(key_list[3], (ITEMS, K), jnp.float32) ** block_scale(key_list[3], (ITEMS, K), ((0, 32),), -0.2, 0.2)), 0.5, 2.0).astype(jnp.bfloat16),
    }


def expect(shp, rte):
    return lax.digamma(shp) - jnp.log(rte), shp / rte


def per_block(operands):
    user_exp, counts, item_exp = operands
    user_f = user_exp.astype(jnp.float32)
    item_f = item_exp.astype(jnp.float32)
    denominator = jnp.einsum("uk,jik->uji", user_f, item_f)
    ratios = (counts.astype(jnp.float32) / denominator).astype(jnp.bfloat16).astype(jnp.float32)
    user_stat = user_f * jnp.einsum("uji,jik->uk", ratios, item_f)
    item_stat = item_f * jnp.einsum("uji,uk->jik", ratios, user_f)
    return user_stat, item_stat


def reference(interactions, matchings, user_shape, item_shape):
    factor_users = float(N_USERS)
    user_shp = user_shape.astype(jnp.float32).reshape(N_USERS, U_DEV, K)
    user_rte = jnp.ones_like(user_shp)
    item_shp = item_shape.astype(jnp.float32).reshape(N_USERS, N_ITEMS, I_BLK, K)
    item_rte = jnp.ones_like(item_shp)
    for stratum in range(STRATA):
        partner = jnp.bitwise_xor(jnp.arange(N_USERS, dtype=jnp.int32), matchings[stratum].astype(jnp.int32))
        user_elog, user_mean = expect(user_shp, user_rte)
        item_elog, item_mean = expect(item_shp, item_rte)
        user_exp = jnp.exp(user_elog).astype(jnp.bfloat16)
        item_exp = jnp.exp(item_elog).astype(jnp.bfloat16)
        counts = interactions[stratum].reshape(N_USERS, U_DEV, N_ITEMS, I_BLK)
        user_stat, item_stat = lax.map(per_block, (user_exp, counts, item_exp[partner]))
        beta_cols = jnp.sum(item_mean[partner], axis=(1, 2))
        theta_cols = jnp.sum(user_mean, axis=1)
        new_user_shp = 0.5 * user_shp + 0.5 * (0.3 + factor_users * user_stat)
        new_user_rte = 0.5 * user_rte + 0.5 * (0.3 + factor_users * beta_cols[:, None, :])
        item_shp = 0.5 * item_shp + 0.5 * (0.3 + factor_users * item_stat[partner])
        item_rte = 0.5 * item_rte + 0.5 * (0.3 + factor_users * theta_cols[partner][:, None, None, :])
        user_shp, user_rte = new_user_shp, new_user_rte
    user_log = (lax.digamma(user_shp) - jnp.log(user_rte)).reshape(USERS, K).astype(jnp.bfloat16)
    item_log = (lax.digamma(item_shp) - jnp.log(item_rte)).reshape(ITEMS, K).astype(jnp.bfloat16)
    return user_log, item_log
```

```python
import functools

import jax
import jax.numpy as jnp
from jax import lax
from jax.experimental import pallas as pl
from jax.experimental.pallas import tpu as pltpu
from jax.sharding import PartitionSpec as P

STRATA = 3
TILE = 128
F32 = jnp.float32
BF16 = jnp.bfloat16


def chunk_rows(rows):
    half = rows // 2 // TILE * TILE
    return [half, rows - half]


def psi_parts(x):
    small = x < 8.0
    w = jnp.where(small, x + 3.5, x - 0.5)
    q = x * (x + 3.0)
    q2 = q + 2.0
    shift = (2.0 * x + 3.0) * (q + q2) / (q * q2)
    s = 1.0 / (w * w)
    g = s * (1.0 / 24.0 - s * (7.0 / 960.0 - s * (31.0 / 8064.0 - s * (127.0 / 30720.0))))
    return w, g - jnp.where(small, shift, 0.0)


def psi_any(x):
    mirrored = x < 0.5
    w, g = psi_parts(jnp.where(mirrored, 1.0 - x, x))
    value = jnp.log(w) + g
    t = x - jnp.floor(x + 0.5)
    u = 3.14159265358979 * t
    v = u * u
    sin = 1.0 / 6227020800.0
    for c in (-1.0 / 39916800.0, 1.0 / 362880.0, -1.0 / 5040.0, 1.0 / 120.0, -1.0 / 6.0, 1.0):
        sin = sin * v + c
    cos = -1.0 / 87178291200.0
    for c in (1.0 / 479001600.0, -1.0 / 3628800.0, 1.0 / 40320.0, -1.0 / 720.0, 1.0 / 24.0, -0.5, 1.0):
        cos = cos * v + c
    value = jnp.where(mirrored, value - 3.14159265358979 * cos / (sin * u), value)
    return jnp.where((x <= 0.0) & (x == jnp.floor(x)), jnp.nan, value)


LOWEST = 0.01


def plain(low_shp, rte):
    return (jnp.min(low_shp) >= LOWEST) & (jnp.min(rte) >= LOWEST)


def folded(x):
    return x.reshape(x.shape[0] // 8, 8, x.shape[1])


def tiles(rows):
    step = TILE if rows % TILE == 0 else rows
    return [(at, step) for at in range(0, rows, step)]


def expect_exp(shp_ref, rows, rte, out_ref):
    inv = 1.0 / rte
    low = None
    total = None
    for at, step in tiles(rows):
        x = folded(shp_ref[at:at + step, :])
        w, g = psi_parts(x)
        value = (w * inv[None]) * jnp.exp(g)
        out_ref[at:at + step, :] = value.reshape(step, -1).astype(BF16)
        part = jnp.sum(x * inv[None], axis=0)
        part_low = jnp.min(x, axis=0)
        total = part if total is None else total + part
        low = part_low if low is None else jnp.minimum(low, part_low)

    @pl.when(jnp.logical_not(plain(low, rte)))
    def _():
        for at, step in tiles(rows):
            x = folded(shp_ref[at:at + step, :])
            value = jnp.exp(psi_any(x) - jnp.log(rte)[None])
            out_ref[at:at + step, :] = value.reshape(step, -1).astype(BF16)

    return total


def expect_log(shp_ref, rows, rte, out_ref):
    log_rte = jnp.log(rte)
    low = None
    for at, step in tiles(rows):
        x = folded(shp_ref[at:at + step, :])
        w, g = psi_parts(x)
        value = (jnp.log(w) - log_rte[None]) + g
        out_ref[at:at + step, :] = value.reshape(step, -1).astype(BF16)
        part_low = jnp.min(x, axis=0)
        low = part_low if low is None else jnp.minimum(low, part_low)

    @pl.when(jnp.logical_not(plain(low, rte)))
    def _():
        for at, step in tiles(rows):
            x = folded(shp_ref[at:at + step, :])
            value = psi_any(x) - log_rte[None]
            out_ref[at:at + step, :] = value.reshape(step, -1).astype(BF16)


def row_sum(x):
    return jnp.broadcast_to(jnp.sum(x, axis=0, keepdims=True), x.shape)


def stratum_kernel(names, *refs, stratum, at, rows, items, factor, first, last):
    ref = dict(zip(names, refs))
    counts = ref["counts"]
    weights = pltpu.make_async_copy(
        ref["interactions"].at[stratum, pl.ds(at, rows), :], counts, ref["sems"].at[0])
    weights.start()
    shp_new, upart, uexp = ref["shp_new"], ref["upart"], ref["uexp"]
    extra = 8 if first else 0

    if stratum == 0:
        start = pltpu.make_async_copy(
            ref["user_shape"].at[pl.ds(at, rows), :], ref["shape_in"], ref["sems"].at[1])
        start.start()
        start.wait()
        rte = jnp.ones((8, shp_new.shape[1]), F32)
        for t, step in tiles(rows):
            shp_new[t:t + step, :] = ref["shape_in"][t:t + step, :].astype(F32)
    else:
        if first:
            beta = row_sum(ref["acc"][0:8, :] + ref["recv"][0:8, :])
            rte = 0.5 * ref["rte_old"][...] + 0.5 * (0.3 + factor * beta)
        else:
            rte = ref["rte"][...]
        for t, step in tiles(rows):
            stat = ref["acc"][extra + t:extra + t + step, :] + ref["recv"][extra + t:extra + t + step, :]
            shp_new[t:t + step, :] = 0.5 * ref["shp_old"][t:t + step, :] + 0.5 * (0.3 + factor * stat)
    if first and stratum > 0:
        ref["rte_new"][...] = rte
    theta = expect_exp(shp_new, rows, rte, uexp)

    if first:
        if stratum == 0:
            item_rte = jnp.ones((8, shp_new.shape[1]), F32)
        else:
            item_rte = ref["item"][items:items + 8, :]
        upart[0:8, :] = expect_exp(ref["item"], items, item_rte, ref["item_exp_new"])
        item_exp = ref["item_exp_new"][...]
    else:
        item_exp = ref["item_exp"][...]
        theta = theta + ref["theta"][...]

    weights.wait()
    for t, step in tiles(rows):
        u = uexp[t:t + step, :]
        denominator = lax.dot_general(u, item_exp, (((1,), (1,)), ((), ())), preferred_element_type=F32)
        ratios = (counts[t:t + step, :].astype(F32) / denominator).astype(BF16)
        counts[t:t + step, :] = ratios
        upart[extra + t:extra + t + step, :] = u.astype(F32) * jnp.dot(
            ratios, item_exp, preferred_element_type=F32)
    istat = lax.dot_general(counts[...], uexp[...], (((0,), (0,)), ((), ())), preferred_element_type=F32)
    if not first:
        istat = istat + ref["istat"][...]
    if last:
        if stratum == 0:
            item_rte = jnp.ones((8, shp_new.shape[1]), F32)
        else:
            item_rte = ref["item"][items:items + 8, :]
        ref["item_new"][0:items, :] = 0.5 * ref["item"][0:items, :] + 0.5 * (
            0.3 + factor * (item_exp.astype(F32) * istat))
        ref["item_new"][items:items + 8, :] = 0.5 * item_rte + 0.5 * (0.3 + factor * row_sum(theta))
    else:
        ref["istat_new"][...] = istat
        ref["theta_new"][...] = theta


def stratum_call(stratum, at, rows, items, depth, factor, first, last, operands):
    extra = 8 if first else 0
    outs = {
        "shp_new": ((rows, depth), F32),
        "upart": ((rows + extra, depth), F32),
    }
    if first and stratum > 0:
        outs["rte_new"] = ((8, depth), F32)
    if first:
        outs["item_exp_new"] = ((items, depth), BF16)
    if last:
        outs["item_new"] = ((items + 8, depth), F32)
    else:
        outs["istat_new"] = ((items, depth), F32)
        outs["theta_new"] = ((8, depth), F32)
    scratch = {
        "counts": pltpu.VMEM((rows, items), BF16),
        "uexp": pltpu.VMEM((rows, depth), BF16),
        "sems": pltpu.SemaphoreType.DMA((2,)),
    }
    if stratum == 0:
        scratch["shape_in"] = pltpu.VMEM((rows, depth), BF16)
    in_specs = [
        pl.BlockSpec(memory_space=pl.ANY if name in ("interactions", "user_shape") else pltpu.VMEM)
        for name in operands]
    names = list(operands) + list(outs) + list(scratch)
    kernel = functools.partial(
        stratum_kernel, names, stratum=stratum, at=at, rows=rows, items=items,
        factor=factor, first=first, last=last)
    results = pl.pallas_call(
        kernel,
        out_shape=[jax.ShapeDtypeStruct(*spec) for spec in outs.values()],
        in_specs=in_specs,
        out_specs=[pl.BlockSpec(memory_space=pltpu.VMEM)] * len(outs),
        scratch_shapes=list(scratch.values()),
        compiler_params=pltpu.CompilerParams(vmem_limit_bytes=32 * 2**20),
        cost_estimate=pl.CostEstimate(
            flops=6 * rows * items * depth, bytes_accessed=rows * (items * 2 + depth * 16),
            transcendentals=rows * (depth + items)),
        name=f"stratum{stratum}_at{at}",
    )(*operands.values())
    return dict(zip(outs, results))


def user_log_kernel(*refs, at, rows, factor, first, filled):
    acc, recv, shp_old, rte_in = refs[:4]
    rest = refs[5:] if filled else refs[4:]
    if first:
        out, rte_out, shp, block, sem = rest
        beta = row_sum(acc[0:8, :] + recv[0:8, :])
        rte = 0.5 * rte_in[...] + 0.5 * (0.3 + factor * beta)
        rte_out[...] = rte
    else:
        out, shp, block, sem = rest
        rte = rte_in[...]
    extra = 8 if first else 0
    for t, step in tiles(rows):
        stat = acc[extra + t:extra + t + step, :] + recv[extra + t:extra + t + step, :]
        shp[t:t + step, :] = 0.5 * shp_old[t:t + step, :] + 0.5 * (0.3 + factor * stat)
    expect_log(shp, rows, rte, block)
    copy = pltpu.make_async_copy(block, out.at[pl.ds(at, rows), :], sem)
    copy.start()
    copy.wait()


def user_log_call(at, rows, total, depth, factor, first, operands, filled):
    vmem = pl.BlockSpec(memory_space=pltpu.VMEM)
    anywhere = pl.BlockSpec(memory_space=pl.ANY)
    out_shape = [jax.ShapeDtypeStruct((total, depth), BF16)]
    out_specs = [anywhere]
    if first:
        out_shape.append(jax.ShapeDtypeStruct((8, depth), F32))
        out_specs.append(vmem)
    operands = list(operands)
    in_specs = [vmem] * 4
    if filled is not None:
        operands.append(filled)
        in_specs.append(anywhere)
    return pl.pallas_call(
        functools.partial(user_log_kernel, at=at, rows=rows, factor=factor, first=first,
                          filled=filled is not None),
        out_shape=out_shape,
        in_specs=in_specs,
        out_specs=out_specs,
        input_output_aliases={} if filled is None else {4: 0},
        scratch_shapes=[pltpu.VMEM((rows, depth), F32), pltpu.VMEM((rows, depth), BF16),
                        pltpu.SemaphoreType.DMA],
        compiler_params=pltpu.CompilerParams(vmem_limit_bytes=32 * 2**20),
        cost_estimate=pl.CostEstimate(
            flops=40 * rows * depth, bytes_accessed=rows * depth * 14, transcendentals=rows * depth),
        name=f"user_log_at{at}",
    )(*operands)


def item_log_kernel(item, out, *, items):
    expect_log(item, items, item[items:items + 8, :], out)


def item_log_call(item, items, depth):
    return pl.pallas_call(
        functools.partial(item_log_kernel, items=items),
        out_shape=jax.ShapeDtypeStruct((items, depth), BF16),
        compiler_params=pltpu.CompilerParams(vmem_limit_bytes=32 * 2**20),
        cost_estimate=pl.CostEstimate(
            flops=40 * items * depth, bytes_accessed=items * depth * 6, transcendentals=items * depth),
        name="item_log",
    )(item)


def swapped(value, axis, mask):
    return lax.ppermute(value, axis, [(a, a ^ mask) for a in range(lax.axis_size(axis))])


def moved(value, mask):
    choices = [functools.partial(swapped, axis="users", mask=m) for m in range(1, lax.axis_size("users"))]
    return lax.switch(mask - 1, choices, value)


def exchanged(value):
    size = lax.axis_size("items")
    if size == 1:
        return value, jnp.zeros_like(value)
    mask = 1
    while mask * 2 < size:
        value = value + swapped(value, "items", mask)
        mask *= 2
    return value, swapped(value, "items", mask)


def per_device(interactions, matchings, user_shape, item_shape):
    group = lax.axis_size("users")
    factor = float(group)
    users, depth = user_shape.shape
    items = item_shape.shape[0]
    sizes = chunk_rows(users)
    starts = [sum(sizes[:i]) for i in range(len(sizes))]
    count = len(sizes)

    item = moved(item_shape.astype(F32), matchings[0])
    rte = jnp.ones((8, depth), F32)
    shp = [None] * count
    sums = [None] * count
    for stratum in range(STRATA):
        carried = {}
        for i, (at, rows) in enumerate(zip(starts, sizes)):
            first, last = i == 0, i == count - 1
            operands = {"interactions": interactions}
            if stratum == 0:
                operands["user_shape"] = user_shape
            else:
                operands["acc"], operands["recv"] = sums[i]
                operands["shp_old"] = shp[i]
                operands["rte_old" if first else "rte"] = rte
            if first or last:
                operands["item"] = item
            if not first:
                operands["item_exp"] = carried["item_exp"]
                operands["theta"] = carried["theta"]
                operands["istat"] = carried["istat"]
            out = stratum_call(stratum, at, rows, items, depth, factor, first, last, operands)
            shp[i] = out["shp_new"]
            sums[i] = exchanged(out["upart"])
            if first:
                rte = out.get("rte_new", rte)
                carried["item_exp"] = out["item_exp_new"]
            if last:
                item_new = out["item_new"]
            else:
                carried["theta"] = out["theta_new"]
                carried["istat"] = out["istat_new"]
        if stratum + 1 < STRATA - 1:
            item = moved(item_new, matchings[stratum] ^ matchings[stratum + 1])
        elif stratum + 1 < STRATA:
            item = moved(item_new, matchings[stratum] ^ (group - 1))
        else:
            item = swapped(item_new, "users", group - 1)
    item_log = item_log_call(item, items, depth)
    user_log = None
    for i, (at, rows) in enumerate(zip(starts, sizes)):
        out = user_log_call(at, rows, users, depth, factor, i == 0, (*sums[i], shp[i], rte), user_log)
        user_log = out[0]
        if i == 0:
            rte = out[1]
    return user_log, item_log


def solution(mesh):
    placed = (P(None, "users", "items"), P(), P("users", None), P(("users", "items"), None))
    return jax.shard_map(
        per_device,
        mesh=mesh,
        in_specs=placed,
        out_specs=(P("users", None), P(("users", "items"), None)),
        check_vma=False,
    )
```

```python
import functools

import jax
import jax.numpy as jnp
from jax import lax
from jax.experimental import pallas as pl
from jax.experimental.pallas import tpu as pltpu
from jax.sharding import PartitionSpec as P

STRATA = 3
TILE = 128
F32 = jnp.float32
BF16 = jnp.bfloat16


def chunk_rows(rows):
    half = rows // 2 // TILE * TILE
    return [half, rows - half]


def psi_parts(x):
    small = x < 8.0
    w = jnp.where(small, x + 3.5, x - 0.5)
    q = x * (x + 3.0)
    q2 = q + 2.0
    bounded = jnp.minimum(w, 1e9)
    square = bounded * bounded
    steps = jnp.where(small, q * q2, 1.0)
    r = 1.0 / (square * steps)
    s = r * steps
    shift = (2.0 * x + 3.0) * (q + q2) * (r * square)
    g = s * (1.0 / 24.0 - s * (7.0 / 960.0 - s * (31.0 / 8064.0 - s * (127.0 / 30720.0))))
    return w, g - jnp.where(small, shift, 0.0)


def psi_any(x):
    mirrored = x < 0.5
    w, g = psi_parts(jnp.where(mirrored, 1.0 - x, x))
    value = jnp.log(w) + g
    t = x - jnp.floor(x + 0.5)
    u = 3.14159265358979 * t
    v = u * u
    sin = 1.0 / 6227020800.0
    for c in (-1.0 / 39916800.0, 1.0 / 362880.0, -1.0 / 5040.0, 1.0 / 120.0, -1.0 / 6.0, 1.0):
        sin = sin * v + c
    cos = -1.0 / 87178291200.0
    for c in (1.0 / 479001600.0, -1.0 / 3628800.0, 1.0 / 40320.0, -1.0 / 720.0, 1.0 / 24.0, -0.5, 1.0):
        cos = cos * v + c
    value = jnp.where(mirrored, value - 3.14159265358979 * cos / (sin * u), value)
    return jnp.where((x <= 0.0) & (x == jnp.floor(x)), jnp.nan, value)


LOWEST = 0.01


def above(low):
    return jnp.min(low) >= LOWEST


def folded(x):
    return x.reshape(x.shape[0] // 8, 8, x.shape[1])


def tiles(rows):
    step = TILE if rows % TILE == 0 else rows
    return [(at, step) for at in range(0, rows, step)]


def exp_tile(x, rte, general):
    shape = x.shape
    x = folded(x)
    if general:
        value = psi_any(x)
        if rte is not None:
            value = value - jnp.log(rte)[None]
        value = jnp.exp(value)
    else:
        w, g = psi_parts(x)
        value = w if rte is None else w * (1.0 / rte)[None]
        value = value * jnp.exp(g)
    mean = x if rte is None else x * (1.0 / rte)[None]
    return value.reshape(shape).astype(BF16), jnp.sum(mean, axis=0), jnp.min(x, axis=0)


def log_tile(x, rte, general):
    shape = x.shape
    x = folded(x)
    if general:
        value = psi_any(x) - jnp.log(rte)[None]
    else:
        w, g = psi_parts(x)
        value = (jnp.log(w) - jnp.log(rte)[None]) + g
    return value.reshape(shape).astype(BF16), jnp.min(x, axis=0)


def row_sum(x):
    return jnp.broadcast_to(jnp.sum(x, axis=0, keepdims=True), x.shape)


VMEM_SPEC = pl.BlockSpec(memory_space=pltpu.VMEM)
SMEM_SPEC = pl.BlockSpec(memory_space=pltpu.SMEM)
HBM_SPEC = pl.BlockSpec(memory_space=pltpu.HBM)
PARAMS = pltpu.CompilerParams(vmem_limit_bytes=24 * 2**20)


def prepare_kernel(matchings, item_shape, item, *choices, last):
    item[...] = item_shape[...].astype(F32)
    choices[0][0] = matchings[0] - 1
    for stratum in range(1, STRATA - 1):
        choices[stratum][0] = jnp.bitwise_xor(matchings[stratum - 1], matchings[stratum]) - 1
    choices[STRATA - 1][0] = jnp.bitwise_xor(matchings[STRATA - 2], last) - 1


def prepare_call(matchings, item_shape, last):
    out = pl.pallas_call(
        functools.partial(prepare_kernel, last=last),
        out_shape=[jax.ShapeDtypeStruct(item_shape.shape, F32)]
        + [jax.ShapeDtypeStruct((1,), jnp.int32)] * STRATA,
        in_specs=[SMEM_SPEC, VMEM_SPEC],
        out_specs=[VMEM_SPEC] + [SMEM_SPEC] * STRATA,
        compiler_params=PARAMS,
        name="prepare",
    )(matchings, item_shape)
    return out[0], [choice[0] for choice in out[1:]]


def start_kernel(shape, uexp, theta):
    rows, depth = shape.shape

    def body(general):
        def step(i, carry):
            total, low = carry
            place = pl.ds(pl.multiple_of(i * TILE, TILE), TILE)
            value, part, part_low = exp_tile(shape[place, :].astype(F32), None, general)
            uexp[place, :] = value
            return total + part, jnp.minimum(low, part_low)

        total, low = lax.fori_loop(
            0, rows // TILE, step, (jnp.zeros((8, depth), F32), jnp.ones((8, depth), F32)))
        theta[...] = total
        return low

    low = body(False)

    @pl.when(jnp.logical_not(above(low)))
    def _():
        body(True)


def start_call(user_shape):
    rows, depth = user_shape.shape
    return pl.pallas_call(
        start_kernel,
        out_shape=[jax.ShapeDtypeStruct((rows, depth), BF16), jax.ShapeDtypeStruct((8, depth), F32)],
        in_specs=[VMEM_SPEC],
        out_specs=[VMEM_SPEC] * 2,
        compiler_params=PARAMS,
        cost_estimate=pl.CostEstimate(
            flops=40 * rows * depth, bytes_accessed=rows * depth * 4, transcendentals=2 * rows * depth),
        name="user_start",
    )(user_shape)


def stratum_kernel(names, *refs, stratum, at, rows, items, factor, first, last):
    ref = dict(zip(names, refs))
    sems = ref["sems"]
    copies = {}

    def fetch(name, source, target):
        copies[name] = pltpu.make_async_copy(source, target, sems.at[len(copies)])
        copies[name].start()

    place = pl.ds(at, rows)
    if first or last:
        fetch("item", ref["item"], ref["item_in"])
    if stratum == 0:
        fetch("uexp", ref["uexp_all"].at[place, :], ref["uexp"])
    if stratum == 1:
        fetch("shape", ref["user_shape"].at[place, :], ref["shape_in"])
    fetch("counts", ref["interactions"].at[stratum, place, :], ref["counts"])
    upart, uexp, counts, ratios = ref["upart"], ref["uexp"], ref["counts"], ref["ratios"]
    extra = 8 if first else 0

    def wait(name, general):
        if not general:
            copies[name].wait()

    def body(general):
        lows = []
        theta = None
        if stratum > 0:
            if first:
                beta = row_sum(ref["acc"][0:8, :] + ref["recv"][0:8, :])
                old = 1.0 if stratum == 1 else ref["rte_old"][...]
                rte = 0.5 * old + 0.5 * (0.3 + factor * beta)
                ref["rte_new"][...] = rte
            else:
                rte = ref["rte"][...]
            lows.append(rte)
            if stratum == 1:
                wait("shape", general)
            for t, step in tiles(rows):
                old = ref["shape_in"][t:t + step, :].astype(F32) if stratum == 1 else ref["shp_old"][t:t + step, :]
                stat = ref["acc"][extra + t:extra + t + step, :] + ref["recv"][extra + t:extra + t + step, :]
                shp = 0.5 * old + 0.5 * (0.3 + factor * stat)
                ref["shp_new"][t:t + step, :] = shp
                value, part, low = exp_tile(shp, rte, general)
                uexp[t:t + step, :] = value
                theta = part if theta is None else theta + part
                lows.append(low)
            if not first:
                theta = theta + ref["theta"][...]
        elif last:
            theta = ref["theta"][...]

        if first or last:
            wait("item", general)
            item = ref["item_in"]
            item_rte = None if stratum == 0 else item[items:items + 8, :]
        if first:
            value, sums, low = exp_tile(item[0:items, :], item_rte, general)
            ref["item_exp_new"][...] = value
            upart[0:8, :] = sums
            lows.append(low)
            if item_rte is not None:
                lows.append(item_rte)
            item_exp = value
        else:
            item_exp = ref["item_exp"][...]

        if stratum == 0:
            wait("uexp", general)
        wait("counts", general)
        for t, step in tiles(rows):
            u = uexp[t:t + step, :]
            denominator = lax.dot_general(u, item_exp, (((1,), (1,)), ((), ())), preferred_element_type=F32)
            ratio = (counts[t:t + step, :].astype(F32) / denominator).astype(BF16)
            ratios[t:t + step, :] = ratio
            upart[extra + t:extra + t + step, :] = u.astype(F32) * jnp.dot(
                ratio, item_exp, preferred_element_type=F32)
        istat = lax.dot_general(ratios[...], uexp[...], (((0,), (0,)), ((), ())), preferred_element_type=F32)
        if not first:
            istat = istat + ref["istat"][...]
        if last:
            old = 1.0 if item_rte is None else item_rte
            ref["item_new"][0:items, :] = 0.5 * item[0:items, :] + 0.5 * (
                0.3 + factor * (item_exp.astype(F32) * istat))
            ref["item_new"][items:items + 8, :] = 0.5 * old + 0.5 * (0.3 + factor * row_sum(theta))
        else:
            ref["istat_new"][...] = istat
            if stratum > 0:
                ref["theta_new"][...] = theta
        return functools.reduce(jnp.minimum, lows) if lows else None

    low = body(False)
    if low is not None:

        @pl.when(jnp.logical_not(above(low)))
        def _():
            body(True)


def stratum_call(stratum, at, rows, items, depth, factor, first, last, operands):
    extra = 8 if first else 0
    outs = {"upart": ((rows + extra, depth), F32)}
    if stratum > 0:
        outs["shp_new"] = ((rows, depth), F32)
    if first and stratum > 0:
        outs["rte_new"] = ((8, depth), F32)
    if first:
        outs["item_exp_new"] = ((items, depth), BF16)
    if last:
        outs["item_new"] = ((items + 8, depth), F32)
    else:
        outs["istat_new"] = ((items, depth), F32)
        if stratum > 0:
            outs["theta_new"] = ((8, depth), F32)
    scratch = {
        "counts": pltpu.VMEM((rows, items), BF16),
        "ratios": pltpu.VMEM((rows, items), BF16),
        "uexp": pltpu.VMEM((rows, depth), BF16),
        "sems": pltpu.SemaphoreType.DMA((3,)),
    }
    if stratum == 1:
        scratch["shape_in"] = pltpu.VMEM((rows, depth), BF16)
    if first or last:
        scratch["item_in"] = pltpu.VMEM(operands["item"].shape, F32)
    in_hbm = ("interactions", "user_shape", "uexp_all", "item")
    names = list(operands) + list(outs) + list(scratch)
    kernel = functools.partial(
        stratum_kernel, names, stratum=stratum, at=at, rows=rows, items=items,
        factor=factor, first=first, last=last)
    results = pl.pallas_call(
        kernel,
        out_shape=[jax.ShapeDtypeStruct(*spec) for spec in outs.values()],
        in_specs=[HBM_SPEC if name in in_hbm else VMEM_SPEC for name in operands],
        out_specs=[VMEM_SPEC] * len(outs),
        scratch_shapes=list(scratch.values()),
        compiler_params=PARAMS,
        cost_estimate=pl.CostEstimate(
            flops=6 * rows * items * depth, bytes_accessed=rows * (items * 2 + depth * 16),
            transcendentals=rows * (depth + items)),
        name=f"stratum{stratum}_at{at}",
    )(*operands.values())
    return dict(zip(outs, results))


def user_log_kernel(*refs, at, rows, factor, first, filled):
    acc, recv, shp_old, rte_in = refs[:4]
    rest = refs[5:] if filled else refs[4:]
    if first:
        out, rte_out, block, sem = rest
        beta = row_sum(acc[0:8, :] + recv[0:8, :])
        rte = 0.5 * rte_in[...] + 0.5 * (0.3 + factor * beta)
        rte_out[...] = rte
    else:
        out, block, sem = rest
        rte = rte_in[...]
    extra = 8 if first else 0

    def body(general):
        low = rte
        for t, step in tiles(rows):
            stat = acc[extra + t:extra + t + step, :] + recv[extra + t:extra + t + step, :]
            shp = 0.5 * shp_old[t:t + step, :] + 0.5 * (0.3 + factor * stat)
            block[t:t + step, :], part_low = log_tile(shp, rte, general)
            low = jnp.minimum(low, part_low)
        return low

    low = body(False)

    @pl.when(jnp.logical_not(above(low)))
    def _():
        body(True)

    copy = pltpu.make_async_copy(block, out.at[pl.ds(at, rows), :], sem)
    copy.start()
    copy.wait()


def user_log_call(at, rows, total, depth, factor, first, operands, filled):
    out_shape = [jax.ShapeDtypeStruct((total, depth), BF16)]
    out_specs = [HBM_SPEC]
    if first:
        out_shape.append(jax.ShapeDtypeStruct((8, depth), F32))
        out_specs.append(VMEM_SPEC)
    operands = list(operands)
    in_specs = [VMEM_SPEC] * 4
    if filled is not None:
        operands.append(filled)
        in_specs.append(HBM_SPEC)
    return pl.pallas_call(
        functools.partial(user_log_kernel, at=at, rows=rows, factor=factor, first=first,
                          filled=filled is not None),
        out_shape=out_shape,
        in_specs=in_specs,
        out_specs=out_specs,
        input_output_aliases={} if filled is None else {4: 0},
        scratch_shapes=[pltpu.VMEM((rows, depth), BF16), pltpu.SemaphoreType.DMA],
        compiler_params=PARAMS,
        cost_estimate=pl.CostEstimate(
            flops=40 * rows * depth, bytes_accessed=rows * depth * 14, transcendentals=rows * depth),
        name=f"user_log_at{at}",
    )(*operands)


def item_log_kernel(item, out, *, items):
    rte = item[items:items + 8, :]

    def body(general):
        out[...], low = log_tile(item[0:items, :], rte, general)
        return low

    low = body(False)

    @pl.when(jnp.logical_not(above(jnp.minimum(low, rte))))
    def _():
        body(True)


def item_log_call(item, items, depth):
    return pl.pallas_call(
        functools.partial(item_log_kernel, items=items),
        out_shape=jax.ShapeDtypeStruct((items, depth), BF16),
        in_specs=[VMEM_SPEC],
        out_specs=VMEM_SPEC,
        compiler_params=PARAMS,
        cost_estimate=pl.CostEstimate(
            flops=40 * items * depth, bytes_accessed=items * depth * 6, transcendentals=items * depth),
        name="item_log",
    )(item)


def swapped(value, axis, mask):
    return lax.ppermute(value, axis, [(a, a ^ mask) for a in range(lax.axis_size(axis))])


def moved(choice, value, beside=None, operands=()):
    def branch(mask, value, *operands):
        arrived = swapped(value, "users", mask)
        return (arrived,) if beside is None else (arrived, *beside(*operands))

    choices = [functools.partial(branch, mask) for mask in range(1, lax.axis_size("users"))]
    return lax.switch(choice, choices, value, *operands)


def exchanged(value):
    size = lax.axis_size("items")
    if size == 1:
        return value, jnp.zeros_like(value)
    mask = 1
    while mask * 2 < size:
        value = value + swapped(value, "items", mask)
        mask *= 2
    return value, swapped(value, "items", mask)


def per_device(interactions, matchings, user_shape, item_shape):
    group = lax.axis_size("users")
    factor = float(group)
    users, depth = user_shape.shape
    items = item_shape.shape[0]
    sizes = chunk_rows(users)
    starts = [sum(sizes[:i]) for i in range(len(sizes))]
    count = len(sizes)

    item, choices = prepare_call(matchings, item_shape, group - 1)
    item, uexp, theta = moved(choices[0], item, start_call, (user_shape,))
    rte = None
    shp = [None] * count
    sums = [None] * count
    for stratum in range(STRATA):
        carried = {"theta": theta}
        for i, (at, rows) in enumerate(zip(starts, sizes)):
            first, last = i == 0, i == count - 1
            operands = {"interactions": interactions}
            if stratum == 0:
                operands["uexp_all"] = uexp
            else:
                operands["acc"], operands["recv"] = sums[i]
                if stratum == 1:
                    operands["user_shape"] = user_shape
                else:
                    operands["shp_old"] = shp[i]
                if not first:
                    operands["rte"] = rte
                elif stratum > 1:
                    operands["rte_old"] = rte
            if first or last:
                operands["item"] = item
            if not first:
                operands["item_exp"] = carried["item_exp"]
                operands["istat"] = carried["istat"]
            if (stratum > 0 and not first) or (stratum == 0 and last):
                operands["theta"] = carried["theta"]
            out = stratum_call(stratum, at, rows, items, depth, factor, first, last, operands)
            shp[i] = out.get("shp_new")
            sums[i] = exchanged(out["upart"])
            if first:
                rte = out.get("rte_new")
                carried["item_exp"] = out["item_exp_new"]
            if last:
                item = out["item_new"]
            else:
                carried["istat"] = out["istat_new"]
                if stratum > 0:
                    carried["theta"] = out["theta_new"]
        if stratum + 1 < STRATA:
            item, = moved(choices[stratum + 1], item)
        else:
            item = swapped(item, "users", group - 1)
    item_log = item_log_call(item, items, depth)
    user_log = None
    for i, (at, rows) in enumerate(zip(starts, sizes)):
        out = user_log_call(at, rows, users, depth, factor, i == 0, (*sums[i], shp[i], rte), user_log)
        user_log = out[0]
        if i == 0:
            rte = out[1]
    return user_log, item_log


def solution(mesh):
    placed = (P(None, "users", "items"), P(), P("users", None), P(("users", "items"), None))
    return jax.shard_map(
        per_device,
        mesh=mesh,
        in_specs=placed,
        out_specs=(P("users", None), P(("users", "items"), None)),
        check_vma=False,
    )
```

```python
import functools

import jax
import jax.numpy as jnp
from jax import lax
from jax.experimental import pallas as pl
from jax.experimental.pallas import tpu as pltpu
from jax.sharding import PartitionSpec as P

STRATA = 3
TILE = 128
F32 = jnp.float32
BF16 = jnp.bfloat16


def chunk_rows(rows):
    half = rows // 2 // TILE * TILE
    return [half, rows - half]


def psi_parts(x):
    small = x < 8.0
    w = jnp.where(small, x + 3.5, x - 0.5)
    q = x * (x + 3.0)
    q2 = q + 2.0
    bounded = jnp.minimum(w, 1e9)
    square = bounded * bounded
    steps = jnp.where(small, q * q2, 1.0)
    r = 1.0 / (square * steps)
    s = r * steps
    shift = (2.0 * x + 3.0) * (q + q2) * (r * square)
    g = s * (1.0 / 24.0 - s * (7.0 / 960.0 - s * (31.0 / 8064.0 - s * (127.0 / 30720.0))))
    return w, g - jnp.where(small, shift, 0.0)


def psi_any(x):
    mirrored = x < 0.5
    w, g = psi_parts(jnp.where(mirrored, 1.0 - x, x))
    value = jnp.log(w) + g
    t = x - jnp.floor(x + 0.5)
    u = 3.14159265358979 * t
    v = u * u
    sin = 1.0 / 6227020800.0
    for c in (-1.0 / 39916800.0, 1.0 / 362880.0, -1.0 / 5040.0, 1.0 / 120.0, -1.0 / 6.0, 1.0):
        sin = sin * v + c
    cos = -1.0 / 87178291200.0
    for c in (1.0 / 479001600.0, -1.0 / 3628800.0, 1.0 / 40320.0, -1.0 / 720.0, 1.0 / 24.0, -0.5, 1.0):
        cos = cos * v + c
    value = jnp.where(mirrored, value - 3.14159265358979 * cos / (sin * u), value)
    return jnp.where((x <= 0.0) & (x == jnp.floor(x)), jnp.nan, value)


LOWEST = 0.01


def above(low):
    return jnp.min(low) >= LOWEST


def folded(x):
    return x.reshape(x.shape[0] // 8, 8, x.shape[1])


def tiles(rows):
    step = TILE if rows % TILE == 0 else rows
    return [(at, step) for at in range(0, rows, step)]


def exp_tile(x, rte, general):
    shape = x.shape
    x = folded(x)
    if general:
        value = psi_any(x)
        if rte is not None:
            value = value - jnp.log(rte)[None]
        value = jnp.exp(value)
    else:
        w, g = psi_parts(x)
        value = w if rte is None else w * (1.0 / rte)[None]
        value = value * jnp.exp(g)
    mean = x if rte is None else x * (1.0 / rte)[None]
    return value.reshape(shape).astype(BF16), jnp.sum(mean, axis=0), jnp.min(x, axis=0)


def log_tile(x, rte, general):
    shape = x.shape
    x = folded(x)
    if general:
        value = psi_any(x) - jnp.log(rte)[None]
    else:
        w, g = psi_parts(x)
        value = (jnp.log(w) - jnp.log(rte)[None]) + g
    return value.reshape(shape).astype(BF16), jnp.min(x, axis=0)


def row_sum(x):
    return jnp.broadcast_to(jnp.sum(x, axis=0, keepdims=True), x.shape)


VMEM_SPEC = pl.BlockSpec(memory_space=pltpu.VMEM)
SMEM_SPEC = pl.BlockSpec(memory_space=pltpu.SMEM)
HBM_SPEC = pl.BlockSpec(memory_space=pltpu.HBM)
PARAMS = pltpu.CompilerParams(vmem_limit_bytes=24 * 2**20)


def in_hbm(x):
    return pltpu.with_memory_space_constraint(x, pltpu.HBM)


def in_vmem(x):
    return pltpu.with_memory_space_constraint(x, pltpu.VMEM)


def prepare_kernel(matchings_hbm, shape_hbm, item, *refs, last):
    choices, (matchings, shape, sems) = refs[:STRATA], refs[STRATA:]
    copies = [
        pltpu.make_async_copy(shape_hbm, shape, sems.at[0]),
        pltpu.make_async_copy(matchings_hbm, matchings, sems.at[1]),
    ]
    for copy in copies:
        copy.start()
    for copy in copies:
        copy.wait()
    item[...] = shape[...].astype(F32)
    choices[0][0] = matchings[0] - 1
    for stratum in range(1, STRATA - 1):
        choices[stratum][0] = jnp.bitwise_xor(matchings[stratum - 1], matchings[stratum]) - 1
    choices[STRATA - 1][0] = jnp.bitwise_xor(matchings[STRATA - 2], last) - 1


def prepare_call(matchings, item_shape, last):
    out = pl.pallas_call(
        functools.partial(prepare_kernel, last=last),
        out_shape=[jax.ShapeDtypeStruct(item_shape.shape, F32)]
        + [jax.ShapeDtypeStruct((1,), jnp.int32)] * STRATA,
        in_specs=[HBM_SPEC, HBM_SPEC],
        out_specs=[VMEM_SPEC] + [SMEM_SPEC] * STRATA,
        scratch_shapes=[pltpu.SMEM(matchings.shape, jnp.int32), pltpu.VMEM(item_shape.shape, BF16),
                        pltpu.SemaphoreType.DMA((2,))],
        compiler_params=PARAMS,
        name="prepare",
    )(in_hbm(matchings), in_hbm(item_shape))
    return out[0], [choice[0] for choice in out[1:]]


def start_kernel(shape, uexp, theta):
    rows, depth = shape.shape

    def body(general):
        def step(i, carry):
            total, low = carry
            place = pl.ds(pl.multiple_of(i * TILE, TILE), TILE)
            value, part, part_low = exp_tile(shape[place, :].astype(F32), None, general)
            uexp[place, :] = value
            return total + part, jnp.minimum(low, part_low)

        total, low = lax.fori_loop(
            0, rows // TILE, step, (jnp.zeros((8, depth), F32), jnp.ones((8, depth), F32)))
        theta[...] = total
        return low

    low = body(False)

    @pl.when(jnp.logical_not(above(low)))
    def _():
        body(True)


def start_call(user_shape):
    rows, depth = user_shape.shape
    return pl.pallas_call(
        start_kernel,
        out_shape=[jax.ShapeDtypeStruct((rows, depth), BF16), jax.ShapeDtypeStruct((8, depth), F32)],
        in_specs=[VMEM_SPEC],
        out_specs=[VMEM_SPEC] * 2,
        compiler_params=PARAMS,
        cost_estimate=pl.CostEstimate(
            flops=40 * rows * depth, bytes_accessed=rows * depth * 4, transcendentals=2 * rows * depth),
        name="user_start",
    )(in_hbm(user_shape))


def stratum_kernel(names, *refs, stratum, at, rows, items, factor, first, last):
    ref = dict(zip(names, refs))
    sems = ref["sems"]
    copies = {}

    def fetch(name, source, target):
        copies[name] = pltpu.make_async_copy(source, target, sems.at[len(copies)])
        copies[name].start()

    place = pl.ds(at, rows)
    if first:
        fetch("item", ref["item"], ref["item_in"])
    fetch("counts", ref["interactions"].at[stratum, place, :], ref["counts"])
    upart, counts, ratios, denominator = ref["upart"], ref["counts"], ref["ratios"], ref["denominator"]
    uexp = ref["uexp_all"].at[place, :] if stratum == 0 else ref["uexp"]
    extra = 8 if first else 0

    def wait(name, general):
        if not general:
            copies[name].wait()

    def body(general):
        lows = []
        theta = None
        if stratum > 0:
            if first:
                beta = row_sum(ref["acc"][0:8, :] + ref["recv"][0:8, :])
                old = 1.0 if stratum == 1 else ref["rte_old"][...]
                rte = 0.5 * old + 0.5 * (0.3 + factor * beta)
                ref["rte_new"][...] = rte
            else:
                rte = ref["rte"][...]
            lows.append(rte)
            for t, step in tiles(rows):
                old = ref["user_shape"][at + t:at + t + step, :].astype(F32) if stratum == 1 else ref["shp_old"][t:t + step, :]
                stat = ref["acc"][extra + t:extra + t + step, :] + ref["recv"][extra + t:extra + t + step, :]
                shp = 0.5 * old + 0.5 * (0.3 + factor * stat)
                ref["shp_new"][t:t + step, :] = shp
                value, part, low = exp_tile(shp, rte, general)
                uexp[t:t + step, :] = value
                theta = part if theta is None else theta + part
                lows.append(low)
            if not first:
                theta = theta + ref["theta"][...]
        elif last:
            theta = ref["theta"][...]

        if first:
            wait("item", general)
            item = ref["item_in"]
            if not last:
                ref["item_kept"][...] = item[...]
        elif last:
            item = ref["item_kept"]
        if first or last:
            item_rte = None if stratum == 0 else item[items:items + 8, :]
        if first:
            value, sums, low = exp_tile(item[0:items, :], item_rte, general)
            ref["item_exp_new"][...] = value
            upart[0:8, :] = sums
            lows.append(low)
            if item_rte is not None:
                lows.append(item_rte)
            item_exp = value
        else:
            item_exp = ref["item_exp"][...]

        denominator[...] = lax.dot_general(
            uexp[...], item_exp, (((1,), (1,)), ((), ())), preferred_element_type=F32)
        wait("counts", general)
        for t, step in tiles(rows):
            ratios[t:t + step, :] = (
                counts[t:t + step, :].astype(F32) / denominator[t:t + step, :]).astype(BF16)
        upart[extra:extra + rows, :] = uexp[...].astype(F32) * jnp.dot(
            ratios[...], item_exp, preferred_element_type=F32)
        istat = lax.dot_general(ratios[...], uexp[...], (((0,), (0,)), ((), ())), preferred_element_type=F32)
        if not first:
            istat = istat + ref["istat"][...]
        if last:
            old = 1.0 if item_rte is None else item_rte
            ref["item_new"][0:items, :] = 0.5 * item[0:items, :] + 0.5 * (
                0.3 + factor * (item_exp.astype(F32) * istat))
            ref["item_new"][items:items + 8, :] = 0.5 * old + 0.5 * (0.3 + factor * row_sum(theta))
        else:
            ref["istat_new"][...] = istat
            if stratum > 0:
                ref["theta_new"][...] = theta
        return functools.reduce(jnp.minimum, lows) if lows else None

    low = body(False)
    if low is not None:

        @pl.when(jnp.logical_not(above(low)))
        def _():
            body(True)


def stratum_call(stratum, at, rows, items, depth, factor, first, last, operands):
    extra = 8 if first else 0
    outs = {"upart": ((rows + extra, depth), F32)}
    if stratum > 0:
        outs["shp_new"] = ((rows, depth), F32)
    if first and stratum > 0:
        outs["rte_new"] = ((8, depth), F32)
    if first:
        outs["item_exp_new"] = ((items, depth), BF16)
    if first and not last:
        outs["item_kept"] = (operands["item"].shape, F32)
    if last:
        outs["item_new"] = ((items + 8, depth), F32)
    else:
        outs["istat_new"] = ((items, depth), F32)
        if stratum > 0:
            outs["theta_new"] = ((8, depth), F32)
    scratch = {
        "counts": pltpu.VMEM((rows, items), BF16),
        "ratios": pltpu.VMEM((rows, items), BF16),
        "denominator": pltpu.VMEM((rows, items), F32),
        "sems": pltpu.SemaphoreType.DMA((2,)),
    }
    if stratum > 0:
        scratch["uexp"] = pltpu.VMEM((rows, depth), BF16)
    if first:
        scratch["item_in"] = pltpu.VMEM(operands["item"].shape, F32)
    hbm = ("interactions", "item")
    operands = {
        name: in_hbm(x) if name in hbm else in_vmem(x) if name == "user_shape" else x
        for name, x in operands.items()}
    names = list(operands) + list(outs) + list(scratch)
    kernel = functools.partial(
        stratum_kernel, names, stratum=stratum, at=at, rows=rows, items=items,
        factor=factor, first=first, last=last)
    results = pl.pallas_call(
        kernel,
        out_shape=[jax.ShapeDtypeStruct(*spec) for spec in outs.values()],
        in_specs=[HBM_SPEC if name in hbm else VMEM_SPEC for name in operands],
        out_specs=[VMEM_SPEC] * len(outs),
        scratch_shapes=list(scratch.values()),
        compiler_params=PARAMS,
        cost_estimate=pl.CostEstimate(
            flops=6 * rows * items * depth, bytes_accessed=rows * (items * 2 + depth * 16),
            transcendentals=rows * (depth + items)),
        name=f"stratum{stratum}_at{at}",
    )(*operands.values())
    return dict(zip(outs, results))


def user_log_kernel(*refs, at, rows, factor, first, filled):
    acc, recv, shp_old, rte_in = refs[:4]
    rest = refs[5:] if filled else refs[4:]
    if first:
        out, rte_out, block, sem = rest
        beta = row_sum(acc[0:8, :] + recv[0:8, :])
        rte = 0.5 * rte_in[...] + 0.5 * (0.3 + factor * beta)
        rte_out[...] = rte
    else:
        out, block, sem = rest
        rte = rte_in[...]
    extra = 8 if first else 0

    def body(general):
        low = rte
        for t, step in tiles(rows):
            stat = acc[extra + t:extra + t + step, :] + recv[extra + t:extra + t + step, :]
            shp = 0.5 * shp_old[t:t + step, :] + 0.5 * (0.3 + factor * stat)
            block[t:t + step, :], part_low = log_tile(shp, rte, general)
            low = jnp.minimum(low, part_low)
        return low

    low = body(False)

    @pl.when(jnp.logical_not(above(low)))
    def _():
        body(True)

    copy = pltpu.make_async_copy(block, out.at[pl.ds(at, rows), :], sem)
    copy.start()
    copy.wait()


def user_log_call(at, rows, total, depth, factor, first, operands, filled):
    out_shape = [jax.ShapeDtypeStruct((total, depth), BF16)]
    out_specs = [HBM_SPEC]
    if first:
        out_shape.append(jax.ShapeDtypeStruct((8, depth), F32))
        out_specs.append(VMEM_SPEC)
    operands = list(operands)
    in_specs = [VMEM_SPEC] * 4
    if filled is not None:
        operands.append(filled)
        in_specs.append(HBM_SPEC)
    return pl.pallas_call(
        functools.partial(user_log_kernel, at=at, rows=rows, factor=factor, first=first,
                          filled=filled is not None),
        out_shape=out_shape,
        in_specs=in_specs,
        out_specs=out_specs,
        input_output_aliases={} if filled is None else {4: 0},
        scratch_shapes=[pltpu.VMEM((rows, depth), BF16), pltpu.SemaphoreType.DMA],
        compiler_params=PARAMS,
        cost_estimate=pl.CostEstimate(
            flops=40 * rows * depth, bytes_accessed=rows * depth * 14, transcendentals=rows * depth),
        name=f"user_log_at{at}",
    )(*operands)


def item_log_kernel(item, _, out, *, items):
    rte = item[items:items + 8, :]

    def body(general):
        out[...], low = log_tile(item[0:items, :], rte, general)
        return low

    low = body(False)

    @pl.when(jnp.logical_not(above(jnp.minimum(low, rte))))
    def _():
        body(True)


def item_log_call(item, after, items, depth):
    return pl.pallas_call(
        functools.partial(item_log_kernel, items=items),
        out_shape=jax.ShapeDtypeStruct((items, depth), BF16),
        in_specs=[VMEM_SPEC, VMEM_SPEC],
        out_specs=VMEM_SPEC,
        compiler_params=PARAMS,
        cost_estimate=pl.CostEstimate(
            flops=40 * items * depth, bytes_accessed=items * depth * 6, transcendentals=items * depth),
        name="item_log",
    )(item, after)


def swapped(value, axis, mask):
    return lax.ppermute(value, axis, [(a, a ^ mask) for a in range(lax.axis_size(axis))])


def moved(choice, value, beside=None, operands=()):
    def branch(mask, value, *operands):
        arrived = swapped(value, "users", mask)
        return (arrived,) if beside is None else (arrived, *beside(*operands))

    choices = [functools.partial(branch, mask) for mask in range(1, lax.axis_size("users"))]
    return lax.switch(choice, choices, value, *operands)


def exchanged(value):
    size = lax.axis_size("items")
    if size == 1:
        return value, jnp.zeros_like(value)
    mask = 1
    while mask * 2 < size:
        value = value + swapped(value, "items", mask)
        mask *= 2
    return value, swapped(value, "items", mask)


def per_device(interactions, matchings, user_shape, item_shape):
    group = lax.axis_size("users")
    factor = float(group)
    users, depth = user_shape.shape
    items = item_shape.shape[0]
    sizes = chunk_rows(users)
    starts = [sum(sizes[:i]) for i in range(len(sizes))]
    count = len(sizes)

    item, choices = prepare_call(matchings, item_shape, group - 1)
    item, uexp, theta = moved(choices[0], item, start_call, (user_shape,))
    rte = None
    shp = [None] * count
    sums = [None] * count
    for stratum in range(STRATA):
        carried = {"theta": theta}
        for i, (at, rows) in enumerate(zip(starts, sizes)):
            first, last = i == 0, i == count - 1
            operands = {"interactions": interactions}
            if stratum == 0:
                operands["uexp_all"] = uexp
            else:
                operands["acc"], operands["recv"] = sums[i]
                if stratum == 1:
                    operands["user_shape"] = user_shape
                else:
                    operands["shp_old"] = shp[i]
                if not first:
                    operands["rte"] = rte
                elif stratum > 1:
                    operands["rte_old"] = rte
            if first:
                operands["item"] = item
            elif last:
                operands["item_kept"] = carried["item_kept"]
            if not first:
                operands["item_exp"] = carried["item_exp"]
                operands["istat"] = carried["istat"]
            if (stratum > 0 and not first) or (stratum == 0 and last):
                operands["theta"] = carried["theta"]
            out = stratum_call(stratum, at, rows, items, depth, factor, first, last, operands)
            shp[i] = out.get("shp_new")
            sums[i] = exchanged(out["upart"])
            if first:
                rte = out.get("rte_new")
                carried["item_exp"] = out["item_exp_new"]
                carried["item_kept"] = out.get("item_kept")
            if last:
                item = out["item_new"]
            else:
                carried["istat"] = out["istat_new"]
                if stratum > 0:
                    carried["theta"] = out["theta_new"]
        if stratum + 1 < STRATA:
            item, = moved(choices[stratum + 1], item)
        else:
            item = swapped(item, "users", group - 1)
    user_log = None
    for i, (at, rows) in enumerate(zip(starts, sizes)):
        out = user_log_call(at, rows, users, depth, factor, i == 0, (*sums[i], shp[i], rte), user_log)
        user_log = out[0]
        if i == 0:
            rte = out[1]
            item_log = item_log_call(item, rte, items, depth)
    return user_log, item_log


def solution(mesh):
    placed = (P(None, "users", "items"), P(), P("users", None), P(("users", "items"), None))
    return jax.shard_map(
        per_device,
        mesh=mesh,
        in_specs=placed,
        out_specs=(P("users", None), P(("users", "items"), None)),
        check_vma=False,
    )
```

```python
import functools

import jax
import jax.numpy as jnp
from jax import lax
from jax.experimental import pallas as pl
from jax.experimental.pallas import tpu as pltpu
from jax.sharding import PartitionSpec as P

STRATA = 3
TILE = 128
F32 = jnp.float32
BF16 = jnp.bfloat16


def chunk_rows(rows):
    first = max(rows // 2 // TILE, 1) * TILE
    return [first, rows - first] if first < rows else [rows]


def tail_rows(rows):
    return 2 * TILE if rows > 4 * TILE else 0


def psi_parts(x):
    small = x < 8.0
    w = jnp.where(small, x + 3.5, x - 0.5)
    q = x * (x + 3.0)
    q2 = q + 2.0
    bounded = jnp.minimum(w, 1e9)
    square = bounded * bounded
    steps = jnp.where(small, q * q2, 1.0)
    r = 1.0 / (square * steps)
    s = r * steps
    shift = (2.0 * x + 3.0) * (q + q2) * (r * square)
    g = s * (1.0 / 24.0 - s * (7.0 / 960.0 - s * (31.0 / 8064.0 - s * (127.0 / 30720.0))))
    return w, g - jnp.where(small, shift, 0.0)


def psi_any(x):
    mirrored = x < 0.5
    w, g = psi_parts(jnp.where(mirrored, 1.0 - x, x))
    value = jnp.log(w) + g
    t = x - jnp.floor(x + 0.5)
    u = 3.14159265358979 * t
    v = u * u
    sin = 1.0 / 6227020800.0
    for c in (-1.0 / 39916800.0, 1.0 / 362880.0, -1.0 / 5040.0, 1.0 / 120.0, -1.0 / 6.0, 1.0):
        sin = sin * v + c
    cos = -1.0 / 87178291200.0
    for c in (1.0 / 479001600.0, -1.0 / 3628800.0, 1.0 / 40320.0, -1.0 / 720.0, 1.0 / 24.0, -0.5, 1.0):
        cos = cos * v + c
    value = jnp.where(mirrored, value - 3.14159265358979 * cos / (sin * u), value)
    return jnp.where((x <= 0.0) & (x == jnp.floor(x)), jnp.nan, value)


LOWEST = 0.01


def above(low):
    return jnp.min(low) >= LOWEST


def folded(x):
    return x.reshape(x.shape[0] // 8, 8, x.shape[1])


def tiles(rows):
    step = TILE if rows % TILE == 0 else rows
    return [(at, step) for at in range(0, rows, step)]


def exp_tile(x, rte, general):
    shape = x.shape
    x = folded(x)
    if general:
        value = psi_any(x)
        if rte is not None:
            value = value - jnp.log(rte)[None]
        value = jnp.exp(value)
    else:
        w, g = psi_parts(x)
        value = w if rte is None else w * (1.0 / rte)[None]
        value = value * jnp.exp(g)
    mean = x if rte is None else x * (1.0 / rte)[None]
    return value.reshape(shape).astype(BF16), jnp.sum(mean, axis=0), jnp.min(x, axis=0)


def log_tile(x, rte, general):
    shape = x.shape
    x = folded(x)
    if general:
        value = psi_any(x) - jnp.log(rte)[None]
    else:
        w, g = psi_parts(x)
        value = (jnp.log(w) - jnp.log(rte)[None]) + g
    return value.reshape(shape).astype(BF16), jnp.min(x, axis=0)


def row_sum(x):
    return jnp.broadcast_to(jnp.sum(x, axis=0, keepdims=True), x.shape)


VMEM_SPEC = pl.BlockSpec(memory_space=pltpu.VMEM)
SMEM_SPEC = pl.BlockSpec(memory_space=pltpu.SMEM)
HBM_SPEC = pl.BlockSpec(memory_space=pltpu.HBM)
PARAMS = pltpu.CompilerParams(vmem_limit_bytes=24 * 2**20)


def in_hbm(x):
    return pltpu.with_memory_space_constraint(x, pltpu.HBM)


def in_vmem(x):
    return pltpu.with_memory_space_constraint(x, pltpu.VMEM)


def prepare_kernel(matchings_hbm, shape_hbm, item, *refs, last):
    choices, (matchings, shape, sems) = refs[:STRATA], refs[STRATA:]
    copies = [
        pltpu.make_async_copy(shape_hbm, shape, sems.at[0]),
        pltpu.make_async_copy(matchings_hbm, matchings, sems.at[1]),
    ]
    for copy in copies:
        copy.start()
    for copy in copies:
        copy.wait()
    item[...] = shape[...].astype(F32)
    choices[0][0] = matchings[0] - 1
    for stratum in range(1, STRATA - 1):
        choices[stratum][0] = jnp.bitwise_xor(matchings[stratum - 1], matchings[stratum]) - 1
    choices[STRATA - 1][0] = jnp.bitwise_xor(matchings[STRATA - 2], last) - 1


def prepare_call(matchings, item_shape, last):
    out = pl.pallas_call(
        functools.partial(prepare_kernel, last=last),
        out_shape=[jax.ShapeDtypeStruct(item_shape.shape, F32)]
        + [pltpu.SMEM((1,), jnp.int32)] * STRATA,
        in_specs=[HBM_SPEC, HBM_SPEC],
        out_specs=[VMEM_SPEC] + [SMEM_SPEC] * STRATA,
        scratch_shapes=[pltpu.SMEM(matchings.shape, jnp.int32), pltpu.VMEM(item_shape.shape, BF16),
                        pltpu.SemaphoreType.DMA((2,))],
        compiler_params=PARAMS,
        name="prepare",
    )(in_hbm(matchings), in_hbm(item_shape))
    return out[0], [choice[0] for choice in out[1:]]


def start_kernel(shape, uexp, theta):
    rows, depth = shape.shape

    def body(general):
        def step(i, carry):
            total, low = carry
            place = pl.ds(pl.multiple_of(i * TILE, TILE), TILE)
            value, part, part_low = exp_tile(shape[place, :].astype(F32), None, general)
            uexp[place, :] = value
            return total + part, jnp.minimum(low, part_low)

        total, low = lax.fori_loop(
            0, rows // TILE, step, (jnp.zeros((8, depth), F32), jnp.ones((8, depth), F32)))
        theta[...] = total
        return low

    low = body(False)

    @pl.when(jnp.logical_not(above(low)))
    def _():
        body(True)


def start_call(user_shape):
    rows, depth = user_shape.shape
    return pl.pallas_call(
        start_kernel,
        out_shape=[jax.ShapeDtypeStruct((rows, depth), BF16), jax.ShapeDtypeStruct((8, depth), F32)],
        in_specs=[VMEM_SPEC],
        out_specs=[VMEM_SPEC] * 2,
        compiler_params=PARAMS,
        cost_estimate=pl.CostEstimate(
            flops=40 * rows * depth, bytes_accessed=rows * depth * 4, transcendentals=2 * rows * depth),
        name="user_start",
    )(in_hbm(user_shape))


def stratum_kernel(names, *refs, stratum, at, rows, items, factor, first, last, tail):
    ref = dict(zip(names, refs))
    sems = ref["sems"]
    copies = {}

    def fetch(name, source, target):
        copies[name] = pltpu.make_async_copy(source, target, sems.at[len(copies)])
        copies[name].start()

    place = pl.ds(at, rows)
    if first:
        fetch("item", ref["item"], ref["item_in"])
    fetch("counts", ref["interactions"].at[stratum, place, :], ref["counts"])
    upart, counts, ratios, denominator = ref["upart"], ref["counts"], ref["ratios"], ref["denominator"]
    uexp = ref["uexp_all"].at[place, :] if stratum == 0 else ref["uexp"]
    extra = 8 if first else 0

    def wait(name, general):
        if not general:
            copies[name].wait()

    def body(general):
        lows = []
        theta = None
        if stratum > 0:
            if first:
                beta = row_sum(ref["acc"][0:8, :] + ref["recv"][0:8, :])
                old = 1.0 if stratum == 1 else ref["rte_old"][...]
                rte = 0.5 * old + 0.5 * (0.3 + factor * beta)
                ref["rte_new"][...] = rte
            else:
                rte = ref["rte"][...]
            lows.append(rte)
            for t, step in tiles(rows):
                old = ref["user_shape"][at + t:at + t + step, :].astype(F32) if stratum == 1 else ref["shp_old"][t:t + step, :]
                stat = ref["acc"][extra + t:extra + t + step, :] + ref["recv"][extra + t:extra + t + step, :]
                shp = 0.5 * old + 0.5 * (0.3 + factor * stat)
                ref["shp_new"][t:t + step, :] = shp
                value, part, low = exp_tile(shp, rte, general)
                uexp[t:t + step, :] = value
                theta = part if theta is None else theta + part
                lows.append(low)
            if not first:
                theta = theta + ref["theta"][...]
        elif last:
            theta = ref["theta"][...]

        if first:
            wait("item", general)
            item = ref["item_in"]
            if not last:
                ref["item_kept"][...] = item[...]
        elif last:
            item = ref["item_kept"]
        if first or last:
            item_rte = None if stratum == 0 else item[items:items + 8, :]
        if first:
            value, sums, low = exp_tile(item[0:items, :], item_rte, general)
            ref["item_exp_new"][...] = value
            upart[0:8, :] = sums
            lows.append(low)
            if item_rte is not None:
                lows.append(item_rte)
            item_exp = value
        else:
            item_exp = ref["item_exp"][...]

        denominator[...] = lax.dot_general(
            uexp[...], item_exp, (((1,), (1,)), ((), ())), preferred_element_type=F32)
        wait("counts", general)
        for t, step in tiles(rows):
            ratios[t:t + step, :] = (
                counts[t:t + step, :].astype(F32) / denominator[t:t + step, :]).astype(BF16)
        user_sums = uexp[...].astype(F32) * jnp.dot(
            ratios[...], item_exp, preferred_element_type=F32)
        upart[extra:extra + rows - tail, :] = user_sums[0:rows - tail, :]
        if tail:
            ref["upart_tail"][...] = user_sums[rows - tail:, :]
        istat = lax.dot_general(ratios[...], uexp[...], (((0,), (0,)), ((), ())), preferred_element_type=F32)
        if not first:
            istat = istat + ref["istat"][...]
        if last:
            old = 1.0 if item_rte is None else item_rte
            ref["item_new"][0:items, :] = 0.5 * item[0:items, :] + 0.5 * (
                0.3 + factor * (item_exp.astype(F32) * istat))
            ref["item_new"][items:items + 8, :] = 0.5 * old + 0.5 * (0.3 + factor * row_sum(theta))
        else:
            ref["istat_new"][...] = istat
            if stratum > 0:
                ref["theta_new"][...] = theta
        return functools.reduce(jnp.minimum, lows) if lows else None

    low = body(False)
    if low is not None:

        @pl.when(jnp.logical_not(above(low)))
        def _():
            body(True)


def stratum_call(stratum, at, rows, items, depth, factor, first, last, tail, operands):
    extra = 8 if first else 0
    outs = {"upart": ((rows + extra - tail, depth), F32)}
    if tail:
        outs["upart_tail"] = ((tail, depth), F32)
    if stratum > 0:
        outs["shp_new"] = ((rows, depth), F32)
    if first and stratum > 0:
        outs["rte_new"] = ((8, depth), F32)
    if first:
        outs["item_exp_new"] = ((items, depth), BF16)
    if first and not last:
        outs["item_kept"] = (operands["item"].shape, F32)
    if last:
        outs["item_new"] = ((items + 8, depth), F32)
    else:
        outs["istat_new"] = ((items, depth), F32)
        if stratum > 0:
            outs["theta_new"] = ((8, depth), F32)
    scratch = {
        "counts": pltpu.VMEM((rows, items), BF16),
        "ratios": pltpu.VMEM((rows, items), BF16),
        "denominator": pltpu.VMEM((rows, items), F32),
        "sems": pltpu.SemaphoreType.DMA((2,)),
    }
    if stratum > 0:
        scratch["uexp"] = pltpu.VMEM((rows, depth), BF16)
    if first:
        scratch["item_in"] = pltpu.VMEM(operands["item"].shape, F32)
    hbm = ("interactions", "item")
    operands = {
        name: in_hbm(x) if name in hbm else in_vmem(x) if name == "user_shape" else x
        for name, x in operands.items()}
    names = list(operands) + list(outs) + list(scratch)
    kernel = functools.partial(
        stratum_kernel, names, stratum=stratum, at=at, rows=rows, items=items,
        factor=factor, first=first, last=last, tail=tail)
    results = pl.pallas_call(
        kernel,
        out_shape=[jax.ShapeDtypeStruct(*spec) for spec in outs.values()],
        in_specs=[HBM_SPEC if name in hbm else VMEM_SPEC for name in operands],
        out_specs=[VMEM_SPEC] * len(outs),
        scratch_shapes=list(scratch.values()),
        compiler_params=PARAMS,
        cost_estimate=pl.CostEstimate(flops=1, bytes_accessed=1, transcendentals=0),
        name=f"stratum{stratum}_at{at}",
    )(*operands.values())
    return dict(zip(outs, results))


def user_log_kernel(*refs, at, rows, shp_at, factor, first, filled):
    acc, recv, shp_old, rte_in = refs[:4]
    rest = refs[5:] if filled else refs[4:]
    if first:
        out, rte_out, block, sem = rest
        beta = row_sum(acc[0:8, :] + recv[0:8, :])
        rte = 0.5 * rte_in[...] + 0.5 * (0.3 + factor * beta)
        rte_out[...] = rte
    else:
        out, block, sem = rest
        rte = rte_in[...]
    extra = 8 if first else 0

    def body(general):
        low = rte
        for t, step in tiles(rows):
            stat = acc[extra + t:extra + t + step, :] + recv[extra + t:extra + t + step, :]
            shp = 0.5 * shp_old[shp_at + t:shp_at + t + step, :] + 0.5 * (0.3 + factor * stat)
            block[t:t + step, :], part_low = log_tile(shp, rte, general)
            low = jnp.minimum(low, part_low)
        return low

    low = body(False)

    @pl.when(jnp.logical_not(above(low)))
    def _():
        body(True)

    copy = pltpu.make_async_copy(block, out.at[pl.ds(at, rows), :], sem)
    copy.start()
    copy.wait()


def user_log_call(at, rows, shp_at, total, depth, factor, first, operands, filled):
    out_shape = [jax.ShapeDtypeStruct((total, depth), BF16)]
    out_specs = [HBM_SPEC]
    if first:
        out_shape.append(jax.ShapeDtypeStruct((8, depth), F32))
        out_specs.append(VMEM_SPEC)
    operands = list(operands)
    in_specs = [VMEM_SPEC] * 4
    if filled is not None:
        operands.append(filled)
        in_specs.append(HBM_SPEC)
    return pl.pallas_call(
        functools.partial(user_log_kernel, at=at, rows=rows, shp_at=shp_at, factor=factor, first=first,
                          filled=filled is not None),
        out_shape=out_shape,
        in_specs=in_specs,
        out_specs=out_specs,
        input_output_aliases={} if filled is None else {4: 0},
        scratch_shapes=[pltpu.VMEM((rows, depth), BF16), pltpu.SemaphoreType.DMA],
        compiler_params=PARAMS,
        cost_estimate=pl.CostEstimate(
            flops=40 * rows * depth, bytes_accessed=rows * depth * 14, transcendentals=rows * depth),
        name=f"user_log_at{at}",
    )(*operands)


def item_log_kernel(item, _, out, *, items):
    rte = item[items:items + 8, :]

    def body(general):
        out[...], low = log_tile(item[0:items, :], rte, general)
        return low

    low = body(False)

    @pl.when(jnp.logical_not(above(jnp.minimum(low, rte))))
    def _():
        body(True)


def item_log_call(item, after, items, depth):
    return pl.pallas_call(
        functools.partial(item_log_kernel, items=items),
        out_shape=jax.ShapeDtypeStruct((items, depth), BF16),
        in_specs=[VMEM_SPEC, VMEM_SPEC],
        out_specs=VMEM_SPEC,
        compiler_params=PARAMS,
        cost_estimate=pl.CostEstimate(
            flops=40 * items * depth, bytes_accessed=items * depth * 6, transcendentals=items * depth),
        name="item_log",
    )(item, after)


def swapped(value, axis, mask):
    return lax.ppermute(value, axis, [(a, a ^ mask) for a in range(lax.axis_size(axis))])


def moved(choice, value, beside=None, operands=()):
    def branch(mask, value, *operands):
        arrived = swapped(value, "users", mask)
        return (arrived,) if beside is None else (arrived, *beside(*operands))

    choices = [functools.partial(branch, mask) for mask in range(1, lax.axis_size("users"))]
    return lax.switch(choice, choices, value, *operands)


def exchanged(value):
    size = lax.axis_size("items")
    if size == 1:
        return value, jnp.zeros_like(value)
    mask = 1
    while mask * 2 < size:
        value = value + swapped(value, "items", mask)
        mask *= 2
    return value, swapped(value, "items", mask)


def per_device(interactions, matchings, user_shape, item_shape):
    group = lax.axis_size("users")
    factor = float(group)
    users, depth = user_shape.shape
    items = item_shape.shape[0]
    sizes = chunk_rows(users)
    starts = [sum(sizes[:i]) for i in range(len(sizes))]
    count = len(sizes)

    item, choices = prepare_call(matchings, item_shape, group - 1)
    item, uexp, theta = moved(choices[0], item, start_call, (user_shape,))
    rte = None
    shp = [None] * count
    sums = [None] * count
    for stratum in range(STRATA):
        carried = {"theta": theta}
        for i, (at, rows) in enumerate(zip(starts, sizes)):
            first, last = i == 0, i == count - 1
            operands = {"interactions": interactions}
            if stratum == 0:
                operands["uexp_all"] = uexp
            else:
                operands["acc"], operands["recv"] = sums[i]
                if stratum == 1:
                    operands["user_shape"] = user_shape
                else:
                    operands["shp_old"] = shp[i]
                if not first:
                    operands["rte"] = rte
                elif stratum > 1:
                    operands["rte_old"] = rte
            if first:
                operands["item"] = item
            elif last:
                operands["item_kept"] = carried["item_kept"]
            if not first:
                operands["item_exp"] = carried["item_exp"]
                operands["istat"] = carried["istat"]
            if (stratum > 0 and not first) or (stratum == 0 and last):
                operands["theta"] = carried["theta"]
            tail = tail_rows(rows) if last and stratum == STRATA - 1 else 0
            out = stratum_call(stratum, at, rows, items, depth, factor, first, last, tail, operands)
            shp[i] = out.get("shp_new")
            sums[i] = exchanged(out["upart"])
            if tail:
                tail_sums = exchanged(out["upart_tail"])
            if first:
                rte = out.get("rte_new")
                carried["item_exp"] = out["item_exp_new"]
                carried["item_kept"] = out.get("item_kept")
            if last:
                item = out["item_new"]
            else:
                carried["istat"] = out["istat_new"]
                if stratum > 0:
                    carried["theta"] = out["theta_new"]
        if stratum + 1 < STRATA:
            item, = moved(choices[stratum + 1], item)
        else:
            item = swapped(item, "users", group - 1)
    user_log = None
    pieces = [(at, rows, 0, sums[i], shp[i]) for i, (at, rows) in enumerate(zip(starts, sizes))]
    if tail:
        at, rows = starts[-1], sizes[-1] - tail
        pieces[-1:] = [(at, rows, 0, sums[-1], shp[-1]), (at + rows, tail, rows, tail_sums, shp[-1])]
    for i, (at, rows, shp_at, piece_sums, piece_shp) in enumerate(pieces):
        out = user_log_call(
            at, rows, shp_at, users, depth, factor, i == 0, (*piece_sums, piece_shp, rte), user_log)
        user_log = out[0]
        if i == 0:
            rte = out[1]
            item_log = item_log_call(item, rte, items, depth)
    return user_log, item_log


def solution(mesh):
    placed = (P(None, "users", "items"), P(), P("users", None), P(("users", "items"), None))
    return jax.shard_map(
        per_device,
        mesh=mesh,
        in_specs=placed,
        out_specs=(P("users", None), P(("users", "items"), None)),
        check_vma=False,
    )
```

```python
import functools

import jax
import jax.numpy as jnp
from jax import lax
from jax.experimental import pallas as pl
from jax.experimental.pallas import tpu as pltpu
from jax.sharding import PartitionSpec as P

STRATA = 3
TILE = 64
F32 = jnp.float32
BF16 = jnp.bfloat16


def chunk_rows(rows):
    first = max(rows // 2 // TILE, 1) * TILE
    return [first, rows - first] if first < rows else [rows]


def tail_rows(rows):
    return rows // 2 // TILE * TILE


def psi_parts(x):
    small = x < 8.0
    w = jnp.where(small, x + 3.5, x - 0.5)
    q = x * (x + 3.0)
    q2 = q + 2.0
    bounded = jnp.minimum(w, 1e9)
    square = bounded * bounded
    steps = jnp.where(small, q * q2, 1.0)
    r = 1.0 / (square * steps)
    s = r * steps
    shift = (2.0 * x + 3.0) * (q + q2) * (r * square)
    g = s * (1.0 / 24.0 - s * (7.0 / 960.0 - s * (31.0 / 8064.0 - s * (127.0 / 30720.0))))
    return w, g - jnp.where(small, shift, 0.0)


def psi_any(x):
    mirrored = x < 0.5
    w, g = psi_parts(jnp.where(mirrored, 1.0 - x, x))
    value = jnp.log(w) + g
    t = x - jnp.floor(x + 0.5)
    u = 3.14159265358979 * t
    v = u * u
    sin = 1.0 / 6227020800.0
    for c in (-1.0 / 39916800.0, 1.0 / 362880.0, -1.0 / 5040.0, 1.0 / 120.0, -1.0 / 6.0, 1.0):
        sin = sin * v + c
    cos = -1.0 / 87178291200.0
    for c in (1.0 / 479001600.0, -1.0 / 3628800.0, 1.0 / 40320.0, -1.0 / 720.0, 1.0 / 24.0, -0.5, 1.0):
        cos = cos * v + c
    value = jnp.where(mirrored, value - 3.14159265358979 * cos / (sin * u), value)
    return jnp.where((x <= 0.0) & (x == jnp.floor(x)), jnp.nan, value)


LOWEST = 0.01


def above(low):
    return jnp.min(low) >= LOWEST


def folded(x):
    return x.reshape(x.shape[0] // 8, 8, x.shape[1])


def tiles(rows):
    step = TILE if rows % TILE == 0 else rows
    return [(at, step) for at in range(0, rows, step)]


def exp_tile(x, rte, general):
    shape = x.shape
    x = folded(x)
    if general:
        value = psi_any(x)
        if rte is not None:
            value = value - jnp.log(rte)[None]
        value = jnp.exp(value)
    else:
        w, g = psi_parts(x)
        value = w if rte is None else w * (1.0 / rte)[None]
        value = value * jnp.exp(g)
    mean = x if rte is None else x * (1.0 / rte)[None]
    return value.reshape(shape).astype(BF16), jnp.sum(mean, axis=0), jnp.min(x, axis=0)


def log_tile(x, rte, general):
    shape = x.shape
    x = folded(x)
    if general:
        value = psi_any(x) - jnp.log(rte)[None]
    else:
        w, g = psi_parts(x)
        value = (jnp.log(w) - jnp.log(rte)[None]) + g
    return value.reshape(shape).astype(BF16), jnp.min(x, axis=0)


def row_sum(x):
    return jnp.broadcast_to(jnp.sum(x, axis=0, keepdims=True), x.shape)


VMEM_SPEC = pl.BlockSpec(memory_space=pltpu.VMEM)
SMEM_SPEC = pl.BlockSpec(memory_space=pltpu.SMEM)
HBM_SPEC = pl.BlockSpec(memory_space=pltpu.HBM)
PARAMS = pltpu.CompilerParams(vmem_limit_bytes=24 * 2**20)


def in_hbm(x):
    return pltpu.with_memory_space_constraint(x, pltpu.HBM)


def in_vmem(x):
    return pltpu.with_memory_space_constraint(x, pltpu.VMEM)


def prepare_kernel(matchings_hbm, shape_hbm, item, *refs, last):
    choices, (matchings, shape, sems) = refs[:STRATA], refs[STRATA:]
    copies = [
        pltpu.make_async_copy(shape_hbm, shape, sems.at[0]),
        pltpu.make_async_copy(matchings_hbm, matchings, sems.at[1]),
    ]
    for copy in copies:
        copy.start()
    for copy in copies:
        copy.wait()
    item[...] = shape[...].astype(F32)
    choices[0][0] = matchings[0] - 1
    for stratum in range(1, STRATA - 1):
        choices[stratum][0] = jnp.bitwise_xor(matchings[stratum - 1], matchings[stratum]) - 1
    choices[STRATA - 1][0] = jnp.bitwise_xor(matchings[STRATA - 2], last) - 1


def prepare_call(matchings, item_shape, last):
    out = pl.pallas_call(
        functools.partial(prepare_kernel, last=last),
        out_shape=[jax.ShapeDtypeStruct(item_shape.shape, F32)]
        + [pltpu.SMEM((1,), jnp.int32)] * STRATA,
        in_specs=[HBM_SPEC, HBM_SPEC],
        out_specs=[VMEM_SPEC] + [SMEM_SPEC] * STRATA,
        scratch_shapes=[pltpu.SMEM(matchings.shape, jnp.int32), pltpu.VMEM(item_shape.shape, BF16),
                        pltpu.SemaphoreType.DMA((2,))],
        compiler_params=PARAMS,
        name="prepare",
    )(in_hbm(matchings), in_hbm(item_shape))
    return out[0], [choice[0] for choice in out[1:]]


def start_kernel(shape_hbm, interactions, uexp, theta, counts, shape, sems):
    rows, depth = shape.shape
    load = pltpu.make_async_copy(shape_hbm, shape, sems.at[0])
    ahead = pltpu.make_async_copy(interactions.at[0, pl.ds(0, counts.shape[0]), :], counts, sems.at[1])
    load.start()
    ahead.start()
    load.wait()

    def body(general):
        def step(i, carry):
            total, low = carry
            place = pl.ds(pl.multiple_of(i * TILE, TILE), TILE)
            value, part, part_low = exp_tile(shape[place, :].astype(F32), None, general)
            uexp[place, :] = value
            return total + part, jnp.minimum(low, part_low)

        total, low = lax.fori_loop(
            0, rows // TILE, step, (jnp.zeros((8, depth), F32), jnp.ones((8, depth), F32)))
        theta[...] = total
        return low

    low = body(False)

    @pl.when(jnp.logical_not(above(low)))
    def _():
        body(True)

    ahead.wait()


def start_call(user_shape, interactions, first_rows):
    rows, depth = user_shape.shape
    items = interactions.shape[2]
    return pl.pallas_call(
        start_kernel,
        out_shape=[pltpu.VMEM((rows, depth), BF16), pltpu.VMEM((8, depth), F32),
                   pltpu.VMEM((first_rows, items), BF16)],
        in_specs=[HBM_SPEC] * 2,
        out_specs=[VMEM_SPEC] * 3,
        scratch_shapes=[pltpu.VMEM((rows, depth), BF16), pltpu.SemaphoreType.DMA((2,))],
        compiler_params=PARAMS,
        cost_estimate=pl.CostEstimate(
            flops=40 * rows * depth, bytes_accessed=rows * depth * 4, transcendentals=2 * rows * depth),
        name="user_start",
    )(in_hbm(user_shape), in_hbm(interactions))


def stratum_kernel(names, *refs, stratum, at, rows, items, factor, first, last, tail, ahead):
    ref = dict(zip(names, refs))
    copies = {}

    def fetch(name, source, target):
        copies[name] = pltpu.make_async_copy(source, target, ref["sems"].at[len(copies)])
        copies[name].start()

    if "item_in" in ref:
        fetch("item", ref["item"], ref["item_in"])
    if ahead:
        fetch("ahead", ref["interactions"].at[ahead[0], pl.ds(ahead[1], ahead[2]), :], ref["counts_ahead"])
    upart, counts, ratios, denominator = ref["upart"], ref["counts"], ref["ratios"], ref["denominator"]
    uexp = ref["uexp_all"].at[pl.ds(at, rows), :] if stratum == 0 else ref["uexp"]
    extra = 8 if first else 0

    def wait(name, general):
        if name in copies and not general:
            copies[name].wait()

    def body(general):
        lows = []
        theta = None
        if stratum > 0:
            if first:
                beta = row_sum(ref["acc"][0:8, :] + ref["recv"][0:8, :])
                old = 1.0 if stratum == 1 else ref["rte_old"][...]
                rte = 0.5 * old + 0.5 * (0.3 + factor * beta)
                ref["rte_new"][...] = rte
            else:
                rte = ref["rte"][...]
            lows.append(rte)
            for t, step in tiles(rows):
                old = ref["user_shape"][at + t:at + t + step, :].astype(F32) if stratum == 1 else ref["shp_old"][t:t + step, :]
                stat = ref["acc"][extra + t:extra + t + step, :] + ref["recv"][extra + t:extra + t + step, :]
                shp = 0.5 * old + 0.5 * (0.3 + factor * stat)
                ref["shp_new"][t:t + step, :] = shp
                value, part, low = exp_tile(shp, rte, general)
                uexp[t:t + step, :] = value
                theta = part if theta is None else theta + part
                lows.append(low)
            if not first:
                theta = theta + ref["theta"][...]
        elif last:
            theta = ref["theta"][...]

        if first:
            wait("item", general)
            item = ref["item_in"] if "item_in" in ref else ref["item"]
            if not last:
                ref["item_kept"][...] = item[...]
        elif last:
            item = ref["item_kept"]
        if first or last:
            item_rte = None if stratum == 0 else item[items:items + 8, :]
        if first:
            value, sums, low = exp_tile(item[0:items, :], item_rte, general)
            ref["item_exp_new"][...] = value
            upart[0:8, :] = sums
            lows.append(low)
            if item_rte is not None:
                lows.append(item_rte)
            item_exp = value
        else:
            item_exp = ref["item_exp"][...]

        denominator[...] = lax.dot_general(
            uexp[...], item_exp, (((1,), (1,)), ((), ())), preferred_element_type=F32)
        for t, step in tiles(rows):
            ratios[t:t + step, :] = (
                counts[t:t + step, :].astype(F32) / denominator[t:t + step, :]).astype(BF16)
        user_sums = uexp[...].astype(F32) * jnp.dot(
            ratios[...], item_exp, preferred_element_type=F32)
        upart[extra:extra + rows - tail, :] = user_sums[0:rows - tail, :]
        if tail:
            ref["upart_tail"][...] = user_sums[rows - tail:, :]
        istat = lax.dot_general(ratios[...], uexp[...], (((0,), (0,)), ((), ())), preferred_element_type=F32)
        if not first:
            istat = istat + ref["istat"][...]
        if last:
            old = 1.0 if item_rte is None else item_rte
            ref["item_new"][0:items, :] = 0.5 * item[0:items, :] + 0.5 * (
                0.3 + factor * (item_exp.astype(F32) * istat))
            ref["item_new"][items:items + 8, :] = 0.5 * old + 0.5 * (0.3 + factor * row_sum(theta))
        else:
            ref["istat_new"][...] = istat
            if stratum > 0:
                ref["theta_new"][...] = theta
        return functools.reduce(jnp.minimum, lows) if lows else None

    low = body(False)
    if low is not None:

        @pl.when(jnp.logical_not(above(low)))
        def _():
            body(True)

    wait("ahead", False)


def stratum_call(stratum, at, rows, items, depth, factor, first, last, tail, ahead, operands):
    extra = 8 if first else 0
    outs = {"upart": ((rows + extra - tail, depth), F32)}
    if tail:
        outs["upart_tail"] = ((tail, depth), F32)
    if stratum > 0:
        outs["shp_new"] = ((rows, depth), F32)
    if first and stratum > 0:
        outs["rte_new"] = ((8, depth), F32)
    if first:
        outs["item_exp_new"] = ((items, depth), BF16)
    if first and not last:
        outs["item_kept"] = (operands["item"].shape, F32)
    if last:
        outs["item_new"] = ((items + 8, depth), F32)
    else:
        outs["istat_new"] = ((items, depth), F32)
        if stratum > 0:
            outs["theta_new"] = ((8, depth), F32)
    if ahead:
        outs["counts_ahead"] = ((ahead[2], items), BF16)
    scratch = {
        "ratios": pltpu.VMEM((rows, items), BF16),
        "denominator": pltpu.VMEM((rows, items), F32),
        "sems": pltpu.SemaphoreType.DMA((2,)),
    }
    if stratum > 0:
        scratch["uexp"] = pltpu.VMEM((rows, depth), BF16)
    if first and stratum > 0:
        scratch["item_in"] = pltpu.VMEM(operands["item"].shape, F32)
    hbm = ("interactions", "item") if stratum > 0 else ("interactions",)
    operands = {
        name: in_hbm(x) if name in hbm else in_vmem(x) if name in ("user_shape", "item") else x
        for name, x in operands.items()}
    names = list(operands) + list(outs) + list(scratch)
    kernel = functools.partial(
        stratum_kernel, names, stratum=stratum, at=at, rows=rows, items=items,
        factor=factor, first=first, last=last, tail=tail, ahead=ahead)
    results = pl.pallas_call(
        kernel,
        out_shape=[jax.ShapeDtypeStruct(*spec) for spec in outs.values()],
        in_specs=[HBM_SPEC if name in hbm else VMEM_SPEC for name in operands],
        out_specs=[VMEM_SPEC] * len(outs),
        scratch_shapes=list(scratch.values()),
        compiler_params=PARAMS,
        cost_estimate=pl.CostEstimate(flops=1, bytes_accessed=1, transcendentals=0),
        name=f"stratum{stratum}_at{at}",
    )(*operands.values())
    return dict(zip(outs, results))


def user_log_kernel(*refs, at, rows, shp_at, factor, first, filled):
    acc, recv, shp_old, rte_in = refs[:4]
    rest = refs[5:] if filled else refs[4:]
    if first:
        out, rte_out, block, sem = rest
        beta = row_sum(acc[0:8, :] + recv[0:8, :])
        rte = 0.5 * rte_in[...] + 0.5 * (0.3 + factor * beta)
        rte_out[...] = rte
    else:
        out, block, sem = rest
        rte = rte_in[...]
    extra = 8 if first else 0

    def body(general):
        low = rte
        for t, step in tiles(rows):
            stat = acc[extra + t:extra + t + step, :] + recv[extra + t:extra + t + step, :]
            shp = 0.5 * shp_old[shp_at + t:shp_at + t + step, :] + 0.5 * (0.3 + factor * stat)
            block[t:t + step, :], part_low = log_tile(shp, rte, general)
            low = jnp.minimum(low, part_low)
        return low

    low = body(False)

    @pl.when(jnp.logical_not(above(low)))
    def _():
        body(True)

    copy = pltpu.make_async_copy(block, out.at[pl.ds(at, rows), :], sem)
    copy.start()
    copy.wait()


def user_log_call(at, rows, shp_at, total, depth, factor, first, operands, filled):
    out_shape = [jax.ShapeDtypeStruct((total, depth), BF16)]
    out_specs = [HBM_SPEC]
    if first:
        out_shape.append(jax.ShapeDtypeStruct((8, depth), F32))
        out_specs.append(VMEM_SPEC)
    operands = list(operands)
    in_specs = [VMEM_SPEC] * 4
    if filled is not None:
        operands.append(filled)
        in_specs.append(HBM_SPEC)
    return pl.pallas_call(
        functools.partial(user_log_kernel, at=at, rows=rows, shp_at=shp_at, factor=factor, first=first,
                          filled=filled is not None),
        out_shape=out_shape,
        in_specs=in_specs,
        out_specs=out_specs,
        input_output_aliases={} if filled is None else {4: 0},
        scratch_shapes=[pltpu.VMEM((rows, depth), BF16), pltpu.SemaphoreType.DMA],
        compiler_params=PARAMS,
        cost_estimate=pl.CostEstimate(
            flops=40 * rows * depth, bytes_accessed=rows * depth * 14, transcendentals=rows * depth),
        name=f"user_log_at{at}",
    )(*operands)


def item_log_kernel(item, _, out, *, items):
    rte = item[items:items + 8, :]

    def body(general):
        out[...], low = log_tile(item[0:items, :], rte, general)
        return low

    low = body(False)

    @pl.when(jnp.logical_not(above(jnp.minimum(low, rte))))
    def _():
        body(True)


def item_log_call(item, after, items, depth):
    return pl.pallas_call(
        functools.partial(item_log_kernel, items=items),
        out_shape=jax.ShapeDtypeStruct((items, depth), BF16),
        in_specs=[VMEM_SPEC, VMEM_SPEC],
        out_specs=VMEM_SPEC,
        compiler_params=PARAMS,
        cost_estimate=pl.CostEstimate(
            flops=40 * items * depth, bytes_accessed=items * depth * 6, transcendentals=items * depth),
        name="item_log",
    )(item, after)


def swapped(value, axis, mask):
    return lax.ppermute(value, axis, [(a, a ^ mask) for a in range(lax.axis_size(axis))])


def moved(choice, value, then=None, operands=()):
    def branch(mask, value, *operands):
        arrived = swapped(value, "users", mask)
        return arrived if then is None else then(arrived, *operands)

    choices = [functools.partial(branch, mask) for mask in range(1, lax.axis_size("users"))]
    return lax.switch(choice, choices, value, *operands)


def exchanged(value):
    size = lax.axis_size("items")
    if size == 1:
        return value, jnp.zeros_like(value)
    mask = 1
    while mask * 2 < size:
        value = value + swapped(value, "items", mask)
        mask *= 2
    return value, swapped(value, "items", mask)


def per_device(interactions, matchings, user_shape, item_shape):
    group = lax.axis_size("users")
    factor = float(group)
    users, depth = user_shape.shape
    items = item_shape.shape[0]
    sizes = chunk_rows(users)
    starts = [sum(sizes[:i]) for i in range(len(sizes))]
    count = len(sizes)

    item, choices = prepare_call(matchings, item_shape, group - 1)
    order = [(s, at, rows) for s in range(STRATA) for at, rows in zip(starts, sizes)]

    def opening(arrived, user_shape, interactions):
        uexp, theta, counts = start_call(user_shape, interactions, sizes[0])
        operands = {"interactions": interactions, "counts": counts, "uexp_all": uexp, "item": arrived}
        if count == 1:
            operands["theta"] = theta
        out = stratum_call(0, 0, sizes[0], items, depth, factor, True, count == 1, 0, order[1], operands)
        return uexp, theta, out

    uexp, theta, opened = moved(choices[0], item, opening, (user_shape, interactions))
    rte = None
    shp = [None] * count
    sums = [None] * count
    for stratum in range(STRATA):
        carried = {"theta": theta}
        for i, (at, rows) in enumerate(zip(starts, sizes)):
            first, last = i == 0, i == count - 1
            step = stratum * count + i
            ahead = order[step + 1] if step + 1 < len(order) else None
            tail = tail_rows(rows) if last and stratum == STRATA - 1 else 0
            operands = {"counts": counts} if step else {}
            if ahead:
                operands["interactions"] = interactions
            if stratum == 0:
                operands["uexp_all"] = uexp
            else:
                operands["acc"], operands["recv"] = sums[i]
                if stratum == 1:
                    operands["user_shape"] = user_shape
                else:
                    operands["shp_old"] = shp[i]
                if not first:
                    operands["rte"] = rte
                elif stratum > 1:
                    operands["rte_old"] = rte
            if first:
                operands["item"] = item
            elif last:
                operands["item_kept"] = carried["item_kept"]
            if not first:
                operands["item_exp"] = carried["item_exp"]
                operands["istat"] = carried["istat"]
            if (stratum > 0 and not first) or (stratum == 0 and last):
                operands["theta"] = carried["theta"]
            if step == 0:
                out = opened
            else:
                out = stratum_call(
                    stratum, at, rows, items, depth, factor, first, last, tail, ahead, operands)
            counts = out.get("counts_ahead")
            shp[i] = out.get("shp_new")
            sums[i] = exchanged(out["upart"])
            if tail:
                tail_sums = exchanged(out["upart_tail"])
            if first:
                rte = out.get("rte_new")
                carried["item_exp"] = out["item_exp_new"]
                carried["item_kept"] = out.get("item_kept")
            if last:
                item = out["item_new"]
            else:
                carried["istat"] = out["istat_new"]
                if stratum > 0:
                    carried["theta"] = out["theta_new"]
        if stratum + 1 < STRATA:
            item = moved(choices[stratum + 1], item)
        else:
            item = swapped(item, "users", group - 1)
    user_log = None
    pieces = [(at, rows, 0, sums[i], shp[i]) for i, (at, rows) in enumerate(zip(starts, sizes))]
    if tail:
        at, rows = starts[-1], sizes[-1] - tail
        pieces[-1:] = [(at, rows, 0, sums[-1], shp[-1]), (at + rows, tail, rows, tail_sums, shp[-1])]
    for i, (at, rows, shp_at, piece_sums, piece_shp) in enumerate(pieces):
        out = user_log_call(
            at, rows, shp_at, users, depth, factor, i == 0, (*piece_sums, piece_shp, rte), user_log)
        user_log = out[0]
        if i == 0:
            rte = out[1]
            item_log = item_log_call(item, rte, items, depth)
    return user_log, item_log


def solution(mesh):
    placed = (P(None, "users", "items"), P(), P("users", None), P(("users", "items"), None))
    return jax.shard_map(
        per_device,
        mesh=mesh,
        in_specs=placed,
        out_specs=(P("users", None), P(("users", "items"), None)),
        check_vma=False,
    )
```

```python
import functools

import jax
import jax.numpy as jnp
from jax import lax
from jax.experimental import pallas as pl
from jax.experimental.pallas import tpu as pltpu
from jax.sharding import PartitionSpec as P

STRATA = 3
TILE = 64
START_TILE = 128
F32 = jnp.float32
BF16 = jnp.bfloat16


def chunk_rows(rows):
    first = max(rows // 2 // TILE, 1) * TILE
    return [first, rows - first] if first < rows else [rows]


def tail_rows(rows):
    return rows // 2 // TILE * TILE


def psi_parts(x):
    small = x < 8.0
    w = jnp.where(small, x + 3.5, x - 0.5)
    q = x * (x + 3.0)
    q2 = q + 2.0
    bounded = jnp.minimum(w, 1e9)
    square = bounded * bounded
    steps = jnp.where(small, q * q2, 1.0)
    r = 1.0 / (square * steps)
    s = r * steps
    shift = (2.0 * x + 3.0) * (q + q2) * (r * square)
    g = s * (1.0 / 24.0 - s * (7.0 / 960.0 - s * (31.0 / 8064.0 - s * (127.0 / 30720.0))))
    return w, g - jnp.where(small, shift, 0.0)


def psi_any(x):
    mirrored = x < 0.5
    w, g = psi_parts(jnp.where(mirrored, 1.0 - x, x))
    value = jnp.log(w) + g
    t = x - jnp.floor(x + 0.5)
    u = 3.14159265358979 * t
    v = u * u
    sin = 1.0 / 6227020800.0
    for c in (-1.0 / 39916800.0, 1.0 / 362880.0, -1.0 / 5040.0, 1.0 / 120.0, -1.0 / 6.0, 1.0):
        sin = sin * v + c
    cos = -1.0 / 87178291200.0
    for c in (1.0 / 479001600.0, -1.0 / 3628800.0, 1.0 / 40320.0, -1.0 / 720.0, 1.0 / 24.0, -0.5, 1.0):
        cos = cos * v + c
    value = jnp.where(mirrored, value - 3.14159265358979 * cos / (sin * u), value)
    return jnp.where((x <= 0.0) & (x == jnp.floor(x)), jnp.nan, value)


LOWEST = 0.01


def above(low):
    return jnp.min(low) >= LOWEST


def folded(x):
    return x.reshape(x.shape[0] // 8, 8, x.shape[1])


def tiles(rows):
    step = TILE if rows % TILE == 0 else rows
    return [(at, step) for at in range(0, rows, step)]


def exp_tile(x, rte, general):
    shape = x.shape
    x = folded(x)
    if general:
        value = psi_any(x)
        if rte is not None:
            value = value - jnp.log(rte)[None]
        value = jnp.exp(value)
    else:
        w, g = psi_parts(x)
        value = w if rte is None else w * (1.0 / rte)[None]
        value = value * jnp.exp(g)
    mean = x if rte is None else x * (1.0 / rte)[None]
    return value.reshape(shape).astype(BF16), jnp.sum(mean, axis=0), jnp.min(x, axis=0)


def log_tile(x, rte, general):
    shape = x.shape
    x = folded(x)
    if general:
        value = psi_any(x) - jnp.log(rte)[None]
    else:
        w, g = psi_parts(x)
        value = (jnp.log(w) - jnp.log(rte)[None]) + g
    return value.reshape(shape).astype(BF16), jnp.min(x, axis=0)


def row_sum(x):
    return jnp.broadcast_to(jnp.sum(x, axis=0, keepdims=True), x.shape)


VMEM_SPEC = pl.BlockSpec(memory_space=pltpu.VMEM)
SMEM_SPEC = pl.BlockSpec(memory_space=pltpu.SMEM)
HBM_SPEC = pl.BlockSpec(memory_space=pltpu.HBM)
PARAMS = pltpu.CompilerParams(vmem_limit_bytes=24 * 2**20)


def in_hbm(x):
    return pltpu.with_memory_space_constraint(x, pltpu.HBM)


def in_vmem(x):
    return pltpu.with_memory_space_constraint(x, pltpu.VMEM)


def prepare_kernel(matchings_hbm, shape_hbm, item, *refs, last):
    choices, (matchings, shape, sems) = refs[:STRATA], refs[STRATA:]
    copies = [
        pltpu.make_async_copy(shape_hbm, shape, sems.at[0]),
        pltpu.make_async_copy(matchings_hbm, matchings, sems.at[1]),
    ]
    for copy in copies:
        copy.start()
    for copy in copies:
        copy.wait()
    item[...] = shape[...].astype(F32)
    choices[0][0] = matchings[0] - 1
    for stratum in range(1, STRATA - 1):
        choices[stratum][0] = jnp.bitwise_xor(matchings[stratum - 1], matchings[stratum]) - 1
    choices[STRATA - 1][0] = jnp.bitwise_xor(matchings[STRATA - 2], last) - 1


def prepare_call(matchings, item_shape, last):
    out = pl.pallas_call(
        functools.partial(prepare_kernel, last=last),
        out_shape=[jax.ShapeDtypeStruct(item_shape.shape, F32)]
        + [pltpu.SMEM((1,), jnp.int32)] * STRATA,
        in_specs=[HBM_SPEC, HBM_SPEC],
        out_specs=[VMEM_SPEC] + [SMEM_SPEC] * STRATA,
        scratch_shapes=[pltpu.SMEM(matchings.shape, jnp.int32), pltpu.VMEM(item_shape.shape, BF16),
                        pltpu.SemaphoreType.DMA((2,))],
        compiler_params=PARAMS,
        name="prepare",
    )(in_hbm(matchings), in_hbm(item_shape))
    return out[0], [choice[0] for choice in out[1:]]


def start_kernel(shape_hbm, interactions, uexp, theta, counts, shape, sems):
    rows, depth = shape.shape
    load = pltpu.make_async_copy(shape_hbm, shape, sems.at[0])
    ahead = pltpu.make_async_copy(interactions.at[0, pl.ds(0, counts.shape[0]), :], counts, sems.at[1])
    load.start()
    ahead.start()
    load.wait()

    def body(general):
        def step(i, carry):
            total, low = carry
            place = pl.ds(pl.multiple_of(i * START_TILE, START_TILE), START_TILE)
            value, part, part_low = exp_tile(shape[place, :].astype(F32), None, general)
            uexp[place, :] = value
            return total + part, jnp.minimum(low, part_low)

        total, low = lax.fori_loop(
            0, rows // START_TILE, step, (jnp.zeros((8, depth), F32), jnp.ones((8, depth), F32)))
        theta[...] = total
        return low

    low = body(False)

    @pl.when(jnp.logical_not(above(low)))
    def _():
        body(True)

    ahead.wait()


def start_call(user_shape, interactions, first_rows):
    rows, depth = user_shape.shape
    items = interactions.shape[2]
    return pl.pallas_call(
        start_kernel,
        out_shape=[pltpu.VMEM((rows, depth), BF16), pltpu.VMEM((8, depth), F32),
                   pltpu.VMEM((first_rows, items), BF16)],
        in_specs=[HBM_SPEC] * 2,
        out_specs=[VMEM_SPEC] * 3,
        scratch_shapes=[pltpu.VMEM((rows, depth), BF16), pltpu.SemaphoreType.DMA((2,))],
        compiler_params=PARAMS,
        cost_estimate=pl.CostEstimate(
            flops=40 * rows * depth, bytes_accessed=rows * depth * 4, transcendentals=2 * rows * depth),
        name="user_start",
    )(in_hbm(user_shape), in_hbm(interactions))


def stratum_kernel(names, *refs, stratum, at, rows, items, factor, first, last, tail, ahead):
    ref = dict(zip(names, refs))
    copies = {}

    def fetch(name, source, target):
        copies[name] = pltpu.make_async_copy(source, target, ref["sems"].at[len(copies)])
        copies[name].start()

    if "item_in" in ref:
        fetch("item", ref["item"], ref["item_in"])
    if ahead:
        fetch("ahead", ref["interactions"].at[ahead[0], pl.ds(ahead[1], ahead[2]), :], ref["counts_ahead"])
    upart, counts, ratios, denominator = ref["upart"], ref["counts"], ref["ratios"], ref["denominator"]
    uexp = ref["uexp_all"].at[pl.ds(at, rows), :] if stratum == 0 else ref["uexp"]
    extra = 8 if first else 0

    def wait(name, general):
        if name in copies and not general:
            copies[name].wait()

    def body(general):
        lows = []
        theta = None
        if stratum > 0:
            if first:
                beta = row_sum(ref["acc"][0:8, :] + ref["recv"][0:8, :])
                old = 1.0 if stratum == 1 else ref["rte_old"][...]
                rte = 0.5 * old + 0.5 * (0.3 + factor * beta)
                ref["rte_new"][...] = rte
            else:
                rte = ref["rte"][...]
            lows.append(rte)
            for t, step in tiles(rows):
                old = ref["user_shape"][at + t:at + t + step, :].astype(F32) if stratum == 1 else ref["shp_old"][t:t + step, :]
                stat = ref["acc"][extra + t:extra + t + step, :] + ref["recv"][extra + t:extra + t + step, :]
                shp = 0.5 * old + 0.5 * (0.3 + factor * stat)
                ref["shp_new"][t:t + step, :] = shp
                value, part, low = exp_tile(shp, rte, general)
                uexp[t:t + step, :] = value
                theta = part if theta is None else theta + part
                lows.append(low)
            if not first:
                theta = theta + ref["theta"][...]
        elif last:
            theta = ref["theta"][...]

        if first:
            wait("item", general)
            item = ref["item_in"] if "item_in" in ref else ref["item"]
            if not last:
                ref["item_kept"][...] = item[...]
        elif last:
            item = ref["item_kept"]
        if first or last:
            item_rte = None if stratum == 0 else item[items:items + 8, :]
        if first:
            value, sums, low = exp_tile(item[0:items, :], item_rte, general)
            ref["item_exp_new"][...] = value
            upart[0:8, :] = sums
            lows.append(low)
            if item_rte is not None:
                lows.append(item_rte)
            item_exp = value
        else:
            item_exp = ref["item_exp"][...]

        denominator[...] = lax.dot_general(
            uexp[...], item_exp, (((1,), (1,)), ((), ())), preferred_element_type=F32)
        for t, step in tiles(rows):
            ratios[t:t + step, :] = (
                counts[t:t + step, :].astype(F32) / denominator[t:t + step, :]).astype(BF16)
        user_sums = uexp[...].astype(F32) * jnp.dot(
            ratios[...], item_exp, preferred_element_type=F32)
        upart[extra:extra + rows - tail, :] = user_sums[0:rows - tail, :]
        if tail:
            ref["upart_tail"][...] = user_sums[rows - tail:, :]
        istat = lax.dot_general(ratios[...], uexp[...], (((0,), (0,)), ((), ())), preferred_element_type=F32)
        if not first:
            istat = istat + ref["istat"][...]
        if last:
            old = 1.0 if item_rte is None else item_rte
            ref["item_new"][0:items, :] = 0.5 * item[0:items, :] + 0.5 * (
                0.3 + factor * (item_exp.astype(F32) * istat))
            ref["item_new"][items:items + 8, :] = 0.5 * old + 0.5 * (0.3 + factor * row_sum(theta))
        else:
            ref["istat_new"][...] = istat
            if stratum > 0:
                ref["theta_new"][...] = theta
        return functools.reduce(jnp.minimum, lows) if lows else None

    low = body(False)
    if low is not None:

        @pl.when(jnp.logical_not(above(low)))
        def _():
            body(True)

    wait("ahead", False)


def stratum_call(stratum, at, rows, items, depth, factor, first, last, tail, ahead, operands):
    extra = 8 if first else 0
    outs = {"upart": ((rows + extra - tail, depth), F32)}
    if tail:
        outs["upart_tail"] = ((tail, depth), F32)
    if stratum > 0:
        outs["shp_new"] = ((rows, depth), F32)
    if first and stratum > 0:
        outs["rte_new"] = ((8, depth), F32)
    if first:
        outs["item_exp_new"] = ((items, depth), BF16)
    if first and not last:
        outs["item_kept"] = (operands["item"].shape, F32)
    if last:
        outs["item_new"] = ((items + 8, depth), F32)
    else:
        outs["istat_new"] = ((items, depth), F32)
        if stratum > 0:
            outs["theta_new"] = ((8, depth), F32)
    if ahead:
        outs["counts_ahead"] = ((ahead[2], items), BF16)
    scratch = {
        "ratios": pltpu.VMEM((rows, items), BF16),
        "denominator": pltpu.VMEM((rows, items), F32),
        "sems": pltpu.SemaphoreType.DMA((2,)),
    }
    if stratum > 0:
        scratch["uexp"] = pltpu.VMEM((rows, depth), BF16)
    if first:
        scratch["item_in"] = pltpu.VMEM(operands["item"].shape, F32)
    hbm = ("interactions", "item")
    operands = {
        name: in_hbm(x) if name in hbm else in_vmem(x) if name == "user_shape" else x
        for name, x in operands.items()}
    names = list(operands) + list(outs) + list(scratch)
    kernel = functools.partial(
        stratum_kernel, names, stratum=stratum, at=at, rows=rows, items=items,
        factor=factor, first=first, last=last, tail=tail, ahead=ahead)
    results = pl.pallas_call(
        kernel,
        out_shape=[jax.ShapeDtypeStruct(*spec) for spec in outs.values()],
        in_specs=[HBM_SPEC if name in hbm else VMEM_SPEC for name in operands],
        out_specs=[VMEM_SPEC] * len(outs),
        scratch_shapes=list(scratch.values()),
        compiler_params=PARAMS,
        cost_estimate=pl.CostEstimate(flops=1, bytes_accessed=1, transcendentals=0),
        name=f"stratum{stratum}_at{at}",
    )(*operands.values())
    return dict(zip(outs, results))


def user_log_kernel(*refs, at, rows, shp_at, factor, first, filled):
    acc, recv, shp_old, rte_in = refs[:4]
    rest = refs[5:] if filled else refs[4:]
    if first:
        out, rte_out, block, sem = rest
        beta = row_sum(acc[0:8, :] + recv[0:8, :])
        rte = 0.5 * rte_in[...] + 0.5 * (0.3 + factor * beta)
        rte_out[...] = rte
    else:
        out, block, sem = rest
        rte = rte_in[...]
    extra = 8 if first else 0

    def body(general):
        low = rte
        for t, step in tiles(rows):
            stat = acc[extra + t:extra + t + step, :] + recv[extra + t:extra + t + step, :]
            shp = 0.5 * shp_old[shp_at + t:shp_at + t + step, :] + 0.5 * (0.3 + factor * stat)
            block[t:t + step, :], part_low = log_tile(shp, rte, general)
            low = jnp.minimum(low, part_low)
        return low

    low = body(False)

    @pl.when(jnp.logical_not(above(low)))
    def _():
        body(True)

    copy = pltpu.make_async_copy(block, out.at[pl.ds(at, rows), :], sem)
    copy.start()
    copy.wait()


def user_log_call(at, rows, shp_at, total, depth, factor, first, operands, filled):
    out_shape = [jax.ShapeDtypeStruct((total, depth), BF16)]
    out_specs = [HBM_SPEC]
    if first:
        out_shape.append(jax.ShapeDtypeStruct((8, depth), F32))
        out_specs.append(VMEM_SPEC)
    operands = list(operands)
    in_specs = [VMEM_SPEC] * 4
    if filled is not None:
        operands.append(filled)
        in_specs.append(HBM_SPEC)
    return pl.pallas_call(
        functools.partial(user_log_kernel, at=at, rows=rows, shp_at=shp_at, factor=factor, first=first,
                          filled=filled is not None),
        out_shape=out_shape,
        in_specs=in_specs,
        out_specs=out_specs,
        input_output_aliases={} if filled is None else {4: 0},
        scratch_shapes=[pltpu.VMEM((rows, depth), BF16), pltpu.SemaphoreType.DMA],
        compiler_params=PARAMS,
        cost_estimate=pl.CostEstimate(
            flops=40 * rows * depth, bytes_accessed=rows * depth * 14, transcendentals=rows * depth),
        name=f"user_log_at{at}",
    )(*operands)


def item_log_kernel(item, _, out, *, items):
    rte = item[items:items + 8, :]

    def body(general):
        out[...], low = log_tile(item[0:items, :], rte, general)
        return low

    low = body(False)

    @pl.when(jnp.logical_not(above(jnp.minimum(low, rte))))
    def _():
        body(True)


def item_log_call(item, after, items, depth):
    return pl.pallas_call(
        functools.partial(item_log_kernel, items=items),
        out_shape=jax.ShapeDtypeStruct((items, depth), BF16),
        in_specs=[VMEM_SPEC, VMEM_SPEC],
        out_specs=VMEM_SPEC,
        compiler_params=PARAMS,
        cost_estimate=pl.CostEstimate(
            flops=40 * items * depth, bytes_accessed=items * depth * 6, transcendentals=items * depth),
        name="item_log",
    )(item, after)


def swapped(value, axis, mask):
    return lax.ppermute(value, axis, [(a, a ^ mask) for a in range(lax.axis_size(axis))])


def moved(choice, value, then=None, operands=()):
    def branch(mask, value, *operands):
        arrived = swapped(value, "users", mask)
        return arrived if then is None else then(arrived, *operands)

    choices = [functools.partial(branch, mask) for mask in range(1, lax.axis_size("users"))]
    return lax.switch(choice, choices, value, *operands)


def exchanged(value):
    size = lax.axis_size("items")
    if size == 1:
        return value, jnp.zeros_like(value)
    mask = 1
    while mask * 2 < size:
        value = value + swapped(value, "items", mask)
        mask *= 2
    return value, swapped(value, "items", mask)


def per_device(interactions, matchings, user_shape, item_shape):
    group = lax.axis_size("users")
    factor = float(group)
    users, depth = user_shape.shape
    items = item_shape.shape[0]
    sizes = chunk_rows(users)
    starts = [sum(sizes[:i]) for i in range(len(sizes))]
    count = len(sizes)

    item, choices = prepare_call(matchings, item_shape, group - 1)
    order = [(s, at, rows) for s in range(STRATA) for at, rows in zip(starts, sizes)]

    def opening(arrived, user_shape, interactions):
        return arrived, start_call(user_shape, interactions, sizes[0])

    item, (uexp, theta, counts) = moved(choices[0], item, opening, (user_shape, interactions))
    rte = None
    shp = [None] * count
    sums = [None] * count
    for stratum in range(STRATA):
        carried = {"theta": theta}
        for i, (at, rows) in enumerate(zip(starts, sizes)):
            first, last = i == 0, i == count - 1
            step = stratum * count + i
            ahead = order[step + 1] if step + 1 < len(order) else None
            tail = tail_rows(rows) if last and stratum == STRATA - 1 else 0
            operands = {"counts": counts}
            if ahead:
                operands["interactions"] = interactions
            if stratum == 0:
                operands["uexp_all"] = uexp
            else:
                operands["acc"], operands["recv"] = sums[i]
                if stratum == 1:
                    operands["user_shape"] = user_shape
                else:
                    operands["shp_old"] = shp[i]
                if not first:
                    operands["rte"] = rte
                elif stratum > 1:
                    operands["rte_old"] = rte
            if first:
                operands["item"] = item
            elif last:
                operands["item_kept"] = carried["item_kept"]
            if not first:
                operands["item_exp"] = carried["item_exp"]
                operands["istat"] = carried["istat"]
            if (stratum > 0 and not first) or (stratum == 0 and last):
                operands["theta"] = carried["theta"]
            out = stratum_call(
                stratum, at, rows, items, depth, factor, first, last, tail, ahead, operands)
            counts = out.get("counts_ahead")
            shp[i] = out.get("shp_new")
            sums[i] = exchanged(out["upart"])
            if tail:
                tail_sums = exchanged(out["upart_tail"])
            if first:
                rte = out.get("rte_new")
                carried["item_exp"] = out["item_exp_new"]
                carried["item_kept"] = out.get("item_kept")
            if last:
                item = out["item_new"]
            else:
                carried["istat"] = out["istat_new"]
                if stratum > 0:
                    carried["theta"] = out["theta_new"]
        if stratum + 1 < STRATA:
            item = moved(choices[stratum + 1], item)
        else:
            item = swapped(item, "users", group - 1)
    user_log = None
    pieces = [(at, rows, 0, sums[i], shp[i]) for i, (at, rows) in enumerate(zip(starts, sizes))]
    if tail:
        at, rows = starts[-1], sizes[-1] - tail
        pieces[-1:] = [(at, rows, 0, sums[-1], shp[-1]), (at + rows, tail, rows, tail_sums, shp[-1])]
    for i, (at, rows, shp_at, piece_sums, piece_shp) in enumerate(pieces):
        out = user_log_call(
            at, rows, shp_at, users, depth, factor, i == 0, (*piece_sums, piece_shp, rte), user_log)
        user_log = out[0]
        if i == 0:
            rte = out[1]
            item_log = item_log_call(item, rte, items, depth)
    return user_log, item_log


def solution(mesh):
    placed = (P(None, "users", "items"), P(), P("users", None), P(("users", "items"), None))
    return jax.shard_map(
        per_device,
        mesh=mesh,
        in_specs=placed,
        out_specs=(P("users", None), P(("users", "items"), None)),
        check_vma=False,
    )
```

```python
import functools

import jax
import jax.numpy as jnp
from jax import lax
from jax.experimental import pallas as pl
from jax.experimental.pallas import tpu as pltpu
from jax.sharding import PartitionSpec as P

STRATA = 3
TILE = 64
START_TILE = 128
F32 = jnp.float32
BF16 = jnp.bfloat16


def chunk_rows(rows):
    first = max(rows // 2 // TILE, 1) * TILE
    return [first, rows - first] if first < rows else [rows]


def tail_rows(rows):
    return rows // 2 // TILE * TILE


def psi_parts(x):
    small = x < 8.0
    w = jnp.where(small, x + 3.5, x - 0.5)
    q = x * (x + 3.0)
    q2 = q + 2.0
    bounded = jnp.minimum(w, 1e9)
    square = bounded * bounded
    steps = jnp.where(small, q * q2, 1.0)
    r = 1.0 / (square * steps)
    s = r * steps
    shift = (2.0 * x + 3.0) * (q + q2) * (r * square)
    g = s * (1.0 / 24.0 - s * (7.0 / 960.0 - s * (31.0 / 8064.0 - s * (127.0 / 30720.0))))
    return w, g - jnp.where(small, shift, 0.0)


def psi_any(x):
    mirrored = x < 0.5
    w, g = psi_parts(jnp.where(mirrored, 1.0 - x, x))
    value = jnp.log(w) + g
    t = x - jnp.floor(x + 0.5)
    u = 3.14159265358979 * t
    v = u * u
    sin = 1.0 / 6227020800.0
    for c in (-1.0 / 39916800.0, 1.0 / 362880.0, -1.0 / 5040.0, 1.0 / 120.0, -1.0 / 6.0, 1.0):
        sin = sin * v + c
    cos = -1.0 / 87178291200.0
    for c in (1.0 / 479001600.0, -1.0 / 3628800.0, 1.0 / 40320.0, -1.0 / 720.0, 1.0 / 24.0, -0.5, 1.0):
        cos = cos * v + c
    value = jnp.where(mirrored, value - 3.14159265358979 * cos / (sin * u), value)
    return jnp.where((x <= 0.0) & (x == jnp.floor(x)), jnp.nan, value)


LOWEST = 0.01


def above(low):
    return jnp.min(low) >= LOWEST


def folded(x):
    return x.reshape(x.shape[0] // 8, 8, x.shape[1])


def tiles(rows):
    step = TILE if rows % TILE == 0 else rows
    return [(at, step) for at in range(0, rows, step)]


def exp_tile(x, rte, general):
    shape = x.shape
    x = folded(x)
    if general:
        value = psi_any(x)
        if rte is not None:
            value = value - jnp.log(rte)[None]
        value = jnp.exp(value)
    else:
        w, g = psi_parts(x)
        value = w if rte is None else w * (1.0 / rte)[None]
        value = value * jnp.exp(g)
    mean = x if rte is None else x * (1.0 / rte)[None]
    return value.reshape(shape).astype(BF16), jnp.sum(mean, axis=0), jnp.min(x, axis=0)


def log_tile(x, rte, general):
    shape = x.shape
    x = folded(x)
    if general:
        value = psi_any(x) - jnp.log(rte)[None]
    else:
        w, g = psi_parts(x)
        value = (jnp.log(w) - jnp.log(rte)[None]) + g
    return value.reshape(shape).astype(BF16), jnp.min(x, axis=0)


def row_sum(x):
    return jnp.broadcast_to(jnp.sum(x, axis=0, keepdims=True), x.shape)


VMEM_SPEC = pl.BlockSpec(memory_space=pltpu.VMEM)
SMEM_SPEC = pl.BlockSpec(memory_space=pltpu.SMEM)
HBM_SPEC = pl.BlockSpec(memory_space=pltpu.HBM)
PARAMS = pltpu.CompilerParams(vmem_limit_bytes=24 * 2**20)


def in_hbm(x):
    return pltpu.with_memory_space_constraint(x, pltpu.HBM)


def in_vmem(x):
    return pltpu.with_memory_space_constraint(x, pltpu.VMEM)


def prepare_kernel(matchings_hbm, shape_hbm, item, *refs, last):
    choices, (matchings, shape, sems) = refs[:STRATA], refs[STRATA:]
    copies = [
        pltpu.make_async_copy(shape_hbm, shape, sems.at[0]),
        pltpu.make_async_copy(matchings_hbm, matchings, sems.at[1]),
    ]
    for copy in copies:
        copy.start()
    for copy in copies:
        copy.wait()
    item[...] = shape[...].astype(F32)
    choices[0][0] = matchings[0] - 1
    for stratum in range(1, STRATA - 1):
        choices[stratum][0] = jnp.bitwise_xor(matchings[stratum - 1], matchings[stratum]) - 1
    choices[STRATA - 1][0] = jnp.bitwise_xor(matchings[STRATA - 2], last) - 1


def prepare_call(matchings, item_shape, last):
    out = pl.pallas_call(
        functools.partial(prepare_kernel, last=last),
        out_shape=[jax.ShapeDtypeStruct(item_shape.shape, F32)]
        + [pltpu.SMEM((1,), jnp.int32)] * STRATA,
        in_specs=[HBM_SPEC, HBM_SPEC],
        out_specs=[VMEM_SPEC] + [SMEM_SPEC] * STRATA,
        scratch_shapes=[pltpu.SMEM(matchings.shape, jnp.int32), pltpu.VMEM(item_shape.shape, BF16),
                        pltpu.SemaphoreType.DMA((2,))],
        compiler_params=PARAMS,
        name="prepare",
    )(in_hbm(matchings), in_hbm(item_shape))
    return out[0], [choice[0] for choice in out[1:]]


def start_kernel(shape_hbm, interactions, uexp, theta, counts, shape, sems):
    rows, depth = shape.shape
    load = pltpu.make_async_copy(shape_hbm, shape, sems.at[0])
    ahead = pltpu.make_async_copy(interactions.at[0, pl.ds(0, counts.shape[0]), :], counts, sems.at[1])
    load.start()
    ahead.start()
    load.wait()

    def body(general):
        def step(i, carry):
            total, low = carry
            place = pl.ds(pl.multiple_of(i * START_TILE, START_TILE), START_TILE)
            value, part, part_low = exp_tile(shape[place, :].astype(F32), None, general)
            uexp[place, :] = value
            return total + part, jnp.minimum(low, part_low)

        total, low = lax.fori_loop(
            0, rows // START_TILE, step, (jnp.zeros((8, depth), F32), jnp.ones((8, depth), F32)))
        theta[...] = total
        return low

    low = body(False)

    @pl.when(jnp.logical_not(above(low)))
    def _():
        body(True)

    ahead.wait()


def start_call(user_shape, interactions, first_rows):
    rows, depth = user_shape.shape
    items = interactions.shape[2]
    return pl.pallas_call(
        start_kernel,
        out_shape=[pltpu.VMEM((rows, depth), BF16), pltpu.VMEM((8, depth), F32),
                   pltpu.VMEM((first_rows, items), BF16)],
        in_specs=[HBM_SPEC] * 2,
        out_specs=[VMEM_SPEC] * 3,
        scratch_shapes=[pltpu.VMEM((rows, depth), BF16), pltpu.SemaphoreType.DMA((2,))],
        compiler_params=PARAMS,
        cost_estimate=pl.CostEstimate(
            flops=40 * rows * depth, bytes_accessed=rows * depth * 4, transcendentals=2 * rows * depth),
        name="user_start",
    )(in_hbm(user_shape), in_hbm(interactions))


def item_sums(ratios, uexp):
    return lax.dot_general(ratios[...], uexp[...], (((0,), (0,)), ((), ())), preferred_element_type=F32)


def stratum_kernel(names, *refs, stratum, at, rows, items, factor, first, last, earlier, tail, ahead):
    ref = dict(zip(names, refs))
    copies = {}

    def fetch(name, source, target):
        copies[name] = pltpu.make_async_copy(source, target, ref["sems"].at[len(copies)])
        copies[name].start()

    if first:
        fetch("item", ref["item"], ref["item_kept"])
    if ahead:
        fetch("ahead", ref["interactions"].at[ahead[0], pl.ds(ahead[1], ahead[2]), :], ref["counts_ahead"])
    upart, counts, ratios, denominator = ref["upart"], ref["counts"], ref["ratios"], ref["denominator"]
    uexp = ref["uexp"]
    if stratum == 0:
        uexp[...] = ref["uexp_all"][at:at + rows, :]
    extra = 8 if first else 0

    def wait(name, general):
        if name in copies and not general:
            copies[name].wait()

    def body(general):
        lows = []
        theta = None
        if stratum > 0:
            if first:
                beta = row_sum(ref["acc"][0:8, :] + ref["recv"][0:8, :])
                old = 1.0 if stratum == 1 else ref["rte_old"][...]
                rte = 0.5 * old + 0.5 * (0.3 + factor * beta)
                ref["rte_new"][...] = rte
            else:
                rte = ref["rte"][...]
            lows.append(rte)
            for t, step in tiles(rows):
                old = ref["user_shape"][at + t:at + t + step, :].astype(F32) if stratum == 1 else ref["shp_old"][t:t + step, :]
                stat = ref["acc"][extra + t:extra + t + step, :] + ref["recv"][extra + t:extra + t + step, :]
                shp = 0.5 * old + 0.5 * (0.3 + factor * stat)
                ref["shp_new"][t:t + step, :] = shp
                value, part, low = exp_tile(shp, rte, general)
                uexp[t:t + step, :] = value
                theta = part if theta is None else theta + part
                lows.append(low)
            if not first:
                theta = theta + ref["theta"][...]
        elif last:
            theta = ref["theta"][...]

        if first:
            wait("item", general)
        if first or last:
            item = ref["item_kept"]
            item_rte = None if stratum == 0 else item[items:items + 8, :]
        if first:
            value, sums, low = exp_tile(item[0:items, :], item_rte, general)
            ref["item_exp_new"][...] = value
            upart[0:8, :] = sums
            lows.append(low)
            if item_rte is not None:
                lows.append(item_rte)
            item_exp = value
        else:
            item_exp = ref["item_exp"][...]

        denominator[...] = lax.dot_general(
            uexp[...], item_exp, (((1,), (1,)), ((), ())), preferred_element_type=F32)
        for t, step in tiles(rows):
            ratios[t:t + step, :] = (
                counts[t:t + step, :].astype(F32) / denominator[t:t + step, :]).astype(BF16)
        user_sums = uexp[...].astype(F32) * jnp.dot(
            ratios[...], item_exp, preferred_element_type=F32)
        upart[extra:extra + rows - tail, :] = user_sums[0:rows - tail, :]
        if tail:
            ref["upart_tail"][...] = user_sums[rows - tail:, :]
        if last:
            istat = item_sums(ratios, uexp)
            for i in range(earlier):
                istat = istat + item_sums(ref[f"ratios{i}"], ref[f"uexp{i}"])
            old = 1.0 if item_rte is None else item_rte
            ref["item_new"][0:items, :] = 0.5 * item[0:items, :] + 0.5 * (
                0.3 + factor * (item_exp.astype(F32) * istat))
            ref["item_new"][items:items + 8, :] = 0.5 * old + 0.5 * (0.3 + factor * row_sum(theta))
        elif stratum > 0:
            ref["theta_new"][...] = theta
        return functools.reduce(jnp.minimum, lows) if lows else None

    low = body(False)
    if low is not None:

        @pl.when(jnp.logical_not(above(low)))
        def _():
            body(True)

    wait("ahead", False)


def stratum_call(stratum, at, rows, items, depth, factor, first, last, earlier, tail, ahead, operands):
    extra = 8 if first else 0
    outs = {"upart": ((rows + extra - tail, depth), F32)}
    if tail:
        outs["upart_tail"] = ((tail, depth), F32)
    if stratum > 0:
        outs["shp_new"] = ((rows, depth), F32)
    if first and stratum > 0:
        outs["rte_new"] = ((8, depth), F32)
    if first:
        outs["item_exp_new"] = ((items, depth), BF16)
    if first:
        outs["item_kept"] = (operands["item"].shape, F32)
    if last:
        outs["item_new"] = ((items + 8, depth), F32)
    else:
        outs["ratios"] = ((rows, items), BF16)
        outs["uexp"] = ((rows, depth), BF16)
        if stratum > 0:
            outs["theta_new"] = ((8, depth), F32)
    if ahead:
        outs["counts_ahead"] = ((ahead[2], items), BF16)
    scratch = {
        "denominator": pltpu.VMEM((rows, items), F32),
        "sems": pltpu.SemaphoreType.DMA((2,)),
    }
    if last:
        scratch["ratios"] = pltpu.VMEM((rows, items), BF16)
        scratch["uexp"] = pltpu.VMEM((rows, depth), BF16)
    hbm = ("interactions", "item")
    operands = {
        name: in_hbm(x) if name in hbm else in_vmem(x) if name == "user_shape" else x
        for name, x in operands.items()}
    names = list(operands) + list(outs) + list(scratch)
    kernel = functools.partial(
        stratum_kernel, names, stratum=stratum, at=at, rows=rows, items=items,
        factor=factor, first=first, last=last, earlier=earlier, tail=tail, ahead=ahead)
    results = pl.pallas_call(
        kernel,
        out_shape=[jax.ShapeDtypeStruct(*spec) for spec in outs.values()],
        in_specs=[HBM_SPEC if name in hbm else VMEM_SPEC for name in operands],
        out_specs=[VMEM_SPEC] * len(outs),
        scratch_shapes=list(scratch.values()),
        compiler_params=PARAMS,
        cost_estimate=pl.CostEstimate(flops=1, bytes_accessed=1, transcendentals=0),
        name=f"stratum{stratum}_at{at}",
    )(*operands.values())
    return dict(zip(outs, results))


def user_log_kernel(*refs, at, rows, shp_at, factor, first, filled):
    acc, recv, shp_old, rte_in = refs[:4]
    rest = refs[5:] if filled else refs[4:]
    out, *rte_out, block, sem = rest
    rte = rte_in[...]
    if first:
        rte = 0.5 * rte + 0.5 * (0.3 + factor * row_sum(acc[0:8, :] + recv[0:8, :]))
    for ref in rte_out:
        ref[...] = rte
    extra = 8 if first else 0

    def body(general):
        low = rte
        for t, step in tiles(rows):
            stat = acc[extra + t:extra + t + step, :] + recv[extra + t:extra + t + step, :]
            shp = 0.5 * shp_old[shp_at + t:shp_at + t + step, :] + 0.5 * (0.3 + factor * stat)
            block[t:t + step, :], part_low = log_tile(shp, rte, general)
            low = jnp.minimum(low, part_low)
        return low

    low = body(False)

    @pl.when(jnp.logical_not(above(low)))
    def _():
        body(True)

    copy = pltpu.make_async_copy(block, out.at[pl.ds(at, rows), :], sem)
    copy.start()
    copy.wait()


def user_log_call(at, rows, shp_at, total, depth, factor, first, operands, filled):
    out_shape = [jax.ShapeDtypeStruct((total, depth), BF16)]
    out_specs = [HBM_SPEC]
    if at + rows < total:
        out_shape.append(jax.ShapeDtypeStruct((8, depth), F32))
        out_specs.append(VMEM_SPEC)
    operands = list(operands)
    in_specs = [VMEM_SPEC] * 4
    if filled is not None:
        operands.append(filled)
        in_specs.append(HBM_SPEC)
    return pl.pallas_call(
        functools.partial(user_log_kernel, at=at, rows=rows, shp_at=shp_at, factor=factor, first=first,
                          filled=filled is not None),
        out_shape=out_shape,
        in_specs=in_specs,
        out_specs=out_specs,
        input_output_aliases={} if filled is None else {4: 0},
        scratch_shapes=[pltpu.VMEM((rows, depth), BF16), pltpu.SemaphoreType.DMA],
        compiler_params=PARAMS,
        cost_estimate=pl.CostEstimate(
            flops=40 * rows * depth, bytes_accessed=rows * depth * 14, transcendentals=rows * depth),
        name=f"user_log_at{at}",
    )(*operands)


def item_log_kernel(item, _, out, *, items):
    rte = item[items:items + 8, :]

    def body(general):
        out[...], low = log_tile(item[0:items, :], rte, general)
        return low

    low = body(False)

    @pl.when(jnp.logical_not(above(jnp.minimum(low, rte))))
    def _():
        body(True)


def item_log_call(item, after, items, depth):
    return pl.pallas_call(
        functools.partial(item_log_kernel, items=items),
        out_shape=jax.ShapeDtypeStruct((items, depth), BF16),
        in_specs=[VMEM_SPEC, VMEM_SPEC],
        out_specs=VMEM_SPEC,
        compiler_params=PARAMS,
        cost_estimate=pl.CostEstimate(
            flops=40 * items * depth, bytes_accessed=items * depth * 6, transcendentals=items * depth),
        name="item_log",
    )(item, after)


def swapped(value, axis, mask):
    return lax.ppermute(value, axis, [(a, a ^ mask) for a in range(lax.axis_size(axis))])


def moved(choice, value, then=None, operands=()):
    def branch(mask, value, *operands):
        arrived = swapped(value, "users", mask)
        return arrived if then is None else then(arrived, *operands)

    choices = [functools.partial(branch, mask) for mask in range(1, lax.axis_size("users"))]
    return lax.switch(choice, choices, value, *operands)


def exchanged(value):
    size = lax.axis_size("items")
    if size == 1:
        return value, jnp.zeros_like(value)
    mask = 1
    while mask * 2 < size:
        value = value + swapped(value, "items", mask)
        mask *= 2
    return value, swapped(value, "items", mask)


def per_device(interactions, matchings, user_shape, item_shape):
    group = lax.axis_size("users")
    factor = float(group)
    users, depth = user_shape.shape
    items = item_shape.shape[0]
    sizes = chunk_rows(users)
    starts = [sum(sizes[:i]) for i in range(len(sizes))]
    count = len(sizes)

    item, choices = prepare_call(matchings, item_shape, group - 1)
    order = [(s, at, rows) for s in range(STRATA) for at, rows in zip(starts, sizes)]

    def opening(arrived, user_shape, interactions):
        return arrived, start_call(user_shape, interactions, sizes[0])

    item, (uexp, theta, counts) = moved(choices[0], item, opening, (user_shape, interactions))
    rte = None
    shp = [None] * count
    sums = [None] * count
    for stratum in range(STRATA):
        carried = {"theta": theta}
        earlier = {}
        for i, (at, rows) in enumerate(zip(starts, sizes)):
            first, last = i == 0, i == count - 1
            step = stratum * count + i
            ahead = order[step + 1] if step + 1 < len(order) else None
            tail = tail_rows(rows) if last and stratum == STRATA - 1 else 0
            operands = {"counts": counts}
            if ahead:
                operands["interactions"] = interactions
            if stratum == 0:
                operands["uexp_all"] = uexp
            else:
                operands["acc"], operands["recv"] = sums[i]
                if stratum == 1:
                    operands["user_shape"] = user_shape
                else:
                    operands["shp_old"] = shp[i]
                if not first:
                    operands["rte"] = rte
                elif stratum > 1:
                    operands["rte_old"] = rte
            if first:
                operands["item"] = item
            elif last:
                operands["item_kept"] = carried["item_kept"]
            if not first:
                operands["item_exp"] = carried["item_exp"]
            if last:
                operands.update(earlier)
            if (stratum > 0 and not first) or (stratum == 0 and last):
                operands["theta"] = carried["theta"]
            out = stratum_call(
                stratum, at, rows, items, depth, factor, first, last, i, tail, ahead, operands)
            counts = out.get("counts_ahead")
            shp[i] = out.get("shp_new")
            sums[i] = exchanged(out["upart"])
            if tail:
                tail_sums = exchanged(out["upart_tail"])
            if first:
                rte = out.get("rte_new")
                carried["item_exp"] = out["item_exp_new"]
                carried["item_kept"] = out["item_kept"]
            if last:
                item = out["item_new"]
            else:
                earlier[f"ratios{i}"], earlier[f"uexp{i}"] = out["ratios"], out["uexp"]
                if stratum > 0:
                    carried["theta"] = out["theta_new"]
        if stratum + 1 < STRATA:
            item = moved(choices[stratum + 1], item)
        else:
            item = swapped(item, "users", group - 1)
    user_log = None
    pieces = [(at, rows, 0, sums[i], shp[i]) for i, (at, rows) in enumerate(zip(starts, sizes))]
    if tail:
        at, rows = starts[-1], sizes[-1] - tail
        pieces[-1:] = [(at, rows, 0, sums[-1], shp[-1]), (at + rows, tail, rows, tail_sums, shp[-1])]
    for i, (at, rows, shp_at, piece_sums, piece_shp) in enumerate(pieces):
        user_log, *rest = user_log_call(
            at, rows, shp_at, users, depth, factor, i == 0, (*piece_sums, piece_shp, rte), user_log)
        rte = rest[0] if rest else rte
        if i == max(len(pieces) - 2, 0):
            item_log = item_log_call(item, rte, items, depth)
    return user_log, item_log


def solution(mesh):
    placed = (P(None, "users", "items"), P(), P("users", None), P(("users", "items"), None))
    return jax.shard_map(
        per_device,
        mesh=mesh,
        in_specs=placed,
        out_specs=(P("users", None), P(("users", "items"), None)),
        check_vma=False,
    )
```

```python
import functools

import jax
import jax.numpy as jnp
from jax import lax
from jax.experimental import pallas as pl
from jax.experimental.pallas import tpu as pltpu
from jax.sharding import PartitionSpec as P

STRATA = 3
TILE = 64
START_TILE = 128
REDO_TILE = 32
F32 = jnp.float32
BF16 = jnp.bfloat16


def chunk_rows(rows):
    first = max(rows // 2 // TILE, 1) * TILE
    return [first, rows - first] if first < rows else [rows]


def tail_rows(rows):
    return rows // 2 // TILE * TILE


def psi_parts(x):
    small = x < 8.0
    w = jnp.where(small, x + 3.5, x - 0.5)
    q = x * (x + 3.0)
    q2 = q + 2.0
    bounded = jnp.minimum(w, 1e9)
    square = bounded * bounded
    steps = jnp.where(small, q * q2, 1.0)
    r = 1.0 / (square * steps)
    s = r * steps
    shift = (2.0 * x + 3.0) * (q + q2) * (r * square)
    g = s * (1.0 / 24.0 - s * (7.0 / 960.0 - s * (31.0 / 8064.0 - s * (127.0 / 30720.0))))
    return w, g - jnp.where(small, shift, 0.0)


def psi_any(x):
    mirrored = x < 0.5
    w, g = psi_parts(jnp.where(mirrored, 1.0 - x, x))
    value = jnp.log(w) + g
    t = x - jnp.floor(x + 0.5)
    u = 3.14159265358979 * t
    v = u * u
    sin = 1.0 / 6227020800.0
    for c in (-1.0 / 39916800.0, 1.0 / 362880.0, -1.0 / 5040.0, 1.0 / 120.0, -1.0 / 6.0, 1.0):
        sin = sin * v + c
    cos = -1.0 / 87178291200.0
    for c in (1.0 / 479001600.0, -1.0 / 3628800.0, 1.0 / 40320.0, -1.0 / 720.0, 1.0 / 24.0, -0.5, 1.0):
        cos = cos * v + c
    value = jnp.where(mirrored, value - 3.14159265358979 * cos / (sin * u), value)
    return jnp.where((x <= 0.0) & (x == jnp.floor(x)), jnp.nan, value)


LOWEST = 0.01


def above(low):
    return jnp.min(low) >= LOWEST


def folded(x):
    return x.reshape(x.shape[0] // 8, 8, x.shape[1])


def tiles(rows):
    step = TILE if rows % TILE == 0 else rows
    return [(at, step) for at in range(0, rows, step)]


def redo_loop(rows, step, carry=None):
    size = REDO_TILE if rows % REDO_TILE == 0 else 8
    return lax.fori_loop(
        0, rows // size, lambda i, c: step(pl.multiple_of(i * size, size), size, c), carry)


def exp_tile(x, rte, general):
    shape = x.shape
    x = folded(x)
    if general:
        value = psi_any(x)
        if rte is not None:
            value = value - jnp.log(rte)[None]
        value = jnp.exp(value)
    else:
        w, g = psi_parts(x)
        value = w if rte is None else w * (1.0 / rte)[None]
        value = value * jnp.exp(g)
    mean = x if rte is None else x * (1.0 / rte)[None]
    return value.reshape(shape).astype(BF16), jnp.sum(mean, axis=0), jnp.min(x, axis=0)


def log_tile(x, rte, general):
    shape = x.shape
    x = folded(x)
    if general:
        value = psi_any(x) - jnp.log(rte)[None]
    else:
        w, g = psi_parts(x)
        value = (jnp.log(w) - jnp.log(rte)[None]) + g
    return value.reshape(shape).astype(BF16), jnp.min(x, axis=0)


def row_sum(x):
    return jnp.broadcast_to(jnp.sum(x, axis=0, keepdims=True), x.shape)


VMEM_SPEC = pl.BlockSpec(memory_space=pltpu.VMEM)
SMEM_SPEC = pl.BlockSpec(memory_space=pltpu.SMEM)
HBM_SPEC = pl.BlockSpec(memory_space=pltpu.HBM)
PARAMS = pltpu.CompilerParams(vmem_limit_bytes=24 * 2**20)


def in_hbm(x):
    return pltpu.with_memory_space_constraint(x, pltpu.HBM)


def in_vmem(x):
    return pltpu.with_memory_space_constraint(x, pltpu.VMEM)


def prepare_kernel(matchings_hbm, shape_hbm, item, *refs, last):
    choices, (matchings, shape, sems) = refs[:STRATA], refs[STRATA:]
    copies = [
        pltpu.make_async_copy(shape_hbm, shape, sems.at[0]),
        pltpu.make_async_copy(matchings_hbm, matchings, sems.at[1]),
    ]
    for copy in copies:
        copy.start()
    for copy in copies:
        copy.wait()
    item[...] = shape[...].astype(F32)
    choices[0][0] = matchings[0] - 1
    for stratum in range(1, STRATA - 1):
        choices[stratum][0] = jnp.bitwise_xor(matchings[stratum - 1], matchings[stratum]) - 1
    choices[STRATA - 1][0] = jnp.bitwise_xor(matchings[STRATA - 2], last) - 1


def prepare_call(matchings, item_shape, last):
    out = pl.pallas_call(
        functools.partial(prepare_kernel, last=last),
        out_shape=[jax.ShapeDtypeStruct(item_shape.shape, F32)]
        + [pltpu.SMEM((1,), jnp.int32)] * STRATA,
        in_specs=[HBM_SPEC, HBM_SPEC],
        out_specs=[VMEM_SPEC] + [SMEM_SPEC] * STRATA,
        scratch_shapes=[pltpu.SMEM(matchings.shape, jnp.int32), pltpu.VMEM(item_shape.shape, BF16),
                        pltpu.SemaphoreType.DMA((2,))],
        compiler_params=PARAMS,
        name="prepare",
    )(in_hbm(matchings), in_hbm(item_shape))
    return out[0], [choice[0] for choice in out[1:]]


def start_kernel(shape_hbm, interactions, uexp, theta, counts, shape, sems):
    rows, depth = shape.shape
    load = pltpu.make_async_copy(shape_hbm, shape, sems.at[0])
    ahead = pltpu.make_async_copy(interactions.at[0, pl.ds(0, counts.shape[0]), :], counts, sems.at[1])
    load.start()
    ahead.start()
    load.wait()

    def step(i, carry):
        total, low = carry
        place = pl.ds(pl.multiple_of(i * START_TILE, START_TILE), START_TILE)
        value, part, part_low = exp_tile(shape[place, :].astype(F32), None, False)
        uexp[place, :] = value
        return total + part, jnp.minimum(low, part_low)

    total, low = lax.fori_loop(
        0, rows // START_TILE, step, (jnp.zeros((8, depth), F32), jnp.ones((8, depth), F32)))
    theta[...] = total

    @pl.when(jnp.logical_not(above(low)))
    def _():
        def redo(at, size, _):
            place = pl.ds(at, size)
            uexp[place, :] = exp_tile(shape[place, :].astype(F32), None, True)[0]

        redo_loop(rows, redo)

    ahead.wait()


def start_call(user_shape, interactions, first_rows):
    rows, depth = user_shape.shape
    items = interactions.shape[2]
    return pl.pallas_call(
        start_kernel,
        out_shape=[pltpu.VMEM((rows, depth), BF16), pltpu.VMEM((8, depth), F32),
                   pltpu.VMEM((first_rows, items), BF16)],
        in_specs=[HBM_SPEC] * 2,
        out_specs=[VMEM_SPEC] * 3,
        scratch_shapes=[pltpu.VMEM((rows, depth), BF16), pltpu.SemaphoreType.DMA((2,))],
        compiler_params=PARAMS,
        cost_estimate=pl.CostEstimate(
            flops=40 * rows * depth, bytes_accessed=rows * depth * 4, transcendentals=2 * rows * depth),
        name="user_start",
    )(in_hbm(user_shape), in_hbm(interactions))


def dot_rows(a, b):
    return lax.dot_general(a, b, (((1,), (1,)), ((), ())), preferred_element_type=F32)


def item_sums(ratios, uexp):
    return lax.dot_general(ratios[...], uexp[...], (((0,), (0,)), ((), ())), preferred_element_type=F32)


def stratum_kernel(names, *refs, stratum, at, rows, items, factor, first, last, earlier, tail, ahead):
    ref = dict(zip(names, refs))
    copies = {}

    def fetch(name, source, target):
        copies[name] = pltpu.make_async_copy(source, target, ref["sems"].at[len(copies)])
        copies[name].start()

    if first:
        fetch("item", ref["item"], ref["item_kept"])
    if ahead:
        fetch("ahead", ref["interactions"].at[ahead[0], pl.ds(ahead[1], ahead[2]), :], ref["counts_ahead"])
    upart, counts, ratios, denominator = ref["upart"], ref["counts"], ref["ratios"], ref["denominator"]
    uexp = ref["uexp"]
    if stratum == 0:
        uexp[...] = ref["uexp_all"][at:at + rows, :]
    extra = 8 if first else 0

    lows = []
    theta = None
    item = ref["item_kept"] if first or last else None

    if stratum > 0:
        if first:
            beta = row_sum(ref["acc"][0:8, :] + ref["recv"][0:8, :])
            old = 1.0 if stratum == 1 else ref["rte_old"][...]
            rte = 0.5 * old + 0.5 * (0.3 + factor * beta)
            ref["rte_new"][...] = rte
        else:
            rte = ref["rte"][...]
        lows.append(rte)
        for t, step in tiles(rows):
            old = ref["user_shape"][at + t:at + t + step, :].astype(F32) if stratum == 1 else ref["shp_old"][t:t + step, :]
            stat = ref["acc"][extra + t:extra + t + step, :] + ref["recv"][extra + t:extra + t + step, :]
            shp = 0.5 * old + 0.5 * (0.3 + factor * stat)
            ref["shp_new"][t:t + step, :] = shp
            value, part, low = exp_tile(shp, rte, False)
            uexp[t:t + step, :] = value
            theta = part if theta is None else theta + part
            lows.append(low)
        if not first:
            theta = theta + ref["theta"][...]
        if not last:
            ref["theta_new"][...] = theta
    elif last:
        theta = ref["theta"][...]

    if first:
        copies["item"].wait()
    if first or last:
        item_rte = None if stratum == 0 else item[items:items + 8, :]
    if first:
        item_exp, sums, low = exp_tile(item[0:items, :], item_rte, False)
        ref["item_exp_new"][...] = item_exp
        upart[0:8, :] = sums
        lows.append(low)
        if item_rte is not None:
            lows.append(item_rte)
    else:
        item_exp = ref["item_exp"][...]

    denominator[...] = dot_rows(uexp[...], item_exp)
    for t, step in tiles(rows):
        ratios[t:t + step, :] = (
            counts[t:t + step, :].astype(F32) / denominator[t:t + step, :]).astype(BF16)
    user_sums = uexp[...].astype(F32) * jnp.dot(ratios[...], item_exp, preferred_element_type=F32)
    upart[extra:extra + rows - tail, :] = user_sums[0:rows - tail, :]
    if tail:
        ref["upart_tail"][...] = user_sums[rows - tail:, :]
    pairs = [(ref[f"ratios{i}"], ref[f"uexp{i}"]) for i in range(earlier)] + [(ratios, uexp)]

    def update_items(istat):
        old = 1.0 if item_rte is None else item_rte
        kept = ref["item_exp_new" if first else "item_exp"][...].astype(F32)
        ref["item_new"][0:items, :] = 0.5 * item[0:items, :] + 0.5 * (0.3 + factor * (kept * istat))
        ref["item_new"][items:items + 8, :] = 0.5 * old + 0.5 * (0.3 + factor * row_sum(theta))

    if last:
        istat = None
        for pair in pairs:
            part = item_sums(*pair)
            istat = part if istat is None else istat + part
        update_items(istat)

    if lows:

        @pl.when(jnp.logical_not(above(functools.reduce(jnp.minimum, lows))))
        def _():
            if stratum > 0:

                def redo_users(at, size, _):
                    place = pl.ds(at, size)
                    uexp[place, :] = exp_tile(ref["shp_new"][place, :], rte, True)[0]

                redo_loop(rows, redo_users)
            if first:

                def redo_items(at, size, _):
                    place = pl.ds(at, size)
                    ref["item_exp_new"][place, :] = exp_tile(item[place, :], item_rte, True)[0]

                redo_loop(items, redo_items)
            kept = ref["item_exp_new" if first else "item_exp"]
            for target, begin, skip, length in (
                (upart, 0, extra, rows - tail), (ref.get("upart_tail"), rows - tail, 0, tail)):

                def redo_sums(at, size, _):
                    place = pl.ds(pl.multiple_of(begin + at, size), size)
                    u = uexp[place, :]
                    ratio = (counts[place, :].astype(F32) / dot_rows(u, kept[...])).astype(BF16)
                    ratios[place, :] = ratio
                    target[pl.ds(pl.multiple_of(skip + at, 8), size), :] = u.astype(F32) * jnp.dot(
                        ratio, kept[...], preferred_element_type=F32)

                if length:
                    redo_loop(length, redo_sums)
            if last:
                total = ref["item_new"].at[pl.ds(0, items), :]
                total[...] = jnp.zeros((items, ref["item_new"].shape[1]), F32)
                for pair in pairs:

                    def redo_stat(at, size, _):
                        place = pl.ds(at, size)
                        total[...] += item_sums(pair[0].at[place, :], pair[1].at[place, :])

                    redo_loop(rows if pair[0] is ratios else pair[0].shape[0], redo_stat)
                update_items(total[...])

    if ahead:
        copies["ahead"].wait()


def stratum_call(stratum, at, rows, items, depth, factor, first, last, earlier, tail, ahead, operands):
    extra = 8 if first else 0
    outs = {"upart": ((rows + extra - tail, depth), F32)}
    if tail:
        outs["upart_tail"] = ((tail, depth), F32)
    if stratum > 0:
        outs["shp_new"] = ((rows, depth), F32)
    if first and stratum > 0:
        outs["rte_new"] = ((8, depth), F32)
    if first:
        outs["item_exp_new"] = ((items, depth), BF16)
    if first:
        outs["item_kept"] = (operands["item"].shape, F32)
    if last:
        outs["item_new"] = ((items + 8, depth), F32)
    else:
        outs["ratios"] = ((rows, items), BF16)
        outs["uexp"] = ((rows, depth), BF16)
        if stratum > 0:
            outs["theta_new"] = ((8, depth), F32)
    if ahead:
        outs["counts_ahead"] = ((ahead[2], items), BF16)
    scratch = {
        "denominator": pltpu.VMEM((rows, items), F32),
        "sems": pltpu.SemaphoreType.DMA((2,)),
    }
    if last:
        scratch["ratios"] = pltpu.VMEM((rows, items), BF16)
        scratch["uexp"] = pltpu.VMEM((rows, depth), BF16)
    hbm = ("interactions", "item")
    operands = {
        name: in_hbm(x) if name in hbm else in_vmem(x) if name == "user_shape" else x
        for name, x in operands.items()}
    names = list(operands) + list(outs) + list(scratch)
    kernel = functools.partial(
        stratum_kernel, names, stratum=stratum, at=at, rows=rows, items=items,
        factor=factor, first=first, last=last, earlier=earlier, tail=tail, ahead=ahead)
    results = pl.pallas_call(
        kernel,
        out_shape=[jax.ShapeDtypeStruct(*spec) for spec in outs.values()],
        in_specs=[HBM_SPEC if name in hbm else VMEM_SPEC for name in operands],
        out_specs=[VMEM_SPEC] * len(outs),
        scratch_shapes=list(scratch.values()),
        compiler_params=PARAMS,
        cost_estimate=pl.CostEstimate(flops=1, bytes_accessed=1, transcendentals=0),
        name=f"stratum{stratum}_at{at}",
    )(*operands.values())
    return dict(zip(outs, results))


def user_log_kernel(*refs, at, rows, shp_at, factor, first, filled):
    acc, recv, shp_old, rte_in = refs[:4]
    rest = refs[5:] if filled else refs[4:]
    out, *rte_out, block, sem = rest
    rte = rte_in[...]
    if first:
        rte = 0.5 * rte + 0.5 * (0.3 + factor * row_sum(acc[0:8, :] + recv[0:8, :]))
    for ref in rte_out:
        ref[...] = rte
    extra = 8 if first else 0

    def shape(t, step):
        stat = acc[pl.ds(extra + t, step), :] + recv[pl.ds(extra + t, step), :]
        return 0.5 * shp_old[pl.ds(shp_at + t, step), :] + 0.5 * (0.3 + factor * stat)

    low = rte
    for t, step in tiles(rows):
        block[t:t + step, :], part_low = log_tile(shape(t, step), rte, False)
        low = jnp.minimum(low, part_low)

    @pl.when(jnp.logical_not(above(low)))
    def _():
        def redo(t, step, _):
            block[pl.ds(t, step), :] = log_tile(shape(pl.multiple_of(t, 8), step), rte, True)[0]

        redo_loop(rows, redo)

    copy = pltpu.make_async_copy(block, out.at[pl.ds(at, rows), :], sem)
    copy.start()
    copy.wait()


def user_log_call(at, rows, shp_at, total, depth, factor, first, operands, filled):
    out_shape = [jax.ShapeDtypeStruct((total, depth), BF16)]
    out_specs = [HBM_SPEC]
    if at + rows < total:
        out_shape.append(jax.ShapeDtypeStruct((8, depth), F32))
        out_specs.append(VMEM_SPEC)
    operands = list(operands)
    in_specs = [VMEM_SPEC] * 4
    if filled is not None:
        operands.append(filled)
        in_specs.append(HBM_SPEC)
    return pl.pallas_call(
        functools.partial(user_log_kernel, at=at, rows=rows, shp_at=shp_at, factor=factor, first=first,
                          filled=filled is not None),
        out_shape=out_shape,
        in_specs=in_specs,
        out_specs=out_specs,
        input_output_aliases={} if filled is None else {4: 0},
        scratch_shapes=[pltpu.VMEM((rows, depth), BF16), pltpu.SemaphoreType.DMA],
        compiler_params=PARAMS,
        cost_estimate=pl.CostEstimate(
            flops=40 * rows * depth, bytes_accessed=rows * depth * 14, transcendentals=rows * depth),
        name=f"user_log_at{at}",
    )(*operands)


def item_log_kernel(item, _, out, *, items):
    rte = item[items:items + 8, :]

    out[...], low = log_tile(item[0:items, :], rte, False)

    @pl.when(jnp.logical_not(above(jnp.minimum(low, rte))))
    def _():
        def redo(t, step, _):
            place = pl.ds(t, step)
            out[place, :] = log_tile(item[place, :], rte, True)[0]

        redo_loop(items, redo)


def item_log_call(item, after, items, depth):
    return pl.pallas_call(
        functools.partial(item_log_kernel, items=items),
        out_shape=jax.ShapeDtypeStruct((items, depth), BF16),
        in_specs=[VMEM_SPEC, VMEM_SPEC],
        out_specs=VMEM_SPEC,
        compiler_params=PARAMS,
        cost_estimate=pl.CostEstimate(
            flops=40 * items * depth, bytes_accessed=items * depth * 6, transcendentals=items * depth),
        name="item_log",
    )(item, after)


def swapped(value, axis, mask):
    return lax.ppermute(value, axis, [(a, a ^ mask) for a in range(lax.axis_size(axis))])


def moved(choice, value, then=None, operands=()):
    def branch(mask, value, *operands):
        arrived = swapped(value, "users", mask)
        return arrived if then is None else then(arrived, *operands)

    choices = [functools.partial(branch, mask) for mask in range(1, lax.axis_size("users"))]
    return lax.switch(choice, choices, value, *operands)


def exchanged(value):
    size = lax.axis_size("items")
    if size == 1:
        return value, jnp.zeros_like(value)
    mask = 1
    while mask * 2 < size:
        value = value + swapped(value, "items", mask)
        mask *= 2
    return value, swapped(value, "items", mask)


def per_device(interactions, matchings, user_shape, item_shape):
    group = lax.axis_size("users")
    factor = float(group)
    users, depth = user_shape.shape
    items = item_shape.shape[0]
    sizes = chunk_rows(users)
    starts = [sum(sizes[:i]) for i in range(len(sizes))]
    count = len(sizes)

    item, choices = prepare_call(matchings, item_shape, group - 1)
    order = [(s, at, rows) for s in range(STRATA) for at, rows in zip(starts, sizes)]

    def opening(arrived, user_shape, interactions):
        return arrived, start_call(user_shape, interactions, sizes[0])

    item, (uexp, theta, counts) = moved(choices[0], item, opening, (user_shape, interactions))
    rte = None
    shp = [None] * count
    sums = [None] * count
    for stratum in range(STRATA):
        carried = {"theta": theta}
        earlier = {}
        for i, (at, rows) in enumerate(zip(starts, sizes)):
            first, last = i == 0, i == count - 1
            step = stratum * count + i
            ahead = order[step + 1] if step + 1 < len(order) else None
            tail = tail_rows(rows) if last and stratum == STRATA - 1 else 0
            operands = {"counts": counts}
            if ahead:
                operands["interactions"] = interactions
            if stratum == 0:
                operands["uexp_all"] = uexp
            else:
                operands["acc"], operands["recv"] = sums[i]
                if stratum == 1:
                    operands["user_shape"] = user_shape
                else:
                    operands["shp_old"] = shp[i]
                if not first:
                    operands["rte"] = rte
                elif stratum > 1:
                    operands["rte_old"] = rte
            if first:
                operands["item"] = item
            elif last:
                operands["item_kept"] = carried["item_kept"]
            if not first:
                operands["item_exp"] = carried["item_exp"]
            if last:
                operands.update(earlier)
            if (stratum > 0 and not first) or (stratum == 0 and last):
                operands["theta"] = carried["theta"]
            out = stratum_call(
                stratum, at, rows, items, depth, factor, first, last, i, tail, ahead, operands)
            counts = out.get("counts_ahead")
            shp[i] = out.get("shp_new")
            sums[i] = exchanged(out["upart"])
            if tail:
                tail_sums = exchanged(out["upart_tail"])
            if first:
                rte = out.get("rte_new")
                carried["item_exp"] = out["item_exp_new"]
                carried["item_kept"] = out["item_kept"]
            if last:
                item = out["item_new"]
            else:
                earlier[f"ratios{i}"], earlier[f"uexp{i}"] = out["ratios"], out["uexp"]
                if stratum > 0:
                    carried["theta"] = out["theta_new"]
        if stratum + 1 < STRATA:
            item = moved(choices[stratum + 1], item)
        else:
            item = swapped(item, "users", group - 1)
    user_log = None
    pieces = [(at, rows, 0, sums[i], shp[i]) for i, (at, rows) in enumerate(zip(starts, sizes))]
    if tail:
        at, rows = starts[-1], sizes[-1] - tail
        pieces[-1:] = [(at, rows, 0, sums[-1], shp[-1]), (at + rows, tail, rows, tail_sums, shp[-1])]
    for i, (at, rows, shp_at, piece_sums, piece_shp) in enumerate(pieces):
        user_log, *rest = user_log_call(
            at, rows, shp_at, users, depth, factor, i == 0, (*piece_sums, piece_shp, rte), user_log)
        rte = rest[0] if rest else rte
        if i == max(len(pieces) - 2, 0):
            item_log = item_log_call(item, rte, items, depth)
    return user_log, item_log


def solution(mesh):
    placed = (P(None, "users", "items"), P(), P("users", None), P(("users", "items"), None))
    return jax.shard_map(
        per_device,
        mesh=mesh,
        in_specs=placed,
        out_specs=(P("users", None), P(("users", "items"), None)),
        check_vma=False,
    )
```

```python
import functools

import jax
import jax.numpy as jnp
from jax import lax
from jax.experimental import pallas as pl
from jax.experimental.pallas import tpu as pltpu
from jax.sharding import PartitionSpec as P

STRATA = 3
TILE = 64
START_TILE = 128
REDO_TILE = 32
F32 = jnp.float32
BF16 = jnp.bfloat16


def chunk_rows(rows):
    first = max(rows // 2 // TILE, 1) * TILE
    return [first, rows - first] if first < rows else [rows]


def tail_rows(rows):
    return rows // 2 // TILE * TILE


def psi_parts(x):
    small = x < 8.0
    w = jnp.where(small, x + 3.5, x - 0.5)
    q = x * (x + 3.0)
    q2 = q + 2.0
    bounded = jnp.minimum(w, 1e9)
    square = bounded * bounded
    steps = jnp.where(small, q * q2, 1.0)
    r = 1.0 / (square * steps)
    s = r * steps
    shift = (2.0 * x + 3.0) * (q + q2) * (r * square)
    g = s * (1.0 / 24.0 - s * (7.0 / 960.0 - s * (31.0 / 8064.0 - s * (127.0 / 30720.0))))
    return w, g - jnp.where(small, shift, 0.0)


def psi_any(x):
    mirrored = x < 0.5
    w, g = psi_parts(jnp.where(mirrored, 1.0 - x, x))
    value = jnp.log(w) + g
    t = x - jnp.floor(x + 0.5)
    u = 3.14159265358979 * t
    v = u * u
    sin = 1.0 / 6227020800.0
    for c in (-1.0 / 39916800.0, 1.0 / 362880.0, -1.0 / 5040.0, 1.0 / 120.0, -1.0 / 6.0, 1.0):
        sin = sin * v + c
    cos = -1.0 / 87178291200.0
    for c in (1.0 / 479001600.0, -1.0 / 3628800.0, 1.0 / 40320.0, -1.0 / 720.0, 1.0 / 24.0, -0.5, 1.0):
        cos = cos * v + c
    value = jnp.where(mirrored, value - 3.14159265358979 * cos / (sin * u), value)
    return jnp.where((x <= 0.0) & (x == jnp.floor(x)), jnp.nan, value)


LOWEST = 0.01


def above(low):
    return jnp.min(low) >= LOWEST


def folded(x):
    return x.reshape(x.shape[0] // 8, 8, x.shape[1])


def tiles(rows):
    step = TILE if rows % TILE == 0 else rows
    return [(at, step) for at in range(0, rows, step)]


def redo_loop(rows, step, carry=None):
    size = REDO_TILE if rows % REDO_TILE == 0 else 8
    return lax.fori_loop(
        0, rows // size, lambda i, c: step(pl.multiple_of(i * size, size), size, c), carry)


def exp_tile(x, rte, general):
    shape = x.shape
    x = folded(x)
    if general:
        value = psi_any(x)
        if rte is not None:
            value = value - jnp.log(rte)[None]
        value = jnp.exp(value)
    else:
        w, g = psi_parts(x)
        value = w if rte is None else w * (1.0 / rte)[None]
        value = value * jnp.exp(g)
    mean = x if rte is None else x * (1.0 / rte)[None]
    return value.reshape(shape).astype(BF16), jnp.sum(mean, axis=0), jnp.min(x, axis=0)


def log_tile(x, rte, general):
    shape = x.shape
    x = folded(x)
    if general:
        value = psi_any(x) - jnp.log(rte)[None]
    else:
        w, g = psi_parts(x)
        value = (jnp.log(w) - jnp.log(rte)[None]) + g
    return value.reshape(shape).astype(BF16), jnp.min(x, axis=0)


def row_sum(x):
    return jnp.broadcast_to(jnp.sum(x, axis=0, keepdims=True), x.shape)


VMEM_SPEC = pl.BlockSpec(memory_space=pltpu.VMEM)
SMEM_SPEC = pl.BlockSpec(memory_space=pltpu.SMEM)
HBM_SPEC = pl.BlockSpec(memory_space=pltpu.HBM)
PARAMS = pltpu.CompilerParams(vmem_limit_bytes=24 * 2**20)


def in_hbm(x):
    return pltpu.with_memory_space_constraint(x, pltpu.HBM)


def in_vmem(x):
    return pltpu.with_memory_space_constraint(x, pltpu.VMEM)


def prepare_kernel(matchings_hbm, shape_hbm, item, *refs, last):
    choices, (matchings, shape, sems) = refs[:STRATA], refs[STRATA:]
    copies = [
        pltpu.make_async_copy(shape_hbm, shape, sems.at[0]),
        pltpu.make_async_copy(matchings_hbm, matchings, sems.at[1]),
    ]
    for copy in copies:
        copy.start()
    for copy in copies:
        copy.wait()
    item[...] = shape[...].astype(F32)
    choices[0][0] = matchings[0] - 1
    for stratum in range(1, STRATA - 1):
        choices[stratum][0] = jnp.bitwise_xor(matchings[stratum - 1], matchings[stratum]) - 1
    choices[STRATA - 1][0] = jnp.bitwise_xor(matchings[STRATA - 2], last) - 1


def prepare_call(matchings, item_shape, last):
    out = pl.pallas_call(
        functools.partial(prepare_kernel, last=last),
        out_shape=[jax.ShapeDtypeStruct(item_shape.shape, F32)]
        + [pltpu.SMEM((1,), jnp.int32)] * STRATA,
        in_specs=[HBM_SPEC, HBM_SPEC],
        out_specs=[VMEM_SPEC] + [SMEM_SPEC] * STRATA,
        scratch_shapes=[pltpu.SMEM(matchings.shape, jnp.int32), pltpu.VMEM(item_shape.shape, BF16),
                        pltpu.SemaphoreType.DMA((2,))],
        compiler_params=PARAMS,
        name="prepare",
    )(in_hbm(matchings), in_hbm(item_shape))
    return out[0], [choice[0] for choice in out[1:]]


def start_kernel(shape_hbm, interactions, theta, counts, *refs):
    uexps, (shape, sems) = refs[:-2], refs[-2:]
    depth = shape.shape[1]
    load = pltpu.make_async_copy(shape_hbm, shape, sems.at[0])
    ahead = pltpu.make_async_copy(interactions.at[0, pl.ds(0, counts.shape[0]), :], counts, sems.at[1])
    load.start()
    ahead.start()
    load.wait()
    total, low = jnp.zeros((8, depth), F32), jnp.ones((8, depth), F32)
    begin = 0
    for uexp in uexps:
        rows = uexp.shape[0]

        def step(i, carry, begin=begin, uexp=uexp):
            at = i * START_TILE
            x = shape[pl.ds(pl.multiple_of(begin + at, START_TILE), START_TILE), :].astype(F32)
            value, part, part_low = exp_tile(x, None, False)
            uexp[pl.ds(pl.multiple_of(at, START_TILE), START_TILE), :] = value
            return carry[0] + part, jnp.minimum(carry[1], part_low)

        total, low = lax.fori_loop(0, rows // START_TILE, step, (total, low))
        begin += rows
    theta[...] = total

    @pl.when(jnp.logical_not(above(low)))
    def _():
        begin = 0
        for uexp in uexps:

            def redo(at, size, _, begin=begin, uexp=uexp):
                x = shape[pl.ds(pl.multiple_of(begin + at, size), size), :].astype(F32)
                uexp[pl.ds(at, size), :] = exp_tile(x, None, True)[0]

            redo_loop(uexp.shape[0], redo)
            begin += uexp.shape[0]

    ahead.wait()


def start_call(user_shape, interactions, sizes):
    rows, depth = user_shape.shape
    items = interactions.shape[2]
    theta, counts, *uexps = pl.pallas_call(
        start_kernel,
        out_shape=[pltpu.VMEM((8, depth), F32), pltpu.VMEM((sizes[0], items), BF16)]
        + [pltpu.VMEM((size, depth), BF16) for size in sizes],
        in_specs=[HBM_SPEC] * 2,
        out_specs=[VMEM_SPEC] * (2 + len(sizes)),
        scratch_shapes=[pltpu.VMEM((rows, depth), BF16), pltpu.SemaphoreType.DMA((2,))],
        compiler_params=PARAMS,
        cost_estimate=pl.CostEstimate(
            flops=40 * rows * depth, bytes_accessed=rows * depth * 4, transcendentals=2 * rows * depth),
        name="user_start",
    )(in_hbm(user_shape), in_hbm(interactions))
    return theta, counts, uexps


def dot_rows(a, b):
    return lax.dot_general(a, b, (((1,), (1,)), ((), ())), preferred_element_type=F32)


def item_sums(ratios, uexp):
    return lax.dot_general(ratios[...], uexp[...], (((0,), (0,)), ((), ())), preferred_element_type=F32)


def stratum_kernel(names, *refs, stratum, at, rows, items, factor, first, last, earlier, tail, ahead):
    ref = dict(zip(names, refs))
    copies = {}

    def fetch(name, source, target):
        copies[name] = pltpu.make_async_copy(source, target, ref["sems"].at[len(copies)])
        copies[name].start()

    if first and stratum > 0:
        fetch("item", ref["item"], ref["item_kept"])
    if ahead:
        fetch("ahead", ref["interactions"].at[ahead[0], pl.ds(ahead[1], ahead[2]), :], ref["counts_ahead"])
    upart, counts, ratios, denominator = ref["upart"], ref["counts"], ref["ratios"], ref["denominator"]
    uexp = ref["uexp"]
    extra = 8 if first else 0

    lows = []
    theta = None
    item = ref["item_kept"] if first or last else None

    if stratum > 0:
        if first:
            beta = row_sum(ref["acc"][0:8, :] + ref["recv"][0:8, :])
            old = 1.0 if stratum == 1 else ref["rte_old"][...]
            rte = 0.5 * old + 0.5 * (0.3 + factor * beta)
            ref["rte_new"][...] = rte
        else:
            rte = ref["rte"][...]
        lows.append(rte)
        for t, step in tiles(rows):
            old = ref["user_shape"][at + t:at + t + step, :].astype(F32) if stratum == 1 else ref["shp_old"][t:t + step, :]
            stat = ref["acc"][extra + t:extra + t + step, :] + ref["recv"][extra + t:extra + t + step, :]
            shp = 0.5 * old + 0.5 * (0.3 + factor * stat)
            ref["shp_new"][t:t + step, :] = shp
            value, part, low = exp_tile(shp, rte, False)
            uexp[t:t + step, :] = value
            theta = part if theta is None else theta + part
            lows.append(low)
        if not first:
            theta = theta + ref["theta"][...]
        if not last:
            ref["theta_new"][...] = theta
    elif last:
        theta = ref["theta"][...]

    if first and stratum > 0:
        copies["item"].wait()
    elif first:
        item[...] = ref["item"][...]
        uexp[...] = ref["uexp_in"][...]
    if first or last:
        item_rte = None if stratum == 0 else item[items:items + 8, :]
    if first:
        item_exp, sums, low = exp_tile(item[0:items, :], item_rte, False)
        ref["item_exp_new"][...] = item_exp
        upart[0:8, :] = sums
        lows.append(low)
        if item_rte is not None:
            lows.append(item_rte)
    else:
        item_exp = ref["item_exp"][...]

    denominator[...] = dot_rows(uexp[...], item_exp)
    for t, step in tiles(rows):
        ratios[t:t + step, :] = (
            counts[t:t + step, :].astype(F32) / denominator[t:t + step, :]).astype(BF16)
    user_sums = uexp[...].astype(F32) * jnp.dot(ratios[...], item_exp, preferred_element_type=F32)
    upart[extra:extra + rows - tail, :] = user_sums[0:rows - tail, :]
    if tail:
        ref["upart_tail"][...] = user_sums[rows - tail:, :]
    pairs = [(ref[f"ratios{i}"], ref[f"uexp{i}"]) for i in range(earlier)] + [(ratios, uexp)]

    def update_items(istat):
        old = 1.0 if item_rte is None else item_rte
        kept = ref["item_exp_new" if first else "item_exp"][...].astype(F32)
        ref["item_new"][0:items, :] = 0.5 * item[0:items, :] + 0.5 * (0.3 + factor * (kept * istat))
        ref["item_new"][items:items + 8, :] = 0.5 * old + 0.5 * (0.3 + factor * row_sum(theta))

    if last:
        istat = None
        for pair in pairs:
            part = item_sums(*pair)
            istat = part if istat is None else istat + part
        update_items(istat)

    if lows:

        @pl.when(jnp.logical_not(above(functools.reduce(jnp.minimum, lows))))
        def _():
            if stratum > 0:

                def redo_users(at, size, _):
                    place = pl.ds(at, size)
                    uexp[place, :] = exp_tile(ref["shp_new"][place, :], rte, True)[0]

                redo_loop(rows, redo_users)
            if first:

                def redo_items(at, size, _):
                    place = pl.ds(at, size)
                    ref["item_exp_new"][place, :] = exp_tile(item[place, :], item_rte, True)[0]

                redo_loop(items, redo_items)
            kept = ref["item_exp_new" if first else "item_exp"]
            for target, begin, skip, length in (
                (upart, 0, extra, rows - tail), (ref.get("upart_tail"), rows - tail, 0, tail)):

                def redo_sums(at, size, _):
                    place = pl.ds(pl.multiple_of(begin + at, size), size)
                    u = uexp[place, :]
                    ratio = (counts[place, :].astype(F32) / dot_rows(u, kept[...])).astype(BF16)
                    ratios[place, :] = ratio
                    target[pl.ds(pl.multiple_of(skip + at, 8), size), :] = u.astype(F32) * jnp.dot(
                        ratio, kept[...], preferred_element_type=F32)

                if length:
                    redo_loop(length, redo_sums)
            if last:
                total = ref["item_new"].at[pl.ds(0, items), :]
                total[...] = jnp.zeros((items, ref["item_new"].shape[1]), F32)
                for pair in pairs:

                    def redo_stat(at, size, _):
                        place = pl.ds(at, size)
                        total[...] += item_sums(pair[0].at[place, :], pair[1].at[place, :])

                    redo_loop(rows if pair[0] is ratios else pair[0].shape[0], redo_stat)
                update_items(total[...])

    if ahead:
        copies["ahead"].wait()


def stratum_call(stratum, at, rows, items, depth, factor, first, last, earlier, tail, ahead, operands):
    extra = 8 if first else 0
    outs = {"upart": ((rows + extra - tail, depth), F32)}
    if tail:
        outs["upart_tail"] = ((tail, depth), F32)
    if stratum > 0:
        outs["shp_new"] = ((rows, depth), F32)
    if first and stratum > 0:
        outs["rte_new"] = ((8, depth), F32)
    if first:
        outs["item_exp_new"] = ((items, depth), BF16)
    if first:
        outs["item_kept"] = (operands["item"].shape, F32)
    if last:
        outs["item_new"] = ((items + 8, depth), F32)
    else:
        outs["ratios"] = ((rows, items), BF16)
        outs["uexp"] = ((rows, depth), BF16)
        if stratum > 0:
            outs["theta_new"] = ((8, depth), F32)
    if ahead:
        outs["counts_ahead"] = ((ahead[2], items), BF16)
    scratch = {
        "denominator": pltpu.VMEM((rows, items), F32),
        "sems": pltpu.SemaphoreType.DMA((2,)),
    }
    if last:
        scratch["ratios"] = pltpu.VMEM((rows, items), BF16)
        if stratum > 0:
            scratch["uexp"] = pltpu.VMEM((rows, depth), BF16)
    hbm = ("interactions", "item") if stratum > 0 else ("interactions",)
    operands = {
        name: in_hbm(x) if name in hbm else in_vmem(x) if name in ("user_shape", "item") else x
        for name, x in operands.items()}
    names = list(operands) + list(outs) + list(scratch)
    kernel = functools.partial(
        stratum_kernel, names, stratum=stratum, at=at, rows=rows, items=items,
        factor=factor, first=first, last=last, earlier=earlier, tail=tail, ahead=ahead)
    results = pl.pallas_call(
        kernel,
        out_shape=[jax.ShapeDtypeStruct(*spec) for spec in outs.values()],
        in_specs=[HBM_SPEC if name in hbm else VMEM_SPEC for name in operands],
        out_specs=[VMEM_SPEC] * len(outs),
        scratch_shapes=list(scratch.values()),
        compiler_params=PARAMS,
        cost_estimate=pl.CostEstimate(flops=1, bytes_accessed=1, transcendentals=0),
        name=f"stratum{stratum}_at{at}",
    )(*operands.values())
    return dict(zip(outs, results))


def user_log_kernel(*refs, at, rows, shp_at, factor, first, filled):
    acc, recv, shp_old, rte_in = refs[:4]
    rest = refs[5:] if filled else refs[4:]
    out, *rte_out, block, sem = rest
    rte = rte_in[...]
    if first:
        rte = 0.5 * rte + 0.5 * (0.3 + factor * row_sum(acc[0:8, :] + recv[0:8, :]))
    for ref in rte_out:
        ref[...] = rte
    extra = 8 if first else 0

    def shape(t, step):
        stat = acc[pl.ds(extra + t, step), :] + recv[pl.ds(extra + t, step), :]
        return 0.5 * shp_old[pl.ds(shp_at + t, step), :] + 0.5 * (0.3 + factor * stat)

    low = rte
    for t, step in tiles(rows):
        block[t:t + step, :], part_low = log_tile(shape(t, step), rte, False)
        low = jnp.minimum(low, part_low)

    @pl.when(jnp.logical_not(above(low)))
    def _():
        def redo(t, step, _):
            block[pl.ds(t, step), :] = log_tile(shape(pl.multiple_of(t, 8), step), rte, True)[0]

        redo_loop(rows, redo)

    copy = pltpu.make_async_copy(block, out.at[pl.ds(at, rows), :], sem)
    copy.start()
    copy.wait()


def user_log_call(at, rows, shp_at, total, depth, factor, first, operands, filled):
    out_shape = [jax.ShapeDtypeStruct((total, depth), BF16)]
    out_specs = [HBM_SPEC]
    if at + rows < total:
        out_shape.append(jax.ShapeDtypeStruct((8, depth), F32))
        out_specs.append(VMEM_SPEC)
    operands = list(operands)
    in_specs = [VMEM_SPEC] * 4
    if filled is not None:
        operands.append(filled)
        in_specs.append(HBM_SPEC)
    return pl.pallas_call(
        functools.partial(user_log_kernel, at=at, rows=rows, shp_at=shp_at, factor=factor, first=first,
                          filled=filled is not None),
        out_shape=out_shape,
        in_specs=in_specs,
        out_specs=out_specs,
        input_output_aliases={} if filled is None else {4: 0},
        scratch_shapes=[pltpu.VMEM((rows, depth), BF16), pltpu.SemaphoreType.DMA],
        compiler_params=PARAMS,
        cost_estimate=pl.CostEstimate(
            flops=40 * rows * depth, bytes_accessed=rows * depth * 14, transcendentals=rows * depth),
        name=f"user_log_at{at}",
    )(*operands)


def item_log_kernel(item, _, out, *, items):
    rte = item[items:items + 8, :]

    out[...], low = log_tile(item[0:items, :], rte, False)

    @pl.when(jnp.logical_not(above(jnp.minimum(low, rte))))
    def _():
        def redo(t, step, _):
            place = pl.ds(t, step)
            out[place, :] = log_tile(item[place, :], rte, True)[0]

        redo_loop(items, redo)


def item_log_call(item, after, items, depth):
    return pl.pallas_call(
        functools.partial(item_log_kernel, items=items),
        out_shape=jax.ShapeDtypeStruct((items, depth), BF16),
        in_specs=[VMEM_SPEC, VMEM_SPEC],
        out_specs=VMEM_SPEC,
        compiler_params=PARAMS,
        cost_estimate=pl.CostEstimate(
            flops=40 * items * depth, bytes_accessed=items * depth * 6, transcendentals=items * depth),
        name="item_log",
    )(item, after)


def swapped(value, axis, mask):
    return lax.ppermute(value, axis, [(a, a ^ mask) for a in range(lax.axis_size(axis))])


def moved(choice, value, then=None, operands=()):
    def branch(mask, value, *operands):
        arrived = swapped(value, "users", mask)
        return arrived if then is None else then(arrived, *operands)

    choices = [functools.partial(branch, mask) for mask in range(1, lax.axis_size("users"))]
    return lax.switch(choice, choices, value, *operands)


def exchanged(value):
    size = lax.axis_size("items")
    if size == 1:
        return value, jnp.zeros_like(value)
    mask = 1
    while mask * 2 < size:
        value = value + swapped(value, "items", mask)
        mask *= 2
    return value, swapped(value, "items", mask)


def per_device(interactions, matchings, user_shape, item_shape):
    group = lax.axis_size("users")
    factor = float(group)
    users, depth = user_shape.shape
    items = item_shape.shape[0]
    sizes = chunk_rows(users)
    starts = [sum(sizes[:i]) for i in range(len(sizes))]
    count = len(sizes)

    item, choices = prepare_call(matchings, item_shape, group - 1)
    order = [(s, at, rows) for s in range(STRATA) for at, rows in zip(starts, sizes)]

    def opening(arrived, user_shape, interactions):
        theta, counts, uexps = start_call(user_shape, interactions, sizes)
        operands = {"counts": counts, "interactions": interactions, "uexp_in": uexps[0], "item": arrived}
        if count == 1:
            operands["theta"] = theta
        out = stratum_call(
            0, 0, sizes[0], items, depth, factor, True, count == 1, 0, 0, order[1], operands)
        return theta, [out["uexp"], *uexps[1:]], out

    theta, uexps, opened = moved(choices[0], item, opening, (user_shape, interactions))
    rte = None
    shp = [None] * count
    sums = [None] * count
    for stratum in range(STRATA):
        carried = {"theta": theta}
        earlier = {}
        for i, (at, rows) in enumerate(zip(starts, sizes)):
            first, last = i == 0, i == count - 1
            step = stratum * count + i
            ahead = order[step + 1] if step + 1 < len(order) else None
            tail = tail_rows(rows) if last and stratum == STRATA - 1 else 0
            operands = {"counts": counts} if step else {}
            if ahead:
                operands["interactions"] = interactions
            if stratum == 0:
                operands["uexp"] = uexps[i]
            else:
                operands["acc"], operands["recv"] = sums[i]
                if stratum == 1:
                    operands["user_shape"] = user_shape
                else:
                    operands["shp_old"] = shp[i]
                if not first:
                    operands["rte"] = rte
                elif stratum > 1:
                    operands["rte_old"] = rte
            if first:
                operands["item"] = item
            elif last:
                operands["item_kept"] = carried["item_kept"]
            if not first:
                operands["item_exp"] = carried["item_exp"]
            if last:
                operands.update(earlier)
            if (stratum > 0 and not first) or (stratum == 0 and last):
                operands["theta"] = carried["theta"]
            if step == 0:
                out = opened
            else:
                out = stratum_call(
                    stratum, at, rows, items, depth, factor, first, last, i, tail, ahead, operands)
            counts = out.get("counts_ahead")
            shp[i] = out.get("shp_new")
            sums[i] = exchanged(out["upart"])
            if tail:
                tail_sums = exchanged(out["upart_tail"])
            if first:
                rte = out.get("rte_new")
                carried["item_exp"] = out["item_exp_new"]
                carried["item_kept"] = out["item_kept"]
            if last:
                item = out["item_new"]
            else:
                earlier[f"ratios{i}"], earlier[f"uexp{i}"] = out["ratios"], out.get("uexp", operands.get("uexp"))
                if stratum > 0:
                    carried["theta"] = out["theta_new"]
        if stratum + 1 < STRATA:
            item = moved(choices[stratum + 1], item)
        else:
            item = swapped(item, "users", group - 1)
    user_log = None
    pieces = [(at, rows, 0, sums[i], shp[i]) for i, (at, rows) in enumerate(zip(starts, sizes))]
    if tail:
        at, rows = starts[-1], sizes[-1] - tail
        pieces[-1:] = [(at, rows, 0, sums[-1], shp[-1]), (at + rows, tail, rows, tail_sums, shp[-1])]
    for i, (at, rows, shp_at, piece_sums, piece_shp) in enumerate(pieces):
        user_log, *rest = user_log_call(
            at, rows, shp_at, users, depth, factor, i == 0, (*piece_sums, piece_shp, rte), user_log)
        rte = rest[0] if rest else rte
        if i == max(len(pieces) - 2, 0):
            item_log = item_log_call(item, rte, items, depth)
    return user_log, item_log


def solution(mesh):
    placed = (P(None, "users", "items"), P(), P("users", None), P(("users", "items"), None))
    return jax.shard_map(
        per_device,
        mesh=mesh,
        in_specs=placed,
        out_specs=(P("users", None), P(("users", "items"), None)),
        check_vma=False,
    )
```

```python
import functools

import jax
import jax.numpy as jnp
from jax import lax
from jax.experimental import pallas as pl
from jax.experimental.pallas import tpu as pltpu
from jax.sharding import PartitionSpec as P

STRATA = 3
TILE = 64
START_TILE = 128
REDO_TILE = 32
F32 = jnp.float32
BF16 = jnp.bfloat16


def chunk_rows(rows):
    first = max(rows * 3 // 5 // START_TILE, 1) * START_TILE
    return [first, rows - first] if first < rows else [rows]


def tail_rows(rows):
    return rows // 2 // TILE * TILE


def psi_parts(x):
    small = x < 8.0
    w = jnp.where(small, x + 3.5, x - 0.5)
    q = x * (x + 3.0)
    q2 = q + 2.0
    bounded = jnp.minimum(w, 1e9)
    square = bounded * bounded
    steps = jnp.where(small, q * q2, 1.0)
    r = 1.0 / (square * steps)
    s = r * steps
    shift = (2.0 * x + 3.0) * (q + q2) * (r * square)
    g = s * (1.0 / 24.0 - s * (7.0 / 960.0 - s * (31.0 / 8064.0 - s * (127.0 / 30720.0))))
    return w, g - jnp.where(small, shift, 0.0)


def psi_any(x):
    mirrored = x < 0.5
    w, g = psi_parts(jnp.where(mirrored, 1.0 - x, x))
    value = jnp.log(w) + g
    t = x - jnp.floor(x + 0.5)
    u = 3.14159265358979 * t
    v = u * u
    sin = 1.0 / 6227020800.0
    for c in (-1.0 / 39916800.0, 1.0 / 362880.0, -1.0 / 5040.0, 1.0 / 120.0, -1.0 / 6.0, 1.0):
        sin = sin * v + c
    cos = -1.0 / 87178291200.0
    for c in (1.0 / 479001600.0, -1.0 / 3628800.0, 1.0 / 40320.0, -1.0 / 720.0, 1.0 / 24.0, -0.5, 1.0):
        cos = cos * v + c
    value = jnp.where(mirrored, value - 3.14159265358979 * cos / (sin * u), value)
    return jnp.where((x <= 0.0) & (x == jnp.floor(x)), jnp.nan, value)


LOWEST = 0.01


def above(low):
    return jnp.min(low) >= LOWEST


def folded(x):
    return x.reshape(x.shape[0] // 8, 8, x.shape[1])


def tiles(rows):
    step = TILE if rows % TILE == 0 else rows
    return [(at, step) for at in range(0, rows, step)]


def redo_loop(rows, step, carry=None):
    size = REDO_TILE if rows % REDO_TILE == 0 else 8
    return lax.fori_loop(
        0, rows // size, lambda i, c: step(pl.multiple_of(i * size, size), size, c), carry)


def exp_tile(x, rte, general):
    shape = x.shape
    x = folded(x)
    if general:
        value = psi_any(x)
        if rte is not None:
            value = value - jnp.log(rte)[None]
        value = jnp.exp(value)
    else:
        w, g = psi_parts(x)
        value = w if rte is None else w * (1.0 / rte)[None]
        value = value * jnp.exp(g)
    mean = x if rte is None else x * (1.0 / rte)[None]
    return value.reshape(shape).astype(BF16), jnp.sum(mean, axis=0), jnp.min(x, axis=0)


def log_tile(x, rte, general):
    shape = x.shape
    x = folded(x)
    if general:
        value = psi_any(x) - jnp.log(rte)[None]
    else:
        w, g = psi_parts(x)
        value = (jnp.log(w) - jnp.log(rte)[None]) + g
    return value.reshape(shape).astype(BF16), jnp.min(x, axis=0)


def row_sum(x):
    return jnp.broadcast_to(jnp.sum(x, axis=0, keepdims=True), x.shape)


VMEM_SPEC = pl.BlockSpec(memory_space=pltpu.VMEM)
SMEM_SPEC = pl.BlockSpec(memory_space=pltpu.SMEM)
HBM_SPEC = pl.BlockSpec(memory_space=pltpu.HBM)
PARAMS = pltpu.CompilerParams(vmem_limit_bytes=24 * 2**20)


def in_hbm(x):
    return pltpu.with_memory_space_constraint(x, pltpu.HBM)


def in_vmem(x):
    return pltpu.with_memory_space_constraint(x, pltpu.VMEM)


def prepare_kernel(matchings_hbm, shape_hbm, item, *refs, last):
    choices, (matchings, shape, sems) = refs[:STRATA], refs[STRATA:]
    copies = [
        pltpu.make_async_copy(shape_hbm, shape, sems.at[0]),
        pltpu.make_async_copy(matchings_hbm, matchings, sems.at[1]),
    ]
    for copy in copies:
        copy.start()
    for copy in copies:
        copy.wait()
    item[...] = shape[...].astype(F32)
    choices[0][0] = matchings[0] - 1
    for stratum in range(1, STRATA - 1):
        choices[stratum][0] = jnp.bitwise_xor(matchings[stratum - 1], matchings[stratum]) - 1
    choices[STRATA - 1][0] = jnp.bitwise_xor(matchings[STRATA - 2], last) - 1


def prepare_call(matchings, item_shape, last):
    out = pl.pallas_call(
        functools.partial(prepare_kernel, last=last),
        out_shape=[jax.ShapeDtypeStruct(item_shape.shape, F32)]
        + [pltpu.SMEM((1,), jnp.int32)] * STRATA,
        in_specs=[HBM_SPEC, HBM_SPEC],
        out_specs=[VMEM_SPEC] + [SMEM_SPEC] * STRATA,
        scratch_shapes=[pltpu.SMEM(matchings.shape, jnp.int32), pltpu.VMEM(item_shape.shape, BF16),
                        pltpu.SemaphoreType.DMA((2,))],
        compiler_params=PARAMS,
        name="prepare",
    )(in_hbm(matchings), in_hbm(item_shape))
    return out[0], [choice[0] for choice in out[1:]]


def start_kernel(shape_hbm, interactions, theta, counts, *refs):
    uexps, (shape, sems) = refs[:-2], refs[-2:]
    depth = shape.shape[1]
    load = pltpu.make_async_copy(shape_hbm, shape, sems.at[0])
    ahead = pltpu.make_async_copy(interactions.at[0, pl.ds(0, counts.shape[0]), :], counts, sems.at[1])
    load.start()
    ahead.start()
    load.wait()
    total, low = jnp.zeros((8, depth), F32), jnp.ones((8, depth), F32)
    begin = 0
    for uexp in uexps:
        rows = uexp.shape[0]

        def step(i, carry, begin=begin, uexp=uexp):
            at = i * START_TILE
            x = shape[pl.ds(pl.multiple_of(begin + at, START_TILE), START_TILE), :].astype(F32)
            value, part, part_low = exp_tile(x, None, False)
            uexp[pl.ds(pl.multiple_of(at, START_TILE), START_TILE), :] = value
            return carry[0] + part, jnp.minimum(carry[1], part_low)

        total, low = lax.fori_loop(0, rows // START_TILE, step, (total, low))
        begin += rows
    theta[...] = total

    @pl.when(jnp.logical_not(above(low)))
    def _():
        begin = 0
        for uexp in uexps:

            def redo(at, size, _, begin=begin, uexp=uexp):
                x = shape[pl.ds(pl.multiple_of(begin + at, size), size), :].astype(F32)
                uexp[pl.ds(at, size), :] = exp_tile(x, None, True)[0]

            redo_loop(uexp.shape[0], redo)
            begin += uexp.shape[0]

    ahead.wait()


def start_call(user_shape, interactions, sizes):
    rows, depth = user_shape.shape
    items = interactions.shape[2]
    theta, counts, *uexps = pl.pallas_call(
        start_kernel,
        out_shape=[pltpu.VMEM((8, depth), F32), pltpu.VMEM((sizes[0], items), BF16)]
        + [pltpu.VMEM((size, depth), BF16) for size in sizes],
        in_specs=[HBM_SPEC] * 2,
        out_specs=[VMEM_SPEC] * (2 + len(sizes)),
        scratch_shapes=[pltpu.VMEM((rows, depth), BF16), pltpu.SemaphoreType.DMA((2,))],
        compiler_params=PARAMS,
        cost_estimate=pl.CostEstimate(
            flops=40 * rows * depth, bytes_accessed=rows * depth * 4, transcendentals=2 * rows * depth),
        name="user_start",
    )(in_hbm(user_shape), in_hbm(interactions))
    return theta, counts, uexps


def dot_rows(a, b):
    return lax.dot_general(a, b, (((1,), (1,)), ((), ())), preferred_element_type=F32)


def item_sums(ratios, uexp):
    return lax.dot_general(ratios[...], uexp[...], (((0,), (0,)), ((), ())), preferred_element_type=F32)


def stratum_kernel(names, *refs, stratum, at, rows, items, factor, first, last, earlier, tail, ahead):
    ref = dict(zip(names, refs))
    copies = {}

    def fetch(name, source, target):
        copies[name] = pltpu.make_async_copy(source, target, ref["sems"].at[len(copies)])
        copies[name].start()

    if first and stratum > 0:
        fetch("item", ref["item"], ref["item_kept"])
    if ahead:
        fetch("ahead", ref["interactions"].at[ahead[0], pl.ds(ahead[1], ahead[2]), :], ref["counts_ahead"])
    upart, counts, ratios, denominator = ref["upart"], ref["counts"], ref["ratios"], ref["denominator"]
    uexp = ref["uexp"]
    extra = 8 if first else 0

    lows = []
    theta = None
    item = ref["item_kept"] if first or last else None

    if stratum > 0:
        if first:
            beta = row_sum(ref["acc"][0:8, :] + ref["recv"][0:8, :])
            old = 1.0 if stratum == 1 else ref["rte_old"][...]
            rte = 0.5 * old + 0.5 * (0.3 + factor * beta)
            ref["rte_new"][...] = rte
        else:
            rte = ref["rte"][...]
        lows.append(rte)
        for t, step in tiles(rows):
            old = ref["user_shape"][at + t:at + t + step, :].astype(F32) if stratum == 1 else ref["shp_old"][t:t + step, :]
            stat = ref["acc"][extra + t:extra + t + step, :] + ref["recv"][extra + t:extra + t + step, :]
            shp = 0.5 * old + 0.5 * (0.3 + factor * stat)
            ref["shp_new"][t:t + step, :] = shp
            value, part, low = exp_tile(shp, rte, False)
            uexp[t:t + step, :] = value
            theta = part if theta is None else theta + part
            lows.append(low)
        if not first:
            theta = theta + ref["theta"][...]
        if not last:
            ref["theta_new"][...] = theta
    elif last:
        theta = ref["theta"][...]

    if first and stratum > 0:
        copies["item"].wait()
    elif first:
        item[...] = ref["item"][...]
        uexp[...] = ref["uexp_in"][...]
    if first or last:
        item_rte = None if stratum == 0 else item[items:items + 8, :]
    if first:
        item_exp, sums, low = exp_tile(item[0:items, :], item_rte, False)
        ref["item_exp_new"][...] = item_exp
        upart[0:8, :] = sums
        lows.append(low)
        if item_rte is not None:
            lows.append(item_rte)
    else:
        item_exp = ref["item_exp"][...]

    denominator[...] = dot_rows(uexp[...], item_exp)
    for t, step in tiles(rows):
        ratios[t:t + step, :] = (
            counts[t:t + step, :].astype(F32) / denominator[t:t + step, :]).astype(BF16)
    user_sums = uexp[...].astype(F32) * jnp.dot(ratios[...], item_exp, preferred_element_type=F32)
    upart[extra:extra + rows - tail, :] = user_sums[0:rows - tail, :]
    if tail:
        ref["upart_tail"][...] = user_sums[rows - tail:, :]
    pairs = [(ref[f"ratios{i}"], ref[f"uexp{i}"]) for i in range(earlier)] + [(ratios, uexp)]

    def update_items(istat):
        old = 1.0 if item_rte is None else item_rte
        kept = ref["item_exp_new" if first else "item_exp"][...].astype(F32)
        ref["item_new"][0:items, :] = 0.5 * item[0:items, :] + 0.5 * (0.3 + factor * (kept * istat))
        ref["item_new"][items:items + 8, :] = 0.5 * old + 0.5 * (0.3 + factor * row_sum(theta))

    if last:
        istat = None
        for pair in pairs:
            part = item_sums(*pair)
            istat = part if istat is None else istat + part
        update_items(istat)

    if lows:

        @pl.when(jnp.logical_not(above(functools.reduce(jnp.minimum, lows))))
        def _():
            if stratum > 0:

                def redo_users(at, size, _):
                    place = pl.ds(at, size)
                    uexp[place, :] = exp_tile(ref["shp_new"][place, :], rte, True)[0]

                redo_loop(rows, redo_users)
            if first:

                def redo_items(at, size, _):
                    place = pl.ds(at, size)
                    ref["item_exp_new"][place, :] = exp_tile(item[place, :], item_rte, True)[0]

                redo_loop(items, redo_items)
            kept = ref["item_exp_new" if first else "item_exp"]
            for target, begin, skip, length in (
                (upart, 0, extra, rows - tail), (ref.get("upart_tail"), rows - tail, 0, tail)):

                def redo_sums(at, size, _):
                    place = pl.ds(pl.multiple_of(begin + at, size), size)
                    u = uexp[place, :]
                    ratio = (counts[place, :].astype(F32) / dot_rows(u, kept[...])).astype(BF16)
                    ratios[place, :] = ratio
                    target[pl.ds(pl.multiple_of(skip + at, 8), size), :] = u.astype(F32) * jnp.dot(
                        ratio, kept[...], preferred_element_type=F32)

                if length:
                    redo_loop(length, redo_sums)
            if last:
                total = ref["item_new"].at[pl.ds(0, items), :]
                total[...] = jnp.zeros((items, ref["item_new"].shape[1]), F32)
                for pair in pairs:

                    def redo_stat(at, size, _):
                        place = pl.ds(at, size)
                        total[...] += item_sums(pair[0].at[place, :], pair[1].at[place, :])

                    redo_loop(rows if pair[0] is ratios else pair[0].shape[0], redo_stat)
                update_items(total[...])

    if ahead:
        copies["ahead"].wait()


def stratum_call(stratum, at, rows, items, depth, factor, first, last, earlier, tail, ahead, operands):
    extra = 8 if first else 0
    outs = {"upart": ((rows + extra - tail, depth), F32)}
    if tail:
        outs["upart_tail"] = ((tail, depth), F32)
    if stratum > 0:
        outs["shp_new"] = ((rows, depth), F32)
    if first and stratum > 0:
        outs["rte_new"] = ((8, depth), F32)
    if first:
        outs["item_exp_new"] = ((items, depth), BF16)
    if first:
        outs["item_kept"] = (operands["item"].shape, F32)
    if last:
        outs["item_new"] = ((items + 8, depth), F32)
    else:
        outs["ratios"] = ((rows, items), BF16)
        outs["uexp"] = ((rows, depth), BF16)
        if stratum > 0:
            outs["theta_new"] = ((8, depth), F32)
    if ahead:
        outs["counts_ahead"] = ((ahead[2], items), BF16)
    scratch = {
        "denominator": pltpu.VMEM((rows, items), F32),
        "sems": pltpu.SemaphoreType.DMA((2,)),
    }
    if last:
        scratch["ratios"] = pltpu.VMEM((rows, items), BF16)
        if stratum > 0:
            scratch["uexp"] = pltpu.VMEM((rows, depth), BF16)
    hbm = ("interactions", "item") if stratum > 0 else ("interactions",)
    operands = {
        name: in_hbm(x) if name in hbm else in_vmem(x) if name in ("user_shape", "item") else x
        for name, x in operands.items()}
    names = list(operands) + list(outs) + list(scratch)
    kernel = functools.partial(
        stratum_kernel, names, stratum=stratum, at=at, rows=rows, items=items,
        factor=factor, first=first, last=last, earlier=earlier, tail=tail, ahead=ahead)
    results = pl.pallas_call(
        kernel,
        out_shape=[jax.ShapeDtypeStruct(*spec) for spec in outs.values()],
        in_specs=[HBM_SPEC if name in hbm else VMEM_SPEC for name in operands],
        out_specs=[VMEM_SPEC] * len(outs),
        scratch_shapes=list(scratch.values()),
        compiler_params=PARAMS,
        cost_estimate=pl.CostEstimate(flops=1, bytes_accessed=1, transcendentals=0),
        name=f"stratum{stratum}_at{at}",
    )(*operands.values())
    return dict(zip(outs, results))


def user_log_kernel(*refs, at, rows, shp_at, factor, first, filled):
    acc, recv, shp_old, rte_in = refs[:4]
    rest = refs[5:] if filled else refs[4:]
    out, *rte_out, block, sem = rest
    rte = rte_in[...]
    if first:
        rte = 0.5 * rte + 0.5 * (0.3 + factor * row_sum(acc[0:8, :] + recv[0:8, :]))
    for ref in rte_out:
        ref[...] = rte
    extra = 8 if first else 0

    def shape(t, step):
        stat = acc[pl.ds(extra + t, step), :] + recv[pl.ds(extra + t, step), :]
        return 0.5 * shp_old[pl.ds(shp_at + t, step), :] + 0.5 * (0.3 + factor * stat)

    low = rte
    for t, step in tiles(rows):
        block[t:t + step, :], part_low = log_tile(shape(t, step), rte, False)
        low = jnp.minimum(low, part_low)

    @pl.when(jnp.logical_not(above(low)))
    def _():
        def redo(t, step, _):
            block[pl.ds(t, step), :] = log_tile(shape(pl.multiple_of(t, 8), step), rte, True)[0]

        redo_loop(rows, redo)

    copy = pltpu.make_async_copy(block, out.at[pl.ds(at, rows), :], sem)
    copy.start()
    copy.wait()


def user_log_call(at, rows, shp_at, total, depth, factor, first, operands, filled):
    out_shape = [jax.ShapeDtypeStruct((total, depth), BF16)]
    out_specs = [HBM_SPEC]
    if at + rows < total:
        out_shape.append(jax.ShapeDtypeStruct((8, depth), F32))
        out_specs.append(VMEM_SPEC)
    operands = list(operands)
    in_specs = [VMEM_SPEC] * 4
    if filled is not None:
        operands.append(filled)
        in_specs.append(HBM_SPEC)
    return pl.pallas_call(
        functools.partial(user_log_kernel, at=at, rows=rows, shp_at=shp_at, factor=factor, first=first,
                          filled=filled is not None),
        out_shape=out_shape,
        in_specs=in_specs,
        out_specs=out_specs,
        input_output_aliases={} if filled is None else {4: 0},
        scratch_shapes=[pltpu.VMEM((rows, depth), BF16), pltpu.SemaphoreType.DMA],
        compiler_params=PARAMS,
        cost_estimate=pl.CostEstimate(
            flops=40 * rows * depth, bytes_accessed=rows * depth * 14, transcendentals=rows * depth),
        name=f"user_log_at{at}",
    )(*operands)


def item_log_kernel(item, _, out, *, items):
    rte = item[items:items + 8, :]

    out[...], low = log_tile(item[0:items, :], rte, False)

    @pl.when(jnp.logical_not(above(jnp.minimum(low, rte))))
    def _():
        def redo(t, step, _):
            place = pl.ds(t, step)
            out[place, :] = log_tile(item[place, :], rte, True)[0]

        redo_loop(items, redo)


def item_log_call(item, after, items, depth):
    return pl.pallas_call(
        functools.partial(item_log_kernel, items=items),
        out_shape=jax.ShapeDtypeStruct((items, depth), BF16),
        in_specs=[VMEM_SPEC, VMEM_SPEC],
        out_specs=VMEM_SPEC,
        compiler_params=PARAMS,
        cost_estimate=pl.CostEstimate(
            flops=40 * items * depth, bytes_accessed=items * depth * 6, transcendentals=items * depth),
        name="item_log",
    )(item, after)


def swapped(value, axis, mask):
    return lax.ppermute(value, axis, [(a, a ^ mask) for a in range(lax.axis_size(axis))])


def moved(choice, value, then=None, operands=()):
    def branch(mask, value, *operands):
        arrived = swapped(value, "users", mask)
        return arrived if then is None else then(arrived, *operands)

    choices = [functools.partial(branch, mask) for mask in range(1, lax.axis_size("users"))]
    return lax.switch(choice, choices, value, *operands)


def exchanged(value):
    size = lax.axis_size("items")
    if size == 1:
        return value, jnp.zeros_like(value)
    mask = 1
    while mask * 2 < size:
        value = value + swapped(value, "items", mask)
        mask *= 2
    return value, swapped(value, "items", mask)


def per_device(interactions, matchings, user_shape, item_shape):
    group = lax.axis_size("users")
    factor = float(group)
    users, depth = user_shape.shape
    items = item_shape.shape[0]
    sizes = chunk_rows(users)
    starts = [sum(sizes[:i]) for i in range(len(sizes))]
    count = len(sizes)

    item, choices = prepare_call(matchings, item_shape, group - 1)
    order = [(s, at, rows) for s in range(STRATA) for at, rows in zip(starts, sizes)]

    def opening(arrived, user_shape, interactions):
        theta, counts, uexps = start_call(user_shape, interactions, sizes)
        operands = {"counts": counts, "interactions": interactions, "uexp_in": uexps[0], "item": arrived}
        if count == 1:
            operands["theta"] = theta
        out = stratum_call(
            0, 0, sizes[0], items, depth, factor, True, count == 1, 0, 0, order[1], operands)
        return theta, [out["uexp"], *uexps[1:]], out

    theta, uexps, opened = moved(choices[0], item, opening, (user_shape, interactions))
    rte = None
    shp = [None] * count
    sums = [None] * count
    for stratum in range(STRATA):
        carried = {"theta": theta}
        earlier = {}
        for i, (at, rows) in enumerate(zip(starts, sizes)):
            first, last = i == 0, i == count - 1
            step = stratum * count + i
            ahead = order[step + 1] if step + 1 < len(order) else None
            tail = tail_rows(rows) if last and stratum == STRATA - 1 else 0
            operands = {"counts": counts} if step else {}
            if ahead:
                operands["interactions"] = interactions
            if stratum == 0:
                operands["uexp"] = uexps[i]
            else:
                operands["acc"], operands["recv"] = sums[i]
                if stratum == 1:
                    operands["user_shape"] = user_shape
                else:
                    operands["shp_old"] = shp[i]
                if not first:
                    operands["rte"] = rte
                elif stratum > 1:
                    operands["rte_old"] = rte
            if first:
                operands["item"] = item
            elif last:
                operands["item_kept"] = carried["item_kept"]
            if not first:
                operands["item_exp"] = carried["item_exp"]
            if last:
                operands.update(earlier)
            if (stratum > 0 and not first) or (stratum == 0 and last):
                operands["theta"] = carried["theta"]
            if step == 0:
                out = opened
            else:
                out = stratum_call(
                    stratum, at, rows, items, depth, factor, first, last, i, tail, ahead, operands)
            counts = out.get("counts_ahead")
            shp[i] = out.get("shp_new")
            sums[i] = exchanged(out["upart"])
            if tail:
                tail_sums = exchanged(out["upart_tail"])
            if first:
                rte = out.get("rte_new")
                carried["item_exp"] = out["item_exp_new"]
                carried["item_kept"] = out["item_kept"]
            if last:
                item = out["item_new"]
            else:
                earlier[f"ratios{i}"], earlier[f"uexp{i}"] = out["ratios"], out.get("uexp", operands.get("uexp"))
                if stratum > 0:
                    carried["theta"] = out["theta_new"]
        if stratum + 1 < STRATA:
            item = moved(choices[stratum + 1], item)
        else:
            item = swapped(item, "users", group - 1)
    user_log = None
    pieces = [(at, rows, 0, sums[i], shp[i]) for i, (at, rows) in enumerate(zip(starts, sizes))]
    if tail:
        at, rows = starts[-1], sizes[-1] - tail
        pieces[-1:] = [(at, rows, 0, sums[-1], shp[-1]), (at + rows, tail, rows, tail_sums, shp[-1])]
    for i, (at, rows, shp_at, piece_sums, piece_shp) in enumerate(pieces):
        user_log, *rest = user_log_call(
            at, rows, shp_at, users, depth, factor, i == 0, (*piece_sums, piece_shp, rte), user_log)
        rte = rest[0] if rest else rte
        if i == max(len(pieces) - 2, 0):
            item_log = item_log_call(item, rte, items, depth)
    return user_log, item_log


def solution(mesh):
    placed = (P(None, "users", "items"), P(), P("users", None), P(("users", "items"), None))
    return jax.shard_map(
        per_device,
        mesh=mesh,
        in_specs=placed,
        out_specs=(P("users", None), P(("users", "items"), None)),
        check_vma=False,
    )
```

```python
import functools

import jax
import jax.numpy as jnp
from jax import lax
from jax.experimental import pallas as pl
from jax.experimental.pallas import tpu as pltpu
from jax.sharding import PartitionSpec as P

STRATA = 3
TILE = 64
START_TILE = 128
REDO_TILE = 32
F32 = jnp.float32
BF16 = jnp.bfloat16


def chunk_rows(rows):
    first = max(rows // 2 // START_TILE, 1) * START_TILE
    return [first, rows - first] if first < rows else [rows]


def last_cuts(rows):
    count = -(-rows // (4 * TILE))
    tiles_of = [rows // TILE // count + (i < rows // TILE % count) for i in range(count)]
    return [n * TILE for n in tiles_of] if rows % TILE == 0 else [rows]


def psi_parts(x):
    small = x < 8.0
    w = jnp.where(small, x + 3.5, x - 0.5)
    q = x * (x + 3.0)
    q2 = q + 2.0
    bounded = jnp.minimum(w, 1e9)
    square = bounded * bounded
    steps = jnp.where(small, q * q2, 1.0)
    r = 1.0 / (square * steps)
    s = r * steps
    shift = (2.0 * x + 3.0) * (q + q2) * (r * square)
    g = s * (1.0 / 24.0 - s * (7.0 / 960.0 - s * (31.0 / 8064.0 - s * (127.0 / 30720.0))))
    return w, g - jnp.where(small, shift, 0.0)


def psi_any(x):
    mirrored = x < 0.5
    w, g = psi_parts(jnp.where(mirrored, 1.0 - x, x))
    value = jnp.log(w) + g
    t = x - jnp.floor(x + 0.5)
    u = 3.14159265358979 * t
    v = u * u
    sin = 1.0 / 6227020800.0
    for c in (-1.0 / 39916800.0, 1.0 / 362880.0, -1.0 / 5040.0, 1.0 / 120.0, -1.0 / 6.0, 1.0):
        sin = sin * v + c
    cos = -1.0 / 87178291200.0
    for c in (1.0 / 479001600.0, -1.0 / 3628800.0, 1.0 / 40320.0, -1.0 / 720.0, 1.0 / 24.0, -0.5, 1.0):
        cos = cos * v + c
    value = jnp.where(mirrored, value - 3.14159265358979 * cos / (sin * u), value)
    return jnp.where((x <= 0.0) & (x == jnp.floor(x)), jnp.nan, value)


LOWEST = 0.01
HIGHEST = 1e30


def usual(rte):
    return jnp.where(rte <= HIGHEST, rte, -1.0)


def above(low):
    return jnp.min(low) >= LOWEST


def folded(x):
    return x.reshape(x.shape[0] // 8, 8, x.shape[1])


def tiles(rows):
    step = TILE if rows % TILE == 0 else rows
    return [(at, step) for at in range(0, rows, step)]


def redo_loop(rows, step, carry=None):
    size = REDO_TILE if rows % REDO_TILE == 0 else 8
    return lax.fori_loop(
        0, rows // size, lambda i, c: step(pl.multiple_of(i * size, size), size, c), carry)


def exp_tile(x, rte, general):
    shape = x.shape
    x = folded(x)
    if general:
        value = psi_any(x)
        if rte is not None:
            value = value - jnp.log(rte)[None]
        value = jnp.exp(value)
    else:
        w, g = psi_parts(x)
        value = w if rte is None else w * (1.0 / rte)[None]
        value = value * jnp.exp(g)
    mean = x if rte is None else x / rte[None] if general else x * (1.0 / rte)[None]
    return value.reshape(shape).astype(BF16), jnp.sum(mean, axis=0), jnp.min(x, axis=0)


def log_tile(x, rte, general):
    shape = x.shape
    x = folded(x)
    if general:
        value = psi_any(x) - jnp.log(rte)[None]
    else:
        w, g = psi_parts(x)
        value = (jnp.log(w) - jnp.log(rte)[None]) + g
    return value.reshape(shape).astype(BF16), jnp.min(x, axis=0)


def row_sum(x):
    return jnp.broadcast_to(jnp.sum(x, axis=0, keepdims=True), x.shape)


VMEM_SPEC = pl.BlockSpec(memory_space=pltpu.VMEM)
SMEM_SPEC = pl.BlockSpec(memory_space=pltpu.SMEM)
HBM_SPEC = pl.BlockSpec(memory_space=pltpu.HBM)
PARAMS = pltpu.CompilerParams(vmem_limit_bytes=24 * 2**20)


def in_hbm(x):
    return pltpu.with_memory_space_constraint(x, pltpu.HBM)


def in_vmem(x):
    return pltpu.with_memory_space_constraint(x, pltpu.VMEM)


def prepare_kernel(matchings_hbm, shape_hbm, item, *refs, last):
    choices, (matchings, shape, sems) = refs[:STRATA], refs[STRATA:]
    copies = [
        pltpu.make_async_copy(shape_hbm, shape, sems.at[0]),
        pltpu.make_async_copy(matchings_hbm, matchings, sems.at[1]),
    ]
    for copy in copies:
        copy.start()
    for copy in copies:
        copy.wait()
    item[...] = shape[...].astype(F32)
    choices[0][0] = matchings[0] - 1
    for stratum in range(1, STRATA - 1):
        choices[stratum][0] = jnp.bitwise_xor(matchings[stratum - 1], matchings[stratum]) - 1
    choices[STRATA - 1][0] = jnp.bitwise_xor(matchings[STRATA - 2], last) - 1


def prepare_call(matchings, item_shape, last):
    out = pl.pallas_call(
        functools.partial(prepare_kernel, last=last),
        out_shape=[jax.ShapeDtypeStruct(item_shape.shape, F32)]
        + [pltpu.SMEM((1,), jnp.int32)] * STRATA,
        in_specs=[HBM_SPEC, HBM_SPEC],
        out_specs=[VMEM_SPEC] + [SMEM_SPEC] * STRATA,
        scratch_shapes=[pltpu.SMEM(matchings.shape, jnp.int32), pltpu.VMEM(item_shape.shape, BF16),
                        pltpu.SemaphoreType.DMA((2,))],
        compiler_params=PARAMS,
        name="prepare",
    )(in_hbm(matchings), in_hbm(item_shape))
    return out[0], [choice[0] for choice in out[1:]]


def start_kernel(shape_hbm, interactions, theta, counts, *refs):
    uexps, (shape, sems) = refs[:-2], refs[-2:]
    depth = shape.shape[1]
    load = pltpu.make_async_copy(shape_hbm, shape, sems.at[0])
    ahead = pltpu.make_async_copy(interactions.at[0, pl.ds(0, counts.shape[0]), :], counts, sems.at[1])
    load.start()
    ahead.start()
    load.wait()
    total, low = jnp.zeros((8, depth), F32), jnp.ones((8, depth), F32)
    begin = 0
    for uexp in uexps:
        rows = uexp.shape[0]

        def step(i, carry, begin=begin, uexp=uexp):
            at = i * START_TILE
            x = shape[pl.ds(pl.multiple_of(begin + at, START_TILE), START_TILE), :].astype(F32)
            value, part, part_low = exp_tile(x, None, False)
            uexp[pl.ds(pl.multiple_of(at, START_TILE), START_TILE), :] = value
            return carry[0] + part, jnp.minimum(carry[1], part_low)

        total, low = lax.fori_loop(0, rows // START_TILE, step, (total, low))
        begin += rows
    theta[...] = total

    @pl.when(jnp.logical_not(above(low)))
    def _():
        begin = 0
        for uexp in uexps:

            def redo(at, size, _, begin=begin, uexp=uexp):
                x = shape[pl.ds(pl.multiple_of(begin + at, size), size), :].astype(F32)
                uexp[pl.ds(at, size), :] = exp_tile(x, None, True)[0]

            redo_loop(uexp.shape[0], redo)
            begin += uexp.shape[0]

    ahead.wait()


def start_call(user_shape, interactions, sizes):
    rows, depth = user_shape.shape
    items = interactions.shape[2]
    theta, counts, *uexps = pl.pallas_call(
        start_kernel,
        out_shape=[pltpu.VMEM((8, depth), F32), pltpu.VMEM((sizes[0], items), BF16)]
        + [pltpu.VMEM((size, depth), BF16) for size in sizes],
        in_specs=[HBM_SPEC] * 2,
        out_specs=[VMEM_SPEC] * (2 + len(sizes)),
        scratch_shapes=[pltpu.VMEM((rows, depth), BF16), pltpu.SemaphoreType.DMA((2,))],
        compiler_params=PARAMS,
        cost_estimate=pl.CostEstimate(
            flops=40 * rows * depth, bytes_accessed=rows * depth * 4, transcendentals=2 * rows * depth),
        name="user_start",
    )(in_hbm(user_shape), in_hbm(interactions))
    return theta, counts, uexps


def dot_rows(a, b):
    return lax.dot_general(a, b, (((1,), (1,)), ((), ())), preferred_element_type=F32)


def item_sums(ratios, uexp):
    return lax.dot_general(ratios[...], uexp[...], (((0,), (0,)), ((), ())), preferred_element_type=F32)


def stratum_kernel(names, *refs, stratum, at, rows, items, factor, first, last, earlier, cuts, ahead):
    ref = dict(zip(names, refs))
    copies = {}

    def fetch(name, source, target):
        copies[name] = pltpu.make_async_copy(source, target, ref["sems"].at[len(copies)])
        copies[name].start()

    if first and stratum > 0:
        fetch("item", ref["item"], ref["item_kept"])
    if ahead:
        fetch("ahead", ref["interactions"].at[ahead[0], pl.ds(ahead[1], ahead[2]), :], ref["counts_ahead"])
    upart, counts, ratios, denominator = ref["upart0"], ref["counts"], ref["ratios"], ref["denominator"]
    uexp = ref["uexp"]
    extra = 8 if first else 0

    lows = []
    theta = None
    item = ref["item_kept"] if first or last else None

    if stratum > 0:
        if first:
            beta = row_sum(ref["acc"][0:8, :] + ref["recv"][0:8, :])
            old = 1.0 if stratum == 1 else ref["rte_old"][...]
            rte = 0.5 * old + 0.5 * (0.3 + factor * beta)
            ref["rte_new"][...] = rte
        else:
            rte = ref["rte"][...]
        lows.append(usual(rte))
        for t, step in tiles(rows):
            old = ref["user_shape"][at + t:at + t + step, :].astype(F32) if stratum == 1 else ref["shp_old"][t:t + step, :]
            stat = ref["acc"][extra + t:extra + t + step, :] + ref["recv"][extra + t:extra + t + step, :]
            shp = 0.5 * old + 0.5 * (0.3 + factor * stat)
            ref["shp_new"][t:t + step, :] = shp
            value, part, low = exp_tile(shp, rte, False)
            uexp[t:t + step, :] = value
            theta = part if theta is None else theta + part
            lows.append(low)
        if not first:
            theta = theta + ref["theta"][...]
        total_mean = ref["theta_new"]
        total_mean[...] = theta
    elif last:
        total_mean = ref["theta"]

    if first and stratum > 0:
        copies["item"].wait()
    elif first:
        item[...] = ref["item"][...]
        uexp[...] = ref["uexp_in"][...]
    if first or last:
        item_rte = None if stratum == 0 else item[items:items + 8, :]
    if first:
        item_exp, sums, low = exp_tile(item[0:items, :], item_rte, False)
        ref["item_exp_new"][...] = item_exp
        upart[0:8, :] = sums
        lows.append(low)
        if item_rte is not None:
            lows.append(usual(item_rte))
    else:
        item_exp = ref["item_exp"][...]

    denominator[...] = dot_rows(uexp[...], item_exp)
    for t, step in tiles(rows):
        ratios[t:t + step, :] = (
            counts[t:t + step, :].astype(F32) / denominator[t:t + step, :]).astype(BF16)
    user_sums = uexp[...].astype(F32) * jnp.dot(ratios[...], item_exp, preferred_element_type=F32)
    parts = []
    for i, length in enumerate(cuts):
        begin, skip = sum(cuts[:i]), 0 if i else extra
        parts.append((ref[f"upart{i}"], begin, skip, length))
        parts[i][0][skip:skip + length, :] = user_sums[begin:begin + length, :]
    pairs = [(ref[f"ratios{i}"], ref[f"uexp{i}"]) for i in range(earlier)] + [(ratios, uexp)]

    def update_items(istat):
        old = 1.0 if item_rte is None else item_rte
        kept = ref["item_exp_new" if first else "item_exp"][...].astype(F32)
        ref["item_new"][0:items, :] = 0.5 * item[0:items, :] + 0.5 * (0.3 + factor * (kept * istat))
        ref["item_new"][items:items + 8, :] = 0.5 * old + 0.5 * (0.3 + factor * row_sum(total_mean[...]))

    if last:
        istat = None
        for pair in pairs:
            part = item_sums(*pair)
            istat = part if istat is None else istat + part
        update_items(istat)

    if lows:

        @pl.when(jnp.logical_not(above(functools.reduce(jnp.minimum, lows))))
        def _():
            if stratum > 0:

                def redo_users(at, size, total):
                    place = pl.ds(at, size)
                    uexp[place, :], part, _ = exp_tile(ref["shp_new"][place, :], rte, True)
                    return total + part

                start = jnp.zeros_like(rte) if first else ref["theta"][...]
                total_mean[...] = redo_loop(rows, redo_users, start)
            if first:

                def redo_items(at, size, total):
                    place = pl.ds(at, size)
                    ref["item_exp_new"][place, :], part, _ = exp_tile(item[place, :], item_rte, True)
                    return total + part

                upart[0:8, :] = redo_loop(items, redo_items, jnp.zeros((8, upart.shape[1]), F32))
            kept = ref["item_exp_new" if first else "item_exp"]
            for target, begin, skip, length in parts:

                def redo_sums(at, size, _, target=target, begin=begin, skip=skip):
                    place = pl.ds(pl.multiple_of(begin + at, size), size)
                    u = uexp[place, :]
                    ratio = (counts[place, :].astype(F32) / dot_rows(u, kept[...])).astype(BF16)
                    ratios[place, :] = ratio
                    target[pl.ds(pl.multiple_of(skip + at, 8), size), :] = u.astype(F32) * jnp.dot(
                        ratio, kept[...], preferred_element_type=F32)

                redo_loop(length, redo_sums)
            if last:
                total = ref["item_new"].at[pl.ds(0, items), :]
                total[...] = jnp.zeros((items, ref["item_new"].shape[1]), F32)
                for pair in pairs:

                    def redo_stat(at, size, _, pair=pair):
                        place = pl.ds(at, size)
                        total[...] += item_sums(pair[0].at[place, :], pair[1].at[place, :])

                    redo_loop(rows if pair[0] is ratios else pair[0].shape[0], redo_stat)
                update_items(total[...])

    if ahead:
        copies["ahead"].wait()


def stratum_call(stratum, at, rows, items, depth, factor, first, last, earlier, cuts, ahead, operands):
    extra = 8 if first else 0
    outs = {f"upart{i}": ((size + (0 if i else extra), depth), F32) for i, size in enumerate(cuts)}
    if stratum > 0:
        outs["shp_new"] = ((rows, depth), F32)
    if first and stratum > 0:
        outs["rte_new"] = ((8, depth), F32)
    if first:
        outs["item_exp_new"] = ((items, depth), BF16)
    if first:
        outs["item_kept"] = (operands["item"].shape, F32)
    if last:
        outs["item_new"] = ((items + 8, depth), F32)
    else:
        outs["ratios"] = ((rows, items), BF16)
        outs["uexp"] = ((rows, depth), BF16)
        if stratum > 0:
            outs["theta_new"] = ((8, depth), F32)
    if ahead:
        outs["counts_ahead"] = ((ahead[2], items), BF16)
    scratch = {
        "denominator": pltpu.VMEM((rows, items), F32),
        "sems": pltpu.SemaphoreType.DMA((2,)),
    }
    if last:
        scratch["ratios"] = pltpu.VMEM((rows, items), BF16)
        if stratum > 0:
            scratch["uexp"] = pltpu.VMEM((rows, depth), BF16)
            scratch["theta_new"] = pltpu.VMEM((8, depth), F32)
    hbm = ("interactions", "item") if stratum > 0 else ("interactions",)
    operands = {
        name: in_hbm(x) if name in hbm else in_vmem(x) if name in ("user_shape", "item") else x
        for name, x in operands.items()}
    names = list(operands) + list(outs) + list(scratch)
    kernel = functools.partial(
        stratum_kernel, names, stratum=stratum, at=at, rows=rows, items=items,
        factor=factor, first=first, last=last, earlier=earlier, cuts=cuts, ahead=ahead)
    results = pl.pallas_call(
        kernel,
        out_shape=[jax.ShapeDtypeStruct(*spec) for spec in outs.values()],
        in_specs=[HBM_SPEC if name in hbm else VMEM_SPEC for name in operands],
        out_specs=[VMEM_SPEC] * len(outs),
        scratch_shapes=list(scratch.values()),
        compiler_params=PARAMS,
        cost_estimate=pl.CostEstimate(flops=1, bytes_accessed=1, transcendentals=0),
        name=f"stratum{stratum}_at{at}",
    )(*operands.values())
    return dict(zip(outs, results))


def user_log_kernel(*refs, at, rows, shp_at, factor, first, filled):
    acc, recv, shp_old, rte_in = refs[:4]
    rest = refs[5:] if filled else refs[4:]
    out, *rte_out, block, sem = rest
    rte = rte_in[...]
    if first:
        rte = 0.5 * rte + 0.5 * (0.3 + factor * row_sum(acc[0:8, :] + recv[0:8, :]))
    for ref in rte_out:
        ref[...] = rte
    extra = 8 if first else 0

    def shape(t, step):
        stat = acc[pl.ds(extra + t, step), :] + recv[pl.ds(extra + t, step), :]
        return 0.5 * shp_old[pl.ds(shp_at + t, step), :] + 0.5 * (0.3 + factor * stat)

    low = rte
    for t, step in tiles(rows):
        block[t:t + step, :], part_low = log_tile(shape(t, step), rte, False)
        low = jnp.minimum(low, part_low)

    @pl.when(jnp.logical_not(above(low)))
    def _():
        def redo(t, step, _):
            block[pl.ds(t, step), :] = log_tile(shape(pl.multiple_of(t, 8), step), rte, True)[0]

        redo_loop(rows, redo)

    copy = pltpu.make_async_copy(block, out.at[pl.ds(at, rows), :], sem)
    copy.start()
    copy.wait()


def user_log_call(at, rows, shp_at, total, depth, factor, first, operands, filled):
    out_shape = [jax.ShapeDtypeStruct((total, depth), BF16)]
    out_specs = [HBM_SPEC]
    if at + rows < total:
        out_shape.append(jax.ShapeDtypeStruct((8, depth), F32))
        out_specs.append(VMEM_SPEC)
    operands = list(operands)
    in_specs = [VMEM_SPEC] * 4
    if filled is not None:
        operands.append(filled)
        in_specs.append(HBM_SPEC)
    return pl.pallas_call(
        functools.partial(user_log_kernel, at=at, rows=rows, shp_at=shp_at, factor=factor, first=first,
                          filled=filled is not None),
        out_shape=out_shape,
        in_specs=in_specs,
        out_specs=out_specs,
        input_output_aliases={} if filled is None else {4: 0},
        scratch_shapes=[pltpu.VMEM((rows, depth), BF16), pltpu.SemaphoreType.DMA],
        compiler_params=PARAMS,
        cost_estimate=pl.CostEstimate(
            flops=40 * rows * depth, bytes_accessed=rows * depth * 14, transcendentals=rows * depth),
        name=f"user_log_at{at}",
    )(*operands)


def item_log_kernel(item, _, out, *, items):
    rte = item[items:items + 8, :]

    out[...], low = log_tile(item[0:items, :], rte, False)

    @pl.when(jnp.logical_not(above(jnp.minimum(low, rte))))
    def _():
        def redo(t, step, _):
            place = pl.ds(t, step)
            out[place, :] = log_tile(item[place, :], rte, True)[0]

        redo_loop(items, redo)


def item_log_call(item, after, items, depth):
    return pl.pallas_call(
        functools.partial(item_log_kernel, items=items),
        out_shape=jax.ShapeDtypeStruct((items, depth), BF16),
        in_specs=[VMEM_SPEC, VMEM_SPEC],
        out_specs=VMEM_SPEC,
        compiler_params=PARAMS,
        cost_estimate=pl.CostEstimate(
            flops=40 * items * depth, bytes_accessed=items * depth * 6, transcendentals=items * depth),
        name="item_log",
    )(item, after)


def swapped(value, axis, mask):
    return lax.ppermute(value, axis, [(a, a ^ mask) for a in range(lax.axis_size(axis))])


def moved(choice, value, then=None, operands=()):
    def branch(mask, value, *operands):
        arrived = swapped(value, "users", mask)
        return arrived if then is None else then(arrived, *operands)

    choices = [functools.partial(branch, mask) for mask in range(1, lax.axis_size("users"))]
    return lax.switch(choice, choices, value, *operands)


def exchanged(value):
    size = lax.axis_size("items")
    if size == 1:
        return value, jnp.zeros_like(value)
    mask = 1
    while mask * 2 < size:
        value = value + swapped(value, "items", mask)
        mask *= 2
    return value, swapped(value, "items", mask)


def per_device(interactions, matchings, user_shape, item_shape):
    group = lax.axis_size("users")
    factor = float(group)
    users, depth = user_shape.shape
    items = item_shape.shape[0]
    sizes = chunk_rows(users)
    starts = [sum(sizes[:i]) for i in range(len(sizes))]
    count = len(sizes)

    item, choices = prepare_call(matchings, item_shape, group - 1)
    order = [(s, at, rows) for s in range(STRATA) for at, rows in zip(starts, sizes)]

    def opening(arrived, user_shape, interactions):
        theta, counts, uexps = start_call(user_shape, interactions, sizes)
        operands = {"counts": counts, "interactions": interactions, "uexp_in": uexps[0], "item": arrived}
        if count == 1:
            operands["theta"] = theta
        out = stratum_call(
            0, 0, sizes[0], items, depth, factor, True, count == 1, 0, sizes[:1], order[1], operands)
        return theta, [out["uexp"], *uexps[1:]], out

    theta, uexps, opened = moved(choices[0], item, opening, (user_shape, interactions))
    rte = None
    shp = [None] * count
    sums = [None] * count
    for stratum in range(STRATA):
        carried = {"theta": theta}
        earlier = {}
        for i, (at, rows) in enumerate(zip(starts, sizes)):
            first, last = i == 0, i == count - 1
            step = stratum * count + i
            ahead = order[step + 1] if step + 1 < len(order) else None
            cuts = last_cuts(rows) if step + 1 == len(order) else [rows]
            operands = {"counts": counts} if step else {}
            if ahead:
                operands["interactions"] = interactions
            if stratum == 0:
                operands["uexp"] = uexps[i]
            else:
                operands["acc"], operands["recv"] = sums[i]
                if stratum == 1:
                    operands["user_shape"] = user_shape
                else:
                    operands["shp_old"] = shp[i]
                if not first:
                    operands["rte"] = rte
                elif stratum > 1:
                    operands["rte_old"] = rte
            if first:
                operands["item"] = item
            elif last:
                operands["item_kept"] = carried["item_kept"]
            if not first:
                operands["item_exp"] = carried["item_exp"]
            if last:
                operands.update(earlier)
            if (stratum > 0 and not first) or (stratum == 0 and last):
                operands["theta"] = carried["theta"]
            if step == 0:
                out = opened
            else:
                out = stratum_call(
                    stratum, at, rows, items, depth, factor, first, last, i, cuts, ahead, operands)
            counts = out.get("counts_ahead")
            shp[i] = out.get("shp_new")
            sums[i] = exchanged(out["upart0"])
            if first:
                rte = out.get("rte_new")
                carried["item_exp"] = out["item_exp_new"]
                carried["item_kept"] = out["item_kept"]
            if last:
                item = out["item_new"]
            else:
                earlier[f"ratios{i}"], earlier[f"uexp{i}"] = out["ratios"], out.get("uexp", operands.get("uexp"))
                if stratum > 0:
                    carried["theta"] = out["theta_new"]
        if stratum + 1 < STRATA:
            item = moved(choices[stratum + 1], item)
        else:
            item = swapped(item, "users", group - 1)
    user_log = None
    pieces = [(at, rows, 0, sums[i], shp[i]) for i, (at, rows) in enumerate(zip(starts, sizes))]
    pieces[-1:] = [
        (starts[-1] + sum(cuts[:i]), size, sum(cuts[:i]), exchanged(out[f"upart{i}"]) if i else sums[-1], shp[-1])
        for i, size in enumerate(cuts)]
    for i, (at, rows, shp_at, piece_sums, piece_shp) in enumerate(pieces):
        user_log, *rest = user_log_call(
            at, rows, shp_at, users, depth, factor, i == 0, (*piece_sums, piece_shp, rte), user_log)
        rte = rest[0] if rest else rte
        if i == max(len(pieces) - 2, 0):
            item_log = item_log_call(item, rte, items, depth)
    return user_log, item_log


def solution(mesh):
    placed = (P(None, "users", "items"), P(), P("users", None), P(("users", "items"), None))
    return jax.shard_map(
        per_device,
        mesh=mesh,
        in_specs=placed,
        out_specs=(P("users", None), P(("users", "items"), None)),
        check_vma=False,
    )
```

```python
import functools

import jax
import jax.numpy as jnp
from jax import lax
from jax.experimental import pallas as pl
from jax.experimental.pallas import tpu as pltpu
from jax.sharding import PartitionSpec as P

STRATA = 3
TILE = 64
START_TILE = 128
REDO_TILE = 32
F32 = jnp.float32
BF16 = jnp.bfloat16


def chunk_rows(rows):
    first = max(rows // 2 // START_TILE, 1) * START_TILE
    return [first, rows - first] if first < rows else [rows]


def last_cuts(rows):
    count = -(-rows // (4 * TILE))
    tiles_of = [rows // TILE // count + (i < rows // TILE % count) for i in range(count)]
    return [n * TILE for n in tiles_of] if rows % TILE == 0 else [rows]


def psi_parts(x):
    small = x < 8.0
    w = jnp.where(small, x + 3.5, x - 0.5)
    q = x * (x + 3.0)
    q2 = q + 2.0
    bounded = jnp.minimum(w, 1e9)
    square = bounded * bounded
    steps = jnp.where(small, q * q2, 1.0)
    r = 1.0 / (square * steps)
    s = r * steps
    shift = (2.0 * x + 3.0) * (q + q2) * (r * square)
    g = s * (1.0 / 24.0 - s * (7.0 / 960.0 - s * (31.0 / 8064.0 - s * (127.0 / 30720.0))))
    return w, g - jnp.where(small, shift, 0.0)


def psi_any(x):
    mirrored = x < 0.5
    w, g = psi_parts(jnp.where(mirrored, 1.0 - x, x))
    value = jnp.log(w) + g
    t = x - jnp.floor(x + 0.5)
    u = 3.14159265358979 * t
    v = u * u
    sin = 1.0 / 6227020800.0
    for c in (-1.0 / 39916800.0, 1.0 / 362880.0, -1.0 / 5040.0, 1.0 / 120.0, -1.0 / 6.0, 1.0):
        sin = sin * v + c
    cos = -1.0 / 87178291200.0
    for c in (1.0 / 479001600.0, -1.0 / 3628800.0, 1.0 / 40320.0, -1.0 / 720.0, 1.0 / 24.0, -0.5, 1.0):
        cos = cos * v + c
    value = jnp.where(mirrored, value - 3.14159265358979 * cos / (sin * u), value)
    return jnp.where((x <= 0.0) & (x == jnp.floor(x)), jnp.nan, value)


LOWEST = 0.01
HIGHEST = 1e30


def usual(rte):
    return jnp.where(rte <= HIGHEST, rte, -1.0)


def above(low):
    return jnp.min(low) >= LOWEST


def folded(x):
    return x.reshape(x.shape[0] // 8, 8, x.shape[1])


def tiles(rows):
    step = TILE if rows % TILE == 0 else rows
    return [(at, step) for at in range(0, rows, step)]


def redo_loop(rows, step, carry=None):
    size = REDO_TILE if rows % REDO_TILE == 0 else 8
    return lax.fori_loop(
        0, rows // size, lambda i, c: step(pl.multiple_of(i * size, size), size, c), carry)


def exp_tile(x, rte, general):
    shape = x.shape
    x = folded(x)
    if general:
        value = psi_any(x)
        if rte is not None:
            value = value - jnp.log(rte)[None]
        value = jnp.exp(value)
    else:
        w, g = psi_parts(x)
        value = w if rte is None else w * (1.0 / rte)[None]
        value = value * jnp.exp(g)
    mean = x if rte is None else x / rte[None] if general else x * (1.0 / rte)[None]
    return value.reshape(shape).astype(BF16), jnp.sum(mean, axis=0), jnp.min(x, axis=0)


def log_tile(x, rte, general):
    shape = x.shape
    x = folded(x)
    if general:
        value = psi_any(x) - jnp.log(rte)[None]
    else:
        w, g = psi_parts(x)
        value = (jnp.log(w) - jnp.log(rte)[None]) + g
    return value.reshape(shape).astype(BF16), jnp.min(x, axis=0)


def row_sum(x):
    return jnp.broadcast_to(jnp.sum(x, axis=0, keepdims=True), x.shape)


VMEM_SPEC = pl.BlockSpec(memory_space=pltpu.VMEM)
SMEM_SPEC = pl.BlockSpec(memory_space=pltpu.SMEM)
HBM_SPEC = pl.BlockSpec(memory_space=pltpu.HBM)
PARAMS = pltpu.CompilerParams(vmem_limit_bytes=24 * 2**20)


def in_hbm(x):
    return pltpu.with_memory_space_constraint(x, pltpu.HBM)


def in_vmem(x):
    return pltpu.with_memory_space_constraint(x, pltpu.VMEM)


def prepare_kernel(matchings_hbm, shape_hbm, item, *refs, last):
    choices, (matchings, shape, sems) = refs[:STRATA], refs[STRATA:]
    copies = [
        pltpu.make_async_copy(shape_hbm, shape, sems.at[0]),
        pltpu.make_async_copy(matchings_hbm, matchings, sems.at[1]),
    ]
    for copy in copies:
        copy.start()
    for copy in copies:
        copy.wait()
    item[...] = shape[...].astype(F32)
    choices[0][0] = matchings[0] - 1
    for stratum in range(1, STRATA - 1):
        choices[stratum][0] = jnp.bitwise_xor(matchings[stratum - 1], matchings[stratum]) - 1
    choices[STRATA - 1][0] = jnp.bitwise_xor(matchings[STRATA - 2], last) - 1


def prepare_call(matchings, item_shape, last):
    out = pl.pallas_call(
        functools.partial(prepare_kernel, last=last),
        out_shape=[jax.ShapeDtypeStruct(item_shape.shape, F32)]
        + [pltpu.SMEM((1,), jnp.int32)] * STRATA,
        in_specs=[HBM_SPEC, HBM_SPEC],
        out_specs=[VMEM_SPEC] + [SMEM_SPEC] * STRATA,
        scratch_shapes=[pltpu.SMEM(matchings.shape, jnp.int32), pltpu.VMEM(item_shape.shape, BF16),
                        pltpu.SemaphoreType.DMA((2,))],
        compiler_params=PARAMS,
        name="prepare",
    )(in_hbm(matchings), in_hbm(item_shape))
    return out[0], [choice[0] for choice in out[1:]]


def start_kernel(shape_hbm, interactions, theta, counts, *refs):
    uexps, (shape, sems) = refs[:-2], refs[-2:]
    depth = shape.shape[1]
    load = pltpu.make_async_copy(shape_hbm, shape, sems.at[0])
    ahead = pltpu.make_async_copy(interactions.at[0, pl.ds(0, counts.shape[0]), :], counts, sems.at[1])
    load.start()
    ahead.start()
    load.wait()
    total, low = jnp.zeros((8, depth), F32), jnp.ones((8, depth), F32)
    begin = 0
    for uexp in uexps:
        rows = uexp.shape[0]

        def step(i, carry, begin=begin, uexp=uexp):
            at = i * START_TILE
            x = shape[pl.ds(pl.multiple_of(begin + at, START_TILE), START_TILE), :].astype(F32)
            value, part, part_low = exp_tile(x, None, False)
            uexp[pl.ds(pl.multiple_of(at, START_TILE), START_TILE), :] = value
            return carry[0] + part, jnp.minimum(carry[1], part_low)

        total, low = lax.fori_loop(0, rows // START_TILE, step, (total, low))
        begin += rows
    theta[...] = total

    @pl.when(jnp.logical_not(above(low)))
    def _():
        begin = 0
        for uexp in uexps:

            def redo(at, size, _, begin=begin, uexp=uexp):
                x = shape[pl.ds(pl.multiple_of(begin + at, size), size), :].astype(F32)
                uexp[pl.ds(at, size), :] = exp_tile(x, None, True)[0]

            redo_loop(uexp.shape[0], redo)
            begin += uexp.shape[0]

    ahead.wait()


def start_call(user_shape, interactions, sizes):
    rows, depth = user_shape.shape
    items = interactions.shape[2]
    theta, counts, *uexps = pl.pallas_call(
        start_kernel,
        out_shape=[pltpu.VMEM((8, depth), F32), pltpu.VMEM((sizes[0], items), BF16)]
        + [pltpu.VMEM((size, depth), BF16) for size in sizes],
        in_specs=[HBM_SPEC] * 2,
        out_specs=[VMEM_SPEC] * (2 + len(sizes)),
        scratch_shapes=[pltpu.VMEM((rows, depth), BF16), pltpu.SemaphoreType.DMA((2,))],
        compiler_params=PARAMS,
        cost_estimate=pl.CostEstimate(
            flops=40 * rows * depth, bytes_accessed=rows * depth * 4, transcendentals=2 * rows * depth),
        name="user_start",
    )(in_hbm(user_shape), in_hbm(interactions))
    return theta, counts, uexps


def dot_rows(a, b):
    return lax.dot_general(a, b, (((1,), (1,)), ((), ())), preferred_element_type=F32)


def item_sums(ratios, uexp):
    return lax.dot_general(ratios[...], uexp[...], (((0,), (0,)), ((), ())), preferred_element_type=F32)


def stratum_kernel(names, *refs, stratum, at, rows, items, factor, first, last, earlier, cuts, ahead):
    ref = dict(zip(names, refs))
    copies = {}

    def fetch(name, source, target):
        copies[name] = pltpu.make_async_copy(source, target, ref["sems"].at[len(copies)])
        copies[name].start()

    if first and stratum > 0:
        fetch("item", ref["item"], ref["item_kept"])
    if ahead:
        fetch("ahead", ref["interactions"].at[ahead[0], pl.ds(ahead[1], ahead[2]), :], ref["counts_ahead"])
    upart, counts, ratios, denominator = ref["upart0"], ref["counts"], ref["ratios"], ref["denominator"]
    uexp = ref["uexp"]
    extra = 8 if first else 0

    lows = []
    theta = None
    item = ref["item_kept"] if first or last else None

    if stratum > 0:
        if first:
            beta = row_sum(ref["acc"][0:8, :] + ref["recv"][0:8, :])
            old = 1.0 if stratum == 1 else ref["rte_old"][...]
            rte = 0.5 * old + 0.5 * (0.3 + factor * beta)
            ref["rte_new"][...] = rte
        else:
            rte = ref["rte"][...]
        lows.append(usual(rte))
        for t, step in tiles(rows):
            old = ref["user_shape"][at + t:at + t + step, :].astype(F32) if stratum == 1 else ref["shp_old"][t:t + step, :]
            stat = ref["acc"][extra + t:extra + t + step, :] + ref["recv"][extra + t:extra + t + step, :]
            shp = 0.5 * old + 0.5 * (0.3 + factor * stat)
            ref["shp_new"][t:t + step, :] = shp
            value, part, low = exp_tile(shp, rte, False)
            uexp[t:t + step, :] = value
            theta = part if theta is None else theta + part
            lows.append(low)
        if not first:
            theta = theta + ref["theta"][...]
        total_mean = ref["theta_new"]
        total_mean[...] = theta
    elif last:
        total_mean = ref["theta"]

    if first and stratum > 0:
        copies["item"].wait()
    elif first:
        item[...] = ref["item"][...]
        uexp[...] = ref["uexp_in"][...]
    if first or last:
        item_rte = None if stratum == 0 else item[items:items + 8, :]
    if first:
        item_exp, sums, low = exp_tile(item[0:items, :], item_rte, False)
        ref["item_exp_new"][...] = item_exp
        upart[0:8, :] = sums
        lows.append(low)
        if item_rte is not None:
            lows.append(usual(item_rte))
    else:
        item_exp = ref["item_exp"][...]

    denominator[...] = dot_rows(uexp[...], item_exp)
    for t, step in tiles(rows):
        ratios[t:t + step, :] = (
            counts[t:t + step, :].astype(F32) / denominator[t:t + step, :]).astype(BF16)
    user_sums = uexp[...].astype(F32) * jnp.dot(ratios[...], item_exp, preferred_element_type=F32)
    parts = []
    for i, length in enumerate(cuts):
        begin, skip = sum(cuts[:i]), 0 if i else extra
        parts.append((ref[f"upart{i}"], begin, skip, length))
        parts[i][0][skip:skip + length, :] = user_sums[begin:begin + length, :]
    pairs = [(ref[f"ratios{i}"], ref[f"uexp{i}"]) for i in range(earlier)] + [(ratios, uexp)]

    def update_items(istat):
        old = 1.0 if item_rte is None else item_rte
        kept = ref["item_exp_new" if first else "item_exp"][...].astype(F32)
        ref["item_new"][0:items, :] = 0.5 * item[0:items, :] + 0.5 * (0.3 + factor * (kept * istat))
        ref["item_new"][items:items + 8, :] = 0.5 * old + 0.5 * (0.3 + factor * row_sum(total_mean[...]))

    if last:
        istat = None
        for pair in pairs:
            part = item_sums(*pair)
            istat = part if istat is None else istat + part
        update_items(istat)

    if lows:

        @pl.when(jnp.logical_not(above(functools.reduce(jnp.minimum, lows))))
        def _():
            if stratum > 0:

                def redo_users(at, size, total):
                    place = pl.ds(at, size)
                    uexp[place, :], part, _ = exp_tile(ref["shp_new"][place, :], rte, True)
                    return total + part

                start = jnp.zeros_like(rte) if first else ref["theta"][...]
                total_mean[...] = redo_loop(rows, redo_users, start)
            if first:

                def redo_items(at, size, total):
                    place = pl.ds(at, size)
                    ref["item_exp_new"][place, :], part, _ = exp_tile(item[place, :], item_rte, True)
                    return total + part

                upart[0:8, :] = redo_loop(items, redo_items, jnp.zeros((8, upart.shape[1]), F32))
            kept = ref["item_exp_new" if first else "item_exp"]
            for target, begin, skip, length in parts:

                def redo_sums(at, size, _, target=target, begin=begin, skip=skip):
                    place = pl.ds(pl.multiple_of(begin + at, size), size)
                    u = uexp[place, :]
                    ratio = (counts[place, :].astype(F32) / dot_rows(u, kept[...])).astype(BF16)
                    ratios[place, :] = ratio
                    target[pl.ds(pl.multiple_of(skip + at, 8), size), :] = u.astype(F32) * jnp.dot(
                        ratio, kept[...], preferred_element_type=F32)

                redo_loop(length, redo_sums)
            if last:
                total = ref["item_new"].at[pl.ds(0, items), :]
                total[...] = jnp.zeros((items, ref["item_new"].shape[1]), F32)
                for pair in pairs:

                    def redo_stat(at, size, _, pair=pair):
                        place = pl.ds(at, size)
                        total[...] += item_sums(pair[0].at[place, :], pair[1].at[place, :])

                    redo_loop(rows if pair[0] is ratios else pair[0].shape[0], redo_stat)
                update_items(total[...])

    if ahead:
        copies["ahead"].wait()


def stratum_call(stratum, at, rows, items, depth, factor, first, last, earlier, cuts, ahead, operands):
    extra = 8 if first else 0
    outs = {f"upart{i}": ((size + (0 if i else extra), depth), F32) for i, size in enumerate(cuts)}
    if stratum > 0:
        outs["shp_new"] = ((rows, depth), F32)
    if first and stratum > 0:
        outs["rte_new"] = ((8, depth), F32)
    if first:
        outs["item_exp_new"] = ((items, depth), BF16)
    if first:
        outs["item_kept"] = (operands["item"].shape, F32)
    if last:
        outs["item_new"] = ((items + 8, depth), F32)
    else:
        outs["ratios"] = ((rows, items), BF16)
        outs["uexp"] = ((rows, depth), BF16)
        if stratum > 0:
            outs["theta_new"] = ((8, depth), F32)
    if ahead:
        outs["counts_ahead"] = ((ahead[2], items), BF16)
    scratch = {
        "denominator": pltpu.VMEM((rows, items), F32),
        "sems": pltpu.SemaphoreType.DMA((2,)),
    }
    if last:
        scratch["ratios"] = pltpu.VMEM((rows, items), BF16)
        if stratum > 0:
            scratch["uexp"] = pltpu.VMEM((rows, depth), BF16)
            scratch["theta_new"] = pltpu.VMEM((8, depth), F32)
    hbm = ("interactions", "item") if stratum > 0 else ("interactions",)
    operands = {
        name: in_hbm(x) if name in hbm else in_vmem(x) if name in ("user_shape", "item") else x
        for name, x in operands.items()}
    names = list(operands) + list(outs) + list(scratch)
    kernel = functools.partial(
        stratum_kernel, names, stratum=stratum, at=at, rows=rows, items=items,
        factor=factor, first=first, last=last, earlier=earlier, cuts=cuts, ahead=ahead)
    results = pl.pallas_call(
        kernel,
        out_shape=[jax.ShapeDtypeStruct(*spec) for spec in outs.values()],
        in_specs=[HBM_SPEC if name in hbm else VMEM_SPEC for name in operands],
        out_specs=[VMEM_SPEC] * len(outs),
        scratch_shapes=list(scratch.values()),
        compiler_params=PARAMS,
        cost_estimate=pl.CostEstimate(flops=1, bytes_accessed=1, transcendentals=0),
        name=f"stratum{stratum}_at{at}",
    )(*operands.values())
    return dict(zip(outs, results))


def user_log_kernel(*refs, at, rows, shp_at, factor, first, filled):
    acc, recv, shp_old, rte_in = refs[:4]
    rest = refs[5:] if filled else refs[4:]
    out, *rte_out, block, sem = rest
    rte = rte_in[...]
    if first:
        rte = 0.5 * rte + 0.5 * (0.3 + factor * row_sum(acc[0:8, :] + recv[0:8, :]))
    for ref in rte_out:
        ref[...] = rte
    extra = 8 if first else 0

    def shape(t, step):
        stat = acc[pl.ds(extra + t, step), :] + recv[pl.ds(extra + t, step), :]
        return 0.5 * shp_old[pl.ds(shp_at + t, step), :] + 0.5 * (0.3 + factor * stat)

    low = rte
    for t, step in tiles(rows):
        block[t:t + step, :], part_low = log_tile(shape(t, step), rte, False)
        low = jnp.minimum(low, part_low)

    @pl.when(jnp.logical_not(above(low)))
    def _():
        def redo(t, step, _):
            block[pl.ds(t, step), :] = log_tile(shape(pl.multiple_of(t, 8), step), rte, True)[0]

        redo_loop(rows, redo)

    copy = pltpu.make_async_copy(block, out.at[pl.ds(at, rows), :], sem)
    copy.start()
    copy.wait()


def user_log_call(at, rows, shp_at, total, depth, factor, first, operands, filled):
    out_shape = [jax.ShapeDtypeStruct((total, depth), BF16)]
    out_specs = [HBM_SPEC]
    if at + rows < total:
        out_shape.append(jax.ShapeDtypeStruct((8, depth), F32))
        out_specs.append(VMEM_SPEC)
    operands = list(operands)
    in_specs = [VMEM_SPEC] * 4
    if filled is not None:
        operands.append(filled)
        in_specs.append(HBM_SPEC)
    return pl.pallas_call(
        functools.partial(user_log_kernel, at=at, rows=rows, shp_at=shp_at, factor=factor, first=first,
                          filled=filled is not None),
        out_shape=out_shape,
        in_specs=in_specs,
        out_specs=out_specs,
        input_output_aliases={} if filled is None else {4: 0},
        scratch_shapes=[pltpu.VMEM((rows, depth), BF16), pltpu.SemaphoreType.DMA],
        compiler_params=PARAMS,
        cost_estimate=pl.CostEstimate(
            flops=40 * rows * depth, bytes_accessed=rows * depth * 14, transcendentals=rows * depth),
        name=f"user_log_at{at}",
    )(*operands)


def item_log_kernel(item, _, out, *, items):
    rte = item[items:items + 8, :]

    out[...], low = log_tile(item[0:items, :], rte, False)

    @pl.when(jnp.logical_not(above(jnp.minimum(low, rte))))
    def _():
        def redo(t, step, _):
            place = pl.ds(t, step)
            out[place, :] = log_tile(item[place, :], rte, True)[0]

        redo_loop(items, redo)


def item_log_call(item, after, items, depth):
    return pl.pallas_call(
        functools.partial(item_log_kernel, items=items),
        out_shape=jax.ShapeDtypeStruct((items, depth), BF16),
        in_specs=[VMEM_SPEC, VMEM_SPEC],
        out_specs=VMEM_SPEC,
        compiler_params=PARAMS,
        cost_estimate=pl.CostEstimate(
            flops=40 * items * depth, bytes_accessed=items * depth * 6, transcendentals=items * depth),
        name="item_log",
    )(item, after)


def swapped(value, axis, mask):
    return lax.ppermute(value, axis, [(a, a ^ mask) for a in range(lax.axis_size(axis))])


def moved(choice, value, then=None, operands=()):
    def branch(mask, value, *operands):
        arrived = swapped(value, "users", mask)
        return arrived if then is None else then(arrived, *operands)

    choices = [functools.partial(branch, mask) for mask in range(1, lax.axis_size("users"))]
    return lax.switch(choice, choices, value, *operands)


def exchanged(value):
    size = lax.axis_size("items")
    if size == 1:
        return value, jnp.zeros_like(value)
    mask = 1
    while mask * 2 < size:
        value = value + swapped(value, "items", mask)
        mask *= 2
    return value, swapped(value, "items", mask)


def per_device(interactions, matchings, user_shape, item_shape):
    group = lax.axis_size("users")
    factor = float(group)
    users, depth = user_shape.shape
    items = item_shape.shape[0]
    sizes = chunk_rows(users)
    starts = [sum(sizes[:i]) for i in range(len(sizes))]
    count = len(sizes)

    item, choices = prepare_call(matchings, item_shape, group - 1)
    order = [(s, at, rows) for s in range(STRATA) for at, rows in zip(starts, sizes)]

    def opening(arrived, user_shape, interactions):
        theta, counts, uexps = start_call(user_shape, interactions, sizes)
        operands = {"counts": counts, "interactions": interactions, "uexp_in": uexps[0], "item": arrived}
        if count == 1:
            operands["theta"] = theta
        out = stratum_call(
            0, 0, sizes[0], items, depth, factor, True, count == 1, 0, sizes[:1], order[1], operands)
        return theta, [out["uexp"], *uexps[1:]], out

    theta, uexps, opened = moved(choices[0], item, opening, (user_shape, interactions))
    rte = None
    shp = [None] * count
    sums = [None] * count
    for stratum in range(STRATA):
        carried = {"theta": theta}
        earlier = {}
        for i, (at, rows) in enumerate(zip(starts, sizes)):
            first, last = i == 0, i == count - 1
            step = stratum * count + i
            ahead = order[step + 1] if step + 1 < len(order) else None
            cuts = last_cuts(rows) if step + 1 == len(order) else [rows]
            operands = {"counts": counts} if step else {}
            if ahead:
                operands["interactions"] = interactions
            if stratum == 0:
                operands["uexp"] = uexps[i]
            else:
                operands["acc"], operands["recv"] = sums[i]
                if stratum == 1:
                    operands["user_shape"] = user_shape
                else:
                    operands["shp_old"] = shp[i]
                if not first:
                    operands["rte"] = rte
                elif stratum > 1:
                    operands["rte_old"] = rte
            if first:
                operands["item"] = item
            elif last:
                operands["item_kept"] = carried["item_kept"]
            if not first:
                operands["item_exp"] = carried["item_exp"]
            if last:
                operands.update(earlier)
            if (stratum > 0 and not first) or (stratum == 0 and last):
                operands["theta"] = carried["theta"]
            if step == 0:
                out = opened
            else:
                out = stratum_call(
                    stratum, at, rows, items, depth, factor, first, last, i, cuts, ahead, operands)
            counts = out.get("counts_ahead")
            shp[i] = out.get("shp_new")
            sums[i] = exchanged(out["upart0"])
            if first:
                rte = out.get("rte_new")
                carried["item_exp"] = out["item_exp_new"]
                carried["item_kept"] = out["item_kept"]
            if last:
                item = out["item_new"]
            else:
                earlier[f"ratios{i}"], earlier[f"uexp{i}"] = out["ratios"], out.get("uexp", operands.get("uexp"))
                if stratum > 0:
                    carried["theta"] = out["theta_new"]
        if stratum + 1 < STRATA:
            item = moved(choices[stratum + 1], item)
        else:
            item = swapped(item, "users", group - 1)
    user_log = None
    pieces = [(at, rows, 0, sums[i], shp[i]) for i, (at, rows) in enumerate(zip(starts, sizes))]
    pieces[-1:] = [
        (starts[-1] + sum(cuts[:i]), size, sum(cuts[:i]), exchanged(out[f"upart{i}"]) if i else sums[-1], shp[-1])
        for i, size in enumerate(cuts)]
    for i, (at, rows, shp_at, piece_sums, piece_shp) in enumerate(pieces):
        user_log, *rest = user_log_call(
            at, rows, shp_at, users, depth, factor, i == 0, (*piece_sums, piece_shp, rte), user_log)
        rte = rest[0] if rest else rte
        if i == max(len(pieces) - 3, 0):
            item_log = item_log_call(item, rte, items, depth)
    return user_log, item_log


def solution(mesh):
    placed = (P(None, "users", "items"), P(), P("users", None), P(("users", "items"), None))
    return jax.shard_map(
        per_device,
        mesh=mesh,
        in_specs=placed,
        out_specs=(P("users", None), P(("users", "items"), None)),
        check_vma=False,
    )
```

```python
import functools

import jax
import jax.numpy as jnp
from jax import lax
from jax.experimental import pallas as pl
from jax.experimental.pallas import tpu as pltpu
from jax.sharding import PartitionSpec as P

STRATA = 3
TILE = 64
START_TILE = 128
REDO_TILE = 32
F32 = jnp.float32
BF16 = jnp.bfloat16


def chunk_rows(rows):
    first = max(rows // 2 // START_TILE, 1) * START_TILE
    return [first, rows - first] if first < rows else [rows]


def last_cuts(rows):
    count = -(-rows // (4 * TILE))
    tiles_of = [rows // TILE // count + (i < rows // TILE % count) for i in range(count)]
    return [n * TILE for n in tiles_of] if rows % TILE == 0 else [rows]


def psi_parts(x):
    small = x < 8.0
    w = jnp.where(small, x + 3.5, x - 0.5)
    q = x * (x + 3.0)
    q2 = q + 2.0
    bounded = jnp.minimum(w, 1e9)
    square = bounded * bounded
    steps = jnp.where(small, q * q2, 1.0)
    r = 1.0 / (square * steps)
    s = r * steps
    shift = (2.0 * x + 3.0) * (q + q2) * (r * square)
    g = s * (1.0 / 24.0 - s * (7.0 / 960.0 - s * (31.0 / 8064.0 - s * (127.0 / 30720.0))))
    return w, g - jnp.where(small, shift, 0.0)


def psi_any(x):
    mirrored = x < 0.5
    w, g = psi_parts(jnp.where(mirrored, 1.0 - x, x))
    value = jnp.log(w) + g
    t = x - jnp.floor(x + 0.5)
    u = 3.14159265358979 * t
    v = u * u
    sin = 1.0 / 6227020800.0
    for c in (-1.0 / 39916800.0, 1.0 / 362880.0, -1.0 / 5040.0, 1.0 / 120.0, -1.0 / 6.0, 1.0):
        sin = sin * v + c
    cos = -1.0 / 87178291200.0
    for c in (1.0 / 479001600.0, -1.0 / 3628800.0, 1.0 / 40320.0, -1.0 / 720.0, 1.0 / 24.0, -0.5, 1.0):
        cos = cos * v + c
    value = jnp.where(mirrored, value - 3.14159265358979 * cos / (sin * u), value)
    return jnp.where((x <= 0.0) & (x == jnp.floor(x)), jnp.nan, value)


LOWEST = 0.01
HIGHEST = 1e30


def usual(rte):
    return jnp.where(rte <= HIGHEST, rte, -1.0)


def above(low):
    return jnp.min(low) >= LOWEST


def folded(x):
    return x.reshape(x.shape[0] // 8, 8, x.shape[1])


def tiles(rows):
    step = TILE if rows % TILE == 0 else rows
    return [(at, step) for at in range(0, rows, step)]


def redo_loop(rows, step, carry=None):
    size = REDO_TILE if rows % REDO_TILE == 0 else 8
    return lax.fori_loop(
        0, rows // size, lambda i, c: step(pl.multiple_of(i * size, size), size, c), carry)


def exp_tile(x, rte, general):
    shape = x.shape
    x = folded(x)
    if general:
        value = psi_any(x)
        if rte is not None:
            value = value - jnp.log(rte)[None]
        value = jnp.exp(value)
    else:
        w, g = psi_parts(x)
        value = w if rte is None else w * (1.0 / rte)[None]
        value = value * jnp.exp(g)
    mean = x if rte is None else x / rte[None] if general else x * (1.0 / rte)[None]
    return value.reshape(shape).astype(BF16), jnp.sum(mean, axis=0), jnp.min(x, axis=0)


def log_tile(x, rte, general):
    shape = x.shape
    x = folded(x)
    if general:
        value = psi_any(x) - jnp.log(rte)[None]
    else:
        w, g = psi_parts(x)
        value = (jnp.log(w) - jnp.log(rte)[None]) + g
    return value.reshape(shape).astype(BF16), jnp.min(x, axis=0)


def row_sum(x):
    return jnp.broadcast_to(jnp.sum(x, axis=0, keepdims=True), x.shape)


VMEM_SPEC = pl.BlockSpec(memory_space=pltpu.VMEM)
SMEM_SPEC = pl.BlockSpec(memory_space=pltpu.SMEM)
HBM_SPEC = pl.BlockSpec(memory_space=pltpu.HBM)
PARAMS = pltpu.CompilerParams(vmem_limit_bytes=24 * 2**20)


def in_hbm(x):
    return pltpu.with_memory_space_constraint(x, pltpu.HBM)


def in_vmem(x):
    return pltpu.with_memory_space_constraint(x, pltpu.VMEM)


def prepare_kernel(matchings_hbm, shape_hbm, item, *refs, last):
    choices, (matchings, shape, sems) = refs[:STRATA], refs[STRATA:]
    copies = [
        pltpu.make_async_copy(shape_hbm, shape, sems.at[0]),
        pltpu.make_async_copy(matchings_hbm, matchings, sems.at[1]),
    ]
    for copy in copies:
        copy.start()
    for copy in copies:
        copy.wait()
    item[...] = shape[...].astype(F32)
    choices[0][0] = matchings[0] - 1
    for stratum in range(1, STRATA - 1):
        choices[stratum][0] = jnp.bitwise_xor(matchings[stratum - 1], matchings[stratum]) - 1
    choices[STRATA - 1][0] = jnp.bitwise_xor(matchings[STRATA - 2], last) - 1


def prepare_call(matchings, item_shape, last):
    out = pl.pallas_call(
        functools.partial(prepare_kernel, last=last),
        out_shape=[jax.ShapeDtypeStruct(item_shape.shape, F32)]
        + [pltpu.SMEM((1,), jnp.int32)] * STRATA,
        in_specs=[HBM_SPEC, HBM_SPEC],
        out_specs=[VMEM_SPEC] + [SMEM_SPEC] * STRATA,
        scratch_shapes=[pltpu.SMEM(matchings.shape, jnp.int32), pltpu.VMEM(item_shape.shape, BF16),
                        pltpu.SemaphoreType.DMA((2,))],
        compiler_params=PARAMS,
        name="prepare",
    )(in_hbm(matchings), in_hbm(item_shape))
    return out[0], [choice[0] for choice in out[1:]]


def start_kernel(shape_hbm, interactions, theta, counts, *refs):
    uexps, (shape, sems) = refs[:-2], refs[-2:]
    depth = shape.shape[1]
    load = pltpu.make_async_copy(shape_hbm, shape, sems.at[0])
    ahead = pltpu.make_async_copy(interactions.at[0, pl.ds(0, counts.shape[0]), :], counts, sems.at[1])
    load.start()
    ahead.start()
    load.wait()
    total, low = jnp.zeros((8, depth), F32), jnp.ones((8, depth), F32)
    begin = 0
    for uexp in uexps:
        rows = uexp.shape[0]

        def step(i, carry, begin=begin, uexp=uexp):
            at = i * START_TILE
            x = shape[pl.ds(pl.multiple_of(begin + at, START_TILE), START_TILE), :].astype(F32)
            value, part, part_low = exp_tile(x, None, False)
            uexp[pl.ds(pl.multiple_of(at, START_TILE), START_TILE), :] = value
            return carry[0] + part, jnp.minimum(carry[1], part_low)

        total, low = lax.fori_loop(0, rows // START_TILE, step, (total, low))
        begin += rows
    theta[...] = total

    @pl.when(jnp.logical_not(above(low)))
    def _():
        begin = 0
        for uexp in uexps:

            def redo(at, size, _, begin=begin, uexp=uexp):
                x = shape[pl.ds(pl.multiple_of(begin + at, size), size), :].astype(F32)
                uexp[pl.ds(at, size), :] = exp_tile(x, None, True)[0]

            redo_loop(uexp.shape[0], redo)
            begin += uexp.shape[0]

    ahead.wait()


def start_call(user_shape, interactions, sizes):
    rows, depth = user_shape.shape
    items = interactions.shape[2]
    theta, counts, *uexps = pl.pallas_call(
        start_kernel,
        out_shape=[pltpu.VMEM((8, depth), F32), pltpu.VMEM((sizes[0], items), BF16)]
        + [pltpu.VMEM((size, depth), BF16) for size in sizes],
        in_specs=[HBM_SPEC] * 2,
        out_specs=[VMEM_SPEC] * (2 + len(sizes)),
        scratch_shapes=[pltpu.VMEM((rows, depth), BF16), pltpu.SemaphoreType.DMA((2,))],
        compiler_params=PARAMS,
        cost_estimate=pl.CostEstimate(
            flops=40 * rows * depth, bytes_accessed=rows * depth * 4, transcendentals=2 * rows * depth),
        name="user_start",
    )(in_hbm(user_shape), in_hbm(interactions))
    return theta, counts, uexps


def dot_rows(a, b):
    return lax.dot_general(a, b, (((1,), (1,)), ((), ())), preferred_element_type=F32)


def item_sums(ratios, uexp):
    return lax.dot_general(ratios[...], uexp[...], (((0,), (0,)), ((), ())), preferred_element_type=F32)


def stratum_kernel(names, *refs, stratum, at, rows, items, factor, first, last, earlier, cuts, ahead):
    ref = dict(zip(names, refs))
    copies = {}

    def fetch(name, source, target):
        copies[name] = pltpu.make_async_copy(source, target, ref["sems"].at[len(copies)])
        copies[name].start()

    if first and stratum > 0:
        fetch("item", ref["item"], ref["item_kept"])
    if ahead:
        fetch("ahead", ref["interactions"].at[ahead[0], pl.ds(ahead[1], ahead[2]), :], ref["counts_ahead"])
    upart, counts, ratios, denominator = ref["upart0"], ref["counts"], ref["ratios"], ref["denominator"]
    uexp = ref["uexp"]
    extra = 8 if first else 0

    lows = []
    theta = None
    item = ref["item_kept"] if first or last else None

    if stratum > 0:
        if first:
            beta = row_sum(ref["acc"][0:8, :] + ref["recv"][0:8, :])
            old = 1.0 if stratum == 1 else ref["rte_old"][...]
            rte = 0.5 * old + 0.5 * (0.3 + factor * beta)
            ref["rte_new"][...] = rte
        else:
            rte = ref["rte"][...]
        lows.append(usual(rte))
        for t, step in tiles(rows):
            old = ref["user_shape"][at + t:at + t + step, :].astype(F32) if stratum == 1 else ref["shp_old"][t:t + step, :]
            stat = ref["acc"][extra + t:extra + t + step, :] + ref["recv"][extra + t:extra + t + step, :]
            shp = 0.5 * old + 0.5 * (0.3 + factor * stat)
            ref["shp_new"][t:t + step, :] = shp
            value, part, low = exp_tile(shp, rte, False)
            uexp[t:t + step, :] = value
            theta = part if theta is None else theta + part
            lows.append(low)
        if not first:
            theta = theta + ref["theta"][...]
        total_mean = ref["theta_new"]
        total_mean[...] = theta
    elif last:
        total_mean = ref["theta"]

    if first and stratum > 0:
        copies["item"].wait()
    elif first:
        item[...] = ref["item"][...]
        uexp[...] = ref["uexp_in"][...]
    if first or last:
        item_rte = None if stratum == 0 else item[items:items + 8, :]
    if first:
        item_exp, sums, low = exp_tile(item[0:items, :], item_rte, False)
        ref["item_exp_new"][...] = item_exp
        upart[0:8, :] = sums
        lows.append(low)
        if item_rte is not None:
            lows.append(usual(item_rte))
    else:
        item_exp = ref["item_exp"][...]

    denominator[...] = dot_rows(uexp[...], item_exp)
    for t, step in tiles(rows):
        ratios[t:t + step, :] = (
            counts[t:t + step, :].astype(F32) / denominator[t:t + step, :]).astype(BF16)
    user_sums = uexp[...].astype(F32) * jnp.dot(ratios[...], item_exp, preferred_element_type=F32)
    parts = []
    for i, length in enumerate(cuts):
        begin, skip = sum(cuts[:i]), 0 if i else extra
        parts.append((ref[f"upart{i}"], begin, skip, length))
        parts[i][0][skip:skip + length, :] = user_sums[begin:begin + length, :]
    pairs = [(ref[f"ratios{i}"], ref[f"uexp{i}"]) for i in range(earlier)] + [(ratios, uexp)]

    def update_items(istat):
        old = 1.0 if item_rte is None else item_rte
        kept = ref["item_exp_new" if first else "item_exp"][...].astype(F32)
        ref["item_new"][0:items, :] = 0.5 * item[0:items, :] + 0.5 * (0.3 + factor * (kept * istat))
        ref["item_new"][items:items + 8, :] = 0.5 * old + 0.5 * (0.3 + factor * row_sum(total_mean[...]))

    if last:
        istat = None
        for pair in pairs:
            part = item_sums(*pair)
            istat = part if istat is None else istat + part
        update_items(istat)

    if lows:

        @pl.when(jnp.logical_not(above(functools.reduce(jnp.minimum, lows))))
        def _():
            if stratum > 0:

                def redo_users(at, size, total):
                    place = pl.ds(at, size)
                    uexp[place, :], part, _ = exp_tile(ref["shp_new"][place, :], rte, True)
                    return total + part

                start = jnp.zeros_like(rte) if first else ref["theta"][...]
                total_mean[...] = redo_loop(rows, redo_users, start)
            if first:

                def redo_items(at, size, total):
                    place = pl.ds(at, size)
                    ref["item_exp_new"][place, :], part, _ = exp_tile(item[place, :], item_rte, True)
                    return total + part

                upart[0:8, :] = redo_loop(items, redo_items, jnp.zeros((8, upart.shape[1]), F32))
            kept = ref["item_exp_new" if first else "item_exp"]
            for target, begin, skip, length in parts:

                def redo_sums(at, size, _, target=target, begin=begin, skip=skip):
                    place = pl.ds(pl.multiple_of(begin + at, size), size)
                    u = uexp[place, :]
                    ratio = (counts[place, :].astype(F32) / dot_rows(u, kept[...])).astype(BF16)
                    ratios[place, :] = ratio
                    target[pl.ds(pl.multiple_of(skip + at, 8), size), :] = u.astype(F32) * jnp.dot(
                        ratio, kept[...], preferred_element_type=F32)

                redo_loop(length, redo_sums)
            if last:
                total = ref["item_new"].at[pl.ds(0, items), :]
                total[...] = jnp.zeros((items, ref["item_new"].shape[1]), F32)
                for pair in pairs:

                    def redo_stat(at, size, _, pair=pair):
                        place = pl.ds(at, size)
                        total[...] += item_sums(pair[0].at[place, :], pair[1].at[place, :])

                    redo_loop(rows if pair[0] is ratios else pair[0].shape[0], redo_stat)
                update_items(total[...])

    if ahead:
        copies["ahead"].wait()


def stratum_call(stratum, at, rows, items, depth, factor, first, last, earlier, cuts, ahead, operands):
    extra = 8 if first else 0
    outs = {f"upart{i}": ((size + (0 if i else extra), depth), F32) for i, size in enumerate(cuts)}
    if stratum > 0:
        outs["shp_new"] = ((rows, depth), F32)
    if first and stratum > 0:
        outs["rte_new"] = ((8, depth), F32)
    if first:
        outs["item_exp_new"] = ((items, depth), BF16)
    if first:
        outs["item_kept"] = (operands["item"].shape, F32)
    if last:
        outs["item_new"] = ((items + 8, depth), F32)
    else:
        outs["ratios"] = ((rows, items), BF16)
        outs["uexp"] = ((rows, depth), BF16)
        if stratum > 0:
            outs["theta_new"] = ((8, depth), F32)
    if ahead:
        outs["counts_ahead"] = ((ahead[2], items), BF16)
    scratch = {
        "denominator": pltpu.VMEM((rows, items), F32),
        "sems": pltpu.SemaphoreType.DMA((2,)),
    }
    if last:
        scratch["ratios"] = pltpu.VMEM((rows, items), BF16)
        if stratum > 0:
            scratch["uexp"] = pltpu.VMEM((rows, depth), BF16)
            scratch["theta_new"] = pltpu.VMEM((8, depth), F32)
    hbm = ("interactions", "item") if stratum > 0 else ("interactions",)
    operands = {
        name: in_hbm(x) if name in hbm else in_vmem(x) if name in ("user_shape", "item") else x
        for name, x in operands.items()}
    names = list(operands) + list(outs) + list(scratch)
    kernel = functools.partial(
        stratum_kernel, names, stratum=stratum, at=at, rows=rows, items=items,
        factor=factor, first=first, last=last, earlier=earlier, cuts=cuts, ahead=ahead)
    results = pl.pallas_call(
        kernel,
        out_shape=[jax.ShapeDtypeStruct(*spec) for spec in outs.values()],
        in_specs=[HBM_SPEC if name in hbm else VMEM_SPEC for name in operands],
        out_specs=[VMEM_SPEC] * len(outs),
        scratch_shapes=list(scratch.values()),
        compiler_params=PARAMS,
        cost_estimate=pl.CostEstimate(flops=1, bytes_accessed=1, transcendentals=0),
        name=f"stratum{stratum}_at{at}",
    )(*operands.values())
    return dict(zip(outs, results))


def user_log_kernel(*refs, at, rows, shp_at, factor, first, filled):
    acc, recv, shp_old, rte_in = refs[:4]
    rest = refs[5:] if filled else refs[4:]
    out, *rte_out, block, sem = rest
    rte = rte_in[...]
    if first:
        rte = 0.5 * rte + 0.5 * (0.3 + factor * row_sum(acc[0:8, :] + recv[0:8, :]))
    for ref in rte_out:
        ref[...] = rte
    extra = 8 if first else 0

    def shape(t, step):
        stat = acc[pl.ds(extra + t, step), :] + recv[pl.ds(extra + t, step), :]
        return 0.5 * shp_old[pl.ds(shp_at + t, step), :] + 0.5 * (0.3 + factor * stat)

    low = rte
    for t, step in tiles(rows):
        block[t:t + step, :], part_low = log_tile(shape(t, step), rte, False)
        low = jnp.minimum(low, part_low)

    @pl.when(jnp.logical_not(above(low)))
    def _():
        def redo(t, step, _):
            block[pl.ds(t, step), :] = log_tile(shape(pl.multiple_of(t, 8), step), rte, True)[0]

        redo_loop(rows, redo)

    copy = pltpu.make_async_copy(block, out.at[pl.ds(at, rows), :], sem)
    copy.start()
    copy.wait()


def user_log_call(at, rows, shp_at, total, depth, factor, first, operands, filled):
    out_shape = [jax.ShapeDtypeStruct((total, depth), BF16)]
    out_specs = [HBM_SPEC]
    if at + rows < total:
        out_shape.append(jax.ShapeDtypeStruct((8, depth), F32))
        out_specs.append(VMEM_SPEC)
    operands = list(operands)
    in_specs = [VMEM_SPEC] * 4
    if filled is not None:
        operands.append(filled)
        in_specs.append(HBM_SPEC)
    return pl.pallas_call(
        functools.partial(user_log_kernel, at=at, rows=rows, shp_at=shp_at, factor=factor, first=first,
                          filled=filled is not None),
        out_shape=out_shape,
        in_specs=in_specs,
        out_specs=out_specs,
        input_output_aliases={} if filled is None else {4: 0},
        scratch_shapes=[pltpu.VMEM((rows, depth), BF16), pltpu.SemaphoreType.DMA],
        compiler_params=PARAMS,
        cost_estimate=pl.CostEstimate(
            flops=40 * rows * depth, bytes_accessed=rows * depth * 14, transcendentals=rows * depth),
        name=f"user_log_at{at}",
    )(*operands)


def item_log_kernel(item, through, out, passed, *, items):
    passed[...] = through[...]
    rte = item[items:items + 8, :]

    out[...], low = log_tile(item[0:items, :], rte, False)

    @pl.when(jnp.logical_not(above(jnp.minimum(low, rte))))
    def _():
        def redo(t, step, _):
            place = pl.ds(t, step)
            out[place, :] = log_tile(item[place, :], rte, True)[0]

        redo_loop(items, redo)


def item_log_call(item, through, items, depth):
    return pl.pallas_call(
        functools.partial(item_log_kernel, items=items),
        out_shape=[jax.ShapeDtypeStruct((items, depth), BF16), jax.ShapeDtypeStruct(through.shape, F32)],
        in_specs=[VMEM_SPEC, VMEM_SPEC],
        out_specs=[VMEM_SPEC, VMEM_SPEC],
        compiler_params=PARAMS,
        cost_estimate=pl.CostEstimate(
            flops=40 * items * depth, bytes_accessed=items * depth * 6, transcendentals=items * depth),
        name="item_log",
    )(item, through)


def swapped(value, axis, mask):
    return lax.ppermute(value, axis, [(a, a ^ mask) for a in range(lax.axis_size(axis))])


def moved(choice, value, then=None, operands=()):
    def branch(mask, value, *operands):
        arrived = swapped(value, "users", mask)
        return arrived if then is None else then(arrived, *operands)

    choices = [functools.partial(branch, mask) for mask in range(1, lax.axis_size("users"))]
    return lax.switch(choice, choices, value, *operands)


def exchanged(value):
    size = lax.axis_size("items")
    if size == 1:
        return value, jnp.zeros_like(value)
    mask = 1
    while mask * 2 < size:
        value = value + swapped(value, "items", mask)
        mask *= 2
    return value, swapped(value, "items", mask)


def per_device(interactions, matchings, user_shape, item_shape):
    group = lax.axis_size("users")
    factor = float(group)
    users, depth = user_shape.shape
    items = item_shape.shape[0]
    sizes = chunk_rows(users)
    starts = [sum(sizes[:i]) for i in range(len(sizes))]
    count = len(sizes)

    item, choices = prepare_call(matchings, item_shape, group - 1)
    order = [(s, at, rows) for s in range(STRATA) for at, rows in zip(starts, sizes)]

    def opening(arrived, user_shape, interactions):
        theta, counts, uexps = start_call(user_shape, interactions, sizes)
        operands = {"counts": counts, "interactions": interactions, "uexp_in": uexps[0], "item": arrived}
        if count == 1:
            operands["theta"] = theta
        out = stratum_call(
            0, 0, sizes[0], items, depth, factor, True, count == 1, 0, sizes[:1], order[1], operands)
        return theta, [out["uexp"], *uexps[1:]], out

    theta, uexps, opened = moved(choices[0], item, opening, (user_shape, interactions))
    rte = None
    shp = [None] * count
    sums = [None] * count
    for stratum in range(STRATA):
        carried = {"theta": theta}
        earlier = {}
        for i, (at, rows) in enumerate(zip(starts, sizes)):
            first, last = i == 0, i == count - 1
            step = stratum * count + i
            ahead = order[step + 1] if step + 1 < len(order) else None
            cuts = last_cuts(rows) if step + 1 == len(order) else [rows]
            operands = {"counts": counts} if step else {}
            if ahead:
                operands["interactions"] = interactions
            if stratum == 0:
                operands["uexp"] = uexps[i]
            else:
                operands["acc"], operands["recv"] = sums[i]
                if stratum == 1:
                    operands["user_shape"] = user_shape
                else:
                    operands["shp_old"] = shp[i]
                if not first:
                    operands["rte"] = rte
                elif stratum > 1:
                    operands["rte_old"] = rte
            if first:
                operands["item"] = item
            elif last:
                operands["item_kept"] = carried["item_kept"]
            if not first:
                operands["item_exp"] = carried["item_exp"]
            if last:
                operands.update(earlier)
            if (stratum > 0 and not first) or (stratum == 0 and last):
                operands["theta"] = carried["theta"]
            if step == 0:
                out = opened
            else:
                out = stratum_call(
                    stratum, at, rows, items, depth, factor, first, last, i, cuts, ahead, operands)
            counts = out.get("counts_ahead")
            shp[i] = out.get("shp_new")
            sums[i] = exchanged(out["upart0"])
            if first:
                rte = out.get("rte_new")
                carried["item_exp"] = out["item_exp_new"]
                carried["item_kept"] = out["item_kept"]
            if last:
                item = out["item_new"]
            else:
                earlier[f"ratios{i}"], earlier[f"uexp{i}"] = out["ratios"], out.get("uexp", operands.get("uexp"))
                if stratum > 0:
                    carried["theta"] = out["theta_new"]
        if stratum + 1 < STRATA:
            item = moved(choices[stratum + 1], item)
        else:
            item = swapped(item, "users", group - 1)
    user_log = None
    pieces = [(at, rows, 0, sums[i], shp[i]) for i, (at, rows) in enumerate(zip(starts, sizes))]
    pieces[-1:] = [
        (starts[-1] + sum(cuts[:i]), size, sum(cuts[:i]), exchanged(out[f"upart{i}"]) if i else sums[-1], shp[-1])
        for i, size in enumerate(cuts)]
    for i, (at, rows, shp_at, piece_sums, piece_shp) in enumerate(pieces):
        user_log, *rest = user_log_call(
            at, rows, shp_at, users, depth, factor, i == 0, (*piece_sums, piece_shp, rte), user_log)
        rte = rest[0] if rest else rte
        if i == max(len(pieces) - 3, 0):
            item_log, rte = item_log_call(item, rte, items, depth)
    return user_log, item_log


def solution(mesh):
    placed = (P(None, "users", "items"), P(), P("users", None), P(("users", "items"), None))
    return jax.shard_map(
        per_device,
        mesh=mesh,
        in_specs=placed,
        out_specs=(P("users", None), P(("users", "items"), None)),
        check_vma=False,
    )
```

```python
import functools

import jax
import jax.numpy as jnp
from jax import lax
from jax.experimental import pallas as pl
from jax.experimental.pallas import tpu as pltpu
from jax.sharding import PartitionSpec as P

STRATA = 3
TILE = 64
START_TILE = 128
REDO_TILE = 32
F32 = jnp.float32
BF16 = jnp.bfloat16


def chunk_rows(rows):
    first = max(rows // 2 // START_TILE, 1) * START_TILE
    return [first, rows - first] if first < rows else [rows]


def last_cuts(rows):
    count = -(-rows // (4 * TILE))
    tiles_of = [rows // TILE // count + (i < rows // TILE % count) for i in range(count)]
    return [n * TILE for n in tiles_of] if rows % TILE == 0 else [rows]


def psi_parts(x):
    small = x < 8.0
    w = jnp.where(small, x + 3.5, x - 0.5)
    q = x * (x + 3.0)
    q2 = q + 2.0
    bounded = jnp.minimum(w, 1e9)
    square = bounded * bounded
    steps = jnp.where(small, q * q2, 1.0)
    r = 1.0 / (square * steps)
    s = r * steps
    shift = (2.0 * x + 3.0) * (q + q2) * (r * square)
    g = s * (1.0 / 24.0 - s * (7.0 / 960.0 - s * (31.0 / 8064.0 - s * (127.0 / 30720.0))))
    return w, g - jnp.where(small, shift, 0.0)


def psi_any(x):
    mirrored = x < 0.5
    w, g = psi_parts(jnp.where(mirrored, 1.0 - x, x))
    value = jnp.log(w) + g
    t = x - jnp.floor(x + 0.5)
    u = 3.14159265358979 * t
    v = u * u
    sin = 1.0 / 6227020800.0
    for c in (-1.0 / 39916800.0, 1.0 / 362880.0, -1.0 / 5040.0, 1.0 / 120.0, -1.0 / 6.0, 1.0):
        sin = sin * v + c
    cos = -1.0 / 87178291200.0
    for c in (1.0 / 479001600.0, -1.0 / 3628800.0, 1.0 / 40320.0, -1.0 / 720.0, 1.0 / 24.0, -0.5, 1.0):
        cos = cos * v + c
    value = jnp.where(mirrored, value - 3.14159265358979 * cos / (sin * u), value)
    return jnp.where((x <= 0.0) & (x == jnp.floor(x)), jnp.nan, value)


LOWEST = 0.01
HIGHEST = 1e30


def usual(rte):
    return jnp.where(rte <= HIGHEST, rte, -1.0)


def above(low):
    return jnp.min(low) >= LOWEST


def folded(x):
    return x.reshape(x.shape[0] // 8, 8, x.shape[1])


def tiles(rows):
    step = TILE if rows % TILE == 0 else rows
    return [(at, step) for at in range(0, rows, step)]


def redo_loop(rows, step, carry=None):
    size = REDO_TILE if rows % REDO_TILE == 0 else 8
    return lax.fori_loop(
        0, rows // size, lambda i, c: step(pl.multiple_of(i * size, size), size, c), carry)


def exp_tile(x, rte, general):
    shape = x.shape
    x = folded(x)
    if general:
        value = psi_any(x)
        if rte is not None:
            value = value - jnp.log(rte)[None]
        value = jnp.exp(value)
    else:
        w, g = psi_parts(x)
        value = w if rte is None else w * (1.0 / rte)[None]
        value = value * jnp.exp(g)
    mean = x if rte is None else x / rte[None] if general else x * (1.0 / rte)[None]
    return value.reshape(shape).astype(BF16), jnp.sum(mean, axis=0), jnp.min(x, axis=0)


def log_tile(x, rte, general):
    shape = x.shape
    x = folded(x)
    if general:
        value = psi_any(x) - jnp.log(rte)[None]
    else:
        w, g = psi_parts(x)
        value = (jnp.log(w) - jnp.log(rte)[None]) + g
    return value.reshape(shape).astype(BF16), jnp.min(x, axis=0)


def row_sum(x):
    return jnp.broadcast_to(jnp.sum(x, axis=0, keepdims=True), x.shape)


VMEM_SPEC = pl.BlockSpec(memory_space=pltpu.VMEM)
SMEM_SPEC = pl.BlockSpec(memory_space=pltpu.SMEM)
HBM_SPEC = pl.BlockSpec(memory_space=pltpu.HBM)
PARAMS = pltpu.CompilerParams(vmem_limit_bytes=24 * 2**20)


def in_hbm(x):
    return pltpu.with_memory_space_constraint(x, pltpu.HBM)


def in_vmem(x):
    return pltpu.with_memory_space_constraint(x, pltpu.VMEM)


def prepare_kernel(matchings_hbm, shape_hbm, item, *refs, last):
    choices, (matchings, shape, sems) = refs[:STRATA], refs[STRATA:]
    copies = [
        pltpu.make_async_copy(shape_hbm, shape, sems.at[0]),
        pltpu.make_async_copy(matchings_hbm, matchings, sems.at[1]),
    ]
    for copy in copies:
        copy.start()
    for copy in copies:
        copy.wait()
    item[...] = shape[...].astype(F32)
    choices[0][0] = matchings[0] - 1
    for stratum in range(1, STRATA - 1):
        choices[stratum][0] = jnp.bitwise_xor(matchings[stratum - 1], matchings[stratum]) - 1
    choices[STRATA - 1][0] = jnp.bitwise_xor(matchings[STRATA - 2], last) - 1


def prepare_call(matchings, item_shape, last):
    out = pl.pallas_call(
        functools.partial(prepare_kernel, last=last),
        out_shape=[jax.ShapeDtypeStruct(item_shape.shape, F32)]
        + [pltpu.SMEM((1,), jnp.int32)] * STRATA,
        in_specs=[HBM_SPEC, HBM_SPEC],
        out_specs=[VMEM_SPEC] + [SMEM_SPEC] * STRATA,
        scratch_shapes=[pltpu.SMEM(matchings.shape, jnp.int32), pltpu.VMEM(item_shape.shape, BF16),
                        pltpu.SemaphoreType.DMA((2,))],
        compiler_params=PARAMS,
        name="prepare",
    )(in_hbm(matchings), in_hbm(item_shape))
    return out[0], [choice[0] for choice in out[1:]]


def start_kernel(shape_hbm, interactions, theta, counts, *refs):
    uexps, (shape, sems) = refs[:-2], refs[-2:]
    depth = shape.shape[1]
    load = pltpu.make_async_copy(shape_hbm, shape, sems.at[0])
    ahead = pltpu.make_async_copy(interactions.at[0, pl.ds(0, counts.shape[0]), :], counts, sems.at[1])
    load.start()
    ahead.start()
    load.wait()
    total, low = jnp.zeros((8, depth), F32), jnp.ones((8, depth), F32)
    begin = 0
    for uexp in uexps:
        rows = uexp.shape[0]

        def step(i, carry, begin=begin, uexp=uexp):
            at = i * START_TILE
            x = shape[pl.ds(pl.multiple_of(begin + at, START_TILE), START_TILE), :].astype(F32)
            value, part, part_low = exp_tile(x, None, False)
            uexp[pl.ds(pl.multiple_of(at, START_TILE), START_TILE), :] = value
            return carry[0] + part, jnp.minimum(carry[1], part_low)

        total, low = lax.fori_loop(0, rows // START_TILE, step, (total, low))
        begin += rows
    theta[...] = total

    @pl.when(jnp.logical_not(above(low)))
    def _():
        begin = 0
        for uexp in uexps:

            def redo(at, size, _, begin=begin, uexp=uexp):
                x = shape[pl.ds(pl.multiple_of(begin + at, size), size), :].astype(F32)
                uexp[pl.ds(at, size), :] = exp_tile(x, None, True)[0]

            redo_loop(uexp.shape[0], redo)
            begin += uexp.shape[0]

    ahead.wait()


def start_call(user_shape, interactions, sizes):
    rows, depth = user_shape.shape
    items = interactions.shape[2]
    theta, counts, *uexps = pl.pallas_call(
        start_kernel,
        out_shape=[pltpu.VMEM((8, depth), F32), pltpu.VMEM((sizes[0], items), BF16)]
        + [pltpu.VMEM((size, depth), BF16) for size in sizes],
        in_specs=[HBM_SPEC] * 2,
        out_specs=[VMEM_SPEC] * (2 + len(sizes)),
        scratch_shapes=[pltpu.VMEM((rows, depth), BF16), pltpu.SemaphoreType.DMA((2,))],
        compiler_params=PARAMS,
        cost_estimate=pl.CostEstimate(
            flops=40 * rows * depth, bytes_accessed=rows * depth * 4, transcendentals=2 * rows * depth),
        name="user_start",
    )(in_hbm(user_shape), in_hbm(interactions))
    return theta, counts, uexps


def dot_rows(a, b):
    return lax.dot_general(a, b, (((1,), (1,)), ((), ())), preferred_element_type=F32)


def item_sums(ratios, uexp):
    return lax.dot_general(ratios[...], uexp[...], (((0,), (0,)), ((), ())), preferred_element_type=F32)


def stratum_kernel(names, *refs, stratum, at, rows, items, factor, first, last, earlier, cuts, ahead):
    ref = dict(zip(names, refs))
    copies = {}

    def fetch(name, source, target):
        copies[name] = pltpu.make_async_copy(source, target, ref["sems"].at[len(copies)])
        copies[name].start()

    if first and stratum > 0:
        fetch("item", ref["item"], ref["item_kept"])
    if ahead:
        fetch("ahead", ref["interactions"].at[ahead[0], pl.ds(ahead[1], ahead[2]), :], ref["counts_ahead"])
    upart, counts, ratios, denominator = ref["upart0"], ref["counts"], ref["ratios"], ref["denominator"]
    uexp = ref["uexp"]
    extra = 8 if first else 0

    lows = []
    theta = None
    item = ref["item_kept"] if first or last else None

    if stratum > 0:
        if first:
            beta = row_sum(ref["acc"][0:8, :] + ref["recv"][0:8, :])
            old = 1.0 if stratum == 1 else ref["rte_old"][...]
            rte = 0.5 * old + 0.5 * (0.3 + factor * beta)
            ref["rte_new"][...] = rte
        else:
            rte = ref["rte"][...]
        lows.append(usual(rte))
        for t, step in tiles(rows):
            old = ref["user_shape"][at + t:at + t + step, :].astype(F32) if stratum == 1 else ref["shp_old"][t:t + step, :]
            stat = ref["acc"][extra + t:extra + t + step, :] + ref["recv"][extra + t:extra + t + step, :]
            shp = 0.5 * old + 0.5 * (0.3 + factor * stat)
            ref["shp_new"][t:t + step, :] = shp
            value, part, low = exp_tile(shp, rte, False)
            uexp[t:t + step, :] = value
            theta = part if theta is None else theta + part
            lows.append(low)
        if not first:
            theta = theta + ref["theta"][...]
        total_mean = ref["theta_new"]
        total_mean[...] = theta
    elif last:
        total_mean = ref["theta"]

    if first and stratum > 0:
        copies["item"].wait()
    elif first:
        item[...] = ref["item"][...]
        uexp[...] = ref["uexp_in"][...]
    if first or last:
        item_rte = None if stratum == 0 else item[items:items + 8, :]
    if first:
        sums = None
        for t, step in tiles(items):
            ref["item_exp_new"][t:t + step, :], part, low = exp_tile(item[t:t + step, :], item_rte, False)
            sums = part if sums is None else sums + part
            lows.append(low)
        upart[0:8, :] = sums
        item_exp = ref["item_exp_new"][...]
        if item_rte is not None:
            lows.append(usual(item_rte))
    else:
        item_exp = ref["item_exp"][...]

    denominator[...] = dot_rows(uexp[...], item_exp)
    for t, step in tiles(rows):
        ratios[t:t + step, :] = (
            counts[t:t + step, :].astype(F32) / denominator[t:t + step, :]).astype(BF16)
    parts = []
    for i, length in enumerate(cuts):
        begin, skip = sum(cuts[:i]), 0 if i else extra
        target = ref[f"upart{i}"]
        parts.append((target, begin, skip, length))
        target[skip:skip + length, :] = jnp.dot(
            ratios[begin:begin + length, :], item_exp, preferred_element_type=F32)
        for t, step in tiles(length):
            target[skip + t:skip + t + step, :] *= uexp[begin + t:begin + t + step, :].astype(F32)
    pairs = [(ref[f"ratios{i}"], ref[f"uexp{i}"]) for i in range(earlier)] + [(ratios, uexp)]

    def update_items(istat):
        old = 1.0 if item_rte is None else item_rte
        kept = ref["item_exp_new" if first else "item_exp"][...].astype(F32)
        ref["item_new"][0:items, :] = 0.5 * item[0:items, :] + 0.5 * (0.3 + factor * (kept * istat))
        ref["item_new"][items:items + 8, :] = 0.5 * old + 0.5 * (0.3 + factor * row_sum(total_mean[...]))

    if last:
        istat = None
        for pair in pairs:
            part = item_sums(*pair)
            istat = part if istat is None else istat + part
        update_items(istat)

    if lows:

        @pl.when(jnp.logical_not(above(functools.reduce(jnp.minimum, lows))))
        def _():
            if stratum > 0:

                def redo_users(at, size, total):
                    place = pl.ds(at, size)
                    uexp[place, :], part, _ = exp_tile(ref["shp_new"][place, :], rte, True)
                    return total + part

                start = jnp.zeros_like(rte) if first else ref["theta"][...]
                total_mean[...] = redo_loop(rows, redo_users, start)
            if first:

                def redo_items(at, size, total):
                    place = pl.ds(at, size)
                    ref["item_exp_new"][place, :], part, _ = exp_tile(item[place, :], item_rte, True)
                    return total + part

                upart[0:8, :] = redo_loop(items, redo_items, jnp.zeros((8, upart.shape[1]), F32))
            kept = ref["item_exp_new" if first else "item_exp"]
            for target, begin, skip, length in parts:

                def redo_sums(at, size, _, target=target, begin=begin, skip=skip):
                    place = pl.ds(pl.multiple_of(begin + at, size), size)
                    u = uexp[place, :]
                    ratio = (counts[place, :].astype(F32) / dot_rows(u, kept[...])).astype(BF16)
                    ratios[place, :] = ratio
                    target[pl.ds(pl.multiple_of(skip + at, 8), size), :] = u.astype(F32) * jnp.dot(
                        ratio, kept[...], preferred_element_type=F32)

                redo_loop(length, redo_sums)
            if last:
                total = ref["item_new"].at[pl.ds(0, items), :]
                total[...] = jnp.zeros((items, ref["item_new"].shape[1]), F32)
                for pair in pairs:

                    def redo_stat(at, size, _, pair=pair):
                        place = pl.ds(at, size)
                        total[...] += item_sums(pair[0].at[place, :], pair[1].at[place, :])

                    redo_loop(rows if pair[0] is ratios else pair[0].shape[0], redo_stat)
                update_items(total[...])

    if ahead:
        copies["ahead"].wait()


def stratum_call(stratum, at, rows, items, depth, factor, first, last, earlier, cuts, ahead, operands):
    extra = 8 if first else 0
    outs = {f"upart{i}": ((size + (0 if i else extra), depth), F32) for i, size in enumerate(cuts)}
    if stratum > 0:
        outs["shp_new"] = ((rows, depth), F32)
    if first and stratum > 0:
        outs["rte_new"] = ((8, depth), F32)
    if first:
        outs["item_exp_new"] = ((items, depth), BF16)
    if first:
        outs["item_kept"] = (operands["item"].shape, F32)
    if last:
        outs["item_new"] = ((items + 8, depth), F32)
    else:
        outs["ratios"] = ((rows, items), BF16)
        outs["uexp"] = ((rows, depth), BF16)
        if stratum > 0:
            outs["theta_new"] = ((8, depth), F32)
    if ahead:
        outs["counts_ahead"] = ((ahead[2], items), BF16)
    scratch = {
        "denominator": pltpu.VMEM((rows, items), F32),
        "sems": pltpu.SemaphoreType.DMA((2,)),
    }
    if last:
        scratch["ratios"] = pltpu.VMEM((rows, items), BF16)
        if stratum > 0:
            scratch["uexp"] = pltpu.VMEM((rows, depth), BF16)
            scratch["theta_new"] = pltpu.VMEM((8, depth), F32)
    hbm = ("interactions", "item") if stratum > 0 else ("interactions",)
    operands = {
        name: in_hbm(x) if name in hbm else in_vmem(x) if name in ("user_shape", "item") else x
        for name, x in operands.items()}
    names = list(operands) + list(outs) + list(scratch)
    kernel = functools.partial(
        stratum_kernel, names, stratum=stratum, at=at, rows=rows, items=items,
        factor=factor, first=first, last=last, earlier=earlier, cuts=cuts, ahead=ahead)
    results = pl.pallas_call(
        kernel,
        out_shape=[jax.ShapeDtypeStruct(*spec) for spec in outs.values()],
        in_specs=[HBM_SPEC if name in hbm else VMEM_SPEC for name in operands],
        out_specs=[VMEM_SPEC] * len(outs),
        scratch_shapes=list(scratch.values()),
        compiler_params=PARAMS,
        cost_estimate=pl.CostEstimate(flops=1, bytes_accessed=1, transcendentals=0),
        name=f"stratum{stratum}_at{at}",
    )(*operands.values())
    return dict(zip(outs, results))


def user_log_kernel(*refs, at, rows, shp_at, factor, first, filled):
    acc, recv, shp_old, rte_in = refs[:4]
    rest = refs[5:] if filled else refs[4:]
    out, *rte_out, block, sem = rest
    rte = rte_in[...]
    if first:
        rte = 0.5 * rte + 0.5 * (0.3 + factor * row_sum(acc[0:8, :] + recv[0:8, :]))
    for ref in rte_out:
        ref[...] = rte
    extra = 8 if first else 0

    def shape(t, step):
        stat = acc[pl.ds(extra + t, step), :] + recv[pl.ds(extra + t, step), :]
        return 0.5 * shp_old[pl.ds(shp_at + t, step), :] + 0.5 * (0.3 + factor * stat)

    low = rte
    for t, step in tiles(rows):
        block[t:t + step, :], part_low = log_tile(shape(t, step), rte, False)
        low = jnp.minimum(low, part_low)

    @pl.when(jnp.logical_not(above(low)))
    def _():
        def redo(t, step, _):
            block[pl.ds(t, step), :] = log_tile(shape(pl.multiple_of(t, 8), step), rte, True)[0]

        redo_loop(rows, redo)

    copy = pltpu.make_async_copy(block, out.at[pl.ds(at, rows), :], sem)
    copy.start()
    copy.wait()


def user_log_call(at, rows, shp_at, total, depth, factor, first, operands, filled):
    out_shape = [jax.ShapeDtypeStruct((total, depth), BF16)]
    out_specs = [HBM_SPEC]
    if at + rows < total:
        out_shape.append(jax.ShapeDtypeStruct((8, depth), F32))
        out_specs.append(VMEM_SPEC)
    operands = list(operands)
    in_specs = [VMEM_SPEC] * 4
    if filled is not None:
        operands.append(filled)
        in_specs.append(HBM_SPEC)
    return pl.pallas_call(
        functools.partial(user_log_kernel, at=at, rows=rows, shp_at=shp_at, factor=factor, first=first,
                          filled=filled is not None),
        out_shape=out_shape,
        in_specs=in_specs,
        out_specs=out_specs,
        input_output_aliases={} if filled is None else {4: 0},
        scratch_shapes=[pltpu.VMEM((rows, depth), BF16), pltpu.SemaphoreType.DMA],
        compiler_params=PARAMS,
        cost_estimate=pl.CostEstimate(
            flops=40 * rows * depth, bytes_accessed=rows * depth * 14, transcendentals=rows * depth),
        name=f"user_log_at{at}",
    )(*operands)


def item_log_kernel(item, through, out, passed, *, items):
    passed[...] = through[...]
    rte = item[items:items + 8, :]

    low = rte
    for t, step in tiles(items):
        out[t:t + step, :], part_low = log_tile(item[t:t + step, :], rte, False)
        low = jnp.minimum(low, part_low)

    @pl.when(jnp.logical_not(above(low)))
    def _():
        def redo(t, step, _):
            place = pl.ds(t, step)
            out[place, :] = log_tile(item[place, :], rte, True)[0]

        redo_loop(items, redo)


def item_log_call(item, through, items, depth):
    return pl.pallas_call(
        functools.partial(item_log_kernel, items=items),
        out_shape=[jax.ShapeDtypeStruct((items, depth), BF16), jax.ShapeDtypeStruct(through.shape, F32)],
        in_specs=[VMEM_SPEC, VMEM_SPEC],
        out_specs=[VMEM_SPEC, VMEM_SPEC],
        compiler_params=PARAMS,
        cost_estimate=pl.CostEstimate(
            flops=40 * items * depth, bytes_accessed=items * depth * 6, transcendentals=items * depth),
        name="item_log",
    )(item, through)


def swapped(value, axis, mask):
    return lax.ppermute(value, axis, [(a, a ^ mask) for a in range(lax.axis_size(axis))])


def moved(choice, value, then=None, operands=()):
    def branch(mask, value, *operands):
        arrived = swapped(value, "users", mask)
        return arrived if then is None else then(arrived, *operands)

    choices = [functools.partial(branch, mask) for mask in range(1, lax.axis_size("users"))]
    return lax.switch(choice, choices, value, *operands)


def exchanged(value):
    size = lax.axis_size("items")
    if size == 1:
        return value, jnp.zeros_like(value)
    mask = 1
    while mask * 2 < size:
        value = value + swapped(value, "items", mask)
        mask *= 2
    return value, swapped(value, "items", mask)


def per_device(interactions, matchings, user_shape, item_shape):
    group = lax.axis_size("users")
    factor = float(group)
    users, depth = user_shape.shape
    items = item_shape.shape[0]
    sizes = chunk_rows(users)
    starts = [sum(sizes[:i]) for i in range(len(sizes))]
    count = len(sizes)

    item, choices = prepare_call(matchings, item_shape, group - 1)
    order = [(s, at, rows) for s in range(STRATA) for at, rows in zip(starts, sizes)]

    def opening(arrived, user_shape, interactions):
        theta, counts, uexps = start_call(user_shape, interactions, sizes)
        operands = {"counts": counts, "interactions": interactions, "uexp_in": uexps[0], "item": arrived}
        if count == 1:
            operands["theta"] = theta
        out = stratum_call(
            0, 0, sizes[0], items, depth, factor, True, count == 1, 0, sizes[:1], order[1], operands)
        return theta, [out["uexp"], *uexps[1:]], out

    theta, uexps, opened = moved(choices[0], item, opening, (user_shape, interactions))
    rte = None
    shp = [None] * count
    sums = [None] * count
    for stratum in range(STRATA):
        carried = {"theta": theta}
        earlier = {}
        for i, (at, rows) in enumerate(zip(starts, sizes)):
            first, last = i == 0, i == count - 1
            step = stratum * count + i
            ahead = order[step + 1] if step + 1 < len(order) else None
            cuts = last_cuts(rows) if step + 1 == len(order) else [rows]
            operands = {"counts": counts} if step else {}
            if ahead:
                operands["interactions"] = interactions
            if stratum == 0:
                operands["uexp"] = uexps[i]
            else:
                operands["acc"], operands["recv"] = sums[i]
                if stratum == 1:
                    operands["user_shape"] = user_shape
                else:
                    operands["shp_old"] = shp[i]
                if not first:
                    operands["rte"] = rte
                elif stratum > 1:
                    operands["rte_old"] = rte
            if first:
                operands["item"] = item
            elif last:
                operands["item_kept"] = carried["item_kept"]
            if not first:
                operands["item_exp"] = carried["item_exp"]
            if last:
                operands.update(earlier)
            if (stratum > 0 and not first) or (stratum == 0 and last):
                operands["theta"] = carried["theta"]
            if step == 0:
                out = opened
            else:
                out = stratum_call(
                    stratum, at, rows, items, depth, factor, first, last, i, cuts, ahead, operands)
            counts = out.get("counts_ahead")
            shp[i] = out.get("shp_new")
            sums[i] = exchanged(out["upart0"])
            if first:
                rte = out.get("rte_new")
                carried["item_exp"] = out["item_exp_new"]
                carried["item_kept"] = out["item_kept"]
            if last:
                item = out["item_new"]
            else:
                earlier[f"ratios{i}"], earlier[f"uexp{i}"] = out["ratios"], out.get("uexp", operands.get("uexp"))
                if stratum > 0:
                    carried["theta"] = out["theta_new"]
        if stratum + 1 < STRATA:
            item = moved(choices[stratum + 1], item)
        else:
            item = swapped(item, "users", group - 1)
    user_log = None
    pieces = [(at, rows, 0, sums[i], shp[i]) for i, (at, rows) in enumerate(zip(starts, sizes))]
    pieces[-1:] = [
        (starts[-1] + sum(cuts[:i]), size, sum(cuts[:i]), exchanged(out[f"upart{i}"]) if i else sums[-1], shp[-1])
        for i, size in enumerate(cuts)]
    for i, (at, rows, shp_at, piece_sums, piece_shp) in enumerate(pieces):
        user_log, *rest = user_log_call(
            at, rows, shp_at, users, depth, factor, i == 0, (*piece_sums, piece_shp, rte), user_log)
        rte = rest[0] if rest else rte
        if i == max(len(pieces) - 3, 0):
            item_log, rte = item_log_call(item, rte, items, depth)
    return user_log, item_log


def solution(mesh):
    placed = (P(None, "users", "items"), P(), P("users", None), P(("users", "items"), None))
    return jax.shard_map(
        per_device,
        mesh=mesh,
        in_specs=placed,
        out_specs=(P("users", None), P(("users", "items"), None)),
        check_vma=False,
    )
```

```python
import functools

import jax
import jax.numpy as jnp
from jax import lax
from jax.experimental import pallas as pl
from jax.experimental.pallas import tpu as pltpu
from jax.sharding import PartitionSpec as P

STRATA = 3
TILE = 64
START_TILE = 128
REDO_TILE = 32
F32 = jnp.float32
BF16 = jnp.bfloat16


def chunk_rows(rows):
    first = max(rows * 3 // 10 // START_TILE, 1) * START_TILE
    return [first, rows - first] if first < rows else [rows]


def last_cuts(rows):
    count = -(-rows // (4 * TILE))
    tiles_of = [rows // TILE // count + (i < rows // TILE % count) for i in range(count)]
    return [n * TILE for n in tiles_of] if rows % TILE == 0 else [rows]


def psi_parts(x):
    small = x < 8.0
    w = jnp.where(small, x + 3.5, x - 0.5)
    q = x * (x + 3.0)
    q2 = q + 2.0
    bounded = jnp.minimum(w, 1e9)
    square = bounded * bounded
    steps = jnp.where(small, q * q2, 1.0)
    r = 1.0 / (square * steps)
    s = r * steps
    shift = (2.0 * x + 3.0) * (q + q2) * (r * square)
    g = s * (1.0 / 24.0 - s * (7.0 / 960.0 - s * (31.0 / 8064.0 - s * (127.0 / 30720.0))))
    return w, g - jnp.where(small, shift, 0.0)


def psi_any(x):
    mirrored = x < 0.5
    w, g = psi_parts(jnp.where(mirrored, 1.0 - x, x))
    value = jnp.log(w) + g
    t = x - jnp.floor(x + 0.5)
    u = 3.14159265358979 * t
    v = u * u
    sin = 1.0 / 6227020800.0
    for c in (-1.0 / 39916800.0, 1.0 / 362880.0, -1.0 / 5040.0, 1.0 / 120.0, -1.0 / 6.0, 1.0):
        sin = sin * v + c
    cos = -1.0 / 87178291200.0
    for c in (1.0 / 479001600.0, -1.0 / 3628800.0, 1.0 / 40320.0, -1.0 / 720.0, 1.0 / 24.0, -0.5, 1.0):
        cos = cos * v + c
    value = jnp.where(mirrored, value - 3.14159265358979 * cos / (sin * u), value)
    return jnp.where((x <= 0.0) & (x == jnp.floor(x)), jnp.nan, value)


LOWEST = 0.01
HIGHEST = 1e30


def usual(rte):
    return jnp.where(rte <= HIGHEST, rte, -1.0)


def above(low):
    return jnp.min(low) >= LOWEST


def folded(x):
    return x.reshape(x.shape[0] // 8, 8, x.shape[1])


def tiles(rows):
    step = TILE if rows % TILE == 0 else rows
    return [(at, step) for at in range(0, rows, step)]


def redo_loop(rows, step, carry=None):
    size = REDO_TILE if rows % REDO_TILE == 0 else 8
    return lax.fori_loop(
        0, rows // size, lambda i, c: step(pl.multiple_of(i * size, size), size, c), carry)


def exp_tile(x, rte, general):
    shape = x.shape
    x = folded(x)
    if general:
        value = psi_any(x)
        if rte is not None:
            value = value - jnp.log(rte)[None]
        value = jnp.exp(value)
    else:
        w, g = psi_parts(x)
        value = w if rte is None else w * (1.0 / rte)[None]
        value = value * jnp.exp(g)
    mean = x if rte is None else x / rte[None] if general else x * (1.0 / rte)[None]
    return value.reshape(shape).astype(BF16), jnp.sum(mean, axis=0), jnp.min(x, axis=0)


def log_tile(x, rte, general):
    shape = x.shape
    x = folded(x)
    if general:
        value = psi_any(x) - jnp.log(rte)[None]
    else:
        w, g = psi_parts(x)
        value = (jnp.log(w) - jnp.log(rte)[None]) + g
    return value.reshape(shape).astype(BF16), jnp.min(x, axis=0)


def row_sum(x):
    return jnp.broadcast_to(jnp.sum(x, axis=0, keepdims=True), x.shape)


VMEM_SPEC = pl.BlockSpec(memory_space=pltpu.VMEM)
SMEM_SPEC = pl.BlockSpec(memory_space=pltpu.SMEM)
HBM_SPEC = pl.BlockSpec(memory_space=pltpu.HBM)
PARAMS = pltpu.CompilerParams(vmem_limit_bytes=24 * 2**20)


def in_hbm(x):
    return pltpu.with_memory_space_constraint(x, pltpu.HBM)


def in_vmem(x):
    return pltpu.with_memory_space_constraint(x, pltpu.VMEM)


def prepare_kernel(matchings_hbm, shape_hbm, item, *refs, last):
    choices, (matchings, shape, sems) = refs[:STRATA], refs[STRATA:]
    copies = [
        pltpu.make_async_copy(shape_hbm, shape, sems.at[0]),
        pltpu.make_async_copy(matchings_hbm, matchings, sems.at[1]),
    ]
    for copy in copies:
        copy.start()
    for copy in copies:
        copy.wait()
    item[...] = shape[...].astype(F32)
    choices[0][0] = matchings[0] - 1
    for stratum in range(1, STRATA - 1):
        choices[stratum][0] = jnp.bitwise_xor(matchings[stratum - 1], matchings[stratum]) - 1
    choices[STRATA - 1][0] = jnp.bitwise_xor(matchings[STRATA - 2], last) - 1


def prepare_call(matchings, item_shape, last):
    out = pl.pallas_call(
        functools.partial(prepare_kernel, last=last),
        out_shape=[jax.ShapeDtypeStruct(item_shape.shape, F32)]
        + [pltpu.SMEM((1,), jnp.int32)] * STRATA,
        in_specs=[HBM_SPEC, HBM_SPEC],
        out_specs=[VMEM_SPEC] + [SMEM_SPEC] * STRATA,
        scratch_shapes=[pltpu.SMEM(matchings.shape, jnp.int32), pltpu.VMEM(item_shape.shape, BF16),
                        pltpu.SemaphoreType.DMA((2,))],
        compiler_params=PARAMS,
        name="prepare",
    )(in_hbm(matchings), in_hbm(item_shape))
    return out[0], [choice[0] for choice in out[1:]]


def start_kernel(shape_hbm, interactions, theta, counts, *refs):
    uexps, (shape, sems) = refs[:-2], refs[-2:]
    depth = shape.shape[1]
    load = pltpu.make_async_copy(shape_hbm, shape, sems.at[0])
    ahead = pltpu.make_async_copy(interactions.at[0, pl.ds(0, counts.shape[0]), :], counts, sems.at[1])
    load.start()
    ahead.start()
    load.wait()
    total, low = jnp.zeros((8, depth), F32), jnp.ones((8, depth), F32)
    begin = 0
    for uexp in uexps:
        rows = uexp.shape[0]

        def step(i, carry, begin=begin, uexp=uexp):
            at = i * START_TILE
            x = shape[pl.ds(pl.multiple_of(begin + at, START_TILE), START_TILE), :].astype(F32)
            value, part, part_low = exp_tile(x, None, False)
            uexp[pl.ds(pl.multiple_of(at, START_TILE), START_TILE), :] = value
            return carry[0] + part, jnp.minimum(carry[1], part_low)

        total, low = lax.fori_loop(0, rows // START_TILE, step, (total, low))
        begin += rows
    theta[...] = total

    @pl.when(jnp.logical_not(above(low)))
    def _():
        begin = 0
        for uexp in uexps:

            def redo(at, size, _, begin=begin, uexp=uexp):
                x = shape[pl.ds(pl.multiple_of(begin + at, size), size), :].astype(F32)
                uexp[pl.ds(at, size), :] = exp_tile(x, None, True)[0]

            redo_loop(uexp.shape[0], redo)
            begin += uexp.shape[0]

    ahead.wait()


def start_call(user_shape, interactions, sizes):
    rows, depth = user_shape.shape
    items = interactions.shape[2]
    theta, counts, *uexps = pl.pallas_call(
        start_kernel,
        out_shape=[pltpu.VMEM((8, depth), F32), pltpu.VMEM((sizes[0], items), BF16)]
        + [pltpu.VMEM((size, depth), BF16) for size in sizes],
        in_specs=[HBM_SPEC] * 2,
        out_specs=[VMEM_SPEC] * (2 + len(sizes)),
        scratch_shapes=[pltpu.VMEM((rows, depth), BF16), pltpu.SemaphoreType.DMA((2,))],
        compiler_params=PARAMS,
        cost_estimate=pl.CostEstimate(
            flops=40 * rows * depth, bytes_accessed=rows * depth * 4, transcendentals=2 * rows * depth),
        name="user_start",
    )(in_hbm(user_shape), in_hbm(interactions))
    return theta, counts, uexps


def dot_rows(a, b):
    return lax.dot_general(a, b, (((1,), (1,)), ((), ())), preferred_element_type=F32)


def item_sums(ratios, uexp):
    return lax.dot_general(ratios[...], uexp[...], (((0,), (0,)), ((), ())), preferred_element_type=F32)


def stratum_kernel(names, *refs, stratum, at, rows, items, factor, first, last, earlier, cuts, ahead):
    ref = dict(zip(names, refs))
    copies = {}

    def fetch(name, source, target):
        copies[name] = pltpu.make_async_copy(source, target, ref["sems"].at[len(copies)])
        copies[name].start()

    if first and stratum > 0:
        fetch("item", ref["item"], ref["item_kept"])
    if ahead:
        fetch("ahead", ref["interactions"].at[ahead[0], pl.ds(ahead[1], ahead[2]), :], ref["counts_ahead"])
    upart, counts, ratios, denominator = ref["upart0"], ref["counts"], ref["ratios"], ref["denominator"]
    uexp = ref["uexp"]
    extra = 8 if first else 0

    lows = []
    theta = None
    item = ref["item_kept"] if first or last else None

    if stratum > 0:
        if first:
            beta = row_sum(ref["acc"][0:8, :] + ref["recv"][0:8, :])
            old = 1.0 if stratum == 1 else ref["rte_old"][...]
            rte = 0.5 * old + 0.5 * (0.3 + factor * beta)
            ref["rte_new"][...] = rte
        else:
            rte = ref["rte"][...]
        lows.append(usual(rte))
        for t, step in tiles(rows):
            old = ref["user_shape"][at + t:at + t + step, :].astype(F32) if stratum == 1 else ref["shp_old"][t:t + step, :]
            stat = ref["acc"][extra + t:extra + t + step, :] + ref["recv"][extra + t:extra + t + step, :]
            shp = 0.5 * old + 0.5 * (0.3 + factor * stat)
            ref["shp_new"][t:t + step, :] = shp
            value, part, low = exp_tile(shp, rte, False)
            uexp[t:t + step, :] = value
            theta = part if theta is None else theta + part
            lows.append(low)
        if not first:
            theta = theta + ref["theta"][...]
        total_mean = ref["theta_new"]
        total_mean[...] = theta
    elif last:
        total_mean = ref["theta"]

    if first and stratum > 0:
        copies["item"].wait()
    elif first:
        item[...] = ref["item"][...]
        uexp[...] = ref["uexp_in"][...]
    if first or last:
        item_rte = None if stratum == 0 else item[items:items + 8, :]
    if first:
        item_exp, sums, low = exp_tile(item[0:items, :], item_rte, False)
        ref["item_exp_new"][...] = item_exp
        upart[0:8, :] = sums
        lows.append(low)
        if item_rte is not None:
            lows.append(usual(item_rte))
    else:
        item_exp = ref["item_exp"][...]

    denominator[...] = dot_rows(uexp[...], item_exp)
    for t, step in tiles(rows):
        ratios[t:t + step, :] = (
            counts[t:t + step, :].astype(F32) / denominator[t:t + step, :]).astype(BF16)
    user_sums = uexp[...].astype(F32) * jnp.dot(ratios[...], item_exp, preferred_element_type=F32)
    parts = []
    for i, length in enumerate(cuts):
        begin, skip = sum(cuts[:i]), 0 if i else extra
        parts.append((ref[f"upart{i}"], begin, skip, length))
        parts[i][0][skip:skip + length, :] = user_sums[begin:begin + length, :]
    pairs = [(ref[f"ratios{i}"], ref[f"uexp{i}"]) for i in range(earlier)] + [(ratios, uexp)]

    def update_items(istat):
        old = 1.0 if item_rte is None else item_rte
        kept = ref["item_exp_new" if first else "item_exp"][...].astype(F32)
        ref["item_new"][0:items, :] = 0.5 * item[0:items, :] + 0.5 * (0.3 + factor * (kept * istat))
        ref["item_new"][items:items + 8, :] = 0.5 * old + 0.5 * (0.3 + factor * row_sum(total_mean[...]))

    if last:
        istat = None
        for pair in pairs:
            part = item_sums(*pair)
            istat = part if istat is None else istat + part
        update_items(istat)

    if lows:

        @pl.when(jnp.logical_not(above(functools.reduce(jnp.minimum, lows))))
        def _():
            if stratum > 0:

                def redo_users(at, size, total):
                    place = pl.ds(at, size)
                    uexp[place, :], part, _ = exp_tile(ref["shp_new"][place, :], rte, True)
                    return total + part

                start = jnp.zeros_like(rte) if first else ref["theta"][...]
                total_mean[...] = redo_loop(rows, redo_users, start)
            if first:

                def redo_items(at, size, total):
                    place = pl.ds(at, size)
                    ref["item_exp_new"][place, :], part, _ = exp_tile(item[place, :], item_rte, True)
                    return total + part

                upart[0:8, :] = redo_loop(items, redo_items, jnp.zeros((8, upart.shape[1]), F32))
            kept = ref["item_exp_new" if first else "item_exp"]
            for target, begin, skip, length in parts:

                def redo_sums(at, size, _, target=target, begin=begin, skip=skip):
                    place = pl.ds(pl.multiple_of(begin + at, size), size)
                    u = uexp[place, :]
                    ratio = (counts[place, :].astype(F32) / dot_rows(u, kept[...])).astype(BF16)
                    ratios[place, :] = ratio
                    target[pl.ds(pl.multiple_of(skip + at, 8), size), :] = u.astype(F32) * jnp.dot(
                        ratio, kept[...], preferred_element_type=F32)

                redo_loop(length, redo_sums)
            if last:
                total = ref["item_new"].at[pl.ds(0, items), :]
                total[...] = jnp.zeros((items, ref["item_new"].shape[1]), F32)
                for pair in pairs:

                    def redo_stat(at, size, _, pair=pair):
                        place = pl.ds(at, size)
                        total[...] += item_sums(pair[0].at[place, :], pair[1].at[place, :])

                    redo_loop(rows if pair[0] is ratios else pair[0].shape[0], redo_stat)
                update_items(total[...])

    if ahead:
        copies["ahead"].wait()


def stratum_call(stratum, at, rows, items, depth, factor, first, last, earlier, cuts, ahead, operands):
    extra = 8 if first else 0
    outs = {f"upart{i}": ((size + (0 if i else extra), depth), F32) for i, size in enumerate(cuts)}
    if stratum > 0:
        outs["shp_new"] = ((rows, depth), F32)
    if first and stratum > 0:
        outs["rte_new"] = ((8, depth), F32)
    if first:
        outs["item_exp_new"] = ((items, depth), BF16)
    if first:
        outs["item_kept"] = (operands["item"].shape, F32)
    if last:
        outs["item_new"] = ((items + 8, depth), F32)
    else:
        outs["ratios"] = ((rows, items), BF16)
        outs["uexp"] = ((rows, depth), BF16)
        if stratum > 0:
            outs["theta_new"] = ((8, depth), F32)
    if ahead:
        outs["counts_ahead"] = ((ahead[2], items), BF16)
    scratch = {
        "denominator": pltpu.VMEM((rows, items), F32),
        "sems": pltpu.SemaphoreType.DMA((2,)),
    }
    if last:
        scratch["ratios"] = pltpu.VMEM((rows, items), BF16)
        if stratum > 0:
            scratch["uexp"] = pltpu.VMEM((rows, depth), BF16)
            scratch["theta_new"] = pltpu.VMEM((8, depth), F32)
    hbm = ("interactions", "item") if stratum > 0 else ("interactions",)
    operands = {
        name: in_hbm(x) if name in hbm else in_vmem(x) if name in ("user_shape", "item") else x
        for name, x in operands.items()}
    names = list(operands) + list(outs) + list(scratch)
    kernel = functools.partial(
        stratum_kernel, names, stratum=stratum, at=at, rows=rows, items=items,
        factor=factor, first=first, last=last, earlier=earlier, cuts=cuts, ahead=ahead)
    results = pl.pallas_call(
        kernel,
        out_shape=[jax.ShapeDtypeStruct(*spec) for spec in outs.values()],
        in_specs=[HBM_SPEC if name in hbm else VMEM_SPEC for name in operands],
        out_specs=[VMEM_SPEC] * len(outs),
        scratch_shapes=list(scratch.values()),
        compiler_params=PARAMS,
        cost_estimate=pl.CostEstimate(
            flops=600 * rows * items * depth, bytes_accessed=rows * 200000, transcendentals=rows * depth),
        name=f"stratum{stratum}_at{at}",
    )(*operands.values())
    return dict(zip(outs, results))


def user_log_kernel(*refs, at, rows, shp_at, factor, first, filled):
    acc, recv, shp_old, rte_in = refs[:4]
    rest = refs[5:] if filled else refs[4:]
    out, *rte_out, block, sem = rest
    rte = rte_in[...]
    if first:
        rte = 0.5 * rte + 0.5 * (0.3 + factor * row_sum(acc[0:8, :] + recv[0:8, :]))
    for ref in rte_out:
        ref[...] = rte
    extra = 8 if first else 0

    def shape(t, step):
        stat = acc[pl.ds(extra + t, step), :] + recv[pl.ds(extra + t, step), :]
        return 0.5 * shp_old[pl.ds(shp_at + t, step), :] + 0.5 * (0.3 + factor * stat)

    low = rte
    for t, step in tiles(rows):
        block[t:t + step, :], part_low = log_tile(shape(t, step), rte, False)
        low = jnp.minimum(low, part_low)

    @pl.when(jnp.logical_not(above(low)))
    def _():
        def redo(t, step, _):
            block[pl.ds(t, step), :] = log_tile(shape(pl.multiple_of(t, 8), step), rte, True)[0]

        redo_loop(rows, redo)

    copy = pltpu.make_async_copy(block, out.at[pl.ds(at, rows), :], sem)
    copy.start()
    copy.wait()


def user_log_call(at, rows, shp_at, total, depth, factor, first, operands, filled):
    out_shape = [jax.ShapeDtypeStruct((total, depth), BF16)]
    out_specs = [HBM_SPEC]
    if at + rows < total:
        out_shape.append(jax.ShapeDtypeStruct((8, depth), F32))
        out_specs.append(VMEM_SPEC)
    operands = list(operands)
    in_specs = [VMEM_SPEC] * 4
    if filled is not None:
        operands.append(filled)
        in_specs.append(HBM_SPEC)
    return pl.pallas_call(
        functools.partial(user_log_kernel, at=at, rows=rows, shp_at=shp_at, factor=factor, first=first,
                          filled=filled is not None),
        out_shape=out_shape,
        in_specs=in_specs,
        out_specs=out_specs,
        input_output_aliases={} if filled is None else {4: 0},
        scratch_shapes=[pltpu.VMEM((rows, depth), BF16), pltpu.SemaphoreType.DMA],
        compiler_params=PARAMS,
        cost_estimate=pl.CostEstimate(
            flops=40 * rows * depth, bytes_accessed=rows * depth * 14, transcendentals=rows * depth),
        name=f"user_log_at{at}",
    )(*operands)


def item_log_kernel(item, through, out, passed, *, items):
    passed[...] = through[...]
    rte = item[items:items + 8, :]

    out[...], low = log_tile(item[0:items, :], rte, False)

    @pl.when(jnp.logical_not(above(jnp.minimum(low, rte))))
    def _():
        def redo(t, step, _):
            place = pl.ds(t, step)
            out[place, :] = log_tile(item[place, :], rte, True)[0]

        redo_loop(items, redo)


def item_log_call(item, through, items, depth):
    return pl.pallas_call(
        functools.partial(item_log_kernel, items=items),
        out_shape=[jax.ShapeDtypeStruct((items, depth), BF16), jax.ShapeDtypeStruct(through.shape, F32)],
        in_specs=[VMEM_SPEC, VMEM_SPEC],
        out_specs=[VMEM_SPEC, VMEM_SPEC],
        compiler_params=PARAMS,
        cost_estimate=pl.CostEstimate(
            flops=40 * items * depth, bytes_accessed=items * depth * 6, transcendentals=items * depth),
        name="item_log",
    )(item, through)


def swapped(value, axis, mask):
    return lax.ppermute(value, axis, [(a, a ^ mask) for a in range(lax.axis_size(axis))])


def moved(choice, value, then=None, operands=()):
    def branch(mask, value, *operands):
        arrived = swapped(value, "users", mask)
        return arrived if then is None else then(arrived, *operands)

    choices = [functools.partial(branch, mask) for mask in range(1, lax.axis_size("users"))]
    return lax.switch(choice, choices, value, *operands)


def exchanged(value):
    size = lax.axis_size("items")
    if size == 1:
        return value, jnp.zeros_like(value)
    mask = 1
    while mask * 2 < size:
        value = value + swapped(value, "items", mask)
        mask *= 2
    return value, swapped(value, "items", mask)


def per_device(interactions, matchings, user_shape, item_shape):
    group = lax.axis_size("users")
    factor = float(group)
    users, depth = user_shape.shape
    items = item_shape.shape[0]
    sizes = chunk_rows(users)
    starts = [sum(sizes[:i]) for i in range(len(sizes))]
    count = len(sizes)

    item, choices = prepare_call(matchings, item_shape, group - 1)
    order = [(s, at, rows) for s in range(STRATA) for at, rows in zip(starts, sizes)]

    def opening(arrived, user_shape, interactions):
        theta, counts, uexps = start_call(user_shape, interactions, sizes)
        operands = {"counts": counts, "interactions": interactions, "uexp_in": uexps[0], "item": arrived}
        if count == 1:
            operands["theta"] = theta
        out = stratum_call(
            0, 0, sizes[0], items, depth, factor, True, count == 1, 0, sizes[:1], order[1], operands)
        return theta, [out["uexp"], *uexps[1:]], out

    theta, uexps, opened = moved(choices[0], item, opening, (user_shape, interactions))
    rte = None
    shp = [None] * count
    sums = [None] * count
    for stratum in range(STRATA):
        carried = {"theta": theta}
        earlier = {}
        for i, (at, rows) in enumerate(zip(starts, sizes)):
            first, last = i == 0, i == count - 1
            step = stratum * count + i
            ahead = order[step + 1] if step + 1 < len(order) else None
            cuts = last_cuts(rows) if step + 1 == len(order) else [rows]
            operands = {"counts": counts} if step else {}
            if ahead:
                operands["interactions"] = interactions
            if stratum == 0:
                operands["uexp"] = uexps[i]
            else:
                operands["acc"], operands["recv"] = sums[i]
                if stratum == 1:
                    operands["user_shape"] = user_shape
                else:
                    operands["shp_old"] = shp[i]
                if not first:
                    operands["rte"] = rte
                elif stratum > 1:
                    operands["rte_old"] = rte
            if first:
                operands["item"] = item
            elif last:
                operands["item_kept"] = carried["item_kept"]
            if not first:
                operands["item_exp"] = carried["item_exp"]
            if last:
                operands.update(earlier)
            if (stratum > 0 and not first) or (stratum == 0 and last):
                operands["theta"] = carried["theta"]
            if step == 0:
                out = opened
            else:
                out = stratum_call(
                    stratum, at, rows, items, depth, factor, first, last, i, cuts, ahead, operands)
            counts = out.get("counts_ahead")
            shp[i] = out.get("shp_new")
            sums[i] = exchanged(out["upart0"])
            if first:
                rte = out.get("rte_new")
                carried["item_exp"] = out["item_exp_new"]
                carried["item_kept"] = out["item_kept"]
            if last:
                item = out["item_new"]
            else:
                earlier[f"ratios{i}"], earlier[f"uexp{i}"] = out["ratios"], out.get("uexp", operands.get("uexp"))
                if stratum > 0:
                    carried["theta"] = out["theta_new"]
        if stratum + 1 < STRATA:
            item = moved(choices[stratum + 1], item)
        else:
            item = swapped(item, "users", group - 1)
    user_log = None
    pieces = [(at, rows, 0, sums[i], shp[i]) for i, (at, rows) in enumerate(zip(starts, sizes))]
    pieces[-1:] = [
        (starts[-1] + sum(cuts[:i]), size, sum(cuts[:i]), exchanged(out[f"upart{i}"]) if i else sums[-1], shp[-1])
        for i, size in enumerate(cuts)]
    for i, (at, rows, shp_at, piece_sums, piece_shp) in enumerate(pieces):
        user_log, *rest = user_log_call(
            at, rows, shp_at, users, depth, factor, i == 0, (*piece_sums, piece_shp, rte), user_log)
        rte = rest[0] if rest else rte
        if i == max(len(pieces) - 3, 0):
            item_log, rte = item_log_call(item, rte, items, depth)
    return user_log, item_log


def solution(mesh):
    placed = (P(None, "users", "items"), P(), P("users", None), P(("users", "items"), None))
    return jax.shard_map(
        per_device,
        mesh=mesh,
        in_specs=placed,
        out_specs=(P("users", None), P(("users", "items"), None)),
        check_vma=False,
    )
```

```python
import functools

import jax
import jax.numpy as jnp
from jax import lax
from jax.experimental import pallas as pl
from jax.experimental.pallas import tpu as pltpu
from jax.sharding import PartitionSpec as P

STRATA = 3
TILE = 64
START_TILE = 128
REDO_TILE = 32
F32 = jnp.float32
BF16 = jnp.bfloat16


def chunk_rows(rows):
    first = max(rows // 2 // START_TILE, 1) * START_TILE
    return [first, rows - first] if first < rows else [rows]


def last_cuts(rows):
    count = -(-rows // (4 * TILE))
    tiles_of = [rows // TILE // count + (i < rows // TILE % count) for i in range(count)]
    return [n * TILE for n in tiles_of] if rows % TILE == 0 else [rows]


def psi_parts(x):
    small = x < 8.0
    w = jnp.where(small, x + 3.5, x - 0.5)
    q = x * (x + 3.0)
    q2 = q + 2.0
    bounded = jnp.minimum(w, 1e9)
    square = bounded * bounded
    steps = jnp.where(small, q * q2, 1.0)
    r = 1.0 / (square * steps)
    s = r * steps
    shift = (2.0 * x + 3.0) * (q + q2) * (r * square)
    g = s * (1.0 / 24.0 - s * (7.0 / 960.0 - s * (31.0 / 8064.0 - s * (127.0 / 30720.0))))
    return w, g - jnp.where(small, shift, 0.0)


def psi_any(x):
    mirrored = x < 0.5
    w, g = psi_parts(jnp.where(mirrored, 1.0 - x, x))
    value = jnp.log(w) + g
    t = x - jnp.floor(x + 0.5)
    u = 3.14159265358979 * t
    v = u * u
    sin = 1.0 / 6227020800.0
    for c in (-1.0 / 39916800.0, 1.0 / 362880.0, -1.0 / 5040.0, 1.0 / 120.0, -1.0 / 6.0, 1.0):
        sin = sin * v + c
    cos = -1.0 / 87178291200.0
    for c in (1.0 / 479001600.0, -1.0 / 3628800.0, 1.0 / 40320.0, -1.0 / 720.0, 1.0 / 24.0, -0.5, 1.0):
        cos = cos * v + c
    value = jnp.where(mirrored, value - 3.14159265358979 * cos / (sin * u), value)
    return jnp.where((x <= 0.0) & (x == jnp.floor(x)), jnp.nan, value)


LOWEST = 0.01
HIGHEST = 1e30


def usual(rte):
    return jnp.where(rte <= HIGHEST, rte, -1.0)


def above(low):
    return jnp.min(low) >= LOWEST


def folded(x):
    return x.reshape(x.shape[0] // 8, 8, x.shape[1])


def tiles(rows):
    step = TILE if rows % TILE == 0 else rows
    return [(at, step) for at in range(0, rows, step)]


def redo_loop(rows, step, carry=None):
    size = REDO_TILE if rows % REDO_TILE == 0 else 8
    return lax.fori_loop(
        0, rows // size, lambda i, c: step(pl.multiple_of(i * size, size), size, c), carry)


def exp_tile(x, rte, general):
    shape = x.shape
    x = folded(x)
    if general:
        value = psi_any(x)
        if rte is not None:
            value = value - jnp.log(rte)[None]
        value = jnp.exp(value)
    else:
        w, g = psi_parts(x)
        value = w if rte is None else w * (1.0 / rte)[None]
        value = value * jnp.exp(g)
    mean = x if rte is None else x / rte[None] if general else x * (1.0 / rte)[None]
    return value.reshape(shape).astype(BF16), jnp.sum(mean, axis=0), jnp.min(x, axis=0)


def log_tile(x, rte, general):
    shape = x.shape
    x = folded(x)
    if general:
        value = psi_any(x) - jnp.log(rte)[None]
    else:
        w, g = psi_parts(x)
        value = (jnp.log(w) - jnp.log(rte)[None]) + g
    return value.reshape(shape).astype(BF16), jnp.min(x, axis=0)


def row_sum(x):
    return jnp.broadcast_to(jnp.sum(x, axis=0, keepdims=True), x.shape)


VMEM_SPEC = pl.BlockSpec(memory_space=pltpu.VMEM)
SMEM_SPEC = pl.BlockSpec(memory_space=pltpu.SMEM)
HBM_SPEC = pl.BlockSpec(memory_space=pltpu.HBM)
PARAMS = pltpu.CompilerParams(vmem_limit_bytes=24 * 2**20)


def in_hbm(x):
    return pltpu.with_memory_space_constraint(x, pltpu.HBM)


def in_vmem(x):
    return pltpu.with_memory_space_constraint(x, pltpu.VMEM)


def prepare_kernel(matchings_hbm, shape_hbm, item, *refs, last):
    choices, (matchings, shape, sems) = refs[:STRATA], refs[STRATA:]
    copies = [
        pltpu.make_async_copy(shape_hbm, shape, sems.at[0]),
        pltpu.make_async_copy(matchings_hbm, matchings, sems.at[1]),
    ]
    for copy in copies:
        copy.start()
    for copy in copies:
        copy.wait()
    item[...] = shape[...].astype(F32)
    choices[0][0] = matchings[0] - 1
    for stratum in range(1, STRATA - 1):
        choices[stratum][0] = jnp.bitwise_xor(matchings[stratum - 1], matchings[stratum]) - 1
    choices[STRATA - 1][0] = jnp.bitwise_xor(matchings[STRATA - 2], last) - 1


def prepare_call(matchings, item_shape, last):
    out = pl.pallas_call(
        functools.partial(prepare_kernel, last=last),
        out_shape=[jax.ShapeDtypeStruct(item_shape.shape, F32)]
        + [pltpu.SMEM((1,), jnp.int32)] * STRATA,
        in_specs=[HBM_SPEC, HBM_SPEC],
        out_specs=[VMEM_SPEC] + [SMEM_SPEC] * STRATA,
        scratch_shapes=[pltpu.SMEM(matchings.shape, jnp.int32), pltpu.VMEM(item_shape.shape, BF16),
                        pltpu.SemaphoreType.DMA((2,))],
        compiler_params=PARAMS,
        name="prepare",
    )(in_hbm(matchings), in_hbm(item_shape))
    return out[0], [choice[0] for choice in out[1:]]


def start_kernel(shape_hbm, interactions, theta, counts, *refs):
    uexps, (shape, sems) = refs[:-2], refs[-2:]
    depth = shape.shape[1]
    load = pltpu.make_async_copy(shape_hbm, shape, sems.at[0])
    ahead = pltpu.make_async_copy(interactions.at[0, pl.ds(0, counts.shape[0]), :], counts, sems.at[1])
    load.start()
    ahead.start()
    load.wait()
    total, low = jnp.zeros((8, depth), F32), jnp.ones((8, depth), F32)
    begin = 0
    for uexp in uexps:
        rows = uexp.shape[0]

        def step(i, carry, begin=begin, uexp=uexp):
            at = i * START_TILE
            x = shape[pl.ds(pl.multiple_of(begin + at, START_TILE), START_TILE), :].astype(F32)
            value, part, part_low = exp_tile(x, None, False)
            uexp[pl.ds(pl.multiple_of(at, START_TILE), START_TILE), :] = value
            return carry[0] + part, jnp.minimum(carry[1], part_low)

        total, low = lax.fori_loop(0, rows // START_TILE, step, (total, low))
        begin += rows
    theta[...] = total

    @pl.when(jnp.logical_not(above(low)))
    def _():
        begin = 0
        for uexp in uexps:

            def redo(at, size, _, begin=begin, uexp=uexp):
                x = shape[pl.ds(pl.multiple_of(begin + at, size), size), :].astype(F32)
                uexp[pl.ds(at, size), :] = exp_tile(x, None, True)[0]

            redo_loop(uexp.shape[0], redo)
            begin += uexp.shape[0]

    ahead.wait()


def start_call(user_shape, interactions, sizes):
    rows, depth = user_shape.shape
    items = interactions.shape[2]
    theta, counts, *uexps = pl.pallas_call(
        start_kernel,
        out_shape=[pltpu.VMEM((8, depth), F32), pltpu.VMEM((sizes[0], items), BF16)]
        + [pltpu.VMEM((size, depth), BF16) for size in sizes],
        in_specs=[HBM_SPEC] * 2,
        out_specs=[VMEM_SPEC] * (2 + len(sizes)),
        scratch_shapes=[pltpu.VMEM((rows, depth), BF16), pltpu.SemaphoreType.DMA((2,))],
        compiler_params=PARAMS,
        cost_estimate=pl.CostEstimate(
            flops=40 * rows * depth, bytes_accessed=rows * depth * 4, transcendentals=2 * rows * depth),
        name="user_start",
    )(in_hbm(user_shape), in_hbm(interactions))
    return theta, counts, uexps


def dot_rows(a, b):
    return lax.dot_general(a, b, (((1,), (1,)), ((), ())), preferred_element_type=F32)


def item_sums(ratios, uexp):
    return lax.dot_general(ratios[...], uexp[...], (((0,), (0,)), ((), ())), preferred_element_type=F32)


def stratum_kernel(names, *refs, stratum, at, rows, items, factor, first, last, earlier, cuts, ahead):
    ref = dict(zip(names, refs))
    copies = {}

    def fetch(name, source, target):
        copies[name] = pltpu.make_async_copy(source, target, ref["sems"].at[len(copies)])
        copies[name].start()

    if first and stratum > 0:
        fetch("item", ref["item"], ref["item_kept"])
    if ahead:
        fetch("ahead", ref["interactions"].at[ahead[0], pl.ds(ahead[1], ahead[2]), :], ref["counts_ahead"])
    upart, counts, ratios, denominator = ref["upart0"], ref["counts"], ref["ratios"], ref["denominator"]
    uexp = ref["uexp"]
    extra = 8 if first else 0

    lows = []
    theta = None
    item = ref["item_kept"] if first or last else None

    if stratum > 0:
        if first:
            beta = row_sum(ref["acc"][0:8, :] + ref["recv"][0:8, :])
            old = 1.0 if stratum == 1 else ref["rte_old"][...]
            rte = 0.5 * old + 0.5 * (0.3 + factor * beta)
            ref["rte_new"][...] = rte
        else:
            rte = ref["rte"][...]
        lows.append(usual(rte))
        for t, step in tiles(rows):
            old = ref["user_shape"][at + t:at + t + step, :].astype(F32) if stratum == 1 else ref["shp_old"][t:t + step, :]
            stat = ref["acc"][extra + t:extra + t + step, :] + ref["recv"][extra + t:extra + t + step, :]
            shp = 0.5 * old + 0.5 * (0.3 + factor * stat)
            ref["shp_new"][t:t + step, :] = shp
            value, part, low = exp_tile(shp, rte, False)
            uexp[t:t + step, :] = value
            theta = part if theta is None else theta + part
            lows.append(low)
        if not first:
            theta = theta + ref["theta"][...]
        total_mean = ref["theta_new"]
        total_mean[...] = theta
    elif last:
        total_mean = ref["theta"]

    if first and stratum > 0:
        copies["item"].wait()
    elif first:
        item[...] = ref["item"][...]
        uexp[...] = ref["uexp_in"][...]
    if first or last:
        item_rte = None if stratum == 0 else item[items:items + 8, :]
    if first:
        item_exp, sums, low = exp_tile(item[0:items, :], item_rte, False)
        ref["item_exp_new"][...] = item_exp
        upart[0:8, :] = sums
        lows.append(low)
        if item_rte is not None:
            lows.append(usual(item_rte))
    else:
        item_exp = ref["item_exp"][...]

    denominator[...] = dot_rows(uexp[...], item_exp)
    for t, step in tiles(rows):
        ratios[t:t + step, :] = (
            counts[t:t + step, :].astype(F32) / denominator[t:t + step, :]).astype(BF16)
    user_sums = uexp[...].astype(F32) * jnp.dot(ratios[...], item_exp, preferred_element_type=F32)
    parts = []
    for i, length in enumerate(cuts):
        begin, skip = sum(cuts[:i]), 0 if i else extra
        parts.append((ref[f"upart{i}"], begin, skip, length))
        parts[i][0][skip:skip + length, :] = user_sums[begin:begin + length, :]
    pairs = [(ref[f"ratios{i}"], ref[f"uexp{i}"]) for i in range(earlier)] + [(ratios, uexp)]

    def update_items(istat):
        old = 1.0 if item_rte is None else item_rte
        kept = ref["item_exp_new" if first else "item_exp"][...].astype(F32)
        ref["item_new"][0:items, :] = 0.5 * item[0:items, :] + 0.5 * (0.3 + factor * (kept * istat))
        ref["item_new"][items:items + 8, :] = 0.5 * old + 0.5 * (0.3 + factor * row_sum(total_mean[...]))

    if last:
        istat = None
        for pair in pairs:
            part = item_sums(*pair)
            istat = part if istat is None else istat + part
        update_items(istat)

    if lows:

        @pl.when(jnp.logical_not(above(functools.reduce(jnp.minimum, lows))))
        def _():
            if stratum > 0:

                def redo_users(at, size, total):
                    place = pl.ds(at, size)
                    uexp[place, :], part, _ = exp_tile(ref["shp_new"][place, :], rte, True)
                    return total + part

                start = jnp.zeros_like(rte) if first else ref["theta"][...]
                total_mean[...] = redo_loop(rows, redo_users, start)
            if first:

                def redo_items(at, size, total):
                    place = pl.ds(at, size)
                    ref["item_exp_new"][place, :], part, _ = exp_tile(item[place, :], item_rte, True)
                    return total + part

                upart[0:8, :] = redo_loop(items, redo_items, jnp.zeros((8, upart.shape[1]), F32))
            kept = ref["item_exp_new" if first else "item_exp"]
            for target, begin, skip, length in parts:

                def redo_sums(at, size, _, target=target, begin=begin, skip=skip):
                    place = pl.ds(pl.multiple_of(begin + at, size), size)
                    u = uexp[place, :]
                    ratio = (counts[place, :].astype(F32) / dot_rows(u, kept[...])).astype(BF16)
                    ratios[place, :] = ratio
                    target[pl.ds(pl.multiple_of(skip + at, 8), size), :] = u.astype(F32) * jnp.dot(
                        ratio, kept[...], preferred_element_type=F32)

                redo_loop(length, redo_sums)
            if last:
                total = ref["item_new"].at[pl.ds(0, items), :]
                total[...] = jnp.zeros((items, ref["item_new"].shape[1]), F32)
                for pair in pairs:

                    def redo_stat(at, size, _, pair=pair):
                        place = pl.ds(at, size)
                        total[...] += item_sums(pair[0].at[place, :], pair[1].at[place, :])

                    redo_loop(rows if pair[0] is ratios else pair[0].shape[0], redo_stat)
                update_items(total[...])

    if ahead:
        copies["ahead"].wait()


def stratum_call(stratum, at, rows, items, depth, factor, first, last, earlier, cuts, ahead, operands):
    extra = 8 if first else 0
    outs = {f"upart{i}": ((size + (0 if i else extra), depth), F32) for i, size in enumerate(cuts)}
    if stratum > 0:
        outs["shp_new"] = ((rows, depth), F32)
    if first and stratum > 0:
        outs["rte_new"] = ((8, depth), F32)
    if first:
        outs["item_exp_new"] = ((items, depth), BF16)
    if first:
        outs["item_kept"] = (operands["item"].shape, F32)
    if last:
        outs["item_new"] = ((items + 8, depth), F32)
    else:
        outs["ratios"] = ((rows, items), BF16)
        outs["uexp"] = ((rows, depth), BF16)
        if stratum > 0:
            outs["theta_new"] = ((8, depth), F32)
    if ahead:
        outs["counts_ahead"] = ((ahead[2], items), BF16)
    scratch = {
        "denominator": pltpu.VMEM((rows, items), F32),
        "sems": pltpu.SemaphoreType.DMA((2,)),
    }
    if last:
        scratch["ratios"] = pltpu.VMEM((rows, items), BF16)
        if stratum > 0:
            scratch["uexp"] = pltpu.VMEM((rows, depth), BF16)
            scratch["theta_new"] = pltpu.VMEM((8, depth), F32)
    hbm = ("interactions", "item") if stratum > 0 else ("interactions",)
    operands = {
        name: in_hbm(x) if name in hbm else in_vmem(x) if name in ("user_shape", "item") else x
        for name, x in operands.items()}
    names = list(operands) + list(outs) + list(scratch)
    kernel = functools.partial(
        stratum_kernel, names, stratum=stratum, at=at, rows=rows, items=items,
        factor=factor, first=first, last=last, earlier=earlier, cuts=cuts, ahead=ahead)
    results = pl.pallas_call(
        kernel,
        out_shape=[jax.ShapeDtypeStruct(*spec) for spec in outs.values()],
        in_specs=[HBM_SPEC if name in hbm else VMEM_SPEC for name in operands],
        out_specs=[VMEM_SPEC] * len(outs),
        scratch_shapes=list(scratch.values()),
        compiler_params=PARAMS,
        cost_estimate=pl.CostEstimate(
            flops=600 * rows * items * depth, bytes_accessed=rows * 200000, transcendentals=rows * depth),
        name=f"stratum{stratum}_at{at}",
    )(*operands.values())
    return dict(zip(outs, results))


def user_log_kernel(*refs, at, rows, shp_at, factor, first, filled):
    acc, recv, shp_old, rte_in = refs[:4]
    rest = refs[5:] if filled else refs[4:]
    out, *rte_out, block, sem = rest
    rte = rte_in[...]
    if first:
        rte = 0.5 * rte + 0.5 * (0.3 + factor * row_sum(acc[0:8, :] + recv[0:8, :]))
    for ref in rte_out:
        ref[...] = rte
    extra = 8 if first else 0

    def shape(t, step):
        stat = acc[pl.ds(extra + t, step), :] + recv[pl.ds(extra + t, step), :]
        return 0.5 * shp_old[pl.ds(shp_at + t, step), :] + 0.5 * (0.3 + factor * stat)

    low = rte
    for t, step in tiles(rows):
        block[t:t + step, :], part_low = log_tile(shape(t, step), rte, False)
        low = jnp.minimum(low, part_low)

    @pl.when(jnp.logical_not(above(low)))
    def _():
        def redo(t, step, _):
            block[pl.ds(t, step), :] = log_tile(shape(pl.multiple_of(t, 8), step), rte, True)[0]

        redo_loop(rows, redo)

    copy = pltpu.make_async_copy(block, out.at[pl.ds(at, rows), :], sem)
    copy.start()
    copy.wait()


def user_log_call(at, rows, shp_at, total, depth, factor, first, operands, filled):
    out_shape = [jax.ShapeDtypeStruct((total, depth), BF16)]
    out_specs = [HBM_SPEC]
    if at + rows < total:
        out_shape.append(jax.ShapeDtypeStruct((8, depth), F32))
        out_specs.append(VMEM_SPEC)
    operands = list(operands)
    in_specs = [VMEM_SPEC] * 4
    if filled is not None:
        operands.append(filled)
        in_specs.append(HBM_SPEC)
    return pl.pallas_call(
        functools.partial(user_log_kernel, at=at, rows=rows, shp_at=shp_at, factor=factor, first=first,
                          filled=filled is not None),
        out_shape=out_shape,
        in_specs=in_specs,
        out_specs=out_specs,
        input_output_aliases={} if filled is None else {4: 0},
        scratch_shapes=[pltpu.VMEM((rows, depth), BF16), pltpu.SemaphoreType.DMA],
        compiler_params=PARAMS,
        cost_estimate=pl.CostEstimate(
            flops=40 * rows * depth, bytes_accessed=rows * depth * 14, transcendentals=rows * depth),
        name=f"user_log_at{at}",
    )(*operands)


def item_log_kernel(item, through, out, passed, *, items):
    passed[...] = through[...]
    rte = item[items:items + 8, :]

    out[...], low = log_tile(item[0:items, :], rte, False)

    @pl.when(jnp.logical_not(above(jnp.minimum(low, rte))))
    def _():
        def redo(t, step, _):
            place = pl.ds(t, step)
            out[place, :] = log_tile(item[place, :], rte, True)[0]

        redo_loop(items, redo)


def item_log_call(item, through, items, depth):
    return pl.pallas_call(
        functools.partial(item_log_kernel, items=items),
        out_shape=[jax.ShapeDtypeStruct((items, depth), BF16), jax.ShapeDtypeStruct(through.shape, F32)],
        in_specs=[VMEM_SPEC, VMEM_SPEC],
        out_specs=[VMEM_SPEC, VMEM_SPEC],
        compiler_params=PARAMS,
        cost_estimate=pl.CostEstimate(
            flops=40 * items * depth, bytes_accessed=items * depth * 6, transcendentals=items * depth),
        name="item_log",
    )(item, through)


def swapped(value, axis, mask):
    return lax.ppermute(value, axis, [(a, a ^ mask) for a in range(lax.axis_size(axis))])


def moved(choice, value, then=None, operands=()):
    def branch(mask, value, *operands):
        arrived = swapped(value, "users", mask)
        return arrived if then is None else then(arrived, *operands)

    choices = [functools.partial(branch, mask) for mask in range(1, lax.axis_size("users"))]
    return lax.switch(choice, choices, value, *operands)


def exchanged(value):
    size = lax.axis_size("items")
    if size == 1:
        return value, jnp.zeros_like(value)
    mask = 1
    while mask * 2 < size:
        value = value + swapped(value, "items", mask)
        mask *= 2
    return value, swapped(value, "items", mask)


def per_device(interactions, matchings, user_shape, item_shape):
    group = lax.axis_size("users")
    factor = float(group)
    users, depth = user_shape.shape
    items = item_shape.shape[0]
    sizes = chunk_rows(users)
    starts = [sum(sizes[:i]) for i in range(len(sizes))]
    count = len(sizes)

    item, choices = prepare_call(matchings, item_shape, group - 1)
    order = [(s, at, rows) for s in range(STRATA) for at, rows in zip(starts, sizes)]

    def opening(arrived, user_shape, interactions):
        theta, counts, uexps = start_call(user_shape, interactions, sizes)
        operands = {"counts": counts, "interactions": interactions, "uexp_in": uexps[0], "item": arrived}
        if count == 1:
            operands["theta"] = theta
        out = stratum_call(
            0, 0, sizes[0], items, depth, factor, True, count == 1, 0, sizes[:1], order[1], operands)
        return theta, [out["uexp"], *uexps[1:]], out

    theta, uexps, opened = moved(choices[0], item, opening, (user_shape, interactions))
    rte = None
    shp = [None] * count
    sums = [None] * count
    for stratum in range(STRATA):
        carried = {"theta": theta}
        earlier = {}
        for i, (at, rows) in enumerate(zip(starts, sizes)):
            first, last = i == 0, i == count - 1
            step = stratum * count + i
            ahead = order[step + 1] if step + 1 < len(order) else None
            cuts = last_cuts(rows) if step + 1 == len(order) else [rows]
            operands = {"counts": counts} if step else {}
            if ahead:
                operands["interactions"] = interactions
            if stratum == 0:
                operands["uexp"] = uexps[i]
            else:
                operands["acc"], operands["recv"] = sums[i]
                if stratum == 1:
                    operands["user_shape"] = user_shape
                else:
                    operands["shp_old"] = shp[i]
                if not first:
                    operands["rte"] = rte
                elif stratum > 1:
                    operands["rte_old"] = rte
            if first:
                operands["item"] = item
            elif last:
                operands["item_kept"] = carried["item_kept"]
            if not first:
                operands["item_exp"] = carried["item_exp"]
            if last:
                operands.update(earlier)
            if (stratum > 0 and not first) or (stratum == 0 and last):
                operands["theta"] = carried["theta"]
            if step == 0:
                out = opened
            else:
                out = stratum_call(
                    stratum, at, rows, items, depth, factor, first, last, i, cuts, ahead, operands)
            counts = out.get("counts_ahead")
            shp[i] = out.get("shp_new")
            sums[i] = exchanged(out["upart0"])
            if first:
                rte = out.get("rte_new")
                carried["item_exp"] = out["item_exp_new"]
                carried["item_kept"] = out["item_kept"]
            if last:
                item = out["item_new"]
            else:
                earlier[f"ratios{i}"], earlier[f"uexp{i}"] = out["ratios"], out.get("uexp", operands.get("uexp"))
                if stratum > 0:
                    carried["theta"] = out["theta_new"]
        if stratum + 1 < STRATA:
            item = moved(choices[stratum + 1], item)
        else:
            item = swapped(item, "users", group - 1)
    user_log = None
    pieces = [(at, rows, 0, sums[i], shp[i]) for i, (at, rows) in enumerate(zip(starts, sizes))]
    pieces[-1:] = [
        (starts[-1] + sum(cuts[:i]), size, sum(cuts[:i]), exchanged(out[f"upart{i}"]) if i else sums[-1], shp[-1])
        for i, size in enumerate(cuts)]
    for i, (at, rows, shp_at, piece_sums, piece_shp) in enumerate(pieces):
        user_log, *rest = user_log_call(
            at, rows, shp_at, users, depth, factor, i == 0, (*piece_sums, piece_shp, rte), user_log)
        rte = rest[0] if rest else rte
        if i == max(len(pieces) - 3, 0):
            item_log, rte = item_log_call(item, rte, items, depth)
    return user_log, item_log


def solution(mesh):
    placed = (P(None, "users", "items"), P(), P("users", None), P(("users", "items"), None))
    return jax.shard_map(
        per_device,
        mesh=mesh,
        in_specs=placed,
        out_specs=(P("users", None), P(("users", "items"), None)),
        check_vma=False,
    )
```

```python
import functools

import jax
import jax.numpy as jnp
from jax import lax
from jax.experimental import pallas as pl
from jax.experimental.pallas import tpu as pltpu
from jax.sharding import PartitionSpec as P

STRATA = 3
TILE = 64
START_TILE = 128
REDO_TILE = 32
F32 = jnp.float32
BF16 = jnp.bfloat16


def chunk_rows(rows):
    first = max(rows // 2 // START_TILE, 1) * START_TILE
    return [first, rows - first] if first < rows else [rows]


def last_cuts(rows):
    count = -(-rows // (4 * TILE))
    tiles_of = [rows // TILE // count + (i < rows // TILE % count) for i in range(count)]
    return [n * TILE for n in tiles_of] if rows % TILE == 0 else [rows]


def psi_parts(x):
    small = x < 8.0
    w = jnp.where(small, x + 3.5, x - 0.5)
    q = x * (x + 3.0)
    q2 = q + 2.0
    bounded = jnp.minimum(w, 1e9)
    square = bounded * bounded
    steps = jnp.where(small, q * q2, 1.0)
    r = 1.0 / (square * steps)
    s = r * steps
    shift = (2.0 * x + 3.0) * (q + q2) * (r * square)
    g = s * (1.0 / 24.0 - s * (7.0 / 960.0 - s * (31.0 / 8064.0 - s * (127.0 / 30720.0))))
    return w, g - jnp.where(small, shift, 0.0)


def psi_any(x):
    mirrored = x < 0.5
    w, g = psi_parts(jnp.where(mirrored, 1.0 - x, x))
    value = jnp.log(w) + g
    t = x - jnp.floor(x + 0.5)
    u = 3.14159265358979 * t
    v = u * u
    sin = 1.0 / 6227020800.0
    for c in (-1.0 / 39916800.0, 1.0 / 362880.0, -1.0 / 5040.0, 1.0 / 120.0, -1.0 / 6.0, 1.0):
        sin = sin * v + c
    cos = -1.0 / 87178291200.0
    for c in (1.0 / 479001600.0, -1.0 / 3628800.0, 1.0 / 40320.0, -1.0 / 720.0, 1.0 / 24.0, -0.5, 1.0):
        cos = cos * v + c
    value = jnp.where(mirrored, value - 3.14159265358979 * cos / (sin * u), value)
    return jnp.where((x <= 0.0) & (x == jnp.floor(x)), jnp.nan, value)


LOWEST = 0.01
HIGHEST = 1e30


def usual(rte):
    return jnp.where(rte <= HIGHEST, rte, -1.0)


def above(low):
    return jnp.min(low) >= LOWEST


def folded(x):
    return x.reshape(x.shape[0] // 8, 8, x.shape[1])


def tiles(rows):
    step = TILE if rows % TILE == 0 else rows
    return [(at, step) for at in range(0, rows, step)]


def redo_loop(rows, step, carry=None):
    size = REDO_TILE if rows % REDO_TILE == 0 else 8
    return lax.fori_loop(
        0, rows // size, lambda i, c: step(pl.multiple_of(i * size, size), size, c), carry)


def exp_tile(x, rte, general):
    shape = x.shape
    x = folded(x)
    if general:
        value = psi_any(x)
        if rte is not None:
            value = value - jnp.log(rte)[None]
        value = jnp.exp(value)
    else:
        w, g = psi_parts(x)
        value = w if rte is None else w * (1.0 / rte)[None]
        value = value * jnp.exp(g)
    mean = x if rte is None else x / rte[None] if general else x * (1.0 / rte)[None]
    return value.reshape(shape).astype(BF16), jnp.sum(mean, axis=0), jnp.min(x, axis=0)


def log_tile(x, rte, general):
    shape = x.shape
    x = folded(x)
    if general:
        value = psi_any(x) - jnp.log(rte)[None]
    else:
        w, g = psi_parts(x)
        value = (jnp.log(w) - jnp.log(rte)[None]) + g
    return value.reshape(shape).astype(BF16), jnp.min(x, axis=0)


def row_sum(x):
    return jnp.broadcast_to(jnp.sum(x, axis=0, keepdims=True), x.shape)


VMEM_SPEC = pl.BlockSpec(memory_space=pltpu.VMEM)
SMEM_SPEC = pl.BlockSpec(memory_space=pltpu.SMEM)
HBM_SPEC = pl.BlockSpec(memory_space=pltpu.HBM)
PARAMS = pltpu.CompilerParams(vmem_limit_bytes=24 * 2**20)


def in_hbm(x):
    return pltpu.with_memory_space_constraint(x, pltpu.HBM)


def in_vmem(x):
    return pltpu.with_memory_space_constraint(x, pltpu.VMEM)


def prepare_kernel(matchings_hbm, shape_hbm, item, *refs, last):
    choices, (matchings, shape, sems) = refs[:STRATA], refs[STRATA:]
    copies = [
        pltpu.make_async_copy(shape_hbm, shape, sems.at[0]),
        pltpu.make_async_copy(matchings_hbm, matchings, sems.at[1]),
    ]
    for copy in copies:
        copy.start()
    for copy in copies:
        copy.wait()
    item[...] = shape[...].astype(F32)
    choices[0][0] = matchings[0] - 1
    for stratum in range(1, STRATA - 1):
        choices[stratum][0] = jnp.bitwise_xor(matchings[stratum - 1], matchings[stratum]) - 1
    choices[STRATA - 1][0] = jnp.bitwise_xor(matchings[STRATA - 2], last) - 1


def prepare_call(matchings, item_shape, last):
    out = pl.pallas_call(
        functools.partial(prepare_kernel, last=last),
        out_shape=[jax.ShapeDtypeStruct(item_shape.shape, F32)]
        + [pltpu.SMEM((1,), jnp.int32)] * STRATA,
        in_specs=[HBM_SPEC, HBM_SPEC],
        out_specs=[VMEM_SPEC] + [SMEM_SPEC] * STRATA,
        scratch_shapes=[pltpu.SMEM(matchings.shape, jnp.int32), pltpu.VMEM(item_shape.shape, BF16),
                        pltpu.SemaphoreType.DMA((2,))],
        compiler_params=PARAMS,
        name="prepare",
    )(in_hbm(matchings), in_hbm(item_shape))
    return out[0], [choice[0] for choice in out[1:]]


def start_kernel(shape_hbm, interactions, theta, *refs, ahead):
    counts, uexps, (shape, sems) = refs[:len(ahead)], refs[len(ahead):-2], refs[-2:]
    depth = shape.shape[1]
    load = pltpu.make_async_copy(shape_hbm, shape, sems.at[0])
    load.start()
    fetches = [
        pltpu.make_async_copy(interactions.at[s, pl.ds(at, rows), :], counts[i], sems.at[i + 1])
        for i, (s, at, rows) in enumerate(ahead)]
    for fetch in fetches:
        fetch.start()
    load.wait()
    total, low = jnp.zeros((8, depth), F32), jnp.ones((8, depth), F32)
    begin = 0
    for uexp in uexps:
        rows = uexp.shape[0]

        def step(i, carry, begin=begin, uexp=uexp):
            at = i * START_TILE
            x = shape[pl.ds(pl.multiple_of(begin + at, START_TILE), START_TILE), :].astype(F32)
            value, part, part_low = exp_tile(x, None, False)
            uexp[pl.ds(pl.multiple_of(at, START_TILE), START_TILE), :] = value
            return carry[0] + part, jnp.minimum(carry[1], part_low)

        total, low = lax.fori_loop(0, rows // START_TILE, step, (total, low))
        begin += rows
    theta[...] = total

    @pl.when(jnp.logical_not(above(low)))
    def _():
        begin = 0
        for uexp in uexps:

            def redo(at, size, _, begin=begin, uexp=uexp):
                x = shape[pl.ds(pl.multiple_of(begin + at, size), size), :].astype(F32)
                uexp[pl.ds(at, size), :] = exp_tile(x, None, True)[0]

            redo_loop(uexp.shape[0], redo)
            begin += uexp.shape[0]

    for fetch in fetches:
        fetch.wait()


def start_call(user_shape, interactions, sizes, ahead):
    rows, depth = user_shape.shape
    items = interactions.shape[2]
    theta, *arrays = pl.pallas_call(
        functools.partial(start_kernel, ahead=ahead),
        out_shape=[pltpu.VMEM((8, depth), F32)]
        + [pltpu.VMEM((fetch[2], items), BF16) for fetch in ahead]
        + [pltpu.VMEM((size, depth), BF16) for size in sizes],
        in_specs=[HBM_SPEC] * 2,
        out_specs=[VMEM_SPEC] * (1 + len(ahead) + len(sizes)),
        scratch_shapes=[pltpu.VMEM((rows, depth), BF16), pltpu.SemaphoreType.DMA((1 + len(ahead),))],
        compiler_params=PARAMS,
        cost_estimate=pl.CostEstimate(
            flops=40 * rows * depth, bytes_accessed=rows * depth * 4, transcendentals=2 * rows * depth),
        name="user_start",
    )(in_hbm(user_shape), in_hbm(interactions))
    return theta, arrays[:len(ahead)], arrays[len(ahead):]


def dot_rows(a, b):
    return lax.dot_general(a, b, (((1,), (1,)), ((), ())), preferred_element_type=F32)


def item_sums(ratios, uexp):
    return lax.dot_general(ratios[...], uexp[...], (((0,), (0,)), ((), ())), preferred_element_type=F32)


def stratum_kernel(names, *refs, stratum, at, rows, items, factor, first, last, earlier, cuts, ahead):
    ref = dict(zip(names, refs))
    copies = {}

    def fetch(name, source, target):
        copies[name] = pltpu.make_async_copy(source, target, ref["sems"].at[len(copies)])
        copies[name].start()

    if first and stratum > 0:
        fetch("item", ref["item"], ref["item_kept"])
    for i, (s, begin, size) in enumerate(ahead):
        fetch(f"ahead{i}", ref["interactions"].at[s, pl.ds(begin, size), :], ref[f"counts_ahead{i}"])
    upart, counts, ratios, denominator = ref["upart0"], ref["counts"], ref["ratios"], ref["denominator"]
    uexp = ref["uexp"]
    extra = 8 if first else 0

    lows = []
    theta = None
    item = ref["item_kept"] if first or last else None

    if stratum > 0:
        if first:
            beta = row_sum(ref["acc"][0:8, :] + ref["recv"][0:8, :])
            old = 1.0 if stratum == 1 else ref["rte_old"][...]
            rte = 0.5 * old + 0.5 * (0.3 + factor * beta)
            ref["rte_new"][...] = rte
        else:
            rte = ref["rte"][...]
        lows.append(usual(rte))
        for t, step in tiles(rows):
            old = ref["user_shape"][at + t:at + t + step, :].astype(F32) if stratum == 1 else ref["shp_old"][t:t + step, :]
            stat = ref["acc"][extra + t:extra + t + step, :] + ref["recv"][extra + t:extra + t + step, :]
            shp = 0.5 * old + 0.5 * (0.3 + factor * stat)
            ref["shp_new"][t:t + step, :] = shp
            value, part, low = exp_tile(shp, rte, False)
            uexp[t:t + step, :] = value
            theta = part if theta is None else theta + part
            lows.append(low)
        if not first:
            theta = theta + ref["theta"][...]
        total_mean = ref["theta_new"]
        total_mean[...] = theta
    elif last:
        total_mean = ref["theta"]

    if first and stratum > 0:
        copies["item"].wait()
    elif first:
        item[...] = ref["item"][...]
        uexp[...] = ref["uexp_in"][...]
    if first or last:
        item_rte = None if stratum == 0 else item[items:items + 8, :]
    if first:
        item_exp, sums, low = exp_tile(item[0:items, :], item_rte, False)
        ref["item_exp_new"][...] = item_exp
        upart[0:8, :] = sums
        lows.append(low)
        if item_rte is not None:
            lows.append(usual(item_rte))
    else:
        item_exp = ref["item_exp"][...]

    denominator[...] = dot_rows(uexp[...], item_exp)
    for t, step in tiles(rows):
        ratios[t:t + step, :] = (
            counts[t:t + step, :].astype(F32) / denominator[t:t + step, :]).astype(BF16)
    user_sums = uexp[...].astype(F32) * jnp.dot(ratios[...], item_exp, preferred_element_type=F32)
    parts = []
    for i, length in enumerate(cuts):
        begin, skip = sum(cuts[:i]), 0 if i else extra
        parts.append((ref[f"upart{i}"], begin, skip, length))
        parts[i][0][skip:skip + length, :] = user_sums[begin:begin + length, :]
    pairs = [(ref[f"ratios{i}"], ref[f"uexp{i}"]) for i in range(earlier)] + [(ratios, uexp)]

    def update_items(istat):
        old = 1.0 if item_rte is None else item_rte
        kept = ref["item_exp_new" if first else "item_exp"][...].astype(F32)
        ref["item_new"][0:items, :] = 0.5 * item[0:items, :] + 0.5 * (0.3 + factor * (kept * istat))
        ref["item_new"][items:items + 8, :] = 0.5 * old + 0.5 * (0.3 + factor * row_sum(total_mean[...]))

    if last:
        istat = None
        for pair in pairs:
            part = item_sums(*pair)
            istat = part if istat is None else istat + part
        update_items(istat)

    if lows:

        @pl.when(jnp.logical_not(above(functools.reduce(jnp.minimum, lows))))
        def _():
            if stratum > 0:

                def redo_users(at, size, total):
                    place = pl.ds(at, size)
                    uexp[place, :], part, _ = exp_tile(ref["shp_new"][place, :], rte, True)
                    return total + part

                start = jnp.zeros_like(rte) if first else ref["theta"][...]
                total_mean[...] = redo_loop(rows, redo_users, start)
            if first:

                def redo_items(at, size, total):
                    place = pl.ds(at, size)
                    ref["item_exp_new"][place, :], part, _ = exp_tile(item[place, :], item_rte, True)
                    return total + part

                upart[0:8, :] = redo_loop(items, redo_items, jnp.zeros((8, upart.shape[1]), F32))
            kept = ref["item_exp_new" if first else "item_exp"]
            for target, begin, skip, length in parts:

                def redo_sums(at, size, _, target=target, begin=begin, skip=skip):
                    place = pl.ds(pl.multiple_of(begin + at, size), size)
                    u = uexp[place, :]
                    ratio = (counts[place, :].astype(F32) / dot_rows(u, kept[...])).astype(BF16)
                    ratios[place, :] = ratio
                    target[pl.ds(pl.multiple_of(skip + at, 8), size), :] = u.astype(F32) * jnp.dot(
                        ratio, kept[...], preferred_element_type=F32)

                redo_loop(length, redo_sums)
            if last:
                total = ref["item_new"].at[pl.ds(0, items), :]
                total[...] = jnp.zeros((items, ref["item_new"].shape[1]), F32)
                for pair in pairs:

                    def redo_stat(at, size, _, pair=pair):
                        place = pl.ds(at, size)
                        total[...] += item_sums(pair[0].at[place, :], pair[1].at[place, :])

                    redo_loop(rows if pair[0] is ratios else pair[0].shape[0], redo_stat)
                update_items(total[...])

    for i in range(len(ahead)):
        copies[f"ahead{i}"].wait()


def stratum_call(stratum, at, rows, items, depth, factor, first, last, earlier, cuts, ahead, operands):
    extra = 8 if first else 0
    outs = {f"upart{i}": ((size + (0 if i else extra), depth), F32) for i, size in enumerate(cuts)}
    if stratum > 0:
        outs["shp_new"] = ((rows, depth), F32)
    if first and stratum > 0:
        outs["rte_new"] = ((8, depth), F32)
    if first:
        outs["item_exp_new"] = ((items, depth), BF16)
    if first:
        outs["item_kept"] = (operands["item"].shape, F32)
    if last:
        outs["item_new"] = ((items + 8, depth), F32)
    else:
        outs["ratios"] = ((rows, items), BF16)
        outs["uexp"] = ((rows, depth), BF16)
        if stratum > 0:
            outs["theta_new"] = ((8, depth), F32)
    for i, fetch in enumerate(ahead):
        outs[f"counts_ahead{i}"] = ((fetch[2], items), BF16)
    scratch = {
        "denominator": pltpu.VMEM((rows, items), F32),
        "sems": pltpu.SemaphoreType.DMA((1 + len(ahead),)),
    }
    if last:
        scratch["ratios"] = pltpu.VMEM((rows, items), BF16)
        if stratum > 0:
            scratch["uexp"] = pltpu.VMEM((rows, depth), BF16)
            scratch["theta_new"] = pltpu.VMEM((8, depth), F32)
    hbm = ("interactions", "item") if stratum > 0 else ("interactions",)
    operands = {
        name: in_hbm(x) if name in hbm else in_vmem(x) if name in ("user_shape", "item") else x
        for name, x in operands.items()}
    names = list(operands) + list(outs) + list(scratch)
    kernel = functools.partial(
        stratum_kernel, names, stratum=stratum, at=at, rows=rows, items=items,
        factor=factor, first=first, last=last, earlier=earlier, cuts=cuts, ahead=ahead)
    results = pl.pallas_call(
        kernel,
        out_shape=[jax.ShapeDtypeStruct(*spec) for spec in outs.values()],
        in_specs=[HBM_SPEC if name in hbm else VMEM_SPEC for name in operands],
        out_specs=[VMEM_SPEC] * len(outs),
        scratch_shapes=list(scratch.values()),
        compiler_params=PARAMS,
        cost_estimate=pl.CostEstimate(
            flops=600 * rows * items * depth, bytes_accessed=rows * 200000, transcendentals=rows * depth),
        name=f"stratum{stratum}_at{at}",
    )(*operands.values())
    return dict(zip(outs, results))


def user_log_kernel(*refs, at, rows, shp_at, factor, first, filled):
    acc, recv, shp_old, rte_in = refs[:4]
    rest = refs[5:] if filled else refs[4:]
    out, *rte_out, block, sem = rest
    rte = rte_in[...]
    if first:
        rte = 0.5 * rte + 0.5 * (0.3 + factor * row_sum(acc[0:8, :] + recv[0:8, :]))
    for ref in rte_out:
        ref[...] = rte
    extra = 8 if first else 0

    def shape(t, step):
        stat = acc[pl.ds(extra + t, step), :] + recv[pl.ds(extra + t, step), :]
        return 0.5 * shp_old[pl.ds(shp_at + t, step), :] + 0.5 * (0.3 + factor * stat)

    low = rte
    for t, step in tiles(rows):
        block[t:t + step, :], part_low = log_tile(shape(t, step), rte, False)
        low = jnp.minimum(low, part_low)

    @pl.when(jnp.logical_not(above(low)))
    def _():
        def redo(t, step, _):
            block[pl.ds(t, step), :] = log_tile(shape(pl.multiple_of(t, 8), step), rte, True)[0]

        redo_loop(rows, redo)

    copy = pltpu.make_async_copy(block, out.at[pl.ds(at, rows), :], sem)
    copy.start()
    copy.wait()


def user_log_call(at, rows, shp_at, total, depth, factor, first, operands, filled):
    out_shape = [jax.ShapeDtypeStruct((total, depth), BF16)]
    out_specs = [HBM_SPEC]
    if at + rows < total:
        out_shape.append(jax.ShapeDtypeStruct((8, depth), F32))
        out_specs.append(VMEM_SPEC)
    operands = list(operands)
    in_specs = [VMEM_SPEC] * 4
    if filled is not None:
        operands.append(filled)
        in_specs.append(HBM_SPEC)
    return pl.pallas_call(
        functools.partial(user_log_kernel, at=at, rows=rows, shp_at=shp_at, factor=factor, first=first,
                          filled=filled is not None),
        out_shape=out_shape,
        in_specs=in_specs,
        out_specs=out_specs,
        input_output_aliases={} if filled is None else {4: 0},
        scratch_shapes=[pltpu.VMEM((rows, depth), BF16), pltpu.SemaphoreType.DMA],
        compiler_params=PARAMS,
        cost_estimate=pl.CostEstimate(
            flops=40 * rows * depth, bytes_accessed=rows * depth * 14, transcendentals=rows * depth),
        name=f"user_log_at{at}",
    )(*operands)


def item_log_kernel(item, through, out, passed, *, items):
    passed[...] = through[...]
    rte = item[items:items + 8, :]

    out[...], low = log_tile(item[0:items, :], rte, False)

    @pl.when(jnp.logical_not(above(jnp.minimum(low, rte))))
    def _():
        def redo(t, step, _):
            place = pl.ds(t, step)
            out[place, :] = log_tile(item[place, :], rte, True)[0]

        redo_loop(items, redo)


def item_log_call(item, through, items, depth):
    return pl.pallas_call(
        functools.partial(item_log_kernel, items=items),
        out_shape=[jax.ShapeDtypeStruct((items, depth), BF16), jax.ShapeDtypeStruct(through.shape, F32)],
        in_specs=[VMEM_SPEC, VMEM_SPEC],
        out_specs=[VMEM_SPEC, VMEM_SPEC],
        compiler_params=PARAMS,
        cost_estimate=pl.CostEstimate(
            flops=40 * items * depth, bytes_accessed=items * depth * 6, transcendentals=items * depth),
        name="item_log",
    )(item, through)


def swapped(value, axis, mask):
    return lax.ppermute(value, axis, [(a, a ^ mask) for a in range(lax.axis_size(axis))])


def moved(choice, value, then=None, operands=()):
    def branch(mask, value, *operands):
        arrived = swapped(value, "users", mask)
        return arrived if then is None else then(arrived, *operands)

    choices = [functools.partial(branch, mask) for mask in range(1, lax.axis_size("users"))]
    return lax.switch(choice, choices, value, *operands)


def exchanged(value):
    size = lax.axis_size("items")
    if size == 1:
        return value, jnp.zeros_like(value)
    mask = 1
    while mask * 2 < size:
        value = value + swapped(value, "items", mask)
        mask *= 2
    return value, swapped(value, "items", mask)


def per_device(interactions, matchings, user_shape, item_shape):
    group = lax.axis_size("users")
    factor = float(group)
    users, depth = user_shape.shape
    items = item_shape.shape[0]
    sizes = chunk_rows(users)
    starts = [sum(sizes[:i]) for i in range(len(sizes))]
    count = len(sizes)

    item, choices = prepare_call(matchings, item_shape, group - 1)
    order = [(s, at, rows) for s in range(STRATA) for at, rows in zip(starts, sizes)]

    def ahead_of(stratum):
        begin = 0 if stratum == 0 else stratum * count + 1
        return order[begin:(stratum + 1) * count + 1]

    def opening(arrived, user_shape, interactions):
        theta, counts, uexps = start_call(user_shape, interactions, sizes, ahead_of(0))
        operands = {"counts": counts[0], "uexp_in": uexps[0], "item": arrived}
        if count == 1:
            operands["theta"] = theta
        out = stratum_call(
            0, 0, sizes[0], items, depth, factor, True, count == 1, 0, sizes[:1], [], operands)
        return theta, [out["uexp"], *uexps[1:]], counts[1:], out

    theta, uexps, fetched, opened = moved(choices[0], item, opening, (user_shape, interactions))
    rte = None
    shp = [None] * count
    sums = [None] * count
    for stratum in range(STRATA):
        carried = {"theta": theta}
        earlier = {}
        for i, (at, rows) in enumerate(zip(starts, sizes)):
            first, last = i == 0, i == count - 1
            step = stratum * count + i
            ahead = ahead_of(stratum) if first and stratum > 0 else []
            cuts = last_cuts(rows) if step + 1 == len(order) else [rows]
            operands = {}
            if step:
                operands["counts"], fetched = fetched[0], fetched[1:]
            if ahead:
                operands["interactions"] = interactions
            if stratum == 0:
                operands["uexp"] = uexps[i]
            else:
                operands["acc"], operands["recv"] = sums[i]
                if stratum == 1:
                    operands["user_shape"] = user_shape
                else:
                    operands["shp_old"] = shp[i]
                if not first:
                    operands["rte"] = rte
                elif stratum > 1:
                    operands["rte_old"] = rte
            if first:
                operands["item"] = item
            elif last:
                operands["item_kept"] = carried["item_kept"]
            if not first:
                operands["item_exp"] = carried["item_exp"]
            if last:
                operands.update(earlier)
            if (stratum > 0 and not first) or (stratum == 0 and last):
                operands["theta"] = carried["theta"]
            if step == 0:
                out = opened
            else:
                out = stratum_call(
                    stratum, at, rows, items, depth, factor, first, last, i, cuts, ahead, operands)
            fetched = [*fetched, *(out[f"counts_ahead{n}"] for n in range(len(ahead)))]
            shp[i] = out.get("shp_new")
            sums[i] = exchanged(out["upart0"])
            if first:
                rte = out.get("rte_new")
                carried["item_exp"] = out["item_exp_new"]
                carried["item_kept"] = out["item_kept"]
            if last:
                item = out["item_new"]
            else:
                earlier[f"ratios{i}"], earlier[f"uexp{i}"] = out["ratios"], out.get("uexp", operands.get("uexp"))
                if stratum > 0:
                    carried["theta"] = out["theta_new"]
        if stratum + 1 < STRATA:
            item = moved(choices[stratum + 1], item)
        else:
            item = swapped(item, "users", group - 1)
    user_log = None
    pieces = [(at, rows, 0, sums[i], shp[i]) for i, (at, rows) in enumerate(zip(starts, sizes))]
    pieces[-1:] = [
        (starts[-1] + sum(cuts[:i]), size, sum(cuts[:i]), exchanged(out[f"upart{i}"]) if i else sums[-1], shp[-1])
        for i, size in enumerate(cuts)]
    for i, (at, rows, shp_at, piece_sums, piece_shp) in enumerate(pieces):
        user_log, *rest = user_log_call(
            at, rows, shp_at, users, depth, factor, i == 0, (*piece_sums, piece_shp, rte), user_log)
        rte = rest[0] if rest else rte
        if i == max(len(pieces) - 3, 0):
            item_log, rte = item_log_call(item, rte, items, depth)
    return user_log, item_log


def solution(mesh):
    placed = (P(None, "users", "items"), P(), P("users", None), P(("users", "items"), None))
    return jax.shard_map(
        per_device,
        mesh=mesh,
        in_specs=placed,
        out_specs=(P("users", None), P(("users", "items"), None)),
        check_vma=False,
    )
```

```python
import functools

import jax
import jax.numpy as jnp
from jax import lax
from jax.experimental import pallas as pl
from jax.experimental.pallas import tpu as pltpu
from jax.sharding import PartitionSpec as P

STRATA = 3
TILE = 64
START_TILE = 128
REDO_TILE = 32
F32 = jnp.float32
BF16 = jnp.bfloat16


def chunk_rows(rows):
    first = max(rows // 2 // START_TILE, 1) * START_TILE
    return [first, rows - first] if first < rows else [rows]


def last_cuts(rows):
    count = -(-rows // (4 * TILE))
    tiles_of = [rows // TILE // count + (i < rows // TILE % count) for i in range(count)]
    return [n * TILE for n in tiles_of] if rows % TILE == 0 else [rows]


def psi_parts(x):
    small = x < 8.0
    w = jnp.where(small, x + 3.5, x - 0.5)
    q = x * (x + 3.0)
    q2 = q + 2.0
    bounded = jnp.minimum(w, 1e9)
    square = bounded * bounded
    steps = jnp.where(small, q * q2, 1.0)
    r = 1.0 / (square * steps)
    s = r * steps
    shift = (2.0 * x + 3.0) * (q + q2) * (r * square)
    g = s * (1.0 / 24.0 - s * (7.0 / 960.0 - s * (31.0 / 8064.0 - s * (127.0 / 30720.0))))
    return w, g - jnp.where(small, shift, 0.0)


def psi_any(x):
    mirrored = x < 0.5
    w, g = psi_parts(jnp.where(mirrored, 1.0 - x, x))
    value = jnp.log(w) + g
    t = x - jnp.floor(x + 0.5)
    u = 3.14159265358979 * t
    v = u * u
    sin = 1.0 / 6227020800.0
    for c in (-1.0 / 39916800.0, 1.0 / 362880.0, -1.0 / 5040.0, 1.0 / 120.0, -1.0 / 6.0, 1.0):
        sin = sin * v + c
    cos = -1.0 / 87178291200.0
    for c in (1.0 / 479001600.0, -1.0 / 3628800.0, 1.0 / 40320.0, -1.0 / 720.0, 1.0 / 24.0, -0.5, 1.0):
        cos = cos * v + c
    value = jnp.where(mirrored, value - 3.14159265358979 * cos / (sin * u), value)
    return jnp.where((x <= 0.0) & (x == jnp.floor(x)), jnp.nan, value)


LOWEST = 0.01
HIGHEST = 1e30


def usual(rte):
    return jnp.where(rte <= HIGHEST, rte, -1.0)


def above(low):
    return jnp.min(low) >= LOWEST


def folded(x):
    return x.reshape(x.shape[0] // 8, 8, x.shape[1])


def tiles(rows):
    step = TILE if rows % TILE == 0 else rows
    return [(at, step) for at in range(0, rows, step)]


def redo_loop(rows, step, carry=None):
    size = REDO_TILE if rows % REDO_TILE == 0 else 8
    return lax.fori_loop(
        0, rows // size, lambda i, c: step(pl.multiple_of(i * size, size), size, c), carry)


def exp_tile(x, rte, general):
    shape = x.shape
    x = folded(x)
    if general:
        value = psi_any(x)
        if rte is not None:
            value = value - jnp.log(rte)[None]
        value = jnp.exp(value)
    else:
        w, g = psi_parts(x)
        value = w if rte is None else w * (1.0 / rte)[None]
        value = value * jnp.exp(g)
    mean = x if rte is None else x / rte[None] if general else x * (1.0 / rte)[None]
    return value.reshape(shape).astype(BF16), jnp.sum(mean, axis=0), jnp.min(x, axis=0)


def log_tile(x, rte, general):
    shape = x.shape
    x = folded(x)
    if general:
        value = psi_any(x) - jnp.log(rte)[None]
    else:
        w, g = psi_parts(x)
        value = (jnp.log(w) - jnp.log(rte)[None]) + g
    return value.reshape(shape).astype(BF16), jnp.min(x, axis=0)


def row_sum(x):
    return jnp.broadcast_to(jnp.sum(x, axis=0, keepdims=True), x.shape)


VMEM_SPEC = pl.BlockSpec(memory_space=pltpu.VMEM)
SMEM_SPEC = pl.BlockSpec(memory_space=pltpu.SMEM)
HBM_SPEC = pl.BlockSpec(memory_space=pltpu.HBM)
PARAMS = pltpu.CompilerParams(vmem_limit_bytes=24 * 2**20)


def in_hbm(x):
    return pltpu.with_memory_space_constraint(x, pltpu.HBM)


def in_vmem(x):
    return pltpu.with_memory_space_constraint(x, pltpu.VMEM)


def prepare_kernel(matchings_hbm, shape_hbm, item, *refs, last):
    choices, (matchings, shape, sems) = refs[:STRATA], refs[STRATA:]
    copies = [
        pltpu.make_async_copy(shape_hbm, shape, sems.at[0]),
        pltpu.make_async_copy(matchings_hbm, matchings, sems.at[1]),
    ]
    for copy in copies:
        copy.start()
    for copy in copies:
        copy.wait()
    item[...] = shape[...].astype(F32)
    choices[0][0] = matchings[0] - 1
    for stratum in range(1, STRATA - 1):
        choices[stratum][0] = jnp.bitwise_xor(matchings[stratum - 1], matchings[stratum]) - 1
    choices[STRATA - 1][0] = jnp.bitwise_xor(matchings[STRATA - 2], last) - 1


def prepare_call(matchings, item_shape, last):
    out = pl.pallas_call(
        functools.partial(prepare_kernel, last=last),
        out_shape=[jax.ShapeDtypeStruct(item_shape.shape, F32)]
        + [pltpu.SMEM((1,), jnp.int32)] * STRATA,
        in_specs=[HBM_SPEC, HBM_SPEC],
        out_specs=[VMEM_SPEC] + [SMEM_SPEC] * STRATA,
        scratch_shapes=[pltpu.SMEM(matchings.shape, jnp.int32), pltpu.VMEM(item_shape.shape, BF16),
                        pltpu.SemaphoreType.DMA((2,))],
        compiler_params=PARAMS,
        name="prepare",
    )(in_hbm(matchings), in_hbm(item_shape))
    return out[0], [choice[0] for choice in out[1:]]


def start_kernel(shape_hbm, interactions, theta, *refs, ahead):
    counts, uexps, (shape, sems) = refs[:len(ahead)], refs[len(ahead):-2], refs[-2:]
    depth = shape.shape[1]
    load = pltpu.make_async_copy(shape_hbm, shape, sems.at[0])
    load.start()
    fetches = [
        pltpu.make_async_copy(interactions.at[s, pl.ds(at, rows), :], counts[i], sems.at[i + 1])
        for i, (s, at, rows) in enumerate(ahead)]
    for fetch in fetches:
        fetch.start()
    load.wait()
    total, low = jnp.zeros((8, depth), F32), jnp.ones((8, depth), F32)
    begin = 0
    for uexp in uexps:
        rows = uexp.shape[0]

        def step(i, carry, begin=begin, uexp=uexp):
            at = i * START_TILE
            x = shape[pl.ds(pl.multiple_of(begin + at, START_TILE), START_TILE), :].astype(F32)
            value, part, part_low = exp_tile(x, None, False)
            uexp[pl.ds(pl.multiple_of(at, START_TILE), START_TILE), :] = value
            return carry[0] + part, jnp.minimum(carry[1], part_low)

        total, low = lax.fori_loop(0, rows // START_TILE, step, (total, low))
        begin += rows
    theta[...] = total

    @pl.when(jnp.logical_not(above(low)))
    def _():
        begin = 0
        for uexp in uexps:

            def redo(at, size, _, begin=begin, uexp=uexp):
                x = shape[pl.ds(pl.multiple_of(begin + at, size), size), :].astype(F32)
                uexp[pl.ds(at, size), :] = exp_tile(x, None, True)[0]

            redo_loop(uexp.shape[0], redo)
            begin += uexp.shape[0]

    for fetch in fetches:
        fetch.wait()


def start_call(user_shape, interactions, sizes, ahead):
    rows, depth = user_shape.shape
    items = interactions.shape[2]
    theta, *arrays = pl.pallas_call(
        functools.partial(start_kernel, ahead=ahead),
        out_shape=[pltpu.VMEM((8, depth), F32)]
        + [pltpu.VMEM((fetch[2], items), BF16) for fetch in ahead]
        + [pltpu.VMEM((size, depth), BF16) for size in sizes],
        in_specs=[HBM_SPEC] * 2,
        out_specs=[VMEM_SPEC] * (1 + len(ahead) + len(sizes)),
        scratch_shapes=[pltpu.VMEM((rows, depth), BF16), pltpu.SemaphoreType.DMA((1 + len(ahead),))],
        compiler_params=PARAMS,
        cost_estimate=pl.CostEstimate(
            flops=40 * rows * depth, bytes_accessed=rows * depth * 4, transcendentals=2 * rows * depth),
        name="user_start",
    )(in_hbm(user_shape), in_hbm(interactions))
    return theta, arrays[:len(ahead)], arrays[len(ahead):]


def dot_rows(a, b):
    return lax.dot_general(a, b, (((1,), (1,)), ((), ())), preferred_element_type=F32)


def item_sums(ratios, uexp):
    return lax.dot_general(ratios[...], uexp[...], (((0,), (0,)), ((), ())), preferred_element_type=F32)


def stratum_kernel(names, *refs, stratum, at, rows, items, factor, first, last, earlier, cuts, ahead):
    ref = dict(zip(names, refs))
    copies = {}

    def fetch(name, source, target):
        copies[name] = pltpu.make_async_copy(source, target, ref["sems"].at[len(copies)])
        copies[name].start()

    for i, (s, begin, size) in enumerate(ahead):
        fetch(f"ahead{i}", ref["interactions"].at[s, pl.ds(begin, size), :], ref[f"counts_ahead{i}"])
    upart, counts, ratios, denominator = ref["upart0"], ref["counts"], ref["ratios"], ref["denominator"]
    uexp = ref["uexp"]
    extra = 8 if first else 0

    lows = []
    theta = None
    item = ref["item_kept"] if first or last else None

    if stratum > 0:
        if first:
            beta = row_sum(ref["acc"][0:8, :] + ref["recv"][0:8, :])
            old = 1.0 if stratum == 1 else ref["rte_old"][...]
            rte = 0.5 * old + 0.5 * (0.3 + factor * beta)
            ref["rte_new"][...] = rte
        else:
            rte = ref["rte"][...]
        lows.append(usual(rte))
        for t, step in tiles(rows):
            old = ref["user_shape"][at + t:at + t + step, :].astype(F32) if stratum == 1 else ref["shp_old"][t:t + step, :]
            stat = ref["acc"][extra + t:extra + t + step, :] + ref["recv"][extra + t:extra + t + step, :]
            shp = 0.5 * old + 0.5 * (0.3 + factor * stat)
            ref["shp_new"][t:t + step, :] = shp
            value, part, low = exp_tile(shp, rte, False)
            uexp[t:t + step, :] = value
            theta = part if theta is None else theta + part
            lows.append(low)
        if not first:
            theta = theta + ref["theta"][...]
        total_mean = ref["theta_new"]
        total_mean[...] = theta
    elif last:
        total_mean = ref["theta"]

    meets = first and stratum == 0
    item_exp_ref = ref["item_exp_new" if meets else "item_exp"]
    if first or last:
        item_rte = None if stratum == 0 else item[items:items + 8, :]
    if first and not meets:
        upart[0:8, :] = ref["item_sums"][...]
    if meets:
        item[...] = ref["item"][...]
        uexp[...] = ref["uexp_in"][...]
        item_exp, sums, low = exp_tile(item[0:items, :], item_rte, False)
        ref["item_exp_new"][...] = item_exp
        upart[0:8, :] = sums
        lows.append(low)
    else:
        item_exp = item_exp_ref[...]

    denominator[...] = dot_rows(uexp[...], item_exp)
    for t, step in tiles(rows):
        ratios[t:t + step, :] = (
            counts[t:t + step, :].astype(F32) / denominator[t:t + step, :]).astype(BF16)
    user_sums = uexp[...].astype(F32) * jnp.dot(ratios[...], item_exp, preferred_element_type=F32)
    parts = []
    for i, length in enumerate(cuts):
        begin, skip = sum(cuts[:i]), 0 if i else extra
        parts.append((ref[f"upart{i}"], begin, skip, length))
        parts[i][0][skip:skip + length, :] = user_sums[begin:begin + length, :]
    pairs = [(ref[f"ratios{i}"], ref[f"uexp{i}"]) for i in range(earlier)] + [(ratios, uexp)]

    def update_items(istat):
        old = 1.0 if item_rte is None else item_rte
        kept = item_exp_ref[...].astype(F32)
        ref["item_new"][0:items, :] = 0.5 * item[0:items, :] + 0.5 * (0.3 + factor * (kept * istat))
        ref["item_new"][items:items + 8, :] = 0.5 * old + 0.5 * (0.3 + factor * row_sum(total_mean[...]))

    if last:
        istat = None
        for pair in pairs:
            part = item_sums(*pair)
            istat = part if istat is None else istat + part
        update_items(istat)

    if lows:

        @pl.when(jnp.logical_not(above(functools.reduce(jnp.minimum, lows))))
        def _():
            if stratum > 0:

                def redo_users(at, size, total):
                    place = pl.ds(at, size)
                    uexp[place, :], part, _ = exp_tile(ref["shp_new"][place, :], rte, True)
                    return total + part

                start = jnp.zeros_like(rte) if first else ref["theta"][...]
                total_mean[...] = redo_loop(rows, redo_users, start)
            if meets:

                def redo_items(at, size, total):
                    place = pl.ds(at, size)
                    ref["item_exp_new"][place, :], part, _ = exp_tile(item[place, :], item_rte, True)
                    return total + part

                upart[0:8, :] = redo_loop(items, redo_items, jnp.zeros((8, upart.shape[1]), F32))
            kept = item_exp_ref
            for target, begin, skip, length in parts:

                def redo_sums(at, size, _, target=target, begin=begin, skip=skip):
                    place = pl.ds(pl.multiple_of(begin + at, size), size)
                    u = uexp[place, :]
                    ratio = (counts[place, :].astype(F32) / dot_rows(u, kept[...])).astype(BF16)
                    ratios[place, :] = ratio
                    target[pl.ds(pl.multiple_of(skip + at, 8), size), :] = u.astype(F32) * jnp.dot(
                        ratio, kept[...], preferred_element_type=F32)

                redo_loop(length, redo_sums)
            if last:
                total = ref["item_new"].at[pl.ds(0, items), :]
                total[...] = jnp.zeros((items, ref["item_new"].shape[1]), F32)
                for pair in pairs:

                    def redo_stat(at, size, _, pair=pair):
                        place = pl.ds(at, size)
                        total[...] += item_sums(pair[0].at[place, :], pair[1].at[place, :])

                    redo_loop(rows if pair[0] is ratios else pair[0].shape[0], redo_stat)
                update_items(total[...])

    for i in range(len(ahead)):
        copies[f"ahead{i}"].wait()


def stratum_call(stratum, at, rows, items, depth, factor, first, last, earlier, cuts, ahead, operands):
    extra = 8 if first else 0
    outs = {f"upart{i}": ((size + (0 if i else extra), depth), F32) for i, size in enumerate(cuts)}
    if stratum > 0:
        outs["shp_new"] = ((rows, depth), F32)
    if first and stratum > 0:
        outs["rte_new"] = ((8, depth), F32)
    if first and stratum == 0:
        outs["item_exp_new"] = ((items, depth), BF16)
    if first and stratum == 0:
        outs["item_kept"] = (operands["item"].shape, F32)
    if last:
        outs["item_new"] = ((items + 8, depth), F32)
    else:
        outs["ratios"] = ((rows, items), BF16)
        outs["uexp"] = ((rows, depth), BF16)
        if stratum > 0:
            outs["theta_new"] = ((8, depth), F32)
    for i, fetch in enumerate(ahead):
        outs[f"counts_ahead{i}"] = ((fetch[2], items), BF16)
    scratch = {
        "denominator": pltpu.VMEM((rows, items), F32),
        "sems": pltpu.SemaphoreType.DMA((1 + len(ahead),)),
    }
    if last:
        scratch["ratios"] = pltpu.VMEM((rows, items), BF16)
        if stratum > 0:
            scratch["uexp"] = pltpu.VMEM((rows, depth), BF16)
            scratch["theta_new"] = pltpu.VMEM((8, depth), F32)
    hbm = ("interactions",)
    operands = {
        name: in_hbm(x) if name in hbm else in_vmem(x) if name in ("user_shape", "item") else x
        for name, x in operands.items()}
    names = list(operands) + list(outs) + list(scratch)
    kernel = functools.partial(
        stratum_kernel, names, stratum=stratum, at=at, rows=rows, items=items,
        factor=factor, first=first, last=last, earlier=earlier, cuts=cuts, ahead=ahead)
    results = pl.pallas_call(
        kernel,
        out_shape=[jax.ShapeDtypeStruct(*spec) for spec in outs.values()],
        in_specs=[HBM_SPEC if name in hbm else VMEM_SPEC for name in operands],
        out_specs=[VMEM_SPEC] * len(outs),
        scratch_shapes=list(scratch.values()),
        compiler_params=PARAMS,
        cost_estimate=pl.CostEstimate(
            flops=600 * rows * items * depth, bytes_accessed=rows * 200000, transcendentals=rows * depth),
        name=f"stratum{stratum}_at{at}",
    )(*operands.values())
    return dict(zip(outs, results))


def meet_kernel(item, kept, item_exp, sums, *, items):
    rte = item[items:items + 8, :]
    kept[items:items + 8, :] = rte

    def step(i, carry):
        place = pl.ds(pl.multiple_of(i * TILE, TILE), TILE)
        x = item[place, :]
        kept[place, :] = x
        item_exp[place, :], part, low = exp_tile(x, rte, False)
        return carry[0] + part, jnp.minimum(carry[1], low)

    sums[...], low = lax.fori_loop(0, items // TILE, step, (jnp.zeros_like(rte), usual(rte)))

    @pl.when(jnp.logical_not(above(low)))
    def _():
        def redo(at, size, total):
            place = pl.ds(at, size)
            item_exp[place, :], part, _ = exp_tile(item[place, :], rte, True)
            return total + part

        sums[...] = redo_loop(items, redo, jnp.zeros_like(rte))


def meet_call(item):
    rows, depth = item.shape
    items = rows - 8
    kept, item_exp, sums = pl.pallas_call(
        functools.partial(meet_kernel, items=items),
        out_shape=[pltpu.VMEM(item.shape, F32), pltpu.VMEM((items, depth), BF16), pltpu.VMEM((8, depth), F32)],
        in_specs=[VMEM_SPEC],
        out_specs=[VMEM_SPEC] * 3,
        compiler_params=PARAMS,
        cost_estimate=pl.CostEstimate(
            flops=40 * items * depth, bytes_accessed=items * depth * 10, transcendentals=2 * items * depth),
        name="meet_items",
    )(in_vmem(item))
    return {"item_kept": kept, "item_exp": item_exp, "item_sums": sums}


def user_log_kernel(*refs, at, rows, shp_at, factor, first, filled):
    acc, recv, shp_old, rte_in = refs[:4]
    rest = refs[5:] if filled else refs[4:]
    out, *rte_out, block, sem = rest
    rte = rte_in[...]
    if first:
        rte = 0.5 * rte + 0.5 * (0.3 + factor * row_sum(acc[0:8, :] + recv[0:8, :]))
    for ref in rte_out:
        ref[...] = rte
    extra = 8 if first else 0

    def shape(t, step):
        stat = acc[pl.ds(extra + t, step), :] + recv[pl.ds(extra + t, step), :]
        return 0.5 * shp_old[pl.ds(shp_at + t, step), :] + 0.5 * (0.3 + factor * stat)

    low = rte
    for t, step in tiles(rows):
        block[t:t + step, :], part_low = log_tile(shape(t, step), rte, False)
        low = jnp.minimum(low, part_low)

    @pl.when(jnp.logical_not(above(low)))
    def _():
        def redo(t, step, _):
            block[pl.ds(t, step), :] = log_tile(shape(pl.multiple_of(t, 8), step), rte, True)[0]

        redo_loop(rows, redo)

    copy = pltpu.make_async_copy(block, out.at[pl.ds(at, rows), :], sem)
    copy.start()
    copy.wait()


def user_log_call(at, rows, shp_at, total, depth, factor, first, operands, filled):
    out_shape = [jax.ShapeDtypeStruct((total, depth), BF16)]
    out_specs = [HBM_SPEC]
    if at + rows < total:
        out_shape.append(jax.ShapeDtypeStruct((8, depth), F32))
        out_specs.append(VMEM_SPEC)
    operands = list(operands)
    in_specs = [VMEM_SPEC] * 4
    if filled is not None:
        operands.append(filled)
        in_specs.append(HBM_SPEC)
    return pl.pallas_call(
        functools.partial(user_log_kernel, at=at, rows=rows, shp_at=shp_at, factor=factor, first=first,
                          filled=filled is not None),
        out_shape=out_shape,
        in_specs=in_specs,
        out_specs=out_specs,
        input_output_aliases={} if filled is None else {4: 0},
        scratch_shapes=[pltpu.VMEM((rows, depth), BF16), pltpu.SemaphoreType.DMA],
        compiler_params=PARAMS,
        cost_estimate=pl.CostEstimate(
            flops=40 * rows * depth, bytes_accessed=rows * depth * 14, transcendentals=rows * depth),
        name=f"user_log_at{at}",
    )(*operands)


def item_log_kernel(item, through, out, passed, *, items):
    passed[...] = through[...]
    rte = item[items:items + 8, :]

    out[...], low = log_tile(item[0:items, :], rte, False)

    @pl.when(jnp.logical_not(above(jnp.minimum(low, rte))))
    def _():
        def redo(t, step, _):
            place = pl.ds(t, step)
            out[place, :] = log_tile(item[place, :], rte, True)[0]

        redo_loop(items, redo)


def item_log_call(item, through, items, depth):
    return pl.pallas_call(
        functools.partial(item_log_kernel, items=items),
        out_shape=[jax.ShapeDtypeStruct((items, depth), BF16), jax.ShapeDtypeStruct(through.shape, F32)],
        in_specs=[VMEM_SPEC, VMEM_SPEC],
        out_specs=[VMEM_SPEC, VMEM_SPEC],
        compiler_params=PARAMS,
        cost_estimate=pl.CostEstimate(
            flops=40 * items * depth, bytes_accessed=items * depth * 6, transcendentals=items * depth),
        name="item_log",
    )(item, through)


def swapped(value, axis, mask):
    return lax.ppermute(value, axis, [(a, a ^ mask) for a in range(lax.axis_size(axis))])


def moved(choice, value, then=None, operands=()):
    def branch(mask, value, *operands):
        arrived = swapped(value, "users", mask)
        return arrived if then is None else then(arrived, *operands)

    choices = [functools.partial(branch, mask) for mask in range(1, lax.axis_size("users"))]
    return lax.switch(choice, choices, value, *operands)


def exchanged(value):
    size = lax.axis_size("items")
    if size == 1:
        return value, jnp.zeros_like(value)
    mask = 1
    while mask * 2 < size:
        value = value + swapped(value, "items", mask)
        mask *= 2
    return value, swapped(value, "items", mask)


def per_device(interactions, matchings, user_shape, item_shape):
    group = lax.axis_size("users")
    factor = float(group)
    users, depth = user_shape.shape
    items = item_shape.shape[0]
    sizes = chunk_rows(users)
    starts = [sum(sizes[:i]) for i in range(len(sizes))]
    count = len(sizes)

    item, choices = prepare_call(matchings, item_shape, group - 1)
    order = [(s, at, rows) for s in range(STRATA) for at, rows in zip(starts, sizes)]

    def ahead_of(stratum):
        begin = 0 if stratum == 0 else stratum * count + 1
        return order[begin:(stratum + 1) * count + 1]

    def opening(arrived, user_shape, interactions):
        theta, counts, uexps = start_call(user_shape, interactions, sizes, ahead_of(0))
        operands = {"counts": counts[0], "uexp_in": uexps[0], "item": arrived}
        if count == 1:
            operands["theta"] = theta
        out = stratum_call(
            0, 0, sizes[0], items, depth, factor, True, count == 1, 0, sizes[:1], [], operands)
        return theta, [out["uexp"], *uexps[1:]], counts[1:], out

    theta, uexps, fetched, opened = moved(choices[0], item, opening, (user_shape, interactions))
    rte = None
    shp = [None] * count
    sums = [None] * count
    for stratum in range(STRATA):
        carried = {"theta": theta} if stratum == 0 else {"theta": theta, **item}
        earlier = {}
        for i, (at, rows) in enumerate(zip(starts, sizes)):
            first, last = i == 0, i == count - 1
            step = stratum * count + i
            ahead = ahead_of(stratum) if first and stratum > 0 else []
            cuts = last_cuts(rows) if step + 1 == len(order) else [rows]
            operands = {}
            if step:
                operands["counts"], fetched = fetched[0], fetched[1:]
            if ahead:
                operands["interactions"] = interactions
            if stratum == 0:
                operands["uexp"] = uexps[i]
            else:
                operands["acc"], operands["recv"] = sums[i]
                if stratum == 1:
                    operands["user_shape"] = user_shape
                else:
                    operands["shp_old"] = shp[i]
                if not first:
                    operands["rte"] = rte
                elif stratum > 1:
                    operands["rte_old"] = rte
            if step:
                operands["item_exp"] = carried["item_exp"]
            if step and (first or last):
                operands["item_kept"] = carried["item_kept"]
            if step and first:
                operands["item_sums"] = carried["item_sums"]
            if last:
                operands.update(earlier)
            if (stratum > 0 and not first) or (stratum == 0 and last):
                operands["theta"] = carried["theta"]
            if step == 0:
                out = opened
            else:
                out = stratum_call(
                    stratum, at, rows, items, depth, factor, first, last, i, cuts, ahead, operands)
            fetched = [*fetched, *(out[f"counts_ahead{n}"] for n in range(len(ahead)))]
            shp[i] = out.get("shp_new")
            sums[i] = exchanged(out["upart0"])
            if first:
                rte = out.get("rte_new")
                if stratum == 0:
                    carried["item_exp"], carried["item_kept"] = out["item_exp_new"], out["item_kept"]
            if last:
                item = out["item_new"]
            else:
                earlier[f"ratios{i}"], earlier[f"uexp{i}"] = out["ratios"], out.get("uexp", operands.get("uexp"))
                if stratum > 0:
                    carried["theta"] = out["theta_new"]
        if stratum + 1 < STRATA:
            item = moved(choices[stratum + 1], item, meet_call)
        else:
            item = swapped(item, "users", group - 1)
    user_log = None
    pieces = [(at, rows, 0, sums[i], shp[i]) for i, (at, rows) in enumerate(zip(starts, sizes))]
    pieces[-1:] = [
        (starts[-1] + sum(cuts[:i]), size, sum(cuts[:i]), exchanged(out[f"upart{i}"]) if i else sums[-1], shp[-1])
        for i, size in enumerate(cuts)]
    for i, (at, rows, shp_at, piece_sums, piece_shp) in enumerate(pieces):
        user_log, *rest = user_log_call(
            at, rows, shp_at, users, depth, factor, i == 0, (*piece_sums, piece_shp, rte), user_log)
        rte = rest[0] if rest else rte
        if i == max(len(pieces) - 3, 0):
            item_log, rte = item_log_call(item, rte, items, depth)
    return user_log, item_log


def solution(mesh):
    placed = (P(None, "users", "items"), P(), P("users", None), P(("users", "items"), None))
    return jax.shard_map(
        per_device,
        mesh=mesh,
        in_specs=placed,
        out_specs=(P("users", None), P(("users", "items"), None)),
        check_vma=False,
    )
```

```python
import functools

import jax
import jax.numpy as jnp
from jax import lax
from jax.experimental import pallas as pl
from jax.experimental.pallas import tpu as pltpu
from jax.sharding import PartitionSpec as P

STRATA = 3
TILE = 64
START_TILE = 128
REDO_TILE = 32
F32 = jnp.float32
BF16 = jnp.bfloat16


def chunk_rows(rows):
    first = max(rows // 2 // START_TILE, 1) * START_TILE
    return [first, rows - first] if first < rows else [rows]


def last_cuts(rows):
    count = -(-rows // (4 * TILE))
    tiles_of = [rows // TILE // count + (i < rows // TILE % count) for i in range(count)]
    return [n * TILE for n in tiles_of] if rows % TILE == 0 else [rows]


def psi_parts(x):
    small = x < 8.0
    w = jnp.where(small, x + 3.5, x - 0.5)
    q = x * (x + 3.0)
    q2 = q + 2.0
    bounded = jnp.minimum(w, 1e9)
    square = bounded * bounded
    steps = jnp.where(small, q * q2, 1.0)
    r = 1.0 / (square * steps)
    s = r * steps
    shift = (2.0 * x + 3.0) * (q + q2) * (r * square)
    g = s * (1.0 / 24.0 - s * (7.0 / 960.0 - s * (31.0 / 8064.0 - s * (127.0 / 30720.0))))
    return w, g - jnp.where(small, shift, 0.0)


def psi_any(x):
    mirrored = x < 0.5
    w, g = psi_parts(jnp.where(mirrored, 1.0 - x, x))
    value = jnp.log(w) + g
    t = x - jnp.floor(x + 0.5)
    u = 3.14159265358979 * t
    v = u * u
    sin = 1.0 / 6227020800.0
    for c in (-1.0 / 39916800.0, 1.0 / 362880.0, -1.0 / 5040.0, 1.0 / 120.0, -1.0 / 6.0, 1.0):
        sin = sin * v + c
    cos = -1.0 / 87178291200.0
    for c in (1.0 / 479001600.0, -1.0 / 3628800.0, 1.0 / 40320.0, -1.0 / 720.0, 1.0 / 24.0, -0.5, 1.0):
        cos = cos * v + c
    value = jnp.where(mirrored, value - 3.14159265358979 * cos / (sin * u), value)
    return jnp.where((x <= 0.0) & (x == jnp.floor(x)), jnp.nan, value)


LOWEST = 0.01
HIGHEST = 1e30


def usual(rte):
    return jnp.where(rte <= HIGHEST, rte, -1.0)


def above(low):
    return jnp.min(low) >= LOWEST


def folded(x):
    return x.reshape(x.shape[0] // 8, 8, x.shape[1])


def tiles(rows):
    step = TILE if rows % TILE == 0 else rows
    return [(at, step) for at in range(0, rows, step)]


def redo_loop(rows, step, carry=None):
    size = REDO_TILE if rows % REDO_TILE == 0 else 8
    return lax.fori_loop(
        0, rows // size, lambda i, c: step(pl.multiple_of(i * size, size), size, c), carry)


def exp_tile(x, rte, general):
    shape = x.shape
    x = folded(x)
    if general:
        value = psi_any(x)
        if rte is not None:
            value = value - jnp.log(rte)[None]
        value = jnp.exp(value)
    else:
        w, g = psi_parts(x)
        value = w if rte is None else w * (1.0 / rte)[None]
        value = value * jnp.exp(g)
    mean = x if rte is None else x / rte[None] if general else x * (1.0 / rte)[None]
    return value.reshape(shape).astype(BF16), jnp.sum(mean, axis=0), jnp.min(x, axis=0)


def log_tile(x, rte, general):
    shape = x.shape
    x = folded(x)
    if general:
        value = psi_any(x) - jnp.log(rte)[None]
    else:
        w, g = psi_parts(x)
        value = (jnp.log(w) - jnp.log(rte)[None]) + g
    return value.reshape(shape).astype(BF16), jnp.min(x, axis=0)


def row_sum(x):
    return jnp.broadcast_to(jnp.sum(x, axis=0, keepdims=True), x.shape)


VMEM_SPEC = pl.BlockSpec(memory_space=pltpu.VMEM)
SMEM_SPEC = pl.BlockSpec(memory_space=pltpu.SMEM)
HBM_SPEC = pl.BlockSpec(memory_space=pltpu.HBM)
PARAMS = pltpu.CompilerParams(vmem_limit_bytes=24 * 2**20)


def in_hbm(x):
    return pltpu.with_memory_space_constraint(x, pltpu.HBM)


def in_vmem(x):
    return pltpu.with_memory_space_constraint(x, pltpu.VMEM)


def prepare_kernel(matchings_hbm, shape_hbm, item, *refs, last):
    choices, (matchings, shape, sems) = refs[:STRATA], refs[STRATA:]
    copies = [
        pltpu.make_async_copy(shape_hbm, shape, sems.at[0]),
        pltpu.make_async_copy(matchings_hbm, matchings, sems.at[1]),
    ]
    for copy in copies:
        copy.start()
    for copy in copies:
        copy.wait()
    item[...] = shape[...].astype(F32)
    choices[0][0] = matchings[0] - 1
    for stratum in range(1, STRATA - 1):
        choices[stratum][0] = jnp.bitwise_xor(matchings[stratum - 1], matchings[stratum]) - 1
    choices[STRATA - 1][0] = jnp.bitwise_xor(matchings[STRATA - 2], last) - 1


def prepare_call(matchings, item_shape, last):
    out = pl.pallas_call(
        functools.partial(prepare_kernel, last=last),
        out_shape=[jax.ShapeDtypeStruct(item_shape.shape, F32)]
        + [pltpu.SMEM((1,), jnp.int32)] * STRATA,
        in_specs=[HBM_SPEC, HBM_SPEC],
        out_specs=[VMEM_SPEC] + [SMEM_SPEC] * STRATA,
        scratch_shapes=[pltpu.SMEM(matchings.shape, jnp.int32), pltpu.VMEM(item_shape.shape, BF16),
                        pltpu.SemaphoreType.DMA((2,))],
        compiler_params=PARAMS,
        name="prepare",
    )(in_hbm(matchings), in_hbm(item_shape))
    return out[0], [choice[0] for choice in out[1:]]


def start_kernel(shape_hbm, interactions, theta, *refs, ahead):
    counts, uexps, (shape, sems) = refs[:len(ahead)], refs[len(ahead):-2], refs[-2:]
    depth = shape.shape[1]
    load = pltpu.make_async_copy(shape_hbm, shape, sems.at[0])
    load.start()
    fetches = [
        pltpu.make_async_copy(interactions.at[s, pl.ds(at, rows), :], counts[i], sems.at[i + 1])
        for i, (s, at, rows) in enumerate(ahead)]
    for fetch in fetches:
        fetch.start()
    load.wait()
    total, low = jnp.zeros((8, depth), F32), jnp.ones((8, depth), F32)
    begin = 0
    for uexp in uexps:
        rows = uexp.shape[0]

        def step(i, carry, begin=begin, uexp=uexp):
            at = i * START_TILE
            x = shape[pl.ds(pl.multiple_of(begin + at, START_TILE), START_TILE), :].astype(F32)
            value, part, part_low = exp_tile(x, None, False)
            uexp[pl.ds(pl.multiple_of(at, START_TILE), START_TILE), :] = value
            return carry[0] + part, jnp.minimum(carry[1], part_low)

        total, low = lax.fori_loop(0, rows // START_TILE, step, (total, low))
        begin += rows
    theta[...] = total

    @pl.when(jnp.logical_not(above(low)))
    def _():
        begin = 0
        for uexp in uexps:

            def redo(at, size, _, begin=begin, uexp=uexp):
                x = shape[pl.ds(pl.multiple_of(begin + at, size), size), :].astype(F32)
                uexp[pl.ds(at, size), :] = exp_tile(x, None, True)[0]

            redo_loop(uexp.shape[0], redo)
            begin += uexp.shape[0]

    for fetch in fetches:
        fetch.wait()


def start_call(user_shape, interactions, sizes, ahead):
    rows, depth = user_shape.shape
    items = interactions.shape[2]
    theta, *arrays = pl.pallas_call(
        functools.partial(start_kernel, ahead=ahead),
        out_shape=[pltpu.VMEM((8, depth), F32)]
        + [pltpu.VMEM((fetch[2], items), BF16) for fetch in ahead]
        + [pltpu.VMEM((size, depth), BF16) for size in sizes],
        in_specs=[HBM_SPEC] * 2,
        out_specs=[VMEM_SPEC] * (1 + len(ahead) + len(sizes)),
        scratch_shapes=[pltpu.VMEM((rows, depth), BF16), pltpu.SemaphoreType.DMA((1 + len(ahead),))],
        compiler_params=PARAMS,
        cost_estimate=pl.CostEstimate(
            flops=40 * rows * depth, bytes_accessed=rows * depth * 4, transcendentals=2 * rows * depth),
        name="user_start",
    )(in_hbm(user_shape), in_hbm(interactions))
    return theta, arrays[:len(ahead)], arrays[len(ahead):]


def fetch_kernel(interactions, *refs, ahead):
    counts, sems = refs[:-1], refs[-1]
    fetches = [
        pltpu.make_async_copy(interactions.at[s, pl.ds(at, rows), :], counts[i], sems.at[i])
        for i, (s, at, rows) in enumerate(ahead)]
    for fetch in fetches:
        fetch.start()
    for fetch in fetches:
        fetch.wait()


def fetch_call(interactions, ahead):
    items = interactions.shape[2]
    return pl.pallas_call(
        functools.partial(fetch_kernel, ahead=ahead),
        out_shape=[pltpu.VMEM((rows, items), BF16) for _, _, rows in ahead],
        in_specs=[HBM_SPEC],
        out_specs=[VMEM_SPEC] * len(ahead),
        scratch_shapes=[pltpu.SemaphoreType.DMA((len(ahead),))],
        compiler_params=PARAMS,
        cost_estimate=pl.CostEstimate(
            flops=0, bytes_accessed=4 * items * sum(rows for _, _, rows in ahead), transcendentals=0),
        name="fetch_weights",
    )(in_hbm(interactions))


def dot_rows(a, b):
    return lax.dot_general(a, b, (((1,), (1,)), ((), ())), preferred_element_type=F32)


def item_sums(ratios, uexp):
    return lax.dot_general(ratios[...], uexp[...], (((0,), (0,)), ((), ())), preferred_element_type=F32)


def stratum_kernel(names, *refs, stratum, at, rows, items, factor, first, last, earlier, cuts):
    ref = dict(zip(names, refs))
    copies = {}

    def fetch(name, source, target):
        copies[name] = pltpu.make_async_copy(source, target, ref["sems"].at[len(copies)])
        copies[name].start()

    if first and stratum > 0:
        fetch("item", ref["item"], ref["item_kept"])
    upart, counts, ratios, denominator = ref["upart0"], ref["counts"], ref["ratios"], ref["denominator"]
    uexp = ref["uexp"]
    extra = 8 if first else 0

    lows = []
    theta = None
    item = ref["item_kept"] if first or last else None

    if stratum > 0:
        if first:
            beta = row_sum(ref["acc"][0:8, :] + ref["recv"][0:8, :])
            old = 1.0 if stratum == 1 else ref["rte_old"][...]
            rte = 0.5 * old + 0.5 * (0.3 + factor * beta)
            ref["rte_new"][...] = rte
        else:
            rte = ref["rte"][...]
        lows.append(usual(rte))
        for t, step in tiles(rows):
            old = ref["user_shape"][at + t:at + t + step, :].astype(F32) if stratum == 1 else ref["shp_old"][t:t + step, :]
            stat = ref["acc"][extra + t:extra + t + step, :] + ref["recv"][extra + t:extra + t + step, :]
            shp = 0.5 * old + 0.5 * (0.3 + factor * stat)
            ref["shp_new"][t:t + step, :] = shp
            value, part, low = exp_tile(shp, rte, False)
            uexp[t:t + step, :] = value
            theta = part if theta is None else theta + part
            lows.append(low)
        if not first:
            theta = theta + ref["theta"][...]
        total_mean = ref["theta_new"]
        total_mean[...] = theta
    elif last:
        total_mean = ref["theta"]

    if first and stratum > 0:
        copies["item"].wait()
    elif first:
        item[...] = ref["item"][...]
        uexp[...] = ref["uexp_in"][...]
    if first or last:
        item_rte = None if stratum == 0 else item[items:items + 8, :]
    if first:
        item_exp, sums, low = exp_tile(item[0:items, :], item_rte, False)
        ref["item_exp_new"][...] = item_exp
        upart[0:8, :] = sums
        lows.append(low)
        if item_rte is not None:
            lows.append(usual(item_rte))
    else:
        item_exp = ref["item_exp"][...]

    denominator[...] = dot_rows(uexp[...], item_exp)
    for t, step in tiles(rows):
        ratios[t:t + step, :] = (
            counts[t:t + step, :].astype(F32) / denominator[t:t + step, :]).astype(BF16)
    user_sums = uexp[...].astype(F32) * jnp.dot(ratios[...], item_exp, preferred_element_type=F32)
    parts = []
    for i, length in enumerate(cuts):
        begin, skip = sum(cuts[:i]), 0 if i else extra
        parts.append((ref[f"upart{i}"], begin, skip, length))
        parts[i][0][skip:skip + length, :] = user_sums[begin:begin + length, :]
    pairs = [(ref[f"ratios{i}"], ref[f"uexp{i}"]) for i in range(earlier)] + [(ratios, uexp)]

    def update_items(istat):
        old = 1.0 if item_rte is None else item_rte
        kept = ref["item_exp_new" if first else "item_exp"][...].astype(F32)
        ref["item_new"][0:items, :] = 0.5 * item[0:items, :] + 0.5 * (0.3 + factor * (kept * istat))
        ref["item_new"][items:items + 8, :] = 0.5 * old + 0.5 * (0.3 + factor * row_sum(total_mean[...]))

    if last:
        istat = None
        for pair in pairs:
            part = item_sums(*pair)
            istat = part if istat is None else istat + part
        update_items(istat)

    if lows:

        @pl.when(jnp.logical_not(above(functools.reduce(jnp.minimum, lows))))
        def _():
            if stratum > 0:

                def redo_users(at, size, total):
                    place = pl.ds(at, size)
                    uexp[place, :], part, _ = exp_tile(ref["shp_new"][place, :], rte, True)
                    return total + part

                start = jnp.zeros_like(rte) if first else ref["theta"][...]
                total_mean[...] = redo_loop(rows, redo_users, start)
            if first:

                def redo_items(at, size, total):
                    place = pl.ds(at, size)
                    ref["item_exp_new"][place, :], part, _ = exp_tile(item[place, :], item_rte, True)
                    return total + part

                upart[0:8, :] = redo_loop(items, redo_items, jnp.zeros((8, upart.shape[1]), F32))
            kept = ref["item_exp_new" if first else "item_exp"]
            for target, begin, skip, length in parts:

                def redo_sums(at, size, _, target=target, begin=begin, skip=skip):
                    place = pl.ds(pl.multiple_of(begin + at, size), size)
                    u = uexp[place, :]
                    ratio = (counts[place, :].astype(F32) / dot_rows(u, kept[...])).astype(BF16)
                    ratios[place, :] = ratio
                    target[pl.ds(pl.multiple_of(skip + at, 8), size), :] = u.astype(F32) * jnp.dot(
                        ratio, kept[...], preferred_element_type=F32)

                redo_loop(length, redo_sums)
            if last:
                total = ref["item_new"].at[pl.ds(0, items), :]
                total[...] = jnp.zeros((items, ref["item_new"].shape[1]), F32)
                for pair in pairs:

                    def redo_stat(at, size, _, pair=pair):
                        place = pl.ds(at, size)
                        total[...] += item_sums(pair[0].at[place, :], pair[1].at[place, :])

                    redo_loop(rows if pair[0] is ratios else pair[0].shape[0], redo_stat)
                update_items(total[...])


def stratum_call(stratum, at, rows, items, depth, factor, first, last, earlier, cuts, operands):
    extra = 8 if first else 0
    outs = {f"upart{i}": ((size + (0 if i else extra), depth), F32) for i, size in enumerate(cuts)}
    if stratum > 0:
        outs["shp_new"] = ((rows, depth), F32)
    if first and stratum > 0:
        outs["rte_new"] = ((8, depth), F32)
    if first:
        outs["item_exp_new"] = ((items, depth), BF16)
    if first:
        outs["item_kept"] = (operands["item"].shape, F32)
    if last:
        outs["item_new"] = ((items + 8, depth), F32)
    else:
        outs["ratios"] = ((rows, items), BF16)
        outs["uexp"] = ((rows, depth), BF16)
        if stratum > 0:
            outs["theta_new"] = ((8, depth), F32)
    scratch = {
        "denominator": pltpu.VMEM((rows, items), F32),
        "sems": pltpu.SemaphoreType.DMA((1,)),
    }
    if last:
        scratch["ratios"] = pltpu.VMEM((rows, items), BF16)
        if stratum > 0:
            scratch["uexp"] = pltpu.VMEM((rows, depth), BF16)
            scratch["theta_new"] = pltpu.VMEM((8, depth), F32)
    hbm = ("item",) if stratum > 0 else ()
    operands = {
        name: in_hbm(x) if name in hbm else in_vmem(x) if name in ("user_shape", "item") else x
        for name, x in operands.items()}
    names = list(operands) + list(outs) + list(scratch)
    kernel = functools.partial(
        stratum_kernel, names, stratum=stratum, at=at, rows=rows, items=items,
        factor=factor, first=first, last=last, earlier=earlier, cuts=cuts)
    results = pl.pallas_call(
        kernel,
        out_shape=[jax.ShapeDtypeStruct(*spec) for spec in outs.values()],
        in_specs=[HBM_SPEC if name in hbm else VMEM_SPEC for name in operands],
        out_specs=[VMEM_SPEC] * len(outs),
        scratch_shapes=list(scratch.values()),
        compiler_params=PARAMS,
        cost_estimate=pl.CostEstimate(
            flops=600 * rows * items * depth, bytes_accessed=rows * 200000, transcendentals=rows * depth),
        name=f"stratum{stratum}_at{at}",
    )(*operands.values())
    return dict(zip(outs, results))


def user_log_kernel(*refs, at, rows, shp_at, factor, first, filled):
    acc, recv, shp_old, rte_in = refs[:4]
    rest = refs[5:] if filled else refs[4:]
    out, *rte_out, block, sem = rest
    rte = rte_in[...]
    if first:
        rte = 0.5 * rte + 0.5 * (0.3 + factor * row_sum(acc[0:8, :] + recv[0:8, :]))
    for ref in rte_out:
        ref[...] = rte
    extra = 8 if first else 0

    def shape(t, step):
        stat = acc[pl.ds(extra + t, step), :] + recv[pl.ds(extra + t, step), :]
        return 0.5 * shp_old[pl.ds(shp_at + t, step), :] + 0.5 * (0.3 + factor * stat)

    low = rte
    for t, step in tiles(rows):
        block[t:t + step, :], part_low = log_tile(shape(t, step), rte, False)
        low = jnp.minimum(low, part_low)

    @pl.when(jnp.logical_not(above(low)))
    def _():
        def redo(t, step, _):
            block[pl.ds(t, step), :] = log_tile(shape(pl.multiple_of(t, 8), step), rte, True)[0]

        redo_loop(rows, redo)

    copy = pltpu.make_async_copy(block, out.at[pl.ds(at, rows), :], sem)
    copy.start()
    copy.wait()


def user_log_call(at, rows, shp_at, total, depth, factor, first, operands, filled):
    out_shape = [jax.ShapeDtypeStruct((total, depth), BF16)]
    out_specs = [HBM_SPEC]
    if at + rows < total:
        out_shape.append(jax.ShapeDtypeStruct((8, depth), F32))
        out_specs.append(VMEM_SPEC)
    operands = list(operands)
    in_specs = [VMEM_SPEC] * 4
    if filled is not None:
        operands.append(filled)
        in_specs.append(HBM_SPEC)
    return pl.pallas_call(
        functools.partial(user_log_kernel, at=at, rows=rows, shp_at=shp_at, factor=factor, first=first,
                          filled=filled is not None),
        out_shape=out_shape,
        in_specs=in_specs,
        out_specs=out_specs,
        input_output_aliases={} if filled is None else {4: 0},
        scratch_shapes=[pltpu.VMEM((rows, depth), BF16), pltpu.SemaphoreType.DMA],
        compiler_params=PARAMS,
        cost_estimate=pl.CostEstimate(
            flops=40 * rows * depth, bytes_accessed=rows * depth * 14, transcendentals=rows * depth),
        name=f"user_log_at{at}",
    )(*operands)


def item_log_kernel(item, through, out, passed, *, items):
    passed[...] = through[...]
    rte = item[items:items + 8, :]

    out[...], low = log_tile(item[0:items, :], rte, False)

    @pl.when(jnp.logical_not(above(jnp.minimum(low, rte))))
    def _():
        def redo(t, step, _):
            place = pl.ds(t, step)
            out[place, :] = log_tile(item[place, :], rte, True)[0]

        redo_loop(items, redo)


def item_log_call(item, through, items, depth):
    return pl.pallas_call(
        functools.partial(item_log_kernel, items=items),
        out_shape=[jax.ShapeDtypeStruct((items, depth), BF16), jax.ShapeDtypeStruct(through.shape, F32)],
        in_specs=[VMEM_SPEC, VMEM_SPEC],
        out_specs=[VMEM_SPEC, VMEM_SPEC],
        compiler_params=PARAMS,
        cost_estimate=pl.CostEstimate(
            flops=40 * items * depth, bytes_accessed=items * depth * 6, transcendentals=items * depth),
        name="item_log",
    )(item, through)


def swapped(value, axis, mask):
    return lax.ppermute(value, axis, [(a, a ^ mask) for a in range(lax.axis_size(axis))])


def moved(choice, value, then=None, operands=()):
    def branch(mask, value, *operands):
        arrived = swapped(value, "users", mask)
        return arrived if then is None else then(arrived, *operands)

    choices = [functools.partial(branch, mask) for mask in range(1, lax.axis_size("users"))]
    return lax.switch(choice, choices, value, *operands)


def exchanged(value):
    size = lax.axis_size("items")
    if size == 1:
        return value, jnp.zeros_like(value)
    mask = 1
    while mask * 2 < size:
        value = value + swapped(value, "items", mask)
        mask *= 2
    return value, swapped(value, "items", mask)


def per_device(interactions, matchings, user_shape, item_shape):
    group = lax.axis_size("users")
    factor = float(group)
    users, depth = user_shape.shape
    items = item_shape.shape[0]
    sizes = chunk_rows(users)
    starts = [sum(sizes[:i]) for i in range(len(sizes))]
    count = len(sizes)

    item, choices = prepare_call(matchings, item_shape, group - 1)
    order = [(s, at, rows) for s in range(STRATA) for at, rows in zip(starts, sizes)]

    def chunks_of(stratum):
        return order[stratum * count:(stratum + 1) * count]

    def opening(arrived, user_shape, interactions):
        theta, counts, uexps = start_call(user_shape, interactions, sizes, chunks_of(0))
        operands = {"counts": counts[0], "uexp_in": uexps[0], "item": arrived}
        if count == 1:
            operands["theta"] = theta
        out = stratum_call(
            0, 0, sizes[0], items, depth, factor, True, count == 1, 0, sizes[:1], operands)
        return theta, [out["uexp"], *uexps[1:]], counts[1:], out

    theta, uexps, fetched, opened = moved(choices[0], item, opening, (user_shape, interactions))
    rte = None
    shp = [None] * count
    sums = [None] * count
    for stratum in range(STRATA):
        carried = {"theta": theta}
        earlier = {}
        for i, (at, rows) in enumerate(zip(starts, sizes)):
            first, last = i == 0, i == count - 1
            step = stratum * count + i
            cuts = last_cuts(rows) if step + 1 == len(order) else [rows]
            operands = {}
            if step:
                operands["counts"], fetched = fetched[0], fetched[1:]
            if stratum == 0:
                operands["uexp"] = uexps[i]
            else:
                operands["acc"], operands["recv"] = sums[i]
                if stratum == 1:
                    operands["user_shape"] = user_shape
                else:
                    operands["shp_old"] = shp[i]
                if not first:
                    operands["rte"] = rte
                elif stratum > 1:
                    operands["rte_old"] = rte
            if first:
                operands["item"] = item
            elif last:
                operands["item_kept"] = carried["item_kept"]
            if not first:
                operands["item_exp"] = carried["item_exp"]
            if last:
                operands.update(earlier)
            if (stratum > 0 and not first) or (stratum == 0 and last):
                operands["theta"] = carried["theta"]
            if step == 0:
                out = opened
            else:
                out = stratum_call(
                    stratum, at, rows, items, depth, factor, first, last, i, cuts, operands)
            shp[i] = out.get("shp_new")
            sums[i] = exchanged(out["upart0"])
            if first:
                rte = out.get("rte_new")
                carried["item_exp"] = out["item_exp_new"]
                carried["item_kept"] = out["item_kept"]
            if last:
                item = out["item_new"]
            else:
                earlier[f"ratios{i}"], earlier[f"uexp{i}"] = out["ratios"], out.get("uexp", operands.get("uexp"))
                if stratum > 0:
                    carried["theta"] = out["theta_new"]
        if stratum + 1 < STRATA:
            def with_weights(arrived, interactions, chunks=chunks_of(stratum + 1)):
                return arrived, fetch_call(interactions, chunks)

            item, fetched = moved(choices[stratum + 1], item, with_weights, (interactions,))
        else:
            item = swapped(item, "users", group - 1)
    user_log = None
    pieces = [(at, rows, 0, sums[i], shp[i]) for i, (at, rows) in enumerate(zip(starts, sizes))]
    pieces[-1:] = [
        (starts[-1] + sum(cuts[:i]), size, sum(cuts[:i]), exchanged(out[f"upart{i}"]) if i else sums[-1], shp[-1])
        for i, size in enumerate(cuts)]
    for i, (at, rows, shp_at, piece_sums, piece_shp) in enumerate(pieces):
        user_log, *rest = user_log_call(
            at, rows, shp_at, users, depth, factor, i == 0, (*piece_sums, piece_shp, rte), user_log)
        rte = rest[0] if rest else rte
        if i == max(len(pieces) - 3, 0):
            item_log, rte = item_log_call(item, rte, items, depth)
    return user_log, item_log


def solution(mesh):
    placed = (P(None, "users", "items"), P(), P("users", None), P(("users", "items"), None))
    return jax.shard_map(
        per_device,
        mesh=mesh,
        in_specs=placed,
        out_specs=(P("users", None), P(("users", "items"), None)),
        check_vma=False,
    )
```

```python
import functools

import jax
import jax.numpy as jnp
from jax import lax
from jax.experimental import pallas as pl
from jax.experimental.pallas import tpu as pltpu
from jax.sharding import PartitionSpec as P

STRATA = 3
TILE = 64
START_TILE = 128
REDO_TILE = 32
F32 = jnp.float32
BF16 = jnp.bfloat16


def chunk_rows(rows):
    first = max(rows // 2 // START_TILE, 1) * START_TILE
    return [first, rows - first] if first < rows else [rows]


def last_cuts(rows):
    count = -(-rows // (4 * TILE))
    tiles_of = [rows // TILE // count + (i < rows // TILE % count) for i in range(count)]
    return [n * TILE for n in tiles_of] if rows % TILE == 0 else [rows]


def psi_parts(x):
    small = x < 8.0
    w = jnp.where(small, x + 3.5, x - 0.5)
    q = x * (x + 3.0)
    q2 = q + 2.0
    bounded = jnp.minimum(w, 1e9)
    square = bounded * bounded
    steps = jnp.where(small, q * q2, 1.0)
    r = 1.0 / (square * steps)
    s = r * steps
    shift = (2.0 * x + 3.0) * (q + q2) * (r * square)
    g = s * (1.0 / 24.0 - s * (7.0 / 960.0 - s * (31.0 / 8064.0 - s * (127.0 / 30720.0))))
    return w, g - jnp.where(small, shift, 0.0)


def psi_any(x):
    mirrored = x < 0.5
    w, g = psi_parts(jnp.where(mirrored, 1.0 - x, x))
    value = jnp.log(w) + g
    t = x - jnp.floor(x + 0.5)
    u = 3.14159265358979 * t
    v = u * u
    sin = 1.0 / 6227020800.0
    for c in (-1.0 / 39916800.0, 1.0 / 362880.0, -1.0 / 5040.0, 1.0 / 120.0, -1.0 / 6.0, 1.0):
        sin = sin * v + c
    cos = -1.0 / 87178291200.0
    for c in (1.0 / 479001600.0, -1.0 / 3628800.0, 1.0 / 40320.0, -1.0 / 720.0, 1.0 / 24.0, -0.5, 1.0):
        cos = cos * v + c
    value = jnp.where(mirrored, value - 3.14159265358979 * cos / (sin * u), value)
    return jnp.where((x <= 0.0) & (x == jnp.floor(x)), jnp.nan, value)


LOWEST = 0.01
HIGHEST = 1e30


def usual(rte):
    return jnp.where(rte <= HIGHEST, rte, -1.0)


def above(low):
    return jnp.min(low) >= LOWEST


def folded(x):
    return x.reshape(x.shape[0] // 8, 8, x.shape[1])


def tiles(rows):
    step = TILE if rows % TILE == 0 else rows
    return [(at, step) for at in range(0, rows, step)]


def redo_loop(rows, step, carry=None):
    size = REDO_TILE if rows % REDO_TILE == 0 else 8
    return lax.fori_loop(
        0, rows // size, lambda i, c: step(pl.multiple_of(i * size, size), size, c), carry)


def exp_tile(x, rte, general):
    shape = x.shape
    x = folded(x)
    if general:
        value = psi_any(x)
        if rte is not None:
            value = value - jnp.log(rte)[None]
        value = jnp.exp(value)
    else:
        w, g = psi_parts(x)
        value = w if rte is None else w * (1.0 / rte)[None]
        value = value * jnp.exp(g)
    mean = x if rte is None else x / rte[None] if general else x * (1.0 / rte)[None]
    return value.reshape(shape).astype(BF16), jnp.sum(mean, axis=0), jnp.min(x, axis=0)


def log_tile(x, rte, general):
    shape = x.shape
    x = folded(x)
    if general:
        value = psi_any(x) - jnp.log(rte)[None]
    else:
        w, g = psi_parts(x)
        value = (jnp.log(w) - jnp.log(rte)[None]) + g
    return value.reshape(shape).astype(BF16), jnp.min(x, axis=0)


def row_sum(x):
    return jnp.broadcast_to(jnp.sum(x, axis=0, keepdims=True), x.shape)


VMEM_SPEC = pl.BlockSpec(memory_space=pltpu.VMEM)
SMEM_SPEC = pl.BlockSpec(memory_space=pltpu.SMEM)
HBM_SPEC = pl.BlockSpec(memory_space=pltpu.HBM)
PARAMS = pltpu.CompilerParams(vmem_limit_bytes=24 * 2**20)


def in_hbm(x):
    return pltpu.with_memory_space_constraint(x, pltpu.HBM)


def in_vmem(x):
    return pltpu.with_memory_space_constraint(x, pltpu.VMEM)


def prepare_kernel(matchings_hbm, shape_hbm, item, *refs, last):
    choices, (matchings, shape, sems) = refs[:STRATA], refs[STRATA:]
    copies = [
        pltpu.make_async_copy(shape_hbm, shape, sems.at[0]),
        pltpu.make_async_copy(matchings_hbm, matchings, sems.at[1]),
    ]
    for copy in copies:
        copy.start()
    for copy in copies:
        copy.wait()
    item[...] = shape[...].astype(F32)
    choices[0][0] = matchings[0] - 1
    for stratum in range(1, STRATA - 1):
        choices[stratum][0] = jnp.bitwise_xor(matchings[stratum - 1], matchings[stratum]) - 1
    choices[STRATA - 1][0] = jnp.bitwise_xor(matchings[STRATA - 2], last) - 1


def prepare_call(matchings, item_shape, last):
    out = pl.pallas_call(
        functools.partial(prepare_kernel, last=last),
        out_shape=[jax.ShapeDtypeStruct(item_shape.shape, F32)]
        + [pltpu.SMEM((1,), jnp.int32)] * STRATA,
        in_specs=[HBM_SPEC, HBM_SPEC],
        out_specs=[VMEM_SPEC] + [SMEM_SPEC] * STRATA,
        scratch_shapes=[pltpu.SMEM(matchings.shape, jnp.int32), pltpu.VMEM(item_shape.shape, BF16),
                        pltpu.SemaphoreType.DMA((2,))],
        compiler_params=PARAMS,
        name="prepare",
    )(in_hbm(matchings), in_hbm(item_shape))
    return out[0], [choice[0] for choice in out[1:]]


def start_kernel(shape_hbm, interactions, theta, *refs, ahead):
    counts, uexps, (shape, sems) = refs[:len(ahead)], refs[len(ahead):-2], refs[-2:]
    depth = shape.shape[1]
    load = pltpu.make_async_copy(shape_hbm, shape, sems.at[0])
    load.start()
    fetches = [
        pltpu.make_async_copy(interactions.at[s, pl.ds(at, rows), :], counts[i], sems.at[i + 1])
        for i, (s, at, rows) in enumerate(ahead)]
    for fetch in fetches:
        fetch.start()
    load.wait()
    total, low = jnp.zeros((8, depth), F32), jnp.ones((8, depth), F32)
    begin = 0
    for uexp in uexps:
        rows = uexp.shape[0]

        def step(i, carry, begin=begin, uexp=uexp):
            at = i * START_TILE
            x = shape[pl.ds(pl.multiple_of(begin + at, START_TILE), START_TILE), :].astype(F32)
            value, part, part_low = exp_tile(x, None, False)
            uexp[pl.ds(pl.multiple_of(at, START_TILE), START_TILE), :] = value
            return carry[0] + part, jnp.minimum(carry[1], part_low)

        total, low = lax.fori_loop(0, rows // START_TILE, step, (total, low))
        begin += rows
    theta[...] = total

    @pl.when(jnp.logical_not(above(low)))
    def _():
        begin = 0
        for uexp in uexps:

            def redo(at, size, _, begin=begin, uexp=uexp):
                x = shape[pl.ds(pl.multiple_of(begin + at, size), size), :].astype(F32)
                uexp[pl.ds(at, size), :] = exp_tile(x, None, True)[0]

            redo_loop(uexp.shape[0], redo)
            begin += uexp.shape[0]

    for fetch in fetches:
        fetch.wait()


def start_call(user_shape, interactions, sizes, ahead):
    rows, depth = user_shape.shape
    items = interactions.shape[2]
    theta, *arrays = pl.pallas_call(
        functools.partial(start_kernel, ahead=ahead),
        out_shape=[pltpu.VMEM((8, depth), F32)]
        + [pltpu.VMEM((fetch[2], items), BF16) for fetch in ahead]
        + [pltpu.VMEM((size, depth), BF16) for size in sizes],
        in_specs=[HBM_SPEC] * 2,
        out_specs=[VMEM_SPEC] * (1 + len(ahead) + len(sizes)),
        scratch_shapes=[pltpu.VMEM((rows, depth), BF16), pltpu.SemaphoreType.DMA((1 + len(ahead),))],
        compiler_params=PARAMS,
        cost_estimate=pl.CostEstimate(
            flops=40 * rows * depth, bytes_accessed=rows * depth * 4, transcendentals=2 * rows * depth),
        name="user_start",
    )(in_hbm(user_shape), in_hbm(interactions))
    return theta, arrays[:len(ahead)], arrays[len(ahead):]


def fetch_kernel(interactions, *refs, ahead):
    counts, sems = refs[:-1], refs[-1]
    fetches = [
        pltpu.make_async_copy(interactions.at[s, pl.ds(at, rows), :], counts[i], sems.at[i])
        for i, (s, at, rows) in enumerate(ahead)]
    for fetch in fetches:
        fetch.start()
    for fetch in fetches:
        fetch.wait()


def fetch_call(interactions, ahead):
    items = interactions.shape[2]
    return pl.pallas_call(
        functools.partial(fetch_kernel, ahead=ahead),
        out_shape=[pltpu.VMEM((rows, items), BF16) for _, _, rows in ahead],
        in_specs=[HBM_SPEC],
        out_specs=[VMEM_SPEC] * len(ahead),
        scratch_shapes=[pltpu.SemaphoreType.DMA((len(ahead),))],
        compiler_params=PARAMS,
        cost_estimate=pl.CostEstimate(
            flops=0, bytes_accessed=4 * items * sum(rows for _, _, rows in ahead), transcendentals=0),
        name="fetch_weights",
    )(in_hbm(interactions))


def dot_rows(a, b):
    return lax.dot_general(a, b, (((1,), (1,)), ((), ())), preferred_element_type=F32)


def item_sums(ratios, uexp):
    return lax.dot_general(ratios[...], uexp[...], (((0,), (0,)), ((), ())), preferred_element_type=F32)


def stratum_kernel(names, *refs, stratum, at, rows, items, factor, first, last, earlier, cuts):
    ref = dict(zip(names, refs))
    upart, counts, ratios, denominator = ref["upart0"], ref["counts"], ref["ratios"], ref["denominator"]
    uexp = ref["uexp"]
    extra = 8 if first else 0

    lows = []
    theta = None
    item = ref["item_kept"] if first or last else None

    if stratum > 0:
        if first:
            beta = row_sum(ref["acc"][0:8, :] + ref["recv"][0:8, :])
            old = 1.0 if stratum == 1 else ref["rte_old"][...]
            rte = 0.5 * old + 0.5 * (0.3 + factor * beta)
            ref["rte_new"][...] = rte
        else:
            rte = ref["rte"][...]
        lows.append(usual(rte))
        for t, step in tiles(rows):
            old = ref["user_shape"][at + t:at + t + step, :].astype(F32) if stratum == 1 else ref["shp_old"][t:t + step, :]
            stat = ref["acc"][extra + t:extra + t + step, :] + ref["recv"][extra + t:extra + t + step, :]
            shp = 0.5 * old + 0.5 * (0.3 + factor * stat)
            ref["shp_new"][t:t + step, :] = shp
            value, part, low = exp_tile(shp, rte, False)
            uexp[t:t + step, :] = value
            theta = part if theta is None else theta + part
            lows.append(low)
        if not first:
            theta = theta + ref["theta"][...]
        total_mean = ref["theta_new"]
        total_mean[...] = theta
    elif last:
        total_mean = ref["theta"]

    meets = first and stratum == 0
    item_exp_ref = ref["item_exp_new" if meets else "item_exp"]
    if first or last:
        item_rte = None if stratum == 0 else item[items:items + 8, :]
    if first and not meets:
        upart[0:8, :] = ref["item_sums"][...]
    if meets:
        item[...] = ref["item"][...]
        uexp[...] = ref["uexp_in"][...]
        item_exp, sums, low = exp_tile(item[0:items, :], item_rte, False)
        ref["item_exp_new"][...] = item_exp
        upart[0:8, :] = sums
        lows.append(low)
    else:
        item_exp = item_exp_ref[...]

    denominator[...] = dot_rows(uexp[...], item_exp)
    for t, step in tiles(rows):
        ratios[t:t + step, :] = (
            counts[t:t + step, :].astype(F32) / denominator[t:t + step, :]).astype(BF16)
    user_sums = uexp[...].astype(F32) * jnp.dot(ratios[...], item_exp, preferred_element_type=F32)
    parts = []
    for i, length in enumerate(cuts):
        begin, skip = sum(cuts[:i]), 0 if i else extra
        parts.append((ref[f"upart{i}"], begin, skip, length))
        parts[i][0][skip:skip + length, :] = user_sums[begin:begin + length, :]
    pairs = [(ref[f"ratios{i}"], ref[f"uexp{i}"]) for i in range(earlier)] + [(ratios, uexp)]

    def update_items(istat):
        old = 1.0 if item_rte is None else item_rte
        kept = item_exp_ref[...].astype(F32)
        ref["item_new"][0:items, :] = 0.5 * item[0:items, :] + 0.5 * (0.3 + factor * (kept * istat))
        ref["item_new"][items:items + 8, :] = 0.5 * old + 0.5 * (0.3 + factor * row_sum(total_mean[...]))

    if last:
        istat = None
        for pair in pairs:
            part = item_sums(*pair)
            istat = part if istat is None else istat + part
        update_items(istat)

    if lows:

        @pl.when(jnp.logical_not(above(functools.reduce(jnp.minimum, lows))))
        def _():
            if stratum > 0:

                def redo_users(at, size, total):
                    place = pl.ds(at, size)
                    uexp[place, :], part, _ = exp_tile(ref["shp_new"][place, :], rte, True)
                    return total + part

                start = jnp.zeros_like(rte) if first else ref["theta"][...]
                total_mean[...] = redo_loop(rows, redo_users, start)
            if meets:

                def redo_items(at, size, total):
                    place = pl.ds(at, size)
                    ref["item_exp_new"][place, :], part, _ = exp_tile(item[place, :], item_rte, True)
                    return total + part

                upart[0:8, :] = redo_loop(items, redo_items, jnp.zeros((8, upart.shape[1]), F32))
            kept = item_exp_ref
            for target, begin, skip, length in parts:

                def redo_sums(at, size, _, target=target, begin=begin, skip=skip):
                    place = pl.ds(pl.multiple_of(begin + at, size), size)
                    u = uexp[place, :]
                    ratio = (counts[place, :].astype(F32) / dot_rows(u, kept[...])).astype(BF16)
                    ratios[place, :] = ratio
                    target[pl.ds(pl.multiple_of(skip + at, 8), size), :] = u.astype(F32) * jnp.dot(
                        ratio, kept[...], preferred_element_type=F32)

                redo_loop(length, redo_sums)
            if last:
                total = ref["item_new"].at[pl.ds(0, items), :]
                total[...] = jnp.zeros((items, ref["item_new"].shape[1]), F32)
                for pair in pairs:

                    def redo_stat(at, size, _, pair=pair):
                        place = pl.ds(at, size)
                        total[...] += item_sums(pair[0].at[place, :], pair[1].at[place, :])

                    redo_loop(rows if pair[0] is ratios else pair[0].shape[0], redo_stat)
                update_items(total[...])


def stratum_call(stratum, at, rows, items, depth, factor, first, last, earlier, cuts, operands):
    extra = 8 if first else 0
    outs = {f"upart{i}": ((size + (0 if i else extra), depth), F32) for i, size in enumerate(cuts)}
    if stratum > 0:
        outs["shp_new"] = ((rows, depth), F32)
    if first and stratum > 0:
        outs["rte_new"] = ((8, depth), F32)
    if first and stratum == 0:
        outs["item_exp_new"] = ((items, depth), BF16)
    if first and stratum == 0:
        outs["item_kept"] = (operands["item"].shape, F32)
    if last:
        outs["item_new"] = ((items + 8, depth), F32)
    else:
        outs["ratios"] = ((rows, items), BF16)
        outs["uexp"] = ((rows, depth), BF16)
        if stratum > 0:
            outs["theta_new"] = ((8, depth), F32)
    scratch = {
        "denominator": pltpu.VMEM((rows, items), F32),
    }
    if last:
        scratch["ratios"] = pltpu.VMEM((rows, items), BF16)
        if stratum > 0:
            scratch["uexp"] = pltpu.VMEM((rows, depth), BF16)
            scratch["theta_new"] = pltpu.VMEM((8, depth), F32)
    operands = {
        name: in_vmem(x) if name in ("user_shape", "item") else x
        for name, x in operands.items()}
    names = list(operands) + list(outs) + list(scratch)
    kernel = functools.partial(
        stratum_kernel, names, stratum=stratum, at=at, rows=rows, items=items,
        factor=factor, first=first, last=last, earlier=earlier, cuts=cuts)
    results = pl.pallas_call(
        kernel,
        out_shape=[jax.ShapeDtypeStruct(*spec) for spec in outs.values()],
        in_specs=[VMEM_SPEC] * len(operands),
        out_specs=[VMEM_SPEC] * len(outs),
        scratch_shapes=list(scratch.values()),
        compiler_params=PARAMS,
        cost_estimate=pl.CostEstimate(
            flops=600 * rows * items * depth, bytes_accessed=rows * 200000, transcendentals=rows * depth),
        name=f"stratum{stratum}_at{at}",
    )(*operands.values())
    return dict(zip(outs, results))


def meet_kernel(item, kept, item_exp, sums, *, items):
    rte = item[items:items + 8, :]
    kept[items:items + 8, :] = rte

    def step(i, carry):
        place = pl.ds(pl.multiple_of(i * TILE, TILE), TILE)
        x = item[place, :]
        kept[place, :] = x
        item_exp[place, :], part, low = exp_tile(x, rte, False)
        return carry[0] + part, jnp.minimum(carry[1], low)

    sums[...], low = lax.fori_loop(0, items // TILE, step, (jnp.zeros_like(rte), usual(rte)))

    @pl.when(jnp.logical_not(above(low)))
    def _():
        def redo(at, size, total):
            place = pl.ds(at, size)
            item_exp[place, :], part, _ = exp_tile(item[place, :], rte, True)
            return total + part

        sums[...] = redo_loop(items, redo, jnp.zeros_like(rte))


def meet_call(item):
    rows, depth = item.shape
    items = rows - 8
    kept, item_exp, sums = pl.pallas_call(
        functools.partial(meet_kernel, items=items),
        out_shape=[pltpu.VMEM(item.shape, F32), pltpu.VMEM((items, depth), BF16), pltpu.VMEM((8, depth), F32)],
        in_specs=[VMEM_SPEC],
        out_specs=[VMEM_SPEC] * 3,
        compiler_params=PARAMS,
        cost_estimate=pl.CostEstimate(
            flops=40 * items * depth, bytes_accessed=items * depth * 10, transcendentals=2 * items * depth),
        name="meet_items",
    )(in_vmem(item))
    return {"item_kept": kept, "item_exp": item_exp, "item_sums": sums}


def user_log_kernel(*refs, at, rows, shp_at, factor, first, filled):
    acc, recv, shp_old, rte_in = refs[:4]
    rest = refs[5:] if filled else refs[4:]
    out, *rte_out, block, sem = rest
    rte = rte_in[...]
    if first:
        rte = 0.5 * rte + 0.5 * (0.3 + factor * row_sum(acc[0:8, :] + recv[0:8, :]))
    for ref in rte_out:
        ref[...] = rte
    extra = 8 if first else 0

    def shape(t, step):
        stat = acc[pl.ds(extra + t, step), :] + recv[pl.ds(extra + t, step), :]
        return 0.5 * shp_old[pl.ds(shp_at + t, step), :] + 0.5 * (0.3 + factor * stat)

    low = rte
    for t, step in tiles(rows):
        block[t:t + step, :], part_low = log_tile(shape(t, step), rte, False)
        low = jnp.minimum(low, part_low)

    @pl.when(jnp.logical_not(above(low)))
    def _():
        def redo(t, step, _):
            block[pl.ds(t, step), :] = log_tile(shape(pl.multiple_of(t, 8), step), rte, True)[0]

        redo_loop(rows, redo)

    copy = pltpu.make_async_copy(block, out.at[pl.ds(at, rows), :], sem)
    copy.start()
    copy.wait()


def user_log_call(at, rows, shp_at, total, depth, factor, first, operands, filled):
    out_shape = [jax.ShapeDtypeStruct((total, depth), BF16)]
    out_specs = [HBM_SPEC]
    if at + rows < total:
        out_shape.append(jax.ShapeDtypeStruct((8, depth), F32))
        out_specs.append(VMEM_SPEC)
    operands = list(operands)
    in_specs = [VMEM_SPEC] * 4
    if filled is not None:
        operands.append(filled)
        in_specs.append(HBM_SPEC)
    return pl.pallas_call(
        functools.partial(user_log_kernel, at=at, rows=rows, shp_at=shp_at, factor=factor, first=first,
                          filled=filled is not None),
        out_shape=out_shape,
        in_specs=in_specs,
        out_specs=out_specs,
        input_output_aliases={} if filled is None else {4: 0},
        scratch_shapes=[pltpu.VMEM((rows, depth), BF16), pltpu.SemaphoreType.DMA],
        compiler_params=PARAMS,
        cost_estimate=pl.CostEstimate(
            flops=40 * rows * depth, bytes_accessed=rows * depth * 14, transcendentals=rows * depth),
        name=f"user_log_at{at}",
    )(*operands)


def item_log_kernel(item, through, out, passed, *, items):
    passed[...] = through[...]
    rte = item[items:items + 8, :]

    out[...], low = log_tile(item[0:items, :], rte, False)

    @pl.when(jnp.logical_not(above(jnp.minimum(low, rte))))
    def _():
        def redo(t, step, _):
            place = pl.ds(t, step)
            out[place, :] = log_tile(item[place, :], rte, True)[0]

        redo_loop(items, redo)


def item_log_call(item, through, items, depth):
    return pl.pallas_call(
        functools.partial(item_log_kernel, items=items),
        out_shape=[jax.ShapeDtypeStruct((items, depth), BF16), jax.ShapeDtypeStruct(through.shape, F32)],
        in_specs=[VMEM_SPEC, VMEM_SPEC],
        out_specs=[VMEM_SPEC, VMEM_SPEC],
        compiler_params=PARAMS,
        cost_estimate=pl.CostEstimate(
            flops=40 * items * depth, bytes_accessed=items * depth * 6, transcendentals=items * depth),
        name="item_log",
    )(item, through)


def swapped(value, axis, mask):
    return lax.ppermute(value, axis, [(a, a ^ mask) for a in range(lax.axis_size(axis))])


def moved(choice, value, then=None, operands=()):
    def branch(mask, value, *operands):
        arrived = swapped(value, "users", mask)
        return arrived if then is None else then(arrived, *operands)

    choices = [functools.partial(branch, mask) for mask in range(1, lax.axis_size("users"))]
    return lax.switch(choice, choices, value, *operands)


def exchanged(value):
    size = lax.axis_size("items")
    if size == 1:
        return value, jnp.zeros_like(value)
    mask = 1
    while mask * 2 < size:
        value = value + swapped(value, "items", mask)
        mask *= 2
    return value, swapped(value, "items", mask)


def per_device(interactions, matchings, user_shape, item_shape):
    group = lax.axis_size("users")
    factor = float(group)
    users, depth = user_shape.shape
    items = item_shape.shape[0]
    sizes = chunk_rows(users)
    starts = [sum(sizes[:i]) for i in range(len(sizes))]
    count = len(sizes)

    item, choices = prepare_call(matchings, item_shape, group - 1)
    order = [(s, at, rows) for s in range(STRATA) for at, rows in zip(starts, sizes)]

    def chunks_of(stratum):
        return order[stratum * count:(stratum + 1) * count]

    def opening(arrived, user_shape, interactions):
        theta, counts, uexps = start_call(user_shape, interactions, sizes, chunks_of(0))
        operands = {"counts": counts[0], "uexp_in": uexps[0], "item": arrived}
        if count == 1:
            operands["theta"] = theta
        out = stratum_call(
            0, 0, sizes[0], items, depth, factor, True, count == 1, 0, sizes[:1], operands)
        return theta, [out["uexp"], *uexps[1:]], counts[1:], out

    theta, uexps, fetched, opened = moved(choices[0], item, opening, (user_shape, interactions))
    rte = None
    shp = [None] * count
    sums = [None] * count
    for stratum in range(STRATA):
        carried = {"theta": theta} if stratum == 0 else {"theta": theta, **item}
        earlier = {}
        for i, (at, rows) in enumerate(zip(starts, sizes)):
            first, last = i == 0, i == count - 1
            step = stratum * count + i
            cuts = last_cuts(rows) if step + 1 == len(order) else [rows]
            operands = {}
            if step:
                operands["counts"], fetched = fetched[0], fetched[1:]
            if stratum == 0:
                operands["uexp"] = uexps[i]
            else:
                operands["acc"], operands["recv"] = sums[i]
                if stratum == 1:
                    operands["user_shape"] = user_shape
                else:
                    operands["shp_old"] = shp[i]
                if not first:
                    operands["rte"] = rte
                elif stratum > 1:
                    operands["rte_old"] = rte
            if step:
                operands["item_exp"] = carried["item_exp"]
            if step and (first or last):
                operands["item_kept"] = carried["item_kept"]
            if step and first:
                operands["item_sums"] = carried["item_sums"]
            if last:
                operands.update(earlier)
            if (stratum > 0 and not first) or (stratum == 0 and last):
                operands["theta"] = carried["theta"]
            if step == 0:
                out = opened
            else:
                out = stratum_call(
                    stratum, at, rows, items, depth, factor, first, last, i, cuts, operands)
            shp[i] = out.get("shp_new")
            sums[i] = exchanged(out["upart0"])
            if first:
                rte = out.get("rte_new")
                if stratum == 0:
                    carried["item_exp"], carried["item_kept"] = out["item_exp_new"], out["item_kept"]
            if last:
                item = out["item_new"]
            else:
                earlier[f"ratios{i}"], earlier[f"uexp{i}"] = out["ratios"], out.get("uexp", operands.get("uexp"))
                if stratum > 0:
                    carried["theta"] = out["theta_new"]
        if stratum + 1 < STRATA:
            def with_weights(arrived, interactions, chunks=chunks_of(stratum + 1)):
                weights = fetch_call(interactions, chunks)
                return meet_call(arrived), weights

            item, fetched = moved(choices[stratum + 1], item, with_weights, (interactions,))
        else:
            item = swapped(item, "users", group - 1)
    user_log = None
    pieces = [(at, rows, 0, sums[i], shp[i]) for i, (at, rows) in enumerate(zip(starts, sizes))]
    pieces[-1:] = [
        (starts[-1] + sum(cuts[:i]), size, sum(cuts[:i]), exchanged(out[f"upart{i}"]) if i else sums[-1], shp[-1])
        for i, size in enumerate(cuts)]
    for i, (at, rows, shp_at, piece_sums, piece_shp) in enumerate(pieces):
        user_log, *rest = user_log_call(
            at, rows, shp_at, users, depth, factor, i == 0, (*piece_sums, piece_shp, rte), user_log)
        rte = rest[0] if rest else rte
        if i == max(len(pieces) - 3, 0):
            item_log, rte = item_log_call(item, rte, items, depth)
    return user_log, item_log


def solution(mesh):
    placed = (P(None, "users", "items"), P(), P("users", None), P(("users", "items"), None))
    return jax.shard_map(
        per_device,
        mesh=mesh,
        in_specs=placed,
        out_specs=(P("users", None), P(("users", "items"), None)),
        check_vma=False,
    )
```

```python
import functools

import jax
import jax.numpy as jnp
from jax import lax
from jax.experimental import pallas as pl
from jax.experimental.pallas import tpu as pltpu
from jax.sharding import PartitionSpec as P

STRATA = 3
TILE = 64
START_TILE = 128
REDO_TILE = 32
F32 = jnp.float32
BF16 = jnp.bfloat16


def chunk_rows(rows):
    first = max(rows // 2 // START_TILE, 1) * START_TILE
    return [first, rows - first] if first < rows else [rows]


def last_cuts(rows):
    largest = 4 * TILE
    return [largest] * (rows // largest) + [rows % largest] * (rows % largest > 0)


def psi_parts(x):
    small = x < 8.0
    w = jnp.where(small, x + 3.5, x - 0.5)
    q = x * (x + 3.0)
    q2 = q + 2.0
    bounded = jnp.minimum(w, 1e9)
    square = bounded * bounded
    steps = jnp.where(small, q * q2, 1.0)
    r = 1.0 / (square * steps)
    s = r * steps
    shift = (2.0 * x + 3.0) * (q + q2) * (r * square)
    g = s * (1.0 / 24.0 - s * (7.0 / 960.0 - s * (31.0 / 8064.0 - s * (127.0 / 30720.0))))
    return w, g - jnp.where(small, shift, 0.0)


def psi_any(x):
    mirrored = x < 0.5
    w, g = psi_parts(jnp.where(mirrored, 1.0 - x, x))
    value = jnp.log(w) + g
    t = x - jnp.floor(x + 0.5)
    u = 3.14159265358979 * t
    v = u * u
    sin = 1.0 / 6227020800.0
    for c in (-1.0 / 39916800.0, 1.0 / 362880.0, -1.0 / 5040.0, 1.0 / 120.0, -1.0 / 6.0, 1.0):
        sin = sin * v + c
    cos = -1.0 / 87178291200.0
    for c in (1.0 / 479001600.0, -1.0 / 3628800.0, 1.0 / 40320.0, -1.0 / 720.0, 1.0 / 24.0, -0.5, 1.0):
        cos = cos * v + c
    value = jnp.where(mirrored, value - 3.14159265358979 * cos / (sin * u), value)
    return jnp.where((x <= 0.0) & (x == jnp.floor(x)), jnp.nan, value)


LOWEST = 0.01
HIGHEST = 1e30


def usual(rte):
    return jnp.where(rte <= HIGHEST, rte, -1.0)


def above(low):
    return jnp.min(low) >= LOWEST


def folded(x):
    return x.reshape(x.shape[0] // 8, 8, x.shape[1])


def tiles(rows):
    step = TILE if rows % TILE == 0 else rows
    return [(at, step) for at in range(0, rows, step)]


def redo_loop(rows, step, carry=None):
    size = REDO_TILE if rows % REDO_TILE == 0 else 8
    return lax.fori_loop(
        0, rows // size, lambda i, c: step(pl.multiple_of(i * size, size), size, c), carry)


def exp_tile(x, rte, general):
    shape = x.shape
    x = folded(x)
    if general:
        value = psi_any(x)
        if rte is not None:
            value = value - jnp.log(rte)[None]
        value = jnp.exp(value)
    else:
        w, g = psi_parts(x)
        value = w if rte is None else w * (1.0 / rte)[None]
        value = value * jnp.exp(g)
    mean = x if rte is None else x / rte[None] if general else x * (1.0 / rte)[None]
    return value.reshape(shape).astype(BF16), jnp.sum(mean, axis=0), jnp.min(x, axis=0)


def log_tile(x, rte, general):
    shape = x.shape
    x = folded(x)
    if general:
        value = psi_any(x) - jnp.log(rte)[None]
    else:
        w, g = psi_parts(x)
        value = (jnp.log(w) - jnp.log(rte)[None]) + g
    return value.reshape(shape).astype(BF16), jnp.min(x, axis=0)


def row_sum(x):
    return jnp.broadcast_to(jnp.sum(x, axis=0, keepdims=True), x.shape)


VMEM_SPEC = pl.BlockSpec(memory_space=pltpu.VMEM)
SMEM_SPEC = pl.BlockSpec(memory_space=pltpu.SMEM)
HBM_SPEC = pl.BlockSpec(memory_space=pltpu.HBM)
PARAMS = pltpu.CompilerParams(vmem_limit_bytes=24 * 2**20)


def in_hbm(x):
    return pltpu.with_memory_space_constraint(x, pltpu.HBM)


def in_vmem(x):
    return pltpu.with_memory_space_constraint(x, pltpu.VMEM)


def prepare_kernel(matchings_hbm, shape_hbm, item, *refs, last):
    choices, (matchings, shape, sems) = refs[:STRATA], refs[STRATA:]
    copies = [
        pltpu.make_async_copy(shape_hbm, shape, sems.at[0]),
        pltpu.make_async_copy(matchings_hbm, matchings, sems.at[1]),
    ]
    for copy in copies:
        copy.start()
    for copy in copies:
        copy.wait()
    item[...] = shape[...].astype(F32)
    choices[0][0] = matchings[0] - 1
    for stratum in range(1, STRATA - 1):
        choices[stratum][0] = jnp.bitwise_xor(matchings[stratum - 1], matchings[stratum]) - 1
    choices[STRATA - 1][0] = jnp.bitwise_xor(matchings[STRATA - 2], last) - 1


def prepare_call(matchings, item_shape, last):
    out = pl.pallas_call(
        functools.partial(prepare_kernel, last=last),
        out_shape=[jax.ShapeDtypeStruct(item_shape.shape, F32)]
        + [pltpu.SMEM((1,), jnp.int32)] * STRATA,
        in_specs=[HBM_SPEC, HBM_SPEC],
        out_specs=[VMEM_SPEC] + [SMEM_SPEC] * STRATA,
        scratch_shapes=[pltpu.SMEM(matchings.shape, jnp.int32), pltpu.VMEM(item_shape.shape, BF16),
                        pltpu.SemaphoreType.DMA((2,))],
        compiler_params=PARAMS,
        name="prepare",
    )(in_hbm(matchings), in_hbm(item_shape))
    return out[0], [choice[0] for choice in out[1:]]


def start_kernel(shape_hbm, interactions, theta, *refs, ahead):
    counts, uexps, (shape, sems) = refs[:len(ahead)], refs[len(ahead):-2], refs[-2:]
    depth = shape.shape[1]
    load = pltpu.make_async_copy(shape_hbm, shape, sems.at[0])
    load.start()
    fetches = [
        pltpu.make_async_copy(interactions.at[s, pl.ds(at, rows), :], counts[i], sems.at[i + 1])
        for i, (s, at, rows) in enumerate(ahead)]
    for fetch in fetches:
        fetch.start()
    load.wait()
    total, low = jnp.zeros((8, depth), F32), jnp.ones((8, depth), F32)
    begin = 0
    for uexp in uexps:
        rows = uexp.shape[0]

        def step(i, carry, begin=begin, uexp=uexp):
            at = i * START_TILE
            x = shape[pl.ds(pl.multiple_of(begin + at, START_TILE), START_TILE), :].astype(F32)
            value, part, part_low = exp_tile(x, None, False)
            uexp[pl.ds(pl.multiple_of(at, START_TILE), START_TILE), :] = value
            return carry[0] + part, jnp.minimum(carry[1], part_low)

        total, low = lax.fori_loop(0, rows // START_TILE, step, (total, low))
        begin += rows
    theta[...] = total

    @pl.when(jnp.logical_not(above(low)))
    def _():
        begin = 0
        for uexp in uexps:

            def redo(at, size, _, begin=begin, uexp=uexp):
                x = shape[pl.ds(pl.multiple_of(begin + at, size), size), :].astype(F32)
                uexp[pl.ds(at, size), :] = exp_tile(x, None, True)[0]

            redo_loop(uexp.shape[0], redo)
            begin += uexp.shape[0]

    for fetch in fetches:
        fetch.wait()


def start_call(user_shape, interactions, sizes, ahead):
    rows, depth = user_shape.shape
    items = interactions.shape[2]
    theta, *arrays = pl.pallas_call(
        functools.partial(start_kernel, ahead=ahead),
        out_shape=[pltpu.VMEM((8, depth), F32)]
        + [pltpu.VMEM((fetch[2], items), BF16) for fetch in ahead]
        + [pltpu.VMEM((size, depth), BF16) for size in sizes],
        in_specs=[HBM_SPEC] * 2,
        out_specs=[VMEM_SPEC] * (1 + len(ahead) + len(sizes)),
        scratch_shapes=[pltpu.VMEM((rows, depth), BF16), pltpu.SemaphoreType.DMA((1 + len(ahead),))],
        compiler_params=PARAMS,
        cost_estimate=pl.CostEstimate(
            flops=40 * rows * depth, bytes_accessed=rows * depth * 4, transcendentals=2 * rows * depth),
        name="user_start",
    )(in_hbm(user_shape), in_hbm(interactions))
    return theta, arrays[:len(ahead)], arrays[len(ahead):]


def fetch_kernel(interactions, *refs, ahead):
    counts, sems = refs[:-1], refs[-1]
    fetches = [
        pltpu.make_async_copy(interactions.at[s, pl.ds(at, rows), :], counts[i], sems.at[i])
        for i, (s, at, rows) in enumerate(ahead)]
    for fetch in fetches:
        fetch.start()
    for fetch in fetches:
        fetch.wait()


def fetch_call(interactions, ahead):
    items = interactions.shape[2]
    return pl.pallas_call(
        functools.partial(fetch_kernel, ahead=ahead),
        out_shape=[pltpu.VMEM((rows, items), BF16) for _, _, rows in ahead],
        in_specs=[HBM_SPEC],
        out_specs=[VMEM_SPEC] * len(ahead),
        scratch_shapes=[pltpu.SemaphoreType.DMA((len(ahead),))],
        compiler_params=PARAMS,
        cost_estimate=pl.CostEstimate(
            flops=0, bytes_accessed=4 * items * sum(rows for _, _, rows in ahead), transcendentals=0),
        name="fetch_weights",
    )(in_hbm(interactions))


def dot_rows(a, b):
    return lax.dot_general(a, b, (((1,), (1,)), ((), ())), preferred_element_type=F32)


def item_sums(ratios, uexp):
    return lax.dot_general(ratios[...], uexp[...], (((0,), (0,)), ((), ())), preferred_element_type=F32)


def stratum_kernel(names, *refs, stratum, at, rows, items, factor, first, last, earlier, cuts):
    ref = dict(zip(names, refs))
    upart, counts, ratios, denominator = ref["upart0"], ref["counts"], ref["ratios"], ref["denominator"]
    uexp = ref["uexp"]
    extra = 8 if first else 0

    lows = []
    theta = None
    item = ref["item_kept"] if first or last else None

    if stratum > 0:
        if first:
            beta = row_sum(ref["acc"][0:8, :] + ref["recv"][0:8, :])
            old = 1.0 if stratum == 1 else ref["rte_old"][...]
            rte = 0.5 * old + 0.5 * (0.3 + factor * beta)
            ref["rte_new"][...] = rte
        else:
            rte = ref["rte"][...]
        lows.append(usual(rte))
        for t, step in tiles(rows):
            old = ref["user_shape"][at + t:at + t + step, :].astype(F32) if stratum == 1 else ref["shp_old"][t:t + step, :]
            stat = ref["acc"][extra + t:extra + t + step, :] + ref["recv"][extra + t:extra + t + step, :]
            shp = 0.5 * old + 0.5 * (0.3 + factor * stat)
            ref["shp_new"][t:t + step, :] = shp
            value, part, low = exp_tile(shp, rte, False)
            uexp[t:t + step, :] = value
            theta = part if theta is None else theta + part
            lows.append(low)
        if not first:
            theta = theta + ref["theta"][...]
        total_mean = ref["theta_new"]
        total_mean[...] = theta
    elif last:
        total_mean = ref["theta"]

    meets = first and stratum == 0
    item_exp_ref = ref["item_exp_new" if meets else "item_exp"]
    if first or last:
        item_rte = None if stratum == 0 else item[items:items + 8, :]
    if first and not meets:
        upart[0:8, :] = ref["item_sums"][...]
    if meets:
        item[...] = ref["item"][...]
        uexp[...] = ref["uexp_in"][...]
        item_exp, sums, low = exp_tile(item[0:items, :], item_rte, False)
        ref["item_exp_new"][...] = item_exp
        upart[0:8, :] = sums
        lows.append(low)
    else:
        item_exp = item_exp_ref[...]

    denominator[...] = dot_rows(uexp[...], item_exp)
    for t, step in tiles(rows):
        ratios[t:t + step, :] = (
            counts[t:t + step, :].astype(F32) / denominator[t:t + step, :]).astype(BF16)
    user_sums = uexp[...].astype(F32) * jnp.dot(ratios[...], item_exp, preferred_element_type=F32)
    parts = []
    for i, length in enumerate(cuts):
        begin, skip = sum(cuts[:i]), 0 if i else extra
        parts.append((ref[f"upart{i}"], begin, skip, length))
        parts[i][0][skip:skip + length, :] = user_sums[begin:begin + length, :]
    pairs = [(ref[f"ratios{i}"], ref[f"uexp{i}"]) for i in range(earlier)] + [(ratios, uexp)]

    def update_items(istat):
        old = 1.0 if item_rte is None else item_rte
        kept = item_exp_ref[...].astype(F32)
        ref["item_new"][0:items, :] = 0.5 * item[0:items, :] + 0.5 * (0.3 + factor * (kept * istat))
        ref["item_new"][items:items + 8, :] = 0.5 * old + 0.5 * (0.3 + factor * row_sum(total_mean[...]))

    if last:
        istat = None
        for pair in pairs:
            part = item_sums(*pair)
            istat = part if istat is None else istat + part
        update_items(istat)

    if lows:

        @pl.when(jnp.logical_not(above(functools.reduce(jnp.minimum, lows))))
        def _():
            if stratum > 0:

                def redo_users(at, size, total):
                    place = pl.ds(at, size)
                    uexp[place, :], part, _ = exp_tile(ref["shp_new"][place, :], rte, True)
                    return total + part

                start = jnp.zeros_like(rte) if first else ref["theta"][...]
                total_mean[...] = redo_loop(rows, redo_users, start)
            if meets:

                def redo_items(at, size, total):
                    place = pl.ds(at, size)
                    ref["item_exp_new"][place, :], part, _ = exp_tile(item[place, :], item_rte, True)
                    return total + part

                upart[0:8, :] = redo_loop(items, redo_items, jnp.zeros((8, upart.shape[1]), F32))
            kept = item_exp_ref
            for target, begin, skip, length in parts:

                def redo_sums(at, size, _, target=target, begin=begin, skip=skip):
                    place = pl.ds(pl.multiple_of(begin + at, size), size)
                    u = uexp[place, :]
                    ratio = (counts[place, :].astype(F32) / dot_rows(u, kept[...])).astype(BF16)
                    ratios[place, :] = ratio
                    target[pl.ds(pl.multiple_of(skip + at, 8), size), :] = u.astype(F32) * jnp.dot(
                        ratio, kept[...], preferred_element_type=F32)

                redo_loop(length, redo_sums)
            if last:
                total = ref["item_new"].at[pl.ds(0, items), :]
                total[...] = jnp.zeros((items, ref["item_new"].shape[1]), F32)
                for pair in pairs:

                    def redo_stat(at, size, _, pair=pair):
                        place = pl.ds(at, size)
                        total[...] += item_sums(pair[0].at[place, :], pair[1].at[place, :])

                    redo_loop(rows if pair[0] is ratios else pair[0].shape[0], redo_stat)
                update_items(total[...])


def stratum_call(stratum, at, rows, items, depth, factor, first, last, earlier, cuts, operands):
    extra = 8 if first else 0
    outs = {f"upart{i}": ((size + (0 if i else extra), depth), F32) for i, size in enumerate(cuts)}
    if stratum > 0:
        outs["shp_new"] = ((rows, depth), F32)
    if first and stratum > 0:
        outs["rte_new"] = ((8, depth), F32)
    if first and stratum == 0:
        outs["item_exp_new"] = ((items, depth), BF16)
    if first and stratum == 0:
        outs["item_kept"] = (operands["item"].shape, F32)
    if last:
        outs["item_new"] = ((items + 8, depth), F32)
    else:
        outs["ratios"] = ((rows, items), BF16)
        outs["uexp"] = ((rows, depth), BF16)
        if stratum > 0:
            outs["theta_new"] = ((8, depth), F32)
    scratch = {
        "denominator": pltpu.VMEM((rows, items), F32),
    }
    if last:
        scratch["ratios"] = pltpu.VMEM((rows, items), BF16)
        if stratum > 0:
            scratch["uexp"] = pltpu.VMEM((rows, depth), BF16)
            scratch["theta_new"] = pltpu.VMEM((8, depth), F32)
    operands = {
        name: in_vmem(x) if name in ("user_shape", "item") else x
        for name, x in operands.items()}
    names = list(operands) + list(outs) + list(scratch)
    kernel = functools.partial(
        stratum_kernel, names, stratum=stratum, at=at, rows=rows, items=items,
        factor=factor, first=first, last=last, earlier=earlier, cuts=cuts)
    results = pl.pallas_call(
        kernel,
        out_shape=[jax.ShapeDtypeStruct(*spec) for spec in outs.values()],
        in_specs=[VMEM_SPEC] * len(operands),
        out_specs=[VMEM_SPEC] * len(outs),
        scratch_shapes=list(scratch.values()),
        compiler_params=PARAMS,
        cost_estimate=pl.CostEstimate(
            flops=600 * rows * items * depth, bytes_accessed=rows * 200000, transcendentals=rows * depth),
        name=f"stratum{stratum}_at{at}",
    )(*operands.values())
    return dict(zip(outs, results))


def meet_kernel(item, kept, item_exp, sums, *, items):
    rte = item[items:items + 8, :]
    kept[items:items + 8, :] = rte

    def step(i, carry):
        place = pl.ds(pl.multiple_of(i * TILE, TILE), TILE)
        x = item[place, :]
        kept[place, :] = x
        item_exp[place, :], part, low = exp_tile(x, rte, False)
        return carry[0] + part, jnp.minimum(carry[1], low)

    sums[...], low = lax.fori_loop(0, items // TILE, step, (jnp.zeros_like(rte), usual(rte)))

    @pl.when(jnp.logical_not(above(low)))
    def _():
        def redo(at, size, total):
            place = pl.ds(at, size)
            item_exp[place, :], part, _ = exp_tile(item[place, :], rte, True)
            return total + part

        sums[...] = redo_loop(items, redo, jnp.zeros_like(rte))


def meet_call(item):
    rows, depth = item.shape
    items = rows - 8
    kept, item_exp, sums = pl.pallas_call(
        functools.partial(meet_kernel, items=items),
        out_shape=[pltpu.VMEM(item.shape, F32), pltpu.VMEM((items, depth), BF16), pltpu.VMEM((8, depth), F32)],
        in_specs=[VMEM_SPEC],
        out_specs=[VMEM_SPEC] * 3,
        compiler_params=PARAMS,
        cost_estimate=pl.CostEstimate(
            flops=40 * items * depth, bytes_accessed=items * depth * 10, transcendentals=2 * items * depth),
        name="meet_items",
    )(in_vmem(item))
    return {"item_kept": kept, "item_exp": item_exp, "item_sums": sums}


def user_log_kernel(*refs, at, rows, shp_at, factor, first, filled):
    acc, recv, shp_old, rte_in = refs[:4]
    rest = refs[5:] if filled else refs[4:]
    out, *rte_out, block, sem = rest
    rte = rte_in[...]
    if first:
        rte = 0.5 * rte + 0.5 * (0.3 + factor * row_sum(acc[0:8, :] + recv[0:8, :]))
    for ref in rte_out:
        ref[...] = rte
    extra = 8 if first else 0

    def shape(t, step):
        stat = acc[pl.ds(extra + t, step), :] + recv[pl.ds(extra + t, step), :]
        return 0.5 * shp_old[pl.ds(shp_at + t, step), :] + 0.5 * (0.3 + factor * stat)

    low = rte
    for t, step in tiles(rows):
        block[t:t + step, :], part_low = log_tile(shape(t, step), rte, False)
        low = jnp.minimum(low, part_low)

    @pl.when(jnp.logical_not(above(low)))
    def _():
        def redo(t, step, _):
            block[pl.ds(t, step), :] = log_tile(shape(pl.multiple_of(t, 8), step), rte, True)[0]

        redo_loop(rows, redo)

    copy = pltpu.make_async_copy(block, out.at[pl.ds(at, rows), :], sem)
    copy.start()
    copy.wait()


def user_log_call(at, rows, shp_at, total, depth, factor, first, operands, filled):
    out_shape = [jax.ShapeDtypeStruct((total, depth), BF16)]
    out_specs = [HBM_SPEC]
    if at + rows < total:
        out_shape.append(jax.ShapeDtypeStruct((8, depth), F32))
        out_specs.append(VMEM_SPEC)
    operands = list(operands)
    in_specs = [VMEM_SPEC] * 4
    if filled is not None:
        operands.append(filled)
        in_specs.append(HBM_SPEC)
    return pl.pallas_call(
        functools.partial(user_log_kernel, at=at, rows=rows, shp_at=shp_at, factor=factor, first=first,
                          filled=filled is not None),
        out_shape=out_shape,
        in_specs=in_specs,
        out_specs=out_specs,
        input_output_aliases={} if filled is None else {4: 0},
        scratch_shapes=[pltpu.VMEM((rows, depth), BF16), pltpu.SemaphoreType.DMA],
        compiler_params=PARAMS,
        cost_estimate=pl.CostEstimate(
            flops=40 * rows * depth, bytes_accessed=rows * depth * 14, transcendentals=rows * depth),
        name=f"user_log_at{at}",
    )(*operands)


def item_log_kernel(item, through, out, passed, *, items):
    passed[...] = through[...]
    rte = item[items:items + 8, :]

    out[...], low = log_tile(item[0:items, :], rte, False)

    @pl.when(jnp.logical_not(above(jnp.minimum(low, rte))))
    def _():
        def redo(t, step, _):
            place = pl.ds(t, step)
            out[place, :] = log_tile(item[place, :], rte, True)[0]

        redo_loop(items, redo)


def item_log_call(item, through, items, depth):
    return pl.pallas_call(
        functools.partial(item_log_kernel, items=items),
        out_shape=[jax.ShapeDtypeStruct((items, depth), BF16), jax.ShapeDtypeStruct(through.shape, F32)],
        in_specs=[VMEM_SPEC, VMEM_SPEC],
        out_specs=[VMEM_SPEC, VMEM_SPEC],
        compiler_params=PARAMS,
        cost_estimate=pl.CostEstimate(
            flops=40 * items * depth, bytes_accessed=items * depth * 6, transcendentals=items * depth),
        name="item_log",
    )(item, through)


def swapped(value, axis, mask):
    return lax.ppermute(value, axis, [(a, a ^ mask) for a in range(lax.axis_size(axis))])


def moved(choice, value, then=None, operands=()):
    def branch(mask, value, *operands):
        arrived = swapped(value, "users", mask)
        return arrived if then is None else then(arrived, *operands)

    choices = [functools.partial(branch, mask) for mask in range(1, lax.axis_size("users"))]
    return lax.switch(choice, choices, value, *operands)


def exchanged(value):
    size = lax.axis_size("items")
    if size == 1:
        return value, jnp.zeros_like(value)
    mask = 1
    while mask * 2 < size:
        value = value + swapped(value, "items", mask)
        mask *= 2
    return value, swapped(value, "items", mask)


def per_device(interactions, matchings, user_shape, item_shape):
    group = lax.axis_size("users")
    factor = float(group)
    users, depth = user_shape.shape
    items = item_shape.shape[0]
    sizes = chunk_rows(users)
    starts = [sum(sizes[:i]) for i in range(len(sizes))]
    count = len(sizes)

    item, choices = prepare_call(matchings, item_shape, group - 1)
    order = [(s, at, rows) for s in range(STRATA) for at, rows in zip(starts, sizes)]

    def chunks_of(stratum):
        return order[stratum * count:(stratum + 1) * count]

    def opening(arrived, user_shape, interactions):
        theta, counts, uexps = start_call(user_shape, interactions, sizes, chunks_of(0))
        operands = {"counts": counts[0], "uexp_in": uexps[0], "item": arrived}
        if count == 1:
            operands["theta"] = theta
        out = stratum_call(
            0, 0, sizes[0], items, depth, factor, True, count == 1, 0, sizes[:1], operands)
        return theta, [out["uexp"], *uexps[1:]], counts[1:], out

    theta, uexps, fetched, opened = moved(choices[0], item, opening, (user_shape, interactions))
    rte = None
    shp = [None] * count
    sums = [None] * count
    for stratum in range(STRATA):
        carried = {"theta": theta} if stratum == 0 else {"theta": theta, **item}
        earlier = {}
        for i, (at, rows) in enumerate(zip(starts, sizes)):
            first, last = i == 0, i == count - 1
            step = stratum * count + i
            cuts = last_cuts(rows) if step + 1 == len(order) else [rows]
            operands = {}
            if step:
                operands["counts"], fetched = fetched[0], fetched[1:]
            if stratum == 0:
                operands["uexp"] = uexps[i]
            else:
                operands["acc"], operands["recv"] = sums[i]
                if stratum == 1:
                    operands["user_shape"] = user_shape
                else:
                    operands["shp_old"] = shp[i]
                if not first:
                    operands["rte"] = rte
                elif stratum > 1:
                    operands["rte_old"] = rte
            if step:
                operands["item_exp"] = carried["item_exp"]
            if step and (first or last):
                operands["item_kept"] = carried["item_kept"]
            if step and first:
                operands["item_sums"] = carried["item_sums"]
            if last:
                operands.update(earlier)
            if (stratum > 0 and not first) or (stratum == 0 and last):
                operands["theta"] = carried["theta"]
            if step == 0:
                out = opened
            else:
                out = stratum_call(
                    stratum, at, rows, items, depth, factor, first, last, i, cuts, operands)
            shp[i] = out.get("shp_new")
            sums[i] = exchanged(out["upart0"])
            if first:
                rte = out.get("rte_new")
                if stratum == 0:
                    carried["item_exp"], carried["item_kept"] = out["item_exp_new"], out["item_kept"]
            if last:
                item = out["item_new"]
            else:
                earlier[f"ratios{i}"], earlier[f"uexp{i}"] = out["ratios"], out.get("uexp", operands.get("uexp"))
                if stratum > 0:
                    carried["theta"] = out["theta_new"]
        if stratum + 1 < STRATA:
            def with_weights(arrived, interactions, chunks=chunks_of(stratum + 1)):
                weights = fetch_call(interactions, chunks)
                return meet_call(arrived), weights

            item, fetched = moved(choices[stratum + 1], item, with_weights, (interactions,))
        else:
            item = swapped(item, "users", group - 1)
    user_log = None
    pieces = [(at, rows, 0, sums[i], shp[i]) for i, (at, rows) in enumerate(zip(starts, sizes))]
    pieces[-1:] = [
        (starts[-1] + sum(cuts[:i]), size, sum(cuts[:i]), exchanged(out[f"upart{i}"]) if i else sums[-1], shp[-1])
        for i, size in enumerate(cuts)]
    for i, (at, rows, shp_at, piece_sums, piece_shp) in enumerate(pieces):
        user_log, *rest = user_log_call(
            at, rows, shp_at, users, depth, factor, i == 0, (*piece_sums, piece_shp, rte), user_log)
        rte = rest[0] if rest else rte
        if i == max(len(pieces) - 3, 0):
            item_log, rte = item_log_call(item, rte, items, depth)
    return user_log, item_log


def solution(mesh):
    placed = (P(None, "users", "items"), P(), P("users", None), P(("users", "items"), None))
    return jax.shard_map(
        per_device,
        mesh=mesh,
        in_specs=placed,
        out_specs=(P("users", None), P(("users", "items"), None)),
        check_vma=False,
    )
```
